32 devices in a mesh: groups: 2 (over y), date: 8 (over z, x), strip: 2 (over core).
Axes of the slice: x: 2, y: 2, z: 4, core: 2. Of those that a mesh axis runs over, the one named last changes fastest.
Arguments:
- slc: bfloat16 [2, 48, 128, 1024], P(None, 'date', 'groups', 'strip'), parts along dimension 2, may hold values from -60 to 60
- pair_list: int32 [192, 2], replicated, may hold values from 0 to 47, as said below
- az_half: int32 [192], replicated, may hold values from 4 to 8
- rng_half: int32 [192], replicated, may hold values from 12 to 16
Outputs:
- coherence: float32 [2, 192, 128, 1024], P(None, 'date', 'groups', 'strip'), parts along dimension 2
The draws below stay inside these ranges and needn't reach their ends.
There are 2 independent parts, one for each index of `groups`. The reference program is written for one: setup_inputs(seed, part) draws one part's arguments, and reference() takes and returns one part's arrays. A program takes and returns all parts, laid end to end along the dimension named above; an argument that names none is the same for every part. Nothing has to cross between parts.
Inputs may be any that keep to these rules, and one draw needn't show every extreme that they name: `pair_list`: row (4) d + j has reference date d. For j < 3 its secondary is d + (j + 1) c_d with a sign c_d of +1 or -1 shared by the 3 rows of date d; row (4) d + 3 has secondary d + e_d g_d with e_d of +1 or -1 and g_d between 22 and 24.
All inputs are finite; a program needn't handle non-finite values.
Results may differ from the reference program's by a relative error of at most 0.0003.
Values may be sent and summed in bfloat16 or wider, within the bound.
No kernel may reach another device: no remote copies, remote signals or barrier semaphores. Data moves between devices by JAX's collectives and lax.ppermute only.
A program may use at most 128 MiB of HBM per device.

```python
import math
import jax
import jax.numpy as jnp
from jax import lax

AZ = 64
HALO = 16
RH_LO = 12
AH_LO = 4
AH_HI = 8
NEAR = 3
DATES = 48
COLS = 1024
PAIRS = 192
ANN_LO = 22


def draw_slc(key, part):
    key = jax.random.fold_in(key, 11)
    scene_key, noise_key, level_key = jax.random.split(key, 3)
    scene = jnp.clip(jax.random.normal(scene_key, (2, 1, AZ, COLS), jnp.float32), -4.0, 4.0)
    noise = jnp.clip(jax.random.normal(noise_key, (2, DATES, AZ, COLS), jnp.float32), -4.0, 4.0)
    level = jnp.exp(jax.random.uniform(level_key, (1, DATES, AZ, COLS), jnp.float32, 0.0, math.log(4.0)))
    return (level * (scene + 0.8 * noise)).astype(jnp.bfloat16)


def draw_pair_list(key, part):
    key = jax.random.fold_in(key, 23)
    side_key, year_key, sign_key = jax.random.split(key, 3)
    date_ids = jnp.arange(DATES, dtype=jnp.int32)
    direction = 2 * jax.random.randint(side_key, (DATES,), 0, 2, dtype=jnp.int32) - 1
    inside = (date_ids + direction * NEAR >= 0) & (date_ids + direction * NEAR < DATES)
    direction = jnp.where(inside, direction, -direction)
    offsets = jnp.arange(1, NEAR + 1, dtype=jnp.int32)
    nearby = date_ids[:, None] + direction[:, None] * offsets[None, :]
    year_gap = ANN_LO + jax.random.randint(year_key, (DATES,), 0, 3, dtype=jnp.int32)
    year_sign = 2 * jax.random.randint(sign_key, (DATES,), 0, 2, dtype=jnp.int32) - 1
    forward = date_ids + year_sign * year_gap
    yearly = jnp.where((forward >= 0) & (forward < DATES), forward, date_ids - year_sign * year_gap)
    partners = jnp.concatenate([nearby, yearly[:, None]], axis=1)
    references = jnp.broadcast_to(date_ids[:, None], partners.shape)
    return jnp.stack([references, partners], axis=-1).reshape(PAIRS, 2)


def set_ends(array, key, smallest, top_value):
    longest = array.shape.index(max(array.shape))
    spots = []
    for shift in (0, 1):
        where = [jax.random.randint(jax.random.fold_in(key, axis), (), 0, length) for axis, length in enumerate(array.shape)]
        where[longest] = (where[longest] + shift) % array.shape[longest]
        spots.append(tuple(where))
    return array.at[spots[0]].set(smallest).at[spots[1]].set(top_value)


def setup_inputs(seed: int = 0, part: int = 0) -> dict:
    streams_of = jax.random.split(jax.random.key(seed), 5)
    own_keys = jax.random.split(jax.random.fold_in(streams_of[4], part), 5)
    return {
        "slc": draw_slc(jax.random.fold_in(jax.random.fold_in(streams_of[4], part), 71), part),
        "pair_list": draw_pair_list(jax.random.fold_in(streams_of[4], 71), part),
        "az_half": set_ends(jax.random.randint(streams_of[2], (PAIRS,), AH_LO, AH_HI + 1), jax.random.fold_in(streams_of[2], 1), AH_LO, AH_HI).astype(jnp.int32),
        "rng_half": set_ends(jax.random.randint(streams_of[3], (PAIRS,), RH_LO, HALO + 1), jax.random.fold_in(streams_of[3], 1), RH_LO, HALO).astype(jnp.int32),
    }


EPSILON = 1e-06

def reference(slc, pair_list, az_half, rng_half):
    padded = jnp.pad(slc, ((0, 0), (0, 0), (0, 0), (HALO, HALO)))
    row_index = jnp.arange(AZ, dtype=jnp.int32)

    def one_pair(pair_entry):
        ref_date, sec_date, height, reach = pair_entry
        first_strip = lax.dynamic_index_in_dim(padded, ref_date, 1, keepdims=False).astype(jnp.float32)
        second_strip = lax.dynamic_index_in_dim(padded, sec_date, 1, keepdims=False).astype(jnp.float32)
        a_real, a_imag = (first_strip[0], first_strip[1])
        b_real, b_imag = (second_strip[0], second_strip[1])
        cross_terms = jnp.stack([a_real * b_real + a_imag * b_imag, a_imag * b_real - a_real * b_imag, a_real * a_real + a_imag * a_imag, b_real * b_real + b_imag * b_imag])
        ranged = jnp.zeros((4, AZ, COLS), jnp.float32)
        for offset in range(-HALO, HALO + 1):
            weight_on = (abs(offset) <= reach).astype(jnp.float32)
            ranged = ranged + weight_on * cross_terms[:, :, HALO + offset:HALO + offset + COLS]
        band_rows = (jnp.abs(row_index[:, None] - row_index[None, :]) <= height).astype(jnp.float32)
        looked = jnp.einsum('ab,qbc->qac', band_rows, ranged, precision=lax.Precision.HIGHEST)
        inverse = lax.rsqrt(looked[2] * looked[3] + EPSILON)
        return jnp.stack([looked[0] * inverse, looked[1] * inverse])
    result = lax.map(one_pair, (pair_list[:, 0], pair_list[:, 1], az_half, rng_half))
    return jnp.transpose(result, (1, 0, 2, 3))
```

```python
import functools

import jax
import jax.numpy as jnp
from jax import lax
from jax.experimental import pallas as pl
from jax.experimental.pallas import tpu as pltpu
from jax.sharding import PartitionSpec as P

HALO = 16
REACH_LO = 12
NEAR = 3
YEAR = 29
EPSILON = 1e-06
TILE = 128
VMEM_BYTES = 40 * 1024 * 1024
ANY = pl.BlockSpec(memory_space=pl.ANY)
SMEM = pl.BlockSpec(memory_space=pltpu.SMEM)


def run_copies(copies):
    for copy in copies:
        copy.start()
    for copy in copies:
        copy.wait()


def outer_kernel(plan, slc_ref, pairs_ref, early_ref, x_ref, z_ref, far_ref, sems):
    me = lax.axis_index("date")
    dates, late = plan["dates"], plan["late"]
    ends, half, per_date = plan["devices"] - 1, plan["devices"] // 2, plan["per_date"]
    first = me * dates
    last_dates = dates - NEAR
    odd = lax.rem(me, 2)
    mate = lax.rem(me + half, 2 * half)
    mate_slot = jnp.where(mate < half, late, 0)
    copies = []
    for k in range(dates - late):
        wanted = pairs_ref[1, (mate * dates + mate_slot + k) * per_date + NEAR] - first
        wanted = jnp.clip(wanted, 0, dates - 1)
        copies.append((slc_ref.at[:, wanted], early_ref.at[:, k]))
    copies.append((slc_ref.at[:, pl.ds(jnp.where(odd == 1, 0, last_dates), NEAR)], x_ref))
    copies.append((slc_ref.at[:, pl.ds(jnp.where(odd == 1, last_dates, 0), NEAR)], z_ref))
    far = jnp.where(me < half, half - 1, half)
    far_slot = jnp.where(me < half, dates - late, 0)
    for k in range(late):
        wanted = pairs_ref[1, (far * dates + far_slot + k) * per_date + NEAR] - first
        wanted = jnp.clip(wanted, 0, dates - 1)
        copies.append((slc_ref.at[:, wanted], far_ref.at[:, k]))
    run_copies([pltpu.make_async_copy(a, b, sems.at[n]) for n, (a, b) in enumerate(copies)])


def rim_kernel(count, *refs):
    sources, out_ref, sems = refs[:count], refs[count], refs[count + 1]
    cols = sources[0].shape[3]
    start = pl.multiple_of(jnp.where(lax.axis_index("strip") == 0, cols - TILE, 0), TILE)
    copies = []
    place = 0
    for n, source in enumerate(sources):
        here = out_ref.at[:, pl.ds(place, source.shape[1])]
        copies.append(
            pltpu.make_async_copy(source.at[:, :, :, pl.ds(start, TILE)], here, sems.at[n])
        )
        place += source.shape[1]
    run_copies(copies)


def rims(*sources):
    planes, _, rows, _ = sources[0].shape
    total = sum(source.shape[1] for source in sources)
    tiles = pl.pallas_call(
        functools.partial(rim_kernel, len(sources)),
        out_shape=jax.ShapeDtypeStruct((planes, total, rows, TILE), sources[0].dtype),
        in_specs=[ANY] * len(sources),
        out_specs=ANY,
        scratch_shapes=[pltpu.SemaphoreType.DMA((len(sources),))],
        name="rim_blocks",
    )(*sources)
    return lax.ppermute(tiles, "strip", [(0, 1), (1, 0)])


def late_kernel(plan, slc_ref, x_ref, z_ref, rim_ref, pairs_ref, out_ref, rim_buf, sems, rim_sems):
    me = lax.axis_index("date")
    strip = lax.axis_index("strip")
    dates, late = plan["dates"], plan["late"]
    half, per_date = plan["devices"] // 2, plan["per_date"]
    rows = plan["rows"]
    odd = lax.rem(me, 2)
    mate = lax.rem(me + half, 2 * half)
    mate_slot = jnp.where(mate < half, 0, dates - late)
    for k in range(late):
        wanted = pairs_ref[1, (mate * dates + mate_slot + k) * per_date + NEAR] - me * dates
        wanted = jnp.clip(wanted, -NEAR, dates + NEAR - 1)
        own = (wanted >= 0) & (wanted < dates)
        below = wanted < 0
        spot = jnp.where(below, wanted + NEAR, wanted - dates)
        from_x = below == (odd == 1)
        place = jnp.where(own, wanted, spot + jnp.where(from_x, dates, dates + NEAR))
        here = [out_ref.at[pl.ds((2 * k + c) * rows, rows)] for c in range(2)]

        def send(source, index):
            for c in range(2):
                pltpu.make_async_copy(source.at[c, index], here[c], sems.at[2 * k + c]).start()

        pl.when(own)(functools.partial(send, slc_ref, jnp.clip(wanted, 0, dates - 1)))
        spot = jnp.clip(spot, 0, NEAR - 1)
        pl.when(jnp.logical_not(own) & from_x)(functools.partial(send, x_ref, spot))
        pl.when(jnp.logical_not(own) & jnp.logical_not(from_x))(
            functools.partial(send, z_ref, spot)
        )
        pltpu.make_async_copy(rim_ref.at[:, place], rim_buf.at[:, k], rim_sems.at[k]).start()
    lane = lax.broadcasted_iota(jnp.int32, (rows, TILE), 1)
    packed = jnp.zeros((rows, TILE), jnp.float32)
    for k in range(late):
        pltpu.make_async_copy(rim_ref.at[:, 0], rim_buf.at[:, k], rim_sems.at[k]).wait()
        for c in range(2):
            spot = (2 * k + c) * HALO
            moved = pltpu.roll(rim_buf[c, k].astype(jnp.float32), spot + strip * HALO, 1)
            packed = jnp.where((lane >= spot) & (lane < spot + HALO), moved, packed)
    packed = packed.astype(jnp.bfloat16)
    base = 2 * late * rows
    rim_rows = plan["rim_rows"]
    for n in range(rows // rim_rows):
        out_ref[base : base + rim_rows, n * TILE : (n + 1) * TILE] = packed[
            n * rim_rows : (n + 1) * rim_rows
        ]
    for n in range(2 * late):
        pltpu.make_async_copy(
            slc_ref.at[0, 0], out_ref.at[pl.ds(n * rows, rows)], sems.at[n]
        ).wait()


def bands_kernel(cols, out_ref):
    strip = lax.axis_index("strip")
    wide = out_ref.shape[2]
    reach = pl.program_id(0) + REACH_LO

    def band(places, targets):
        return (jnp.abs(places - targets) <= reach).astype(jnp.float32).astype(jnp.bfloat16)

    shape = (wide, wide)
    row = lax.broadcasted_iota(jnp.int32, shape, 0)
    col = lax.broadcasted_iota(jnp.int32, shape, 1)
    out_ref[0, 0:wide] = band(row, col)
    shape = (TILE, wide)
    row = lax.broadcasted_iota(jnp.int32, shape, 0)
    col = lax.broadcasted_iota(jnp.int32, shape, 1)
    beyond = jnp.where(strip == 0, cols + row, row - TILE)
    middle = TILE // 2
    first = band(jnp.where(row < middle, wide + row, beyond), col)
    second = band(jnp.where(row < middle, beyond, wide - TILE + row), col + wide)
    for n, part in enumerate((first, first, second, second)):
        out_ref[0, wide + n * TILE : wide + (n + 1) * TILE] = part


def split(values):
    high = values.astype(jnp.bfloat16)
    low = (values - high.astype(jnp.float32)).astype(jnp.bfloat16)
    return high, low


def cross_terms(a_real, a_imag, b_real, b_imag):
    a_real, a_imag, b_real, b_imag = [
        part.astype(jnp.float32) for part in (a_real, a_imag, b_real, b_imag)
    ]
    return (
        a_real * b_real + a_imag * b_imag,
        a_imag * b_real - a_real * b_imag,
        a_real * a_real + a_imag * a_imag,
        b_real * b_real + b_imag * b_imag,
    )


def coherence(a_main, a_rim, b_main, b_rim, bands, height, store, scratch):
    high_ref, low_ref, side_ref, stack_ref = scratch
    rows, cols = a_main(0).shape
    wide = cols // 2
    lane = lax.broadcasted_iota(jnp.int32, (rows, TILE), 1)
    inner = lane < TILE // 2
    mains = cross_terms(a_main(0), a_main(1), b_main(0), b_main(1))
    edges = cross_terms(a_rim(0), a_rim(1), b_rim(0), b_rim(1))
    for f in range(4):
        here = slice(f * rows, (f + 1) * rows)
        high, low = split(mains[f])
        high_ref[here] = high
        low_ref[here] = low
        first = jnp.where(inner, mains[f][:, wide : wide + TILE], edges[f])
        second = jnp.where(inner, edges[f], mains[f][:, wide - TILE : wide])
        for n, part in enumerate((first, second)):
            high, low = split(part)
            side_ref[n, here, 0:TILE] = high
            side_ref[n, here, TILE : 2 * TILE] = low
    for n in range(2):
        there = slice(n * wide, (n + 1) * wide)
        inside = bands(0, wide)
        ranged = jnp.dot(high_ref[:, there], inside, preferred_element_type=jnp.float32)
        ranged += jnp.dot(low_ref[:, there], inside, preferred_element_type=jnp.float32)
        ranged += jnp.dot(
            side_ref[n],
            bands(wide + 2 * n * TILE, wide + 2 * (n + 1) * TILE),
            preferred_element_type=jnp.float32,
        )
        high, low = split(ranged)
        for f in range(4):
            stack_ref[f, 0:rows, there] = high[f * rows : (f + 1) * rows]
            stack_ref[f, rows : 2 * rows, there] = low[f * rows : (f + 1) * rows]
    row = lax.broadcasted_iota(jnp.int32, (rows, 2 * rows), 0)
    col = lax.broadcasted_iota(jnp.int32, (rows, 2 * rows), 1)
    col = jnp.where(col < rows, col, col - rows)
    band = (jnp.abs(row - col) <= height).astype(jnp.float32).astype(jnp.bfloat16)
    looked = [
        jnp.dot(band, stack_ref[f], preferred_element_type=jnp.float32) for f in range(4)
    ]
    inverse = lax.rsqrt(looked[2] * looked[3] + EPSILON)
    store(0, looked[0] * inverse)
    store(1, looked[1] * inverse)


def work_scratch(rows, cols):
    return [
        pltpu.VMEM((4 * rows, cols), jnp.bfloat16),
        pltpu.VMEM((4 * rows, cols), jnp.bfloat16),
        pltpu.VMEM((2, 4 * rows, 2 * TILE), jnp.bfloat16),
        pltpu.VMEM((4, 2 * rows, cols), jnp.bfloat16),
    ]


def near_kernel(plan, who_ref, pairs_ref, az_ref, rng_ref, slc_hbm, x_hbm, z_hbm, rim_hbm,
                bands_ref, out_ref, ext, rim, sems, *scratch):
    step = pl.program_id(0)
    dates, per_date = plan["dates"], plan["per_date"]
    me, flip = who_ref[0], who_ref[2]

    @pl.when(step == 0)
    def _():
        x_at = jnp.where(flip == 1, 0, dates + NEAR)
        z_at = jnp.where(flip == 1, dates + NEAR, 0)
        run_copies(
            [
                pltpu.make_async_copy(slc_hbm, ext.at[:, pl.ds(NEAR, dates)], sems.at[0]),
                pltpu.make_async_copy(x_hbm, ext.at[:, pl.ds(x_at, NEAR)], sems.at[1]),
                pltpu.make_async_copy(z_hbm, ext.at[:, pl.ds(z_at, NEAR)], sems.at[2]),
                pltpu.make_async_copy(
                    rim_hbm.at[:, pl.ds(0, dates)], rim.at[:, pl.ds(NEAR, dates)], sems.at[3]
                ),
                pltpu.make_async_copy(
                    rim_hbm.at[:, pl.ds(dates, NEAR)], rim.at[:, pl.ds(x_at, NEAR)], sems.at[4]
                ),
                pltpu.make_async_copy(
                    rim_hbm.at[:, pl.ds(dates + NEAR, NEAR)],
                    rim.at[:, pl.ds(z_at, NEAR)],
                    sems.at[5],
                ),
            ]
        )

    slot = step // NEAR
    pair = (me * dates + slot) * per_date + lax.rem(step, NEAR)
    other = jnp.clip(pairs_ref[1, pair] - me * dates + NEAR, 0, dates + 2 * NEAR - 1)
    own = slot + NEAR
    width = jnp.clip(rng_ref[pair] - REACH_LO, 0, HALO - REACH_LO)

    def store(c, values):
        out_ref[c, 0, 0] = values

    coherence(
        lambda c: ext[c, own],
        lambda c: rim[c, own],
        lambda c: ext[c, other],
        lambda c: rim[c, other],
        lambda a, b: bands_ref[width, a:b],
        az_ref[pair],
        store,
        scratch,
    )


def annual_kernel(plan, who_ref, pairs_ref, az_ref, rng_ref, slc_ref, own_rim_ref, early_ref,
                  far_ref, rim_ref, far_rim_ref, bands_ref, _, out_ref, *scratch):
    step = pl.program_id(0)
    dates, per_date = plan["dates"], plan["per_date"]
    me, base, lower = who_ref[0], who_ref[3], who_ref[4]
    date = me * dates + base + step
    pair = date * per_date + NEAR
    partner = pairs_ref[1, pair]
    from_far = jnp.where(lower == 1, partner < date, partner > date) & (who_ref[5] == 1)

    def store(c, values):
        out_ref[c, 0, 0] = values

    coherence(
        lambda c: slc_ref[c, 0],
        lambda c: own_rim_ref[c, 0],
        lambda c: jnp.where(from_far, far_ref[c, 0], early_ref[c, 0]),
        lambda c: jnp.where(from_far, far_rim_ref[c, 0], rim_ref[c, 0]),
        lambda a, b: bands_ref[0, a:b],
        az_ref[pair],
        store,
        scratch,
    )


def last_kernel(plan, who_ref, pairs_ref, az_ref, rng_ref, slc_ref, own_rim_ref, late_ref,
                late_rim_ref, bands_ref, _, out_ref, *scratch):
    step = pl.program_id(0)
    dates, per_date, rows = plan["dates"], plan["per_date"], plan["rows"]
    pair = (who_ref[0] * dates + who_ref[6] + step) * per_date + NEAR
    tiles = late_rim_ref.shape[1] // TILE

    def store(c, values):
        out_ref[c, 0, 0] = values

    def late_rim(c):
        packed = jnp.concatenate(
            [late_rim_ref[:, n * TILE : (n + 1) * TILE] for n in range(tiles)], axis=0
        )
        shift = 2 * TILE - (2 * step + c + who_ref[1]) * HALO
        return pltpu.roll(packed.astype(jnp.float32), lax.rem(shift, TILE), 1)

    coherence(
        lambda c: slc_ref[c, 0],
        lambda c: own_rim_ref[c, 0],
        lambda c: late_ref[c * rows : (c + 1) * rows],
        late_rim,
        lambda a, b: bands_ref[0, a:b],
        az_ref[pair],
        store,
        scratch,
    )


def arrivals_by_distance(slc, pair_list, plan):
    dates, per_date, devices = plan["dates"], plan["per_date"], plan["devices"]
    total = dates * devices
    me = lax.axis_index("date")
    annual_of = pair_list[:, 1].reshape(total, per_date)[:, per_date - 1]
    sums = [None] * dates
    for direction in (1, -1):
        by_distance = {}
        for slot in range(dates):
            for gap in range(plan["year"], plan["year"] + 3):
                distance = (slot + direction * gap) // dates
                by_distance.setdefault(distance, set()).add(slot)
        for distance in sorted(by_distance):
            slots = sorted(by_distance[distance])
            wanted_by = (me - distance) * dates + jnp.array(slots, dtype=jnp.int32)
            inside = (wanted_by >= 0) & (wanted_by < total)
            local = jnp.take(annual_of, jnp.clip(wanted_by, 0, total - 1)) - me * dates
            usable = inside & (local >= 0) & (local < dates)
            packed = jnp.take(slc, jnp.clip(local, 0, dates - 1), axis=1)
            packed = jnp.where(usable[None, :, None, None], packed, jnp.zeros_like(packed))
            route = [(i + distance, i) for i in range(devices) if 0 <= i + distance < devices]
            arrived = lax.ppermute(packed, "date", route)
            for n, slot in enumerate(slots):
                part = arrived[:, n]
                sums[slot] = part if sums[slot] is None else sums[slot] + part
    return jnp.stack(sums, axis=1)


def body(slc, pair_list, az_half, rng_half):
    planes, dates, rows, cols = slc.shape
    devices = lax.axis_size("date")
    total = dates * devices
    per_date = pair_list.shape[0] // total
    year = min(YEAR, total // 2 - 2)
    half = devices // 2
    late = half * dates - year
    plan = {
        "dates": dates,
        "devices": devices,
        "per_date": per_date,
        "year": year,
        "late": late,
        "rows": rows,
        "rim_rows": rows * TILE // cols,
    }
    me, strip = lax.axis_index("date"), lax.axis_index("strip")
    odd = lax.rem(me, 2)
    lower = (me < half).astype(jnp.int32)
    opposite = devices % 2 == 0 and 0 < late <= NEAR and 2 * late <= dates
    pairs = pair_list.T
    dtype = slc.dtype
    params = pltpu.CompilerParams(vmem_limit_bytes=VMEM_BYTES)

    def images(count):
        return jax.ShapeDtypeStruct((planes, count, rows, cols), dtype)

    if opposite:
        early, beside_x, beside_z, far = pl.pallas_call(
            functools.partial(outer_kernel, plan),
            out_shape=(images(dates - late), images(NEAR), images(NEAR), images(late)),
            in_specs=[ANY, SMEM],
            out_specs=(ANY,) * 4,
            scratch_shapes=[pltpu.SemaphoreType.DMA((dates + 2,))],
            name="outgoing_images",
        )(slc, pairs)
        early = lax.ppermute(
            early, "date", [(i, (i + half) % devices) for i in range(devices)]
        )
        beside_x = lax.ppermute(beside_x, "date", [(i, i ^ 1) for i in range(devices)])
        steps = [(i, i + 1) for i in range(1, devices - 1, 2)]
        beside_z = lax.ppermute(beside_z, "date", steps + [(b, a) for a, b in steps])
        far = lax.ppermute(far, "date", [(0, half - 1), (devices - 1, half)])
        flip = odd
        base = jnp.where(lower == 1, late, 0)
        last_base = jnp.where(lower == 1, 0, dates - late)
        any_far = 1
    else:
        early = arrivals_by_distance(slc, pair_list, plan)
        ups = [(i, i + 1) for i in range(devices - 1)]
        beside_x = lax.ppermute(slc[:, :NEAR], "date", [(b, a) for a, b in ups])
        beside_z = lax.ppermute(slc[:, dates - NEAR :], "date", ups)
        far = early[:, :1]
        flip, base, last_base, any_far = 0, 0, 0, 0
    who = jnp.stack(
        [jnp.asarray(v, jnp.int32) for v in (me, strip, flip, base, lower, any_far, last_base)]
    )
    rim = rims(slc, beside_x, beside_z)
    if opposite:
        late_rows = 2 * late * rows + plan["rim_rows"]
        payload = pl.pallas_call(
            functools.partial(late_kernel, plan),
            out_shape=jax.ShapeDtypeStruct((late_rows, cols), dtype),
            in_specs=[ANY] * 4 + [SMEM],
            out_specs=pl.BlockSpec(memory_space=pltpu.VMEM),
            scratch_shapes=[
                pltpu.VMEM((2, late, rows, TILE), dtype),
                pltpu.SemaphoreType.DMA((2 * late,)),
                pltpu.SemaphoreType.DMA((late,)),
            ],
            compiler_params=params,
            name="late_images",
        )(slc, beside_x, beside_z, rim, pairs)
        payload = lax.ppermute(
            payload, "date", [(i, (i + half) % devices) for i in range(devices)]
        )
    wide = cols // 2
    widths = HALO - REACH_LO + 1
    band_rows = wide + 4 * TILE
    bands = pl.pallas_call(
        functools.partial(bands_kernel, cols),
        grid=(widths,),
        out_shape=jax.ShapeDtypeStruct((widths, band_rows, wide), jnp.bfloat16),
        out_specs=pl.BlockSpec((1, band_rows, wide), lambda n: (n, 0, 0)),
        name="range_bands",
    )()
    out_shape = jax.ShapeDtypeStruct((planes, dates, per_date, rows, cols), jnp.float32)
    block = (planes, 1, 1, rows, cols)
    scalars = (who, pairs, az_half, rng_half)
    dims = ext = dates + 2 * NEAR

    def cost(count):
        return pl.CostEstimate(
            flops=count * 4 * rows * cols * 2000,
            bytes_accessed=count * planes * rows * cols * 4,
            transcendentals=0,
        )

    out = pl.pallas_call(
        functools.partial(near_kernel, plan),
        grid_spec=pltpu.PrefetchScalarGridSpec(
            num_scalar_prefetch=4,
            grid=(dates * NEAR,),
            in_specs=[ANY] * 4
            + [pl.BlockSpec((widths, band_rows, wide), lambda n, *_: (0, 0, 0))],
            out_specs=pl.BlockSpec(block, lambda n, *_: (0, n // NEAR, lax.rem(n, NEAR), 0, 0)),
            scratch_shapes=[
                pltpu.VMEM((planes, ext, rows, cols), dtype),
                pltpu.VMEM((planes, ext, rows, TILE), dtype),
                pltpu.SemaphoreType.DMA((6,)),
            ]
            + work_scratch(rows, cols),
        ),
        out_shape=out_shape,
        compiler_params=params,
        cost_estimate=cost(dates * NEAR),
        name="near_pairs",
    )(*scalars, slc, beside_x, beside_z, rim, bands)

    early_count = early.shape[1]
    far_count = far.shape[1]
    early_rim = rims(early, far)

    def own_slot(n, who_ref, *_):
        return (0, who_ref[3] + n, 0, 0)

    def far_slot(n, who_ref):
        skip = jnp.where(who_ref[4] == 1, early_count - far_count, 0)
        return jnp.clip(n - skip, 0, far_count - 1)

    def band_block(start):
        def of(n, who_ref, pairs_ref, az_ref, rng_ref):
            pair = (who_ref[0] * dates + who_ref[start] + n) * per_date + NEAR
            return (jnp.clip(rng_ref[pair] - REACH_LO, 0, widths - 1), 0, 0)

        return pl.BlockSpec((1, band_rows, wide), of)

    image, strip_rim = (planes, 1, rows, cols), (planes, 1, rows, TILE)
    out = pl.pallas_call(
        functools.partial(annual_kernel, plan),
        grid_spec=pltpu.PrefetchScalarGridSpec(
            num_scalar_prefetch=4,
            grid=(early_count,),
            in_specs=[
                pl.BlockSpec(image, own_slot),
                pl.BlockSpec(strip_rim, own_slot),
                pl.BlockSpec(image, lambda n, *_: (0, n, 0, 0)),
                pl.BlockSpec(image, lambda n, who_ref, *_: (0, far_slot(n, who_ref), 0, 0)),
                pl.BlockSpec(strip_rim, lambda n, *_: (0, n, 0, 0)),
                pl.BlockSpec(
                    strip_rim,
                    lambda n, who_ref, *_: (0, early_count + far_slot(n, who_ref), 0, 0),
                ),
                band_block(3),
                ANY,
            ],
            out_specs=pl.BlockSpec(
                block, lambda n, who_ref, *_: (0, who_ref[3] + n, NEAR, 0, 0)
            ),
            scratch_shapes=work_scratch(rows, cols),
        ),
        out_shape=out_shape,
        input_output_aliases={11: 0},
        compiler_params=params,
        cost_estimate=cost(early_count),
        name="annual_pairs",
    )(*scalars, slc, rim, early, far, early_rim, early_rim, bands, out)

    if opposite:
        rim_rows = plan["rim_rows"]

        def last_slot(n, who_ref, *_):
            return (0, who_ref[6] + n, 0, 0)

        out = pl.pallas_call(
            functools.partial(last_kernel, plan),
            grid_spec=pltpu.PrefetchScalarGridSpec(
                num_scalar_prefetch=4,
                grid=(late,),
                in_specs=[
                    pl.BlockSpec(image, last_slot),
                    pl.BlockSpec(strip_rim, last_slot),
                    pl.BlockSpec((2 * rows, cols), lambda n, *_: (n, 0)),
                    pl.BlockSpec(
                        (rim_rows, cols), lambda n, *_: (2 * late * rows // rim_rows, 0)
                    ),
                    band_block(6),
                    ANY,
                ],
                out_specs=pl.BlockSpec(
                    block, lambda n, who_ref, *_: (0, who_ref[6] + n, NEAR, 0, 0)
                ),
                scratch_shapes=work_scratch(rows, cols),
            ),
            out_shape=out_shape,
            input_output_aliases={9: 0},
            compiler_params=params,
            cost_estimate=cost(late),
            name="last_pairs",
        )(*scalars, slc, rim, payload, payload, bands, out)
    return out.reshape(planes, dates * per_date, rows, cols)


def solution(mesh):
    placed = (P(None, "date", "groups", "strip"), P(), P(), P())
    return jax.shard_map(
        body,
        mesh=mesh,
        in_specs=placed,
        out_specs=P(None, "date", "groups", "strip"),
        check_vma=False,
    )
```

```python
import functools

import jax
import jax.numpy as jnp
from jax import lax
from jax.experimental import pallas as pl
from jax.experimental.pallas import tpu as pltpu
from jax.sharding import PartitionSpec as P

HALO = 16
REACH_LO = 12
NEAR = 3
YEAR = 29
EPSILON = 1e-06
TILE = 128
VMEM_BYTES = 20 * 1024 * 1024
SMALL_BYTES = 4 * 1024 * 1024
ANY = pl.BlockSpec(memory_space=pl.ANY)
SMEM = pl.BlockSpec(memory_space=pltpu.SMEM)
VMEM = pl.BlockSpec(memory_space=pltpu.VMEM)
HBM = pl.BlockSpec(memory_space=pltpu.HBM)


def small_params():
    return pltpu.CompilerParams(vmem_limit_bytes=SMALL_BYTES)


def run_copies(copies):
    for copy in copies:
        copy.start()
    for copy in copies:
        copy.wait()


def wanted_image(plan, pairs_ref, device, slot):
    dates = plan["dates"]
    date = device * dates + slot
    return pairs_ref[1, date * plan["per_date"] + NEAR] - lax.axis_index("date") * dates


def gather_strips(tiles, strip):
    lane = lax.broadcasted_iota(jnp.int32, tiles[0].shape, 1)
    packed = jnp.zeros(tiles[0].shape, jnp.float32)
    for n, tile in enumerate(tiles):
        spot = n * HALO
        moved = pltpu.roll(tile.astype(jnp.float32), spot + strip * HALO, 1)
        packed = jnp.where((lane >= spot) & (lane < spot + HALO), moved, packed)
    return packed.astype(jnp.bfloat16)


def place_strip(packed, n, strip):
    shift = 2 * TILE - (n + strip) * HALO
    return pltpu.roll(packed.astype(jnp.float32), lax.rem(shift, TILE), 1).astype(jnp.bfloat16)


def early_kernel(plan, slc_ref, pairs_ref, early_ref, strips_ref, sems):
    me, strip = lax.axis_index("date"), lax.axis_index("strip")
    dates, late, cols = plan["dates"], plan["late"], plan["cols"]
    half = plan["devices"] // 2
    mate = lax.rem(me + half, 2 * half)
    mate_slot = jnp.where(mate < half, late, 0)
    copies = []
    for k in range(dates - late):
        wanted = jnp.clip(wanted_image(plan, pairs_ref, mate, mate_slot + k), 0, dates - 1)
        copies.append(
            pltpu.make_async_copy(slc_ref.at[:, wanted], early_ref.at[:, k], sems.at[k])
        )
    run_copies(copies)
    tiles = []
    for k in range(dates - late):
        for c in range(2):
            left, right = early_ref[c, k, :, :TILE], early_ref[c, k, :, cols - TILE :]
            tiles.append(jnp.where(strip == 1, left, right))
    strips_ref[...] = gather_strips(tiles, 1 - strip)


def beside_kernel(plan, slc_ref, x_ref, z_ref, sems):
    odd = lax.rem(lax.axis_index("date"), 2)
    last = plan["dates"] - NEAR
    run_copies(
        [
            pltpu.make_async_copy(
                slc_ref.at[:, pl.ds(jnp.where(odd == 1, 0, last), NEAR)], x_ref, sems.at[0]
            ),
            pltpu.make_async_copy(
                slc_ref.at[:, pl.ds(jnp.where(odd == 1, last, 0), NEAR)], z_ref, sems.at[1]
            ),
        ]
    )


def rim_kernel(count, *refs):
    sources, out_ref, sems = refs[:count], refs[count], refs[count + 1]
    cols = sources[0].shape[3]
    start = pl.multiple_of(jnp.where(lax.axis_index("strip") == 0, cols - TILE, 0), TILE)
    copies = []
    place = 0
    for n, source in enumerate(sources):
        here = out_ref.at[:, pl.ds(place, source.shape[1])]
        copies.append(
            pltpu.make_async_copy(source.at[:, :, :, pl.ds(start, TILE)], here, sems.at[n])
        )
        place += source.shape[1]
    run_copies(copies)


def rims(*sources):
    planes, _, rows, _ = sources[0].shape
    total = sum(source.shape[1] for source in sources)
    tiles = pl.pallas_call(
        functools.partial(rim_kernel, len(sources)),
        out_shape=jax.ShapeDtypeStruct((planes, total, rows, TILE), sources[0].dtype),
        in_specs=[HBM] + [ANY] * (len(sources) - 1),
        out_specs=VMEM,
        scratch_shapes=[pltpu.SemaphoreType.DMA((len(sources),))],
        compiler_params=small_params(),
        name="rim_blocks",
    )(*sources)
    return lax.ppermute(tiles, "strip", [(0, 1), (1, 0)])


def late_kernel(plan, slc_ref, x_ref, z_ref, rim_ref, pairs_ref, late_ref, far_ref, rim_buf, sems,
                rim_sems):
    me, strip = lax.axis_index("date"), lax.axis_index("strip")
    dates, late, rows, cols = plan["dates"], plan["late"], plan["rows"], plan["cols"]
    half = plan["devices"] // 2
    odd = lax.rem(me, 2)
    mate = lax.rem(me + half, 2 * half)
    far = jnp.where(me < half, half - 1, half)
    routes = (
        (late_ref, mate, jnp.where(mate < half, 0, dates - late)),
        (far_ref, far, jnp.where(me < half, dates - late, 0)),
    )
    for r, (out_ref, device, slot) in enumerate(routes):
        for k in range(late):
            wanted = wanted_image(plan, pairs_ref, device, slot + k)
            wanted = jnp.clip(wanted, -NEAR, dates + NEAR - 1)
            own = (wanted >= 0) & (wanted < dates)
            below = wanted < 0
            spot = jnp.where(below, wanted + NEAR, wanted - dates)
            from_x = below == (odd == 1)
            place = jnp.where(own, wanted, spot + jnp.where(from_x, dates, dates + NEAR))

            def send(source, index):
                for c in range(2):
                    here = out_ref.at[pl.ds((2 * k + c) * rows, rows)]
                    pltpu.make_async_copy(source.at[c, index], here, sems.at[r, k, c]).start()

            pl.when(own)(functools.partial(send, slc_ref, jnp.clip(wanted, 0, dates - 1)))
            spot = jnp.clip(spot, 0, NEAR - 1)
            pl.when(jnp.logical_not(own) & from_x)(functools.partial(send, x_ref, spot))
            pl.when(jnp.logical_not(own) & jnp.logical_not(from_x))(
                functools.partial(send, z_ref, spot)
            )
            pltpu.make_async_copy(
                rim_ref.at[:, place], rim_buf.at[r, :, k], rim_sems.at[r, k]
            ).start()
    base, rim_rows = 2 * late * rows, plan["rim_rows"]
    for r, (out_ref, _, _) in enumerate(routes):
        for k in range(late):
            pltpu.make_async_copy(
                rim_ref.at[:, 0], rim_buf.at[r, :, k], rim_sems.at[r, k]
            ).wait()
        tiles = [rim_buf[r, c, k] for k in range(late) for c in range(2)]
        packed = gather_strips(tiles, strip)
        for n in range(rows // rim_rows):
            out_ref[base : base + rim_rows, n * TILE : (n + 1) * TILE] = packed[
                n * rim_rows : (n + 1) * rim_rows
            ]
        for k in range(late):
            for c in range(2):
                here = out_ref.at[pl.ds((2 * k + c) * rows, rows)]
                pltpu.make_async_copy(slc_ref.at[0, 0], here, sems.at[r, k, c]).wait()


def unpack_late(ref, n, strip, rows):
    packed = jnp.concatenate(
        [ref[:, t * TILE : (t + 1) * TILE] for t in range(ref.shape[1] // TILE)], axis=0
    )
    return place_strip(packed, n, strip)


def bands_kernel(cols, out_ref):
    strip = lax.axis_index("strip")
    wide = out_ref.shape[2]
    reach = pl.program_id(0) + REACH_LO

    def band(places, targets):
        return (jnp.abs(places - targets) <= reach).astype(jnp.float32).astype(jnp.bfloat16)

    shape = (wide, wide)
    row = lax.broadcasted_iota(jnp.int32, shape, 0)
    col = lax.broadcasted_iota(jnp.int32, shape, 1)
    out_ref[0, 0:wide] = band(row, col)
    shape = (TILE, wide)
    row = lax.broadcasted_iota(jnp.int32, shape, 0)
    col = lax.broadcasted_iota(jnp.int32, shape, 1)
    beyond = jnp.where(strip == 0, cols + row, row - TILE)
    middle = TILE // 2
    first = band(jnp.where(row < middle, wide + row, beyond), col)
    second = band(jnp.where(row < middle, beyond, wide - TILE + row), col + wide)
    for n, part in enumerate((first, first, second, second)):
        out_ref[0, wide + n * TILE : wide + (n + 1) * TILE] = part


def split(values):
    high = values.astype(jnp.bfloat16)
    low = (values - high.astype(jnp.float32)).astype(jnp.bfloat16)
    return high, low


def cross_terms(a_real, a_imag, b_real, b_imag):
    a_real, a_imag, b_real, b_imag = [
        part.astype(jnp.float32) for part in (a_real, a_imag, b_real, b_imag)
    ]
    return (
        a_real * b_real + a_imag * b_imag,
        a_imag * b_real - a_real * b_imag,
        a_real * a_real + a_imag * a_imag,
        b_real * b_real + b_imag * b_imag,
    )


def coherence(a_main, a_rim, b_main, b_rim, bands, height, store, scratch):
    high_ref, low_ref, side_ref, stack_ref = scratch
    rows, cols = a_main(0).shape
    wide = cols // 2
    lane = lax.broadcasted_iota(jnp.int32, (rows, TILE), 1)
    inner = lane < TILE // 2
    mains = cross_terms(a_main(0), a_main(1), b_main(0), b_main(1))
    edges = cross_terms(a_rim(0), a_rim(1), b_rim(0), b_rim(1))
    for f in range(4):
        here = slice(f * rows, (f + 1) * rows)
        high, low = split(mains[f])
        high_ref[here] = high
        low_ref[here] = low
        first = jnp.where(inner, mains[f][:, wide : wide + TILE], edges[f])
        second = jnp.where(inner, edges[f], mains[f][:, wide - TILE : wide])
        for n, part in enumerate((first, second)):
            high, low = split(part)
            side_ref[n, here, 0:TILE] = high
            side_ref[n, here, TILE : 2 * TILE] = low
    for n in range(2):
        there = slice(n * wide, (n + 1) * wide)
        inside = bands(0, wide)
        ranged = jnp.dot(high_ref[:, there], inside, preferred_element_type=jnp.float32)
        ranged += jnp.dot(low_ref[:, there], inside, preferred_element_type=jnp.float32)
        ranged += jnp.dot(
            side_ref[n],
            bands(wide + 2 * n * TILE, wide + 2 * (n + 1) * TILE),
            preferred_element_type=jnp.float32,
        )
        high, low = split(ranged)
        for f in range(4):
            stack_ref[f, 0:rows, there] = high[f * rows : (f + 1) * rows]
            stack_ref[f, rows : 2 * rows, there] = low[f * rows : (f + 1) * rows]
    row = lax.broadcasted_iota(jnp.int32, (rows, 2 * rows), 0)
    col = lax.broadcasted_iota(jnp.int32, (rows, 2 * rows), 1)
    col = jnp.where(col < rows, col, col - rows)
    band = (jnp.abs(row - col) <= height).astype(jnp.float32).astype(jnp.bfloat16)
    looked = [
        jnp.dot(band, stack_ref[f], preferred_element_type=jnp.float32) for f in range(4)
    ]
    inverse = lax.rsqrt(looked[2] * looked[3] + EPSILON)
    store(0, looked[0] * inverse)
    store(1, looked[1] * inverse)


def work_scratch(rows, cols):
    return [
        pltpu.VMEM((4 * rows, cols), jnp.bfloat16),
        pltpu.VMEM((4 * rows, cols), jnp.bfloat16),
        pltpu.VMEM((2, 4 * rows, 2 * TILE), jnp.bfloat16),
        pltpu.VMEM((4, 2 * rows, cols), jnp.bfloat16),
    ]


def near_kernel(plan, who_ref, pairs_ref, az_ref, rng_ref, slc_hbm, x_hbm, z_hbm, rim_hbm,
                bands_ref, out_ref, ext, rim, sems, *scratch):
    step = pl.program_id(0)
    dates, per_date = plan["dates"], plan["per_date"]
    me, flip = who_ref[0], who_ref[2]

    @pl.when(step == 0)
    def _():
        x_at = jnp.where(flip == 1, 0, dates + NEAR)
        z_at = jnp.where(flip == 1, dates + NEAR, 0)
        run_copies(
            [
                pltpu.make_async_copy(slc_hbm, ext.at[:, pl.ds(NEAR, dates)], sems.at[0]),
                pltpu.make_async_copy(x_hbm, ext.at[:, pl.ds(x_at, NEAR)], sems.at[1]),
                pltpu.make_async_copy(z_hbm, ext.at[:, pl.ds(z_at, NEAR)], sems.at[2]),
                pltpu.make_async_copy(
                    rim_hbm.at[:, pl.ds(0, dates)], rim.at[:, pl.ds(NEAR, dates)], sems.at[3]
                ),
                pltpu.make_async_copy(
                    rim_hbm.at[:, pl.ds(dates, NEAR)], rim.at[:, pl.ds(x_at, NEAR)], sems.at[4]
                ),
                pltpu.make_async_copy(
                    rim_hbm.at[:, pl.ds(dates + NEAR, NEAR)],
                    rim.at[:, pl.ds(z_at, NEAR)],
                    sems.at[5],
                ),
            ]
        )

    slot = step // NEAR
    pair = (me * dates + slot) * per_date + lax.rem(step, NEAR)
    other = jnp.clip(pairs_ref[1, pair] - me * dates + NEAR, 0, dates + 2 * NEAR - 1)
    own = slot + NEAR
    width = jnp.clip(rng_ref[pair] - REACH_LO, 0, HALO - REACH_LO)

    def store(c, values):
        out_ref[c, 0, 0] = values

    coherence(
        lambda c: ext[c, own],
        lambda c: rim[c, own],
        lambda c: ext[c, other],
        lambda c: rim[c, other],
        lambda a, b: bands_ref[width, a:b],
        az_ref[pair],
        store,
        scratch,
    )


def annual_kernel(plan, who_ref, pairs_ref, az_ref, rng_ref, slc_ref, own_rim_ref, early_ref,
                  strips_ref, far_ref, far_rim_ref, bands_ref, _, out_ref, *scratch):
    step = pl.program_id(0)
    dates, per_date, rows = plan["dates"], plan["per_date"], plan["rows"]
    strip = who_ref[1]
    date = who_ref[0] * dates + who_ref[3] + step
    pair = date * per_date + NEAR
    partner = pairs_ref[1, pair]
    from_far = jnp.where(who_ref[4] == 1, partner < date, partner > date)
    far = far_step(plan, step, who_ref[4])

    def store(c, values):
        out_ref[c, 0, 0] = values

    def main(c):
        return jnp.where(from_far, far_ref[c * rows : (c + 1) * rows], early_ref[c, 0])

    def rim(c):
        return jnp.where(
            from_far,
            unpack_late(far_rim_ref, 2 * far + c, strip, rows),
            place_strip(strips_ref[...], 2 * step + c, strip),
        )

    coherence(
        lambda c: slc_ref[c, 0],
        lambda c: own_rim_ref[c, 0],
        main,
        rim,
        lambda a, b: bands_ref[0, a:b],
        az_ref[pair],
        store,
        scratch,
    )


def far_step(plan, step, lower):
    skip = jnp.where(lower == 1, plan["dates"] - 2 * plan["late"], 0)
    return jnp.clip(step - skip, 0, plan["late"] - 1)


def last_kernel(plan, who_ref, pairs_ref, az_ref, rng_ref, slc_ref, own_rim_ref, late_ref,
                late_rim_ref, bands_ref, _, out_ref, *scratch):
    step = pl.program_id(0)
    dates, per_date, rows = plan["dates"], plan["per_date"], plan["rows"]
    pair = (who_ref[0] * dates + who_ref[5] + step) * per_date + NEAR

    def store(c, values):
        out_ref[c, 0, 0] = values

    coherence(
        lambda c: slc_ref[c, 0],
        lambda c: own_rim_ref[c, 0],
        lambda c: late_ref[c * rows : (c + 1) * rows],
        lambda c: unpack_late(late_rim_ref, 2 * step + c, who_ref[1], rows),
        lambda a, b: bands_ref[0, a:b],
        az_ref[pair],
        store,
        scratch,
    )


def plain_kernel(plan, who_ref, pairs_ref, az_ref, rng_ref, slc_ref, own_rim_ref, other_ref,
                 other_rim_ref, bands_ref, _, out_ref, *scratch):
    date = who_ref[0] * plan["dates"] + pl.program_id(0)

    def store(c, values):
        out_ref[c, 0, 0] = values

    coherence(
        lambda c: slc_ref[c, 0],
        lambda c: own_rim_ref[c, 0],
        lambda c: other_ref[c, 0],
        lambda c: other_rim_ref[c, 0],
        lambda a, b: bands_ref[0, a:b],
        az_ref[date * plan["per_date"] + NEAR],
        store,
        scratch,
    )


def arrivals_by_distance(slc, pair_list, plan):
    dates, per_date, devices = plan["dates"], plan["per_date"], plan["devices"]
    total = dates * devices
    me = lax.axis_index("date")
    annual_of = pair_list[:, 1].reshape(total, per_date)[:, per_date - 1]
    sums = [None] * dates
    for direction in (1, -1):
        by_distance = {}
        for slot in range(dates):
            for gap in range(plan["year"], plan["year"] + 3):
                distance = (slot + direction * gap) // dates
                by_distance.setdefault(distance, set()).add(slot)
        for distance in sorted(by_distance):
            slots = sorted(by_distance[distance])
            wanted_by = (me - distance) * dates + jnp.array(slots, dtype=jnp.int32)
            inside = (wanted_by >= 0) & (wanted_by < total)
            local = jnp.take(annual_of, jnp.clip(wanted_by, 0, total - 1)) - me * dates
            usable = inside & (local >= 0) & (local < dates)
            packed = jnp.take(slc, jnp.clip(local, 0, dates - 1), axis=1)
            packed = jnp.where(usable[None, :, None, None], packed, jnp.zeros_like(packed))
            route = [(i + distance, i) for i in range(devices) if 0 <= i + distance < devices]
            arrived = lax.ppermute(packed, "date", route)
            for n, slot in enumerate(slots):
                part = arrived[:, n]
                sums[slot] = part if sums[slot] is None else sums[slot] + part
    return jnp.stack(sums, axis=1)


def body(slc, pair_list, az_half, rng_half):
    planes, dates, rows, cols = slc.shape
    devices = lax.axis_size("date")
    total = dates * devices
    per_date = pair_list.shape[0] // total
    year = min(YEAR, total // 2 - 2)
    half = devices // 2
    late = half * dates - year
    rim_rows = rows * TILE // cols
    plan = {
        "dates": dates,
        "devices": devices,
        "per_date": per_date,
        "year": year,
        "late": late,
        "rows": rows,
        "cols": cols,
        "rim_rows": rim_rows,
    }
    me, strip = lax.axis_index("date"), lax.axis_index("strip")
    lower = (me < half).astype(jnp.int32)
    opposite = devices % 2 == 0 and 0 < late <= NEAR and 2 * late <= dates
    opposite = opposite and 2 * (dates - late) * HALO <= TILE
    pairs = pair_list.T
    dtype = slc.dtype
    params = pltpu.CompilerParams(vmem_limit_bytes=VMEM_BYTES)

    def images(count):
        return jax.ShapeDtypeStruct((planes, count, rows, cols), dtype)

    if opposite:
        swap = [(i, (i + half) % devices) for i in range(devices)]
        early, strips = pl.pallas_call(
            functools.partial(early_kernel, plan),
            out_shape=(images(dates - late), jax.ShapeDtypeStruct((rows, TILE), dtype)),
            in_specs=[HBM, SMEM],
            out_specs=(VMEM, VMEM),
            scratch_shapes=[pltpu.SemaphoreType.DMA((dates - late,))],
            compiler_params=small_params(),
            name="early_images",
        )(slc, pairs)
        slc, early, strips = lax.optimization_barrier((slc, early, strips))
        beside_x, beside_z = pl.pallas_call(
            functools.partial(beside_kernel, plan),
            out_shape=(images(NEAR), images(NEAR)),
            in_specs=[HBM],
            out_specs=(VMEM, VMEM),
            scratch_shapes=[pltpu.SemaphoreType.DMA((2,))],
            compiler_params=small_params(),
            name="beside_images",
        )(slc)
        early = lax.ppermute(early, "date", swap)
        strips = lax.ppermute(
            strips, ("date", "strip"), [(2 * a + s, 2 * b + 1 - s) for a, b in swap for s in (0, 1)]
        )
        beside_x = lax.ppermute(beside_x, "date", [(i, i ^ 1) for i in range(devices)])
        steps = [(i, i + 1) for i in range(1, devices - 1, 2)]
        beside_z = lax.ppermute(beside_z, "date", steps + [(b, a) for a, b in steps])
        flip = lax.rem(me, 2)
        base = jnp.where(lower == 1, late, 0)
        last_base = jnp.where(lower == 1, 0, dates - late)
    else:
        annual = arrivals_by_distance(slc, pair_list, plan)
        ups = [(i, i + 1) for i in range(devices - 1)]
        beside_x = lax.ppermute(slc[:, :NEAR], "date", [(b, a) for a, b in ups])
        beside_z = lax.ppermute(slc[:, dates - NEAR :], "date", ups)
        flip, base, last_base = 0, 0, 0
    who = jnp.stack(
        [jnp.asarray(v, jnp.int32) for v in (me, strip, flip, base, lower, last_base)]
    )
    rim = rims(slc, beside_x, beside_z)
    if opposite:
        late_shape = jax.ShapeDtypeStruct((2 * late * rows + rim_rows, cols), dtype)
        payload, far = pl.pallas_call(
            functools.partial(late_kernel, plan),
            out_shape=(late_shape, late_shape),
            in_specs=[HBM] + [ANY] * 3 + [SMEM],
            out_specs=(VMEM, VMEM),
            scratch_shapes=[
                pltpu.VMEM((2, 2, late, rows, TILE), dtype),
                pltpu.SemaphoreType.DMA((2, late, 2)),
                pltpu.SemaphoreType.DMA((2, late)),
            ],
            compiler_params=small_params(),
            name="late_images",
        )(slc, beside_x, beside_z, rim, pairs)
        payload = lax.ppermute(payload, "date", swap)
        far = lax.ppermute(far, "date", [(0, half - 1), (devices - 1, half)])
    wide = cols // 2
    widths = HALO - REACH_LO + 1
    band_rows = wide + 4 * TILE
    bands = pl.pallas_call(
        functools.partial(bands_kernel, cols),
        grid=(widths,),
        out_shape=jax.ShapeDtypeStruct((widths, band_rows, wide), jnp.bfloat16),
        out_specs=pl.BlockSpec((1, band_rows, wide), lambda n: (n, 0, 0)),
        compiler_params=small_params(),
        name="range_bands",
    )()
    out_shape = jax.ShapeDtypeStruct((planes, dates, per_date, rows, cols), jnp.float32)
    block = (planes, 1, 1, rows, cols)
    scalars = (who, pairs, az_half, rng_half)
    ext = dates + 2 * NEAR

    def cost(count):
        return pl.CostEstimate(
            flops=count,
            bytes_accessed=count,
            transcendentals=0,
        )

    out = pl.pallas_call(
        functools.partial(near_kernel, plan),
        grid_spec=pltpu.PrefetchScalarGridSpec(
            num_scalar_prefetch=4,
            grid=(dates * NEAR,),
            in_specs=[HBM]
            + [ANY] * 3
            + [pl.BlockSpec((widths, band_rows, wide), lambda n, *_: (0, 0, 0))],
            out_specs=pl.BlockSpec(block, lambda n, *_: (0, n // NEAR, lax.rem(n, NEAR), 0, 0)),
            scratch_shapes=[
                pltpu.VMEM((planes, ext, rows, cols), dtype),
                pltpu.VMEM((planes, ext, rows, TILE), dtype),
                pltpu.SemaphoreType.DMA((6,)),
            ]
            + work_scratch(rows, cols),
        ),
        out_shape=out_shape,
        compiler_params=params,
        cost_estimate=cost(dates * NEAR),
        name="near_pairs",
    )(*scalars, slc, beside_x, beside_z, rim, bands)

    image, strip_rim = (planes, 1, rows, cols), (planes, 1, rows, TILE)

    def own_slot(start):
        return lambda n, who_ref, *_: (0, who_ref[start] + n, 0, 0)

    def band_block(start):
        def of(n, who_ref, pairs_ref, az_ref, rng_ref):
            pair = (who_ref[0] * dates + who_ref[start] + n) * per_date + NEAR
            return (jnp.clip(rng_ref[pair] - REACH_LO, 0, widths - 1), 0, 0)

        return pl.BlockSpec((1, band_rows, wide), of)

    def annual_pairs(kernel, start, count, others, specs, name):
        return pl.pallas_call(
            functools.partial(kernel, plan),
            grid_spec=pltpu.PrefetchScalarGridSpec(
                num_scalar_prefetch=4,
                grid=(count,),
                in_specs=[
                    pl.BlockSpec(image, own_slot(start)),
                    pl.BlockSpec(strip_rim, own_slot(start)),
                    *specs,
                    band_block(start),
                    ANY,
                ],
                out_specs=pl.BlockSpec(
                    block, lambda n, who_ref, *_: (0, who_ref[start] + n, NEAR, 0, 0)
                ),
                scratch_shapes=work_scratch(rows, cols),
            ),
            out_shape=out_shape,
            input_output_aliases={len(specs) + 7: 0},
            compiler_params=params,
            cost_estimate=cost(count),
            name=name,
        )(*scalars, slc, rim, *others, bands, out)

    rim_place = pl.BlockSpec((rim_rows, cols), lambda n, *_: (2 * late * rows // rim_rows, 0))
    if opposite:
        specs = [
            pl.BlockSpec(image, lambda n, *_: (0, n, 0, 0)),
            pl.BlockSpec((rows, TILE), lambda n, *_: (0, 0)),
            pl.BlockSpec(
                (2 * rows, cols), lambda n, who_ref, *_: (far_step(plan, n, who_ref[4]), 0)
            ),
            rim_place,
        ]
        out = annual_pairs(
            annual_kernel, 3, dates - late, (early, strips, far, far), specs, "annual_pairs"
        )
        specs = [pl.BlockSpec((2 * rows, cols), lambda n, *_: (n, 0)), rim_place]
        out = annual_pairs(last_kernel, 5, late, (payload, payload), specs, "last_pairs")
    else:
        specs = [pl.BlockSpec(image, own_slot(3)), pl.BlockSpec(strip_rim, own_slot(3))]
        out = annual_pairs(
            plain_kernel, 3, dates, (annual, rims(annual)), specs, "annual_pairs"
        )
    return out.reshape(planes, dates * per_date, rows, cols)


def solution(mesh):
    placed = (P(None, "date", "groups", "strip"), P(), P(), P())
    return jax.shard_map(
        body,
        mesh=mesh,
        in_specs=placed,
        out_specs=P(None, "date", "groups", "strip"),
        check_vma=False,
    )
```

```python
import functools

import jax
import jax.numpy as jnp
from jax import lax
from jax.experimental import pallas as pl
from jax.experimental.pallas import tpu as pltpu
from jax.sharding import PartitionSpec as P

HALO = 16
REACH_LO = 12
NEAR = 3
YEAR = 29
EPSILON = 1e-06
TILE = 128
INNER = TILE // 2
ANY = pl.BlockSpec(memory_space=pl.ANY)
SMEM = pl.BlockSpec(memory_space=pltpu.SMEM)
VMEM = pl.BlockSpec(memory_space=pltpu.VMEM)


def limit(mebibytes):
    return pltpu.CompilerParams(vmem_limit_bytes=mebibytes * 1024 * 1024)


def run_copies(copies):
    for copy in copies:
        copy.start()
    for copy in copies:
        copy.wait()


def gather_strips(tiles, side):
    lane = lax.broadcasted_iota(jnp.int32, tiles[0].shape, 1)
    packed = jnp.zeros(tiles[0].shape, jnp.float32)
    for n, tile in enumerate(tiles):
        spot = n * HALO
        moved = pltpu.roll(tile.astype(jnp.float32), spot + side * HALO, 1)
        packed = jnp.where((lane >= spot) & (lane < spot + HALO), moved, packed)
    return packed.astype(jnp.bfloat16)


def place_strip(packed, n, side):
    shift = 2 * TILE - (n + side) * HALO
    return pltpu.roll(packed.astype(jnp.float32), lax.rem(shift, TILE), 1).astype(jnp.bfloat16)


def write_strips(out_ref, packed):
    rows, cols = packed.shape[0], out_ref.shape[1]
    part = rows * TILE // cols
    base = out_ref.shape[0] - part
    for n in range(rows // part):
        out_ref[base:, n * TILE : (n + 1) * TILE] = packed[n * part : (n + 1) * part]


def read_strips(ref, rows):
    cols = ref.shape[1]
    base = ref.shape[0] - rows * TILE // cols
    return jnp.concatenate(
        [ref[base:, n * TILE : (n + 1) * TILE] for n in range(cols // TILE)], axis=0
    )


def early_kernel(plan, slc_ref, pairs_ref, early_ref, strips_ref, rim_ref, sems):
    me, strip = lax.axis_index("date"), lax.axis_index("strip")
    dates, late, cols = plan["dates"], plan["late"], plan["cols"]
    half = plan["devices"] // 2
    mate = lax.rem(me + half, 2 * half)
    mate_slot = jnp.where(mate < half, late, 0)
    start = pl.multiple_of(jnp.where(strip == 0, cols - TILE, 0), TILE)
    copies = [
        pltpu.make_async_copy(
            slc_ref.at[:, :, :, pl.ds(start, TILE)], rim_ref, sems.at[dates - late]
        )
    ]
    for k in range(dates - late):
        date = mate * dates + mate_slot + k
        wanted = pairs_ref[1, date * plan["per_date"] + NEAR] - me * dates
        wanted = jnp.clip(wanted, 0, dates - 1)
        copies.append(
            pltpu.make_async_copy(slc_ref.at[:, wanted], early_ref.at[:, k], sems.at[k])
        )
    run_copies(copies)
    tiles = []
    for k in range(dates - late):
        for c in range(2):
            left, right = early_ref[c, k, :, :TILE], early_ref[c, k, :, cols - TILE :]
            tiles.append(jnp.where(strip == 1, left, right))
    strips_ref[...] = gather_strips(tiles, 1 - strip)


def rim_kernel(slc_ref, rim_ref, sem):
    cols = slc_ref.shape[3]
    start = pl.multiple_of(jnp.where(lax.axis_index("strip") == 0, cols - TILE, 0), TILE)
    run_copies([pltpu.make_async_copy(slc_ref.at[:, :, :, pl.ds(start, TILE)], rim_ref, sem)])


def beside_kernel(plan, slc_ref, rim_ref, inner_ref, outer_ref, sems):
    me, strip = lax.axis_index("date"), lax.axis_index("strip")
    dates, rows = plan["dates"], plan["rows"]
    upper = me >= plan["devices"] // 2
    last = dates - NEAR
    copies = []
    firsts = (jnp.where(upper, last, 0), jnp.where(upper, 0, last))
    for r, (out_ref, first) in enumerate(zip((inner_ref, outer_ref), firsts)):
        for k in range(NEAR):
            for c in range(2):
                here = out_ref.at[pl.ds((2 * k + c) * rows, rows)]
                copies.append(
                    pltpu.make_async_copy(slc_ref.at[c, first + k], here, sems.at[r, k, c])
                )
    for copy in copies:
        copy.start()
    for out_ref, first in zip((inner_ref, outer_ref), firsts):
        tiles = [rim_ref[c, first + k] for k in range(NEAR) for c in range(2)]
        write_strips(out_ref, gather_strips(tiles, strip))
    for copy in copies:
        copy.wait()


def late_kernel(plan, slc_ref, rim_ref, inner_ref, meta_ref, _, late_ref, tiles_ref):
    me, strip = lax.axis_index("date"), lax.axis_index("strip")
    dates, late, rows = plan["dates"], plan["late"], plan["rows"]
    half = plan["devices"] // 2
    mate = lax.rem(me + half, 2 * half)
    mate_slot = jnp.where(mate < half, 0, dates - late)
    packed = read_strips(inner_ref, rows)
    for k in range(late):
        date = mate * dates + mate_slot + k
        wanted = meta_ref[date * plan["per_date"] + NEAR] - me * dates
        own = (wanted >= 0) & (wanted < dates)
        own_at = jnp.clip(wanted, 0, dates - 1)
        other_at = jnp.clip(jnp.where(me < half, wanted - dates, wanted + NEAR), 0, NEAR - 1)
        for c in range(2):
            here = pl.ds((2 * k + c) * rows, rows)

            @pl.when(own)
            def _():
                late_ref[here] = slc_ref[c, own_at]
                tiles_ref[k, c] = rim_ref[c, own_at]

            @pl.when(jnp.logical_not(own))
            def _():
                there = pl.multiple_of((2 * other_at + c) * rows, rows)
                late_ref[here] = inner_ref[pl.ds(there, rows)]
                tiles_ref[k, c] = place_strip(packed, 2 * other_at + c, strip)

    tiles = [tiles_ref[k, c] for k in range(late) for c in range(2)]
    write_strips(late_ref, gather_strips(tiles, strip))


def bands_kernel(cols, out_ref):
    strip = lax.axis_index("strip")
    wide = out_ref.shape[3]
    reach = pl.program_id(0) + REACH_LO

    def band(places, targets):
        return (jnp.abs(places - targets) <= reach).astype(jnp.float32).astype(jnp.bfloat16)

    def indices(shape):
        return lax.broadcasted_iota(jnp.int32, shape, 0), lax.broadcasted_iota(jnp.int32, shape, 1)

    inside = band(*indices((wide, wide)))
    row, col = indices((TILE, wide))
    beyond = jnp.where(strip == 0, cols + row, row - TILE)
    first = band(jnp.where(row < INNER, wide + row, beyond), col)
    second = band(jnp.where(row < INNER, beyond, wide - TILE + row), col + wide)
    for n, part in enumerate((first, second)):
        out_ref[0, n, 0:wide] = inside
        out_ref[0, n, wide : 2 * wide] = inside
        out_ref[0, n, 2 * wide : 2 * wide + TILE] = part
        out_ref[0, n, 2 * wide + TILE : 2 * wide + 2 * TILE] = part


def split(values):
    high = values.astype(jnp.bfloat16)
    low = (values - high.astype(jnp.float32)).astype(jnp.bfloat16)
    return high, low


def put(ref, here, t, values):
    wide = 2 * TILE
    depth = 2 * wide + 2 * TILE
    for low, part in enumerate(split(values)):
        side = [n * depth + 2 * wide + low * TILE for n in range(2)]
        if t < 4:
            at = (t // 2) * depth + low * wide + (t % 2) * TILE
            ref[*here, at : at + TILE] = part
        if t == 2:
            ref[*here, side[0] : side[0] + INNER] = part[:, :INNER]
        if t == 1:
            ref[*here, side[1] + INNER : side[1] + TILE] = part[:, INNER:]
        if t == 4:
            ref[*here, side[0] + INNER : side[0] + TILE] = part[:, INNER:]
            ref[*here, side[1] : side[1] + INNER] = part[:, :INNER]


def tile_of(main, rim, t):
    return [
        (rim(c) if t == 4 else main(c, slice(t * TILE, (t + 1) * TILE))).astype(jnp.float32)
        for c in range(2)
    ]


class Pairs:
    def __init__(self, plan, meta_ref, slc_ref, rim_ref, bands_ref, powers_ref, out_ref, scratch):
        self.plan, self.meta_ref = plan, meta_ref
        self.slc_ref, self.rim_ref = slc_ref, rim_ref
        self.bands_ref, self.powers_ref, self.out_ref = bands_ref, powers_ref, out_ref
        (self.left_ref, self.stack_ref, self.other_ref, self.other_rim_ref, self.stage_ref,
         self.count_ref, self.sems) = scratch
        self.me, self.strip = lax.axis_index("date"), lax.axis_index("strip")
        self.count_ref[0] = 0

    def partner(self, pair):
        return self.meta_ref[pair]

    def own_other(self, index):
        return (
            lambda c, cols: self.slc_ref[c, index, :, cols],
            lambda c: self.rim_ref[c, index],
        )

    def fetched_other(self):
        return (
            lambda c, cols: self.other_ref[c, :, cols],
            lambda c: self.other_rim_ref[c],
        )

    def fetch_payload(self, ref, index):
        rows = self.plan["rows"]
        packed = read_strips(ref, rows)
        for c in range(2):
            at = pl.multiple_of((2 * index + c) * rows, rows)
            self.other_ref[c] = ref[pl.ds(at, rows)]
            self.other_rim_ref[c] = place_strip(packed, 2 * index + c, self.strip)

    def out_copy(self, slot, pair):
        return pltpu.make_async_copy(
            self.stage_ref.at[slot], self.out_ref.at[:, pair], self.sems.at[slot]
        )

    def finish(self):
        count = self.count_ref[0]

        @pl.when(count >= 1)
        def _():
            self.out_copy(lax.rem(count + 1, 2), 0).wait()

        @pl.when(count >= 2)
        def _():
            self.out_copy(lax.rem(count, 2), 0).wait()

    def run(self, slot, kind, other, other_power=None):
        plan, left_ref, stack_ref = self.plan, self.left_ref, self.stack_ref
        rows, dates, per_date = plan["rows"], plan["dates"], plan["per_date"]
        count = self.count_ref[0]
        stage = lax.rem(count, 2)

        @pl.when(count >= 2)
        def _():
            self.out_copy(stage, 0).wait()

        pair = (self.me * dates + slot) * per_date + kind
        height = self.meta_ref[plan["pairs"] + pair]
        width = self.meta_ref[2 * plan["pairs"] + pair] - REACH_LO
        width = jnp.clip(width, 0, HALO - REACH_LO)
        part = [(pl.ds(f * rows, rows),) for f in range(4)]
        left_ref[*part[2]] = self.powers_ref[slot]
        if other_power is not None:
            left_ref[*part[3]] = self.powers_ref[other_power]
        first = self.own_other(slot)
        for t in range(5):
            a_real, a_imag = tile_of(*first, t)
            b_real, b_imag = tile_of(*other, t)
            put(left_ref, part[0], t, a_real * b_real + a_imag * b_imag)
            put(left_ref, part[1], t, a_imag * b_real - a_real * b_imag)
            if other_power is None:
                put(left_ref, part[3], t, b_real * b_real + b_imag * b_imag)
        depth = self.bands_ref.shape[2]
        wide = self.bands_ref.shape[3]
        for n in range(2):
            ranged = jnp.dot(
                left_ref[:, n * depth : (n + 1) * depth],
                self.bands_ref[width, n],
                preferred_element_type=jnp.float32,
            )
            for low, values in enumerate(split(ranged)):
                for f in range(4):
                    stack_ref[f, low * rows : (low + 1) * rows, n * wide : (n + 1) * wide] = values[
                        f * rows : (f + 1) * rows
                    ]
        row = lax.broadcasted_iota(jnp.int32, (rows, 2 * rows), 0)
        col = lax.broadcasted_iota(jnp.int32, (rows, 2 * rows), 1)
        col = jnp.where(col < rows, col, col - rows)
        band = (jnp.abs(row - col) <= height).astype(jnp.float32).astype(jnp.bfloat16)
        looked = [
            jnp.dot(band, stack_ref[f], preferred_element_type=jnp.float32) for f in range(4)
        ]
        inverse = lax.rsqrt(looked[2] * looked[3] + EPSILON)
        for c in range(2):
            self.stage_ref[stage, c] = looked[c] * inverse
        self.out_copy(stage, slot * per_date + kind).start()
        self.count_ref[0] = count + 1


def own_kernel(plan, meta_ref, slc_ref, rim_ref, bands_ref, out_ref, powers_ref, *scratch):
    pairs = Pairs(plan, meta_ref, slc_ref, rim_ref, bands_ref, powers_ref, out_ref, scratch)
    dates = plan["dates"]

    def power(slot, carry):
        for t in range(5):
            real, imag = tile_of(*pairs.own_other(slot), t)
            put(powers_ref, (slot, slice(None)), t, real * real + imag * imag)
        return carry

    lax.fori_loop(0, dates, power, 0)

    def step(n, carry):
        slot, kind = n // NEAR, lax.rem(n, NEAR)
        pair = (pairs.me * dates + slot) * plan["per_date"] + kind
        local = pairs.partner(pair) - pairs.me * dates

        @pl.when((local >= 0) & (local < dates))
        def _():
            pairs.run(slot, kind, pairs.own_other(local), local)

        return carry

    lax.fori_loop(0, dates * NEAR, step, 0)
    pairs.finish()


def rest_kernel(plan, meta_ref, slc_ref, rim_ref, bands_ref, powers_ref, inner_ref, outer_ref,
                middle_ref, _, out_ref, *scratch):
    pairs = Pairs(plan, meta_ref, slc_ref, rim_ref, bands_ref, powers_ref, out_ref, scratch)
    dates, half = plan["dates"], plan["devices"] // 2
    upper = pairs.me >= half
    if plan["halves"]:
        in_middle = jnp.where(upper, pairs.me == half, pairs.me == half - 1)
    else:
        upper, in_middle = True, False

    def step(n, carry):
        slot, kind = n // NEAR, lax.rem(n, NEAR)
        pair = (pairs.me * dates + slot) * plan["per_date"] + kind
        local = pairs.partner(pair) - pairs.me * dates
        below = local < 0
        index = jnp.clip(jnp.where(below, local + NEAR, local - dates), 0, NEAR - 1)
        inner = below == upper

        @pl.when(below | (local >= dates))
        def _():
            middle = inner & in_middle
            pl.when(middle)(lambda: pairs.fetch_payload(middle_ref, index))
            pl.when(inner & jnp.logical_not(middle))(
                lambda: pairs.fetch_payload(inner_ref, index)
            )
            pl.when(jnp.logical_not(inner))(lambda: pairs.fetch_payload(outer_ref, index))
            pairs.run(slot, kind, pairs.fetched_other())

        return carry

    lax.fori_loop(0, dates * NEAR, step, 0)
    pairs.finish()


def annual_kernel(plan, is_late, meta_ref, slc_ref, rim_ref, bands_ref, powers_ref, inner_ref,
                  outer_ref, images_ref, strips_ref, _, out_ref, *scratch):
    pairs = Pairs(plan, meta_ref, slc_ref, rim_ref, bands_ref, powers_ref, out_ref, scratch)
    dates, late, rows = plan["dates"], plan["late"], plan["rows"]
    half = plan["devices"] // 2
    me, split_date = pairs.me, half * dates
    lower = me < half
    if is_late:
        base, count = jnp.where(lower, 0, dates - late), late
    else:
        base, count = jnp.where(lower, late, 0), dates - late

    def fetch_early(k):
        packed = strips_ref[...]
        for c in range(2):
            pairs.other_ref[c] = images_ref[c, k]
            pairs.other_rim_ref[c] = place_strip(packed, 2 * k + c, pairs.strip)

    def step(k, carry):
        slot = base + k
        date = me * dates + slot
        other = pairs.partner(date * plan["per_date"] + NEAR)
        far = (other < split_date) == lower
        from_inner = jnp.where(lower, me != 0, me == half)
        inner_at = jnp.where(lower, other, other - (2 * split_date - NEAR))
        outer_at = jnp.where(lower, other - (split_date - NEAR), other - split_date)

        @pl.when(far & from_inner)
        def _():
            pairs.fetch_payload(inner_ref, jnp.clip(inner_at, 0, NEAR - 1))

        @pl.when(far & jnp.logical_not(from_inner))
        def _():
            pairs.fetch_payload(outer_ref, jnp.clip(outer_at, 0, NEAR - 1))

        @pl.when(jnp.logical_not(far))
        def _():
            if is_late:
                pairs.fetch_payload(images_ref, k)
            else:
                fetch_early(k)

        pairs.run(slot, NEAR, pairs.fetched_other())
        return carry

    lax.fori_loop(0, count, step, 0)
    pairs.finish()


def plain_kernel(plan, meta_ref, slc_ref, rim_ref, bands_ref, powers_ref, images_ref,
                 image_rim_ref, _, out_ref, *scratch):
    pairs = Pairs(plan, meta_ref, slc_ref, rim_ref, bands_ref, powers_ref, out_ref, scratch)

    def step(slot, carry):
        other = (
            lambda c, cols: images_ref[c, slot, :, cols],
            lambda c: image_rim_ref[c, slot],
        )
        pairs.run(slot, NEAR, other)
        return carry

    lax.fori_loop(0, plan["dates"], step, 0)
    pairs.finish()


def arrivals_by_distance(slc, pair_list, plan):
    dates, per_date, devices = plan["dates"], plan["per_date"], plan["devices"]
    total = dates * devices
    me = lax.axis_index("date")
    annual_of = pair_list[:, 1].reshape(total, per_date)[:, per_date - 1]
    sums = [None] * dates
    for direction in (1, -1):
        by_distance = {}
        for slot in range(dates):
            for gap in range(plan["year"], plan["year"] + 3):
                distance = (slot + direction * gap) // dates
                by_distance.setdefault(distance, set()).add(slot)
        for distance in sorted(by_distance):
            slots = sorted(by_distance[distance])
            wanted_by = (me - distance) * dates + jnp.array(slots, dtype=jnp.int32)
            inside = (wanted_by >= 0) & (wanted_by < total)
            local = jnp.take(annual_of, jnp.clip(wanted_by, 0, total - 1)) - me * dates
            usable = inside & (local >= 0) & (local < dates)
            packed = jnp.take(slc, jnp.clip(local, 0, dates - 1), axis=1)
            packed = jnp.where(usable[None, :, None, None], packed, jnp.zeros_like(packed))
            route = [(i + distance, i) for i in range(devices) if 0 <= i + distance < devices]
            arrived = lax.ppermute(packed, "date", route)
            for n, slot in enumerate(slots):
                part = arrived[:, n]
                sums[slot] = part if sums[slot] is None else sums[slot] + part
    return jnp.stack(sums, axis=1)


def payload_of(images, rim, strip):
    planes, count, rows, cols = images.shape
    edges = jnp.where(strip == 0, rim[..., :HALO], rim[..., TILE - HALO :])
    edges = jnp.transpose(edges, (2, 1, 0, 3)).reshape(rows, count * planes * HALO)
    edges = jnp.pad(edges, ((0, 0), (0, TILE - edges.shape[1])))
    part = rows * TILE // cols
    edges = jnp.transpose(edges.reshape(rows // part, part, TILE), (1, 0, 2)).reshape(part, cols)
    stacked = jnp.transpose(images, (1, 0, 2, 3)).reshape(count * planes * rows, cols)
    return jnp.concatenate([stacked, edges], axis=0)


def body(slc, pair_list, az_half, rng_half):
    planes, dates, rows, cols = slc.shape
    devices = lax.axis_size("date")
    total = dates * devices
    per_date = pair_list.shape[0] // total
    year = min(YEAR, total // 2 - 2)
    half = devices // 2
    late = half * dates - year
    halves = devices % 2 == 0 and 0 < late <= NEAR and 2 * late <= dates
    halves = halves and 2 * (dates - late) * HALO <= TILE
    plan = {
        "dates": dates,
        "devices": devices,
        "per_date": per_date,
        "year": year,
        "late": late,
        "rows": rows,
        "cols": cols,
        "pairs": total * per_date,
        "halves": halves,
    }
    dtype = slc.dtype
    rim_rows = rows * TILE // cols
    meta = jnp.concatenate([pair_list[:, 1], az_half, rng_half])
    swap_strips = [(0, 1), (1, 0)]

    def images(count):
        return jax.ShapeDtypeStruct((planes, count, rows, cols), dtype)

    def rim_shape(count):
        return jax.ShapeDtypeStruct((planes, count, rows, TILE), dtype)

    def payload_shape(count):
        return jax.ShapeDtypeStruct((planes * count * rows + rim_rows, cols), dtype)

    def swapped_rims(values):
        out = pl.pallas_call(
            rim_kernel,
            out_shape=rim_shape(values.shape[1]),
            in_specs=[ANY],
            out_specs=VMEM,
            scratch_shapes=[pltpu.SemaphoreType.DMA],
            compiler_params=limit(4),
            name="rim_blocks",
        )(values)
        return lax.ppermute(out, "strip", swap_strips)

    wide = cols // 2
    widths = HALO - REACH_LO + 1
    band_shape = (2, 2 * wide + 2 * TILE, wide)
    bands = pl.pallas_call(
        functools.partial(bands_kernel, cols),
        grid=(widths,),
        out_shape=jax.ShapeDtypeStruct((widths, *band_shape), jnp.bfloat16),
        out_specs=pl.BlockSpec((1, *band_shape), lambda n: (n, 0, 0, 0)),
        compiler_params=limit(4),
        name="range_bands",
    )()
    if halves:
        swap = [(i, (i + half) % devices) for i in range(devices)]
        early, strips, rim = pl.pallas_call(
            functools.partial(early_kernel, plan),
            out_shape=(
                images(dates - late),
                jax.ShapeDtypeStruct((rows, TILE), dtype),
                rim_shape(dates),
            ),
            in_specs=[ANY, SMEM],
            out_specs=(VMEM, VMEM, VMEM),
            scratch_shapes=[pltpu.SemaphoreType.DMA((dates - late + 1,))],
            compiler_params=limit(56),
            name="early_images",
        )(slc, pair_list.T)
        early = lax.ppermute(early, "date", swap)
        rim = lax.ppermute(rim, "strip", swap_strips)
        strips = lax.ppermute(
            strips, ("date", "strip"), [(2 * a + s, 2 * b + 1 - s) for a, b in swap for s in (0, 1)]
        )
        inner, outer = pl.pallas_call(
            functools.partial(beside_kernel, plan),
            out_shape=(payload_shape(NEAR), payload_shape(NEAR)),
            in_specs=[ANY, VMEM],
            out_specs=(VMEM, VMEM),
            scratch_shapes=[pltpu.SemaphoreType.DMA((2, NEAR, 2))],
            compiler_params=limit(4),
            name="beside_images",
        )(slc, rim)
        down = [(i, (i - 1) % half) for i in range(half)]
        down += [(half + i, half + (i + 1) % half) for i in range(half)]
        middle = lax.ppermute(outer, "date", [(half - 1, half), (half, half - 1)])
        inner = lax.ppermute(inner, "date", down)
        outer = lax.ppermute(outer, "date", [(b, a) for a, b in down])
    else:
        rim = swapped_rims(slc)
        annual = arrivals_by_distance(slc, pair_list, plan)
        strip = lax.axis_index("strip")
        ups = [(i, i + 1) for i in range(devices - 1)]
        inner = payload_of(slc[:, dates - NEAR :], rim[:, dates - NEAR :], strip)
        outer = payload_of(slc[:, :NEAR], rim[:, :NEAR], strip)
        inner = lax.ppermute(inner, "date", ups)
        outer = lax.ppermute(outer, "date", [(b, a) for a, b in ups])
        middle = inner

    out_shape = jax.ShapeDtypeStruct((planes, dates * per_date, rows, cols), jnp.float32)
    depth = 2 * band_shape[1]
    scratch = [
        pltpu.VMEM((4 * rows, depth), jnp.bfloat16),
        pltpu.VMEM((4, 2 * rows, cols), jnp.bfloat16),
        pltpu.VMEM((planes, rows, cols), dtype),
        pltpu.VMEM((planes, rows, TILE), dtype),
        pltpu.VMEM((2, planes, rows, cols), jnp.float32),
        pltpu.SMEM((1,), jnp.int32),
        pltpu.SemaphoreType.DMA((2,)),
    ]

    def cost(flops):
        return pl.CostEstimate(flops=flops, bytes_accessed=1, transcendentals=0)

    out, powers = pl.pallas_call(
        functools.partial(own_kernel, plan),
        out_shape=(out_shape, jax.ShapeDtypeStruct((dates, rows, depth), jnp.bfloat16)),
        in_specs=[SMEM, VMEM, VMEM, VMEM],
        out_specs=(ANY, VMEM),
        scratch_shapes=scratch,
        compiler_params=limit(24),
        cost_estimate=cost(20_000_000_000),
        name="own_pairs",
    )(meta, slc, rim, bands)

    def more_pairs(kernel, out, others, name):
        return pl.pallas_call(
            functools.partial(kernel, plan),
            out_shape=out_shape,
            in_specs=[SMEM] + [VMEM] * (4 + len(others)) + [ANY],
            out_specs=ANY,
            scratch_shapes=scratch,
            input_output_aliases={5 + len(others): 0},
            compiler_params=limit(24),
            cost_estimate=cost(1),
            name=name,
        )(meta, slc, rim, bands, powers, *others, out)

    if halves:
        payload = pl.pallas_call(
            functools.partial(late_kernel, plan),
            out_shape=payload_shape(late),
            in_specs=[VMEM, VMEM, VMEM, SMEM, ANY],
            out_specs=VMEM,
            scratch_shapes=[pltpu.VMEM((late, planes, rows, TILE), dtype)],
            compiler_params=limit(4),
            name="late_images",
        )(slc, rim, inner, meta, powers)
        payload = lax.ppermute(payload, "date", swap)
    out = more_pairs(rest_kernel, out, (inner, outer, middle), "near_pairs")
    if halves:
        kernel = lambda plan, *refs: annual_kernel(plan, False, *refs)
        out = more_pairs(kernel, out, (inner, outer, early, strips), "annual_pairs")
        kernel = lambda plan, *refs: annual_kernel(plan, True, *refs)
        out = more_pairs(kernel, out, (inner, outer, payload, strips), "last_pairs")
    else:
        out = more_pairs(plain_kernel, out, (annual, swapped_rims(annual)), "annual_pairs")
    return out


def solution(mesh):
    placed = (P(None, "date", "groups", "strip"), P(), P(), P())
    return jax.shard_map(
        body,
        mesh=mesh,
        in_specs=placed,
        out_specs=P(None, "date", "groups", "strip"),
        check_vma=False,
    )
```

```python
import functools

import jax
import jax.numpy as jnp
from jax import lax
from jax.experimental import pallas as pl
from jax.experimental.pallas import tpu as pltpu
from jax.sharding import PartitionSpec as P

HALO = 16
REACH_LO = 12
NEAR = 3
YEAR = 29
EPSILON = 1e-06
TILE = 128
INNER = TILE // 2
ANY = pl.BlockSpec(memory_space=pl.ANY)
SMEM = pl.BlockSpec(memory_space=pltpu.SMEM)
VMEM = pl.BlockSpec(memory_space=pltpu.VMEM)


def limit(mebibytes):
    return pltpu.CompilerParams(vmem_limit_bytes=mebibytes * 1024 * 1024)


def run_copies(copies):
    for copy in copies:
        copy.start()
    for copy in copies:
        copy.wait()


def gather_strips(tiles, side):
    lane = lax.broadcasted_iota(jnp.int32, tiles[0].shape, 1)
    packed = jnp.zeros(tiles[0].shape, jnp.float32)
    for n, tile in enumerate(tiles):
        spot = n * HALO
        moved = pltpu.roll(tile.astype(jnp.float32), spot + side * HALO, 1)
        packed = jnp.where((lane >= spot) & (lane < spot + HALO), moved, packed)
    return packed.astype(jnp.bfloat16)


def place_strip(packed, n, side):
    shift = 2 * TILE - (n + side) * HALO
    return pltpu.roll(packed.astype(jnp.float32), lax.rem(shift, TILE), 1).astype(jnp.bfloat16)


def write_strips(out_ref, packed):
    rows, cols = packed.shape[0], out_ref.shape[1]
    part = rows * TILE // cols
    base = out_ref.shape[0] - part
    for n in range(rows // part):
        out_ref[base:, n * TILE : (n + 1) * TILE] = packed[n * part : (n + 1) * part]


def read_strips(ref, rows):
    cols = ref.shape[1]
    base = ref.shape[0] - rows * TILE // cols
    return jnp.concatenate(
        [ref[base:, n * TILE : (n + 1) * TILE] for n in range(cols // TILE)], axis=0
    )


def early_kernel(plan, slc_ref, pairs_ref, early_ref, strips_ref, rim_ref, sems):
    me, strip = lax.axis_index("date"), lax.axis_index("strip")
    dates, late, cols = plan["dates"], plan["late"], plan["cols"]
    half = plan["devices"] // 2
    mate = lax.rem(me + half, 2 * half)
    mate_slot = jnp.where(mate < half, late, 0)
    start = pl.multiple_of(jnp.where(strip == 0, cols - TILE, 0), TILE)
    copies = [
        pltpu.make_async_copy(
            slc_ref.at[:, :, :, pl.ds(start, TILE)], rim_ref, sems.at[dates - late]
        )
    ]
    for k in range(dates - late):
        date = mate * dates + mate_slot + k
        wanted = pairs_ref[1, date * plan["per_date"] + NEAR] - me * dates
        wanted = jnp.clip(wanted, 0, dates - 1)
        copies.append(
            pltpu.make_async_copy(slc_ref.at[:, wanted], early_ref.at[:, k], sems.at[k])
        )
    run_copies(copies)
    tiles = []
    for k in range(dates - late):
        for c in range(2):
            left, right = early_ref[c, k, :, :TILE], early_ref[c, k, :, cols - TILE :]
            tiles.append(jnp.where(strip == 1, left, right))
    strips_ref[...] = gather_strips(tiles, 1 - strip)


def rim_kernel(slc_ref, rim_ref, sem):
    cols = slc_ref.shape[3]
    start = pl.multiple_of(jnp.where(lax.axis_index("strip") == 0, cols - TILE, 0), TILE)
    run_copies([pltpu.make_async_copy(slc_ref.at[:, :, :, pl.ds(start, TILE)], rim_ref, sem)])


def beside_kernel(plan, slc_ref, rim_ref, inner_ref, outer_ref, sems):
    me, strip = lax.axis_index("date"), lax.axis_index("strip")
    dates, rows = plan["dates"], plan["rows"]
    upper = me >= plan["devices"] // 2
    last = dates - NEAR
    copies = []
    firsts = (jnp.where(upper, last, 0), jnp.where(upper, 0, last))
    for r, (out_ref, first) in enumerate(zip((inner_ref, outer_ref), firsts)):
        for k in range(NEAR):
            for c in range(2):
                here = out_ref.at[pl.ds((2 * k + c) * rows, rows)]
                copies.append(
                    pltpu.make_async_copy(slc_ref.at[c, first + k], here, sems.at[r, k, c])
                )
    for copy in copies:
        copy.start()
    for out_ref, first in zip((inner_ref, outer_ref), firsts):
        tiles = [rim_ref[c, first + k] for k in range(NEAR) for c in range(2)]
        write_strips(out_ref, gather_strips(tiles, strip))
    for copy in copies:
        copy.wait()


def late_kernel(plan, slc_ref, rim_ref, inner_ref, pairs_ref, *refs):
    late_ref, tiles_ref = refs[-2:]
    me, strip = lax.axis_index("date"), lax.axis_index("strip")
    dates, late, rows = plan["dates"], plan["late"], plan["rows"]
    half = plan["devices"] // 2
    mate = lax.rem(me + half, 2 * half)
    mate_slot = jnp.where(mate < half, 0, dates - late)
    packed = read_strips(inner_ref, rows)
    for k in range(late):
        date = mate * dates + mate_slot + k
        wanted = pairs_ref[1, date * plan["per_date"] + NEAR] - me * dates
        own = (wanted >= 0) & (wanted < dates)
        own_at = jnp.clip(wanted, 0, dates - 1)
        other_at = jnp.clip(jnp.where(me < half, wanted - dates, wanted + NEAR), 0, NEAR - 1)
        for c in range(2):
            here = pl.ds((2 * k + c) * rows, rows)

            @pl.when(own)
            def _():
                late_ref[here] = slc_ref[c, own_at]
                tiles_ref[k, c] = rim_ref[c, own_at]

            @pl.when(jnp.logical_not(own))
            def _():
                there = pl.multiple_of((2 * other_at + c) * rows, rows)
                late_ref[here] = inner_ref[pl.ds(there, rows)]
                tiles_ref[k, c] = place_strip(packed, 2 * other_at + c, strip)

    tiles = [tiles_ref[k, c] for k in range(late) for c in range(2)]
    write_strips(late_ref, gather_strips(tiles, strip))


def bands_kernel(cols, out_ref):
    strip = lax.axis_index("strip")
    wide = out_ref.shape[3]
    reach = pl.program_id(0) + REACH_LO

    def band(places, targets):
        return (jnp.abs(places - targets) <= reach).astype(jnp.float32).astype(jnp.bfloat16)

    def indices(shape):
        return lax.broadcasted_iota(jnp.int32, shape, 0), lax.broadcasted_iota(jnp.int32, shape, 1)

    inside = band(*indices((wide, wide)))
    row, col = indices((TILE, wide))
    beyond = jnp.where(strip == 0, cols + row, row - TILE)
    first = band(jnp.where(row < INNER, wide + row, beyond), col)
    second = band(jnp.where(row < INNER, beyond, wide - TILE + row), col + wide)
    for n, part in enumerate((first, second)):
        out_ref[0, n, 0:wide] = inside
        out_ref[0, n, wide : 2 * wide] = inside
        out_ref[0, n, 2 * wide : 2 * wide + TILE] = part
        out_ref[0, n, 2 * wide + TILE : 2 * wide + 2 * TILE] = part


def split(values):
    high = values.astype(jnp.bfloat16)
    low = (values - high.astype(jnp.float32)).astype(jnp.bfloat16)
    return high, low


def put(ref, here, t, values):
    wide = 2 * TILE
    depth = 2 * wide + 2 * TILE
    for low, part in enumerate(split(values)):
        side = [n * depth + 2 * wide + low * TILE for n in range(2)]
        if t < 4:
            at = (t // 2) * depth + low * wide + (t % 2) * TILE
            ref[*here, at : at + TILE] = part
        if t == 2:
            ref[*here, side[0] : side[0] + INNER] = part[:, :INNER]
        if t == 1:
            ref[*here, side[1] + INNER : side[1] + TILE] = part[:, INNER:]
        if t == 4:
            ref[*here, side[0] + INNER : side[0] + TILE] = part[:, INNER:]
            ref[*here, side[1] : side[1] + INNER] = part[:, :INNER]


def tile_of(main, rim, t):
    return [
        (rim(c) if t == 4 else main(c, slice(t * TILE, (t + 1) * TILE))).astype(jnp.float32)
        for c in range(2)
    ]


class Pairs:
    def __init__(self, plan, lists, slc_ref, rim_ref, bands_ref, powers_ref, out_ref, scratch):
        self.plan = plan
        self.pairs_ref, self.az_ref, self.rng_ref = lists
        self.slc_ref, self.rim_ref = slc_ref, rim_ref
        self.bands_ref, self.powers_ref, self.out_ref = bands_ref, powers_ref, out_ref
        (self.left_ref, self.stack_ref, self.other_ref, self.other_rim_ref, self.stage_ref,
         self.count_ref, self.sems) = scratch
        self.me, self.strip = lax.axis_index("date"), lax.axis_index("strip")
        self.count_ref[0] = 0

    def partner(self, pair):
        return self.pairs_ref[1, pair]

    def own_other(self, index):
        return (
            lambda c, cols: self.slc_ref[c, index, :, cols],
            lambda c: self.rim_ref[c, index],
        )

    def fetched_other(self):
        return (
            lambda c, cols: self.other_ref[c, :, cols],
            lambda c: self.other_rim_ref[c],
        )

    def fetch_payload(self, ref, index):
        rows = self.plan["rows"]
        packed = read_strips(ref, rows)
        for c in range(2):
            at = pl.multiple_of((2 * index + c) * rows, rows)
            self.other_ref[c] = ref[pl.ds(at, rows)]
            self.other_rim_ref[c] = place_strip(packed, 2 * index + c, self.strip)

    def out_copy(self, slot, pair):
        return pltpu.make_async_copy(
            self.stage_ref.at[slot], self.out_ref.at[:, pair], self.sems.at[slot]
        )

    def finish(self):
        count = self.count_ref[0]

        @pl.when(count >= 1)
        def _():
            self.out_copy(lax.rem(count + 1, 2), 0).wait()

        @pl.when(count >= 2)
        def _():
            self.out_copy(lax.rem(count, 2), 0).wait()

    def run(self, slot, kind, other, other_power=None):
        plan, left_ref, stack_ref = self.plan, self.left_ref, self.stack_ref
        rows, dates, per_date = plan["rows"], plan["dates"], plan["per_date"]
        count = self.count_ref[0]
        stage = lax.rem(count, 2)

        @pl.when(count >= 2)
        def _():
            self.out_copy(stage, 0).wait()

        pair = (self.me * dates + slot) * per_date + kind
        height = self.az_ref[pair]
        width = jnp.clip(self.rng_ref[pair] - REACH_LO, 0, HALO - REACH_LO)
        part = [(pl.ds(f * rows, rows),) for f in range(4)]
        left_ref[*part[2]] = self.powers_ref[slot]
        if other_power is not None:
            left_ref[*part[3]] = self.powers_ref[other_power]
        first = self.own_other(slot)
        for t in range(5):
            a_real, a_imag = tile_of(*first, t)
            b_real, b_imag = tile_of(*other, t)
            put(left_ref, part[0], t, a_real * b_real + a_imag * b_imag)
            put(left_ref, part[1], t, a_imag * b_real - a_real * b_imag)
            if other_power is None:
                put(left_ref, part[3], t, b_real * b_real + b_imag * b_imag)
        depth = self.bands_ref.shape[2]
        wide = self.bands_ref.shape[3]
        for n in range(2):
            ranged = jnp.dot(
                left_ref[:, n * depth : (n + 1) * depth],
                self.bands_ref[width, n],
                preferred_element_type=jnp.float32,
            )
            for low, values in enumerate(split(ranged)):
                for f in range(4):
                    stack_ref[f, low * rows : (low + 1) * rows, n * wide : (n + 1) * wide] = values[
                        f * rows : (f + 1) * rows
                    ]
        row = lax.broadcasted_iota(jnp.int32, (rows, 2 * rows), 0)
        col = lax.broadcasted_iota(jnp.int32, (rows, 2 * rows), 1)
        col = jnp.where(col < rows, col, col - rows)
        band = (jnp.abs(row - col) <= height).astype(jnp.float32).astype(jnp.bfloat16)
        looked = [
            jnp.dot(band, stack_ref[f], preferred_element_type=jnp.float32) for f in range(4)
        ]
        inverse = lax.rsqrt(looked[2] * looked[3] + EPSILON)
        for c in range(2):
            self.stage_ref[stage, c] = looked[c] * inverse
        self.out_copy(stage, slot * per_date + kind).start()
        self.count_ref[0] = count + 1


def own_kernel(plan, lists, slc_ref, rim_ref, bands_ref, out_ref, powers_ref, *scratch):
    pairs = Pairs(plan, lists, slc_ref, rim_ref, bands_ref, powers_ref, out_ref, scratch)
    dates = plan["dates"]

    def power(slot, carry):
        for t in range(5):
            real, imag = tile_of(*pairs.own_other(slot), t)
            put(powers_ref, (slot, slice(None)), t, real * real + imag * imag)
        return carry

    lax.fori_loop(0, dates, power, 0)

    def step(n, carry):
        slot, kind = n // NEAR, lax.rem(n, NEAR)
        pair = (pairs.me * dates + slot) * plan["per_date"] + kind
        local = pairs.partner(pair) - pairs.me * dates

        @pl.when((local >= 0) & (local < dates))
        def _():
            pairs.run(slot, kind, pairs.own_other(local), local)

        return carry

    lax.fori_loop(0, dates * NEAR, step, 0)
    pairs.finish()


def rest_kernel(plan, lists, slc_ref, rim_ref, bands_ref, powers_ref, inner_ref, outer_ref,
                middle_ref, _, out_ref, *scratch):
    pairs = Pairs(plan, lists, slc_ref, rim_ref, bands_ref, powers_ref, out_ref, scratch)
    dates, half = plan["dates"], plan["devices"] // 2
    upper = pairs.me >= half
    if plan["halves"]:
        in_middle = jnp.where(upper, pairs.me == half, pairs.me == half - 1)
    else:
        upper, in_middle = True, False

    def step(n, carry):
        slot, kind = n // NEAR, lax.rem(n, NEAR)
        pair = (pairs.me * dates + slot) * plan["per_date"] + kind
        local = pairs.partner(pair) - pairs.me * dates
        below = local < 0
        index = jnp.clip(jnp.where(below, local + NEAR, local - dates), 0, NEAR - 1)
        inner = below == upper

        @pl.when(below | (local >= dates))
        def _():
            middle = inner & in_middle
            pl.when(middle)(lambda: pairs.fetch_payload(middle_ref, index))
            pl.when(inner & jnp.logical_not(middle))(
                lambda: pairs.fetch_payload(inner_ref, index)
            )
            pl.when(jnp.logical_not(inner))(lambda: pairs.fetch_payload(outer_ref, index))
            pairs.run(slot, kind, pairs.fetched_other())

        return carry

    lax.fori_loop(0, dates * NEAR, step, 0)
    pairs.finish()


def annual_kernel(plan, is_late, lists, slc_ref, rim_ref, bands_ref, powers_ref, inner_ref,
                  outer_ref, images_ref, strips_ref, _, out_ref, *scratch):
    pairs = Pairs(plan, lists, slc_ref, rim_ref, bands_ref, powers_ref, out_ref, scratch)
    dates, late, rows = plan["dates"], plan["late"], plan["rows"]
    half = plan["devices"] // 2
    me, split_date = pairs.me, half * dates
    lower = me < half
    mate = jnp.where(lower, 1, 0)
    if is_late:
        base, count = jnp.where(lower, 0, dates - late), late
    else:
        base, count = jnp.where(lower, late, 0), dates - late

    def fetch_early(k):
        packed = strips_ref[...]
        for c in range(2):
            pairs.other_ref[c] = images_ref[mate, c, k]
            pairs.other_rim_ref[c] = place_strip(packed, 2 * k + c, pairs.strip)

    def step(k, carry):
        slot = base + k
        date = me * dates + slot
        other = pairs.partner(date * plan["per_date"] + NEAR)
        far = (other < split_date) == lower
        from_inner = jnp.where(lower, me != 0, me == half)
        inner_at = jnp.where(lower, other, other - (2 * split_date - NEAR))
        outer_at = jnp.where(lower, other - (split_date - NEAR), other - split_date)

        @pl.when(far & from_inner)
        def _():
            pairs.fetch_payload(inner_ref, jnp.clip(inner_at, 0, NEAR - 1))

        @pl.when(far & jnp.logical_not(from_inner))
        def _():
            pairs.fetch_payload(outer_ref, jnp.clip(outer_at, 0, NEAR - 1))

        @pl.when(jnp.logical_not(far))
        def _():
            if is_late:
                pairs.fetch_payload(images_ref.at[mate], k)
            else:
                fetch_early(k)

        pairs.run(slot, NEAR, pairs.fetched_other())
        return carry

    lax.fori_loop(0, count, step, 0)
    pairs.finish()


def plain_kernel(plan, lists, slc_ref, rim_ref, bands_ref, powers_ref, images_ref,
                 image_rim_ref, _, out_ref, *scratch):
    pairs = Pairs(plan, lists, slc_ref, rim_ref, bands_ref, powers_ref, out_ref, scratch)

    def step(slot, carry):
        other = (
            lambda c, cols: images_ref[c, slot, :, cols],
            lambda c: image_rim_ref[c, slot],
        )
        pairs.run(slot, NEAR, other)
        return carry

    lax.fori_loop(0, plan["dates"], step, 0)
    pairs.finish()


def arrivals_by_distance(slc, pair_list, plan):
    dates, per_date, devices = plan["dates"], plan["per_date"], plan["devices"]
    total = dates * devices
    me = lax.axis_index("date")
    annual_of = pair_list[:, 1].reshape(total, per_date)[:, per_date - 1]
    sums = [None] * dates
    for direction in (1, -1):
        by_distance = {}
        for slot in range(dates):
            for gap in range(plan["year"], plan["year"] + 3):
                distance = (slot + direction * gap) // dates
                by_distance.setdefault(distance, set()).add(slot)
        for distance in sorted(by_distance):
            slots = sorted(by_distance[distance])
            wanted_by = (me - distance) * dates + jnp.array(slots, dtype=jnp.int32)
            inside = (wanted_by >= 0) & (wanted_by < total)
            local = jnp.take(annual_of, jnp.clip(wanted_by, 0, total - 1)) - me * dates
            usable = inside & (local >= 0) & (local < dates)
            packed = jnp.take(slc, jnp.clip(local, 0, dates - 1), axis=1)
            packed = jnp.where(usable[None, :, None, None], packed, jnp.zeros_like(packed))
            route = [(i + distance, i) for i in range(devices) if 0 <= i + distance < devices]
            arrived = lax.ppermute(packed, "date", route)
            for n, slot in enumerate(slots):
                part = arrived[:, n]
                sums[slot] = part if sums[slot] is None else sums[slot] + part
    return jnp.stack(sums, axis=1)


def payload_of(images, rim, strip):
    planes, count, rows, cols = images.shape
    edges = jnp.where(strip == 0, rim[..., :HALO], rim[..., TILE - HALO :])
    edges = jnp.transpose(edges, (2, 1, 0, 3)).reshape(rows, count * planes * HALO)
    edges = jnp.pad(edges, ((0, 0), (0, TILE - edges.shape[1])))
    part = rows * TILE // cols
    edges = jnp.transpose(edges.reshape(rows // part, part, TILE), (1, 0, 2)).reshape(part, cols)
    stacked = jnp.transpose(images, (1, 0, 2, 3)).reshape(count * planes * rows, cols)
    return jnp.concatenate([stacked, edges], axis=0)


def body(slc, pair_list, az_half, rng_half):
    planes, dates, rows, cols = slc.shape
    devices = lax.axis_size("date")
    total = dates * devices
    per_date = pair_list.shape[0] // total
    year = min(YEAR, total // 2 - 2)
    half = devices // 2
    late = half * dates - year
    halves = devices % 2 == 0 and 0 < late <= NEAR and 2 * late <= dates
    halves = halves and 2 * (dates - late) * HALO <= TILE
    plan = {
        "dates": dates,
        "devices": devices,
        "per_date": per_date,
        "year": year,
        "late": late,
        "rows": rows,
        "cols": cols,
        "pairs": total * per_date,
        "halves": halves,
    }
    dtype = slc.dtype
    rim_rows = rows * TILE // cols
    lists = (pair_list.T, az_half, rng_half)
    swap_strips = [(0, 1), (1, 0)]

    def images(count):
        return jax.ShapeDtypeStruct((planes, count, rows, cols), dtype)

    def rim_shape(count):
        return jax.ShapeDtypeStruct((planes, count, rows, TILE), dtype)

    def payload_shape(count):
        return jax.ShapeDtypeStruct((planes * count * rows + rim_rows, cols), dtype)

    def swapped_rims(values):
        out = pl.pallas_call(
            rim_kernel,
            out_shape=rim_shape(values.shape[1]),
            in_specs=[ANY],
            out_specs=VMEM,
            scratch_shapes=[pltpu.SemaphoreType.DMA],
            compiler_params=limit(4),
            name="rim_blocks",
        )(values)
        return lax.ppermute(out, "strip", swap_strips)

    wide = cols // 2
    widths = HALO - REACH_LO + 1
    band_shape = (2, 2 * wide + 2 * TILE, wide)
    bands = pl.pallas_call(
        functools.partial(bands_kernel, cols),
        grid=(widths,),
        out_shape=jax.ShapeDtypeStruct((widths, *band_shape), jnp.bfloat16),
        out_specs=pl.BlockSpec((1, *band_shape), lambda n: (n, 0, 0, 0)),
        compiler_params=limit(4),
        name="range_bands",
    )()
    if halves:
        swap = [(i, (i + half) % devices) for i in range(devices)]
        mates = [[i, i + half] for i in range(half)]
        early, strips, rim = pl.pallas_call(
            functools.partial(early_kernel, plan),
            out_shape=(
                images(dates - late),
                jax.ShapeDtypeStruct((rows, TILE), dtype),
                rim_shape(dates),
            ),
            in_specs=[ANY, SMEM],
            out_specs=(VMEM, VMEM, VMEM),
            scratch_shapes=[pltpu.SemaphoreType.DMA((dates - late + 1,))],
            compiler_params=limit(56),
            name="early_images",
        )(slc, lists[0])
        early = lax.all_gather(early, "date", axis_index_groups=mates)
        rim = lax.ppermute(rim, "strip", swap_strips)
        strips = lax.ppermute(
            strips, ("date", "strip"), [(2 * a + s, 2 * b + 1 - s) for a, b in swap for s in (0, 1)]
        )
        inner, outer = pl.pallas_call(
            functools.partial(beside_kernel, plan),
            out_shape=(payload_shape(NEAR), payload_shape(NEAR)),
            in_specs=[ANY, VMEM],
            out_specs=(VMEM, VMEM),
            scratch_shapes=[pltpu.SemaphoreType.DMA((2, NEAR, 2))],
            compiler_params=limit(56),
            name="beside_images",
        )(slc, rim)
        down = [(i, (i - 1) % half) for i in range(half)]
        down += [(half + i, half + (i + 1) % half) for i in range(half)]
        middle = lax.ppermute(outer, "date", [(half - 1, half), (half, half - 1)])
        inner = lax.ppermute(inner, "date", down)
        outer = lax.ppermute(outer, "date", [(b, a) for a, b in down])
    else:
        rim = swapped_rims(slc)
        annual = arrivals_by_distance(slc, pair_list, plan)
        strip = lax.axis_index("strip")
        ups = [(i, i + 1) for i in range(devices - 1)]
        inner = payload_of(slc[:, dates - NEAR :], rim[:, dates - NEAR :], strip)
        outer = payload_of(slc[:, :NEAR], rim[:, :NEAR], strip)
        inner = lax.ppermute(inner, "date", ups)
        outer = lax.ppermute(outer, "date", [(b, a) for a, b in ups])
        middle = inner

    out_shape = jax.ShapeDtypeStruct((planes, dates * per_date, rows, cols), jnp.float32)
    depth = 2 * band_shape[1]
    scratch = [
        pltpu.VMEM((4 * rows, depth), jnp.bfloat16),
        pltpu.VMEM((4, 2 * rows, cols), jnp.bfloat16),
        pltpu.VMEM((planes, rows, cols), dtype),
        pltpu.VMEM((planes, rows, TILE), dtype),
        pltpu.VMEM((2, planes, rows, cols), jnp.float32),
        pltpu.SMEM((1,), jnp.int32),
        pltpu.SemaphoreType.DMA((2,)),
    ]

    def cost(flops):
        return pl.CostEstimate(flops=flops, bytes_accessed=1, transcendentals=0)

    out, powers = pl.pallas_call(
        lambda *refs: own_kernel(plan, refs[:3], *refs[3:]),
        out_shape=(out_shape, jax.ShapeDtypeStruct((dates, rows, depth), jnp.bfloat16)),
        in_specs=[SMEM] * 3 + [VMEM] * 3,
        out_specs=(ANY, VMEM),
        scratch_shapes=scratch,
        compiler_params=limit(24),
        cost_estimate=cost(20_000_000_000),
        name="own_pairs",
    )(*lists, slc, rim, bands)

    def more_pairs(kernel, out, others, name):
        return pl.pallas_call(
            lambda *refs: kernel(plan, refs[:3], *refs[3:]),
            out_shape=out_shape,
            in_specs=[SMEM] * 3 + [VMEM] * (4 + len(others)) + [ANY],
            out_specs=ANY,
            scratch_shapes=scratch,
            input_output_aliases={7 + len(others): 0},
            compiler_params=limit(24),
            cost_estimate=cost(1),
            name=name,
        )(*lists, slc, rim, bands, powers, *others, out)

    if halves:
        payload = pl.pallas_call(
            functools.partial(late_kernel, plan),
            out_shape=payload_shape(late),
            in_specs=[VMEM, VMEM, VMEM, SMEM, ANY, ANY],
            out_specs=VMEM,
            scratch_shapes=[pltpu.VMEM((late, planes, rows, TILE), dtype)],
            compiler_params=limit(4),
            name="late_images",
        )(slc, rim, inner, lists[0], powers, strips)
        payload = lax.all_gather(payload, "date", axis_index_groups=mates)
    out = more_pairs(rest_kernel, out, (inner, outer, middle), "near_pairs")
    if halves:
        kernel = lambda plan, *refs: annual_kernel(plan, False, *refs)
        out = more_pairs(kernel, out, (inner, outer, early, strips), "annual_pairs")
        kernel = lambda plan, *refs: annual_kernel(plan, True, *refs)
        out = more_pairs(kernel, out, (inner, outer, payload, strips), "last_pairs")
    else:
        out = more_pairs(plain_kernel, out, (annual, swapped_rims(annual)), "annual_pairs")
    return out


def solution(mesh):
    placed = (P(None, "date", "groups", "strip"), P(), P(), P())
    return jax.shard_map(
        body,
        mesh=mesh,
        in_specs=placed,
        out_specs=P(None, "date", "groups", "strip"),
        check_vma=False,
    )
```

```python
import functools

import jax
import jax.numpy as jnp
from jax import lax
from jax.experimental import pallas as pl
from jax.experimental.pallas import tpu as pltpu
from jax.sharding import PartitionSpec as P

HALO = 16
REACH_LO = 12
NEAR = 3
YEAR = 29
EPSILON = 1e-06
TILE = 128
INNER = TILE // 2
WORK_MIB = 16
FIRST_MIB = 56
ANY = pl.BlockSpec(memory_space=pl.ANY)
SMEM = pl.BlockSpec(memory_space=pltpu.SMEM)
VMEM = pl.BlockSpec(memory_space=pltpu.VMEM)


def limit(mebibytes):
    return pltpu.CompilerParams(vmem_limit_bytes=mebibytes * 1024 * 1024)


def run_copies(copies):
    for copy in copies:
        copy.start()
    for copy in copies:
        copy.wait()


def gather_strips(tiles, side):
    lane = lax.broadcasted_iota(jnp.int32, tiles[0].shape, 1)
    packed = jnp.zeros(tiles[0].shape, jnp.float32)
    for n, tile in enumerate(tiles):
        spot = n * HALO
        moved = pltpu.roll(tile.astype(jnp.float32), spot + side * HALO, 1)
        packed = jnp.where((lane >= spot) & (lane < spot + HALO), moved, packed)
    return packed.astype(jnp.bfloat16)


def place_strip(packed, n, side):
    shift = 2 * TILE - (n + side) * HALO
    return pltpu.roll(packed.astype(jnp.float32), lax.rem(shift, TILE), 1).astype(jnp.bfloat16)


def write_strips(out_ref, packed):
    rows, cols = packed.shape[0], out_ref.shape[1]
    part = rows * TILE // cols
    base = out_ref.shape[0] - part
    for n in range(rows // part):
        out_ref[base:, n * TILE : (n + 1) * TILE] = packed[n * part : (n + 1) * part]


def read_strips(ref, rows):
    cols = ref.shape[1]
    base = ref.shape[0] - rows * TILE // cols
    return jnp.concatenate(
        [ref[base:, n * TILE : (n + 1) * TILE] for n in range(cols // TILE)], axis=0
    )


def wanted_images(plan, pairs_ref):
    me = lax.axis_index("date")
    dates, half = plan["dates"], plan["devices"] // 2
    mate = lax.rem(me + half, 2 * half)
    wanted = []
    for k in range(dates - plan["late"]):
        date = mate * dates + jnp.where(mate < half, plan["late"], 0) + k
        at = pairs_ref[1, date * plan["per_date"] + NEAR] - me * dates
        wanted.append(jnp.clip(at, 0, dates - 1))
    return wanted


def image_copies(slc_ref, wanted, early_ref, sems):
    return [
        pltpu.make_async_copy(slc_ref.at[:, at], early_ref.at[:, k], sems.at[k])
        for k, at in enumerate(wanted)
    ]


def early_kernel(plan, slc_ref, pairs_ref, early_ref, rim_ref, strips_ref, tiles_ref, sems,
                 tile_sems, rim_sem):
    strip, cols = lax.axis_index("strip"), plan["cols"]
    start = pl.multiple_of(jnp.where(strip == 0, cols - TILE, 0), TILE)
    wanted = wanted_images(plan, pairs_ref)
    rim_copy = pltpu.make_async_copy(slc_ref.at[:, :, :, pl.ds(start, TILE)], rim_ref, rim_sem)
    early_copies = image_copies(slc_ref, wanted, early_ref, sems)
    tile_copies = [
        pltpu.make_async_copy(
            slc_ref.at[:, at, :, pl.ds(start, TILE)], tiles_ref.at[k], tile_sems.at[k]
        )
        for k, at in enumerate(wanted)
    ]
    for copy in tile_copies + [rim_copy]:
        copy.start()

    @pl.when(strip == 0)
    def _():
        for copy in early_copies:
            copy.start()

    for copy in tile_copies:
        copy.wait()
    tiles = [tiles_ref[k, c] for k in range(len(wanted)) for c in range(2)]
    strips_ref[...] = gather_strips(tiles, 1 - strip)
    rim_copy.wait()

    @pl.when(strip == 0)
    def _():
        for copy in early_copies:
            copy.wait()


def rim_kernel(slc_ref, rim_ref, sem):
    cols = slc_ref.shape[3]
    start = pl.multiple_of(jnp.where(lax.axis_index("strip") == 0, cols - TILE, 0), TILE)
    run_copies([pltpu.make_async_copy(slc_ref.at[:, :, :, pl.ds(start, TILE)], rim_ref, sem)])


def beside_kernel(plan, slc_ref, pairs_ref, rim_ref, inner_ref, outer_ref, early_ref, sems,
                  early_sems):
    me, strip = lax.axis_index("date"), lax.axis_index("strip")
    dates, rows = plan["dates"], plan["rows"]
    upper = me >= plan["devices"] // 2
    last = dates - NEAR
    copies = []
    firsts = (jnp.where(upper, last, 0), jnp.where(upper, 0, last))
    for r, (out_ref, first) in enumerate(zip((inner_ref, outer_ref), firsts)):
        for k in range(NEAR):
            for c in range(2):
                here = out_ref.at[pl.ds((2 * k + c) * rows, rows)]
                copies.append(
                    pltpu.make_async_copy(slc_ref.at[c, first + k], here, sems.at[r, k, c])
                )
    for copy in copies:
        copy.start()
    early_copies = image_copies(
        slc_ref, wanted_images(plan, pairs_ref), early_ref, early_sems
    )

    @pl.when(strip == 1)
    def _():
        for copy in early_copies:
            copy.start()

    for out_ref, first in zip((inner_ref, outer_ref), firsts):
        tiles = [rim_ref[c, first + k] for k in range(NEAR) for c in range(2)]
        write_strips(out_ref, gather_strips(tiles, strip))
    for copy in copies:
        copy.wait()

    @pl.when(strip == 1)
    def _():
        for copy in early_copies:
            copy.wait()


def late_kernel(plan, slc_ref, rim_ref, inner_ref, pairs_ref, *refs):
    late_ref, tiles_ref = refs[-2:]
    me, strip = lax.axis_index("date"), lax.axis_index("strip")
    dates, late, rows = plan["dates"], plan["late"], plan["rows"]
    half = plan["devices"] // 2
    mate = lax.rem(me + half, 2 * half)
    mate_slot = jnp.where(mate < half, 0, dates - late)
    packed = read_strips(inner_ref, rows)
    for k in range(late):
        date = mate * dates + mate_slot + k
        wanted = pairs_ref[1, date * plan["per_date"] + NEAR] - me * dates
        own = (wanted >= 0) & (wanted < dates)
        own_at = jnp.clip(wanted, 0, dates - 1)
        other_at = jnp.clip(jnp.where(me < half, wanted - dates, wanted + NEAR), 0, NEAR - 1)
        for c in range(2):
            here = pl.ds((2 * k + c) * rows, rows)

            @pl.when(own)
            def _():
                late_ref[here] = slc_ref[c, own_at]
                tiles_ref[k, c] = rim_ref[c, own_at]

            @pl.when(jnp.logical_not(own))
            def _():
                there = pl.multiple_of((2 * other_at + c) * rows, rows)
                late_ref[here] = inner_ref[pl.ds(there, rows)]
                tiles_ref[k, c] = place_strip(packed, 2 * other_at + c, strip)

    tiles = [tiles_ref[k, c] for k in range(late) for c in range(2)]
    write_strips(late_ref, gather_strips(tiles, strip))


def bands_kernel(cols, out_ref):
    strip = lax.axis_index("strip")
    wide = out_ref.shape[3]
    reach = pl.program_id(0) + REACH_LO

    def band(places, targets):
        return (jnp.abs(places - targets) <= reach).astype(jnp.float32).astype(jnp.bfloat16)

    def indices(shape):
        return lax.broadcasted_iota(jnp.int32, shape, 0), lax.broadcasted_iota(jnp.int32, shape, 1)

    inside = band(*indices((wide, wide)))
    row, col = indices((TILE, wide))
    beyond = jnp.where(strip == 0, cols + row, row - TILE)
    first = band(jnp.where(row < INNER, wide + row, beyond), col)
    second = band(jnp.where(row < INNER, beyond, wide - TILE + row), col + wide)
    for n, part in enumerate((first, second)):
        out_ref[0, n, 0:wide] = inside
        out_ref[0, n, wide : 2 * wide] = inside
        out_ref[0, n, 2 * wide : 2 * wide + TILE] = part
        out_ref[0, n, 2 * wide + TILE : 2 * wide + 2 * TILE] = part


def split(values):
    high = values.astype(jnp.bfloat16)
    low = (values - high.astype(jnp.float32)).astype(jnp.bfloat16)
    return high, low


def put(ref, here, t, values):
    wide = 2 * TILE
    depth = 2 * wide + 2 * TILE
    for low, part in enumerate(split(values)):
        side = [n * depth + 2 * wide + low * TILE for n in range(2)]
        if t < 4:
            at = (t // 2) * depth + low * wide + (t % 2) * TILE
            ref[*here, at : at + TILE] = part
        if t == 2:
            ref[*here, side[0] : side[0] + INNER] = part[:, :INNER]
        if t == 1:
            ref[*here, side[1] + INNER : side[1] + TILE] = part[:, INNER:]
        if t == 4:
            ref[*here, side[0] + INNER : side[0] + TILE] = part[:, INNER:]
            ref[*here, side[1] : side[1] + INNER] = part[:, :INNER]


def tile_of(main, rim, t):
    return [
        (rim(c) if t == 4 else main(c, slice(t * TILE, (t + 1) * TILE))).astype(jnp.float32)
        for c in range(2)
    ]


class Pairs:
    def __init__(self, plan, lists, slc_ref, rim_ref, bands_ref, powers_ref, out_ref, scratch):
        self.plan = plan
        self.pairs_ref, self.az_ref, self.rng_ref = lists
        self.slc_ref, self.rim_ref = slc_ref, rim_ref
        self.bands_ref, self.powers_ref, self.out_ref = bands_ref, powers_ref, out_ref
        (self.left_ref, self.stack_ref, self.other_ref, self.other_rim_ref, self.stage_ref,
         self.list_ref, self.sems) = scratch
        self.me, self.strip = lax.axis_index("date"), lax.axis_index("strip")

    def partner(self, pair):
        return self.pairs_ref[1, pair]

    def near_item(self, n):
        slot, kind = n // NEAR, lax.rem(n, NEAR)
        dates = self.plan["dates"]
        pair = (self.me * dates + slot) * self.plan["per_date"] + kind
        return slot, kind, self.partner(pair) - self.me * dates

    def near_list(self, own):
        count = 0
        for n in range(self.plan["dates"] * NEAR):
            local = self.near_item(n)[2]
            inside = (local >= 0) & (local < self.plan["dates"])
            self.list_ref[count] = n
            count = count + jnp.where(inside == own, 1, 0)
        return count

    def own_other(self, index):
        return (
            lambda c, cols: self.slc_ref[c, index, :, cols],
            lambda c: self.rim_ref[c, index],
        )

    def fetched_other(self, x):
        return (
            lambda c, cols: self.other_ref[x, c, :, cols],
            lambda c: self.other_rim_ref[x, c],
        )

    def fetch_payload(self, x, ref, index):
        rows = self.plan["rows"]
        packed = read_strips(ref, rows)
        for c in range(2):
            at = pl.multiple_of((2 * index + c) * rows, rows)
            self.other_ref[x, c] = ref[pl.ds(at, rows)]
            self.other_rim_ref[x, c] = place_strip(packed, 2 * index + c, self.strip)

    def out_copy(self, stage, x, pair):
        return pltpu.make_async_copy(
            self.stage_ref.at[stage, x], self.out_ref.at[:, pair], self.sems.at[stage, x]
        )

    def run(self, count, work):
        steps = (count + 1) // 2

        def step(n, carry):
            stage = lax.rem(n, 2)

            @pl.when(n >= 2)
            def _():
                for x in range(2):
                    self.out_copy(stage, x, 0).wait()

            items = [work(x, jnp.minimum(2 * n + x, count - 1)) for x in range(2)]
            self.compute(stage, items)
            for x, (slot, kind, _, _) in enumerate(items):
                copy = self.out_copy(stage, x, slot * self.plan["per_date"] + kind)
                pl.when(2 * n + x < count)(copy.start)
            return carry

        lax.fori_loop(0, steps, step, 0)
        for back in (2, 1):
            for x in range(2):
                used = (steps >= back) & (2 * (steps - back) + x < count)
                pl.when(used)(self.out_copy(lax.rem(steps + back, 2), x, 0).wait)

    def compute(self, stage, items):
        plan = self.plan
        rows, dates, per_date = plan["rows"], plan["dates"], plan["per_date"]
        part = [(pl.ds(f * rows, rows),) for f in range(4)]
        depth = self.bands_ref.shape[2]
        wide = self.bands_ref.shape[3]
        heights, widths = [], []
        for slot, kind, _, _ in items:
            pair = (self.me * dates + slot) * per_date + kind
            heights.append(self.az_ref[pair])
            widths.append(jnp.clip(self.rng_ref[pair] - REACH_LO, 0, HALO - REACH_LO))
        for x, (slot, kind, other, other_power) in enumerate(items):
            left_ref = self.left_ref.at[x]
            left_ref[*part[2]] = self.powers_ref[slot]
            if other_power is not None:
                left_ref[*part[3]] = self.powers_ref[other_power]
            first = self.own_other(slot)
            for t in range(5):
                a_real, a_imag = tile_of(*first, t)
                b_real, b_imag = tile_of(*other, t)
                put(left_ref, part[0], t, a_real * b_real + a_imag * b_imag)
                put(left_ref, part[1], t, a_imag * b_real - a_real * b_imag)
                if other_power is None:
                    put(left_ref, part[3], t, b_real * b_real + b_imag * b_imag)
        for n in range(2):
            for x in range(2):
                ranged = jnp.dot(
                    self.left_ref[x, :, n * depth : (n + 1) * depth],
                    self.bands_ref[widths[x], n],
                    preferred_element_type=jnp.float32,
                )
                there = slice(n * wide, (n + 1) * wide)
                for low, values in enumerate(split(ranged)):
                    for f in range(4):
                        self.stack_ref[x, f, low * rows : (low + 1) * rows, there] = values[
                            f * rows : (f + 1) * rows
                        ]
        row = lax.broadcasted_iota(jnp.int32, (rows, 2 * rows), 0)
        col = lax.broadcasted_iota(jnp.int32, (rows, 2 * rows), 1)
        col = jnp.where(col < rows, col, col - rows)
        for x in range(2):
            band = (jnp.abs(row - col) <= heights[x]).astype(jnp.float32).astype(jnp.bfloat16)
            looked = [
                jnp.dot(band, self.stack_ref[x, f], preferred_element_type=jnp.float32)
                for f in range(4)
            ]
            inverse = lax.rsqrt(looked[2] * looked[3] + EPSILON)
            for c in range(2):
                self.stage_ref[stage, x, c] = looked[c] * inverse


def own_kernel(plan, lists, slc_ref, rim_ref, bands_ref, out_ref, powers_ref, *scratch):
    pairs = Pairs(plan, lists, slc_ref, rim_ref, bands_ref, powers_ref, out_ref, scratch)
    dates = plan["dates"]

    def power(slot, carry):
        for t in range(5):
            real, imag = tile_of(*pairs.own_other(slot), t)
            put(powers_ref, (slot, slice(None)), t, real * real + imag * imag)
        return carry

    lax.fori_loop(0, dates, power, 0)

    def work(x, n):
        slot, kind, local = pairs.near_item(pairs.list_ref[n])
        return slot, kind, pairs.own_other(local), local

    pairs.run(pairs.near_list(True), work)


def rest_kernel(plan, lists, slc_ref, rim_ref, bands_ref, powers_ref, inner_ref, outer_ref,
                middle_ref, _, out_ref, *scratch):
    pairs = Pairs(plan, lists, slc_ref, rim_ref, bands_ref, powers_ref, out_ref, scratch)
    dates, half = plan["dates"], plan["devices"] // 2
    if plan["halves"]:
        upper = pairs.me >= half
        in_middle = jnp.where(upper, pairs.me == half, pairs.me == half - 1)
    else:
        upper, in_middle = True, False

    def work(x, n):
        slot, kind, local = pairs.near_item(pairs.list_ref[n])
        below = local < 0
        index = jnp.clip(jnp.where(below, local + NEAR, local - dates), 0, NEAR - 1)
        inner = below == upper
        middle = inner & in_middle
        sources = (
            (jnp.logical_not(inner), outer_ref),
            (inner & jnp.logical_not(middle), inner_ref),
            (middle, middle_ref),
        )
        for chosen, ref in sources:
            pl.when(chosen)(functools.partial(pairs.fetch_payload, x, ref, index))
        return slot, kind, pairs.fetched_other(x), None

    pairs.run(pairs.near_list(False), work)


def annual_kernel(plan, is_late, lists, slc_ref, rim_ref, bands_ref, powers_ref, inner_ref,
                  outer_ref, images_ref, more_ref, strips_ref, _, out_ref, *scratch):
    pairs = Pairs(plan, lists, slc_ref, rim_ref, bands_ref, powers_ref, out_ref, scratch)
    dates, late = plan["dates"], plan["late"]
    half = plan["devices"] // 2
    me, split_date = pairs.me, half * dates
    lower = me < half
    if is_late:
        base, count = jnp.where(lower, 0, dates - late), late
    else:
        base, count = jnp.where(lower, late, 0), dates - late

    def fetch_early(x, k, ref):
        packed = strips_ref[...]
        for c in range(2):
            pairs.other_ref[x, c] = ref[c, k]
            pairs.other_rim_ref[x, c] = place_strip(packed, 2 * k + c, pairs.strip)

    def work(x, k):
        slot = base + k
        date = me * dates + slot
        other = pairs.partner(date * plan["per_date"] + NEAR)
        far = (other < split_date) == lower
        from_inner = jnp.where(lower, me != 0, me == half)
        inner_at = jnp.where(lower, other, other - (2 * split_date - NEAR))
        outer_at = jnp.where(lower, other - (split_date - NEAR), other - split_date)
        inner_at, outer_at = jnp.clip(inner_at, 0, NEAR - 1), jnp.clip(outer_at, 0, NEAR - 1)
        fetch = pairs.fetch_payload
        pl.when(far & from_inner)(lambda: fetch(x, inner_ref, inner_at))
        pl.when(far & jnp.logical_not(from_inner))(lambda: fetch(x, outer_ref, outer_at))
        near_side = jnp.logical_not(far)
        if is_late:
            pl.when(near_side)(lambda: fetch(x, images_ref, k))
        else:
            first = pairs.strip == 0
            pl.when(near_side & first)(lambda: fetch_early(x, k, images_ref))
            pl.when(near_side & jnp.logical_not(first))(lambda: fetch_early(x, k, more_ref))
        return slot, NEAR, pairs.fetched_other(x), None

    pairs.run(count, work)


def plain_kernel(plan, lists, slc_ref, rim_ref, bands_ref, powers_ref, images_ref,
                 image_rim_ref, _, out_ref, *scratch):
    pairs = Pairs(plan, lists, slc_ref, rim_ref, bands_ref, powers_ref, out_ref, scratch)

    def work(x, slot):
        other = (
            lambda c, cols: images_ref[c, slot, :, cols],
            lambda c: image_rim_ref[c, slot],
        )
        return slot, NEAR, other, None

    pairs.run(plan["dates"], work)


def arrivals_by_distance(slc, pair_list, plan):
    dates, per_date, devices = plan["dates"], plan["per_date"], plan["devices"]
    total = dates * devices
    me = lax.axis_index("date")
    annual_of = pair_list[:, 1].reshape(total, per_date)[:, per_date - 1]
    sums = [None] * dates
    for direction in (1, -1):
        by_distance = {}
        for slot in range(dates):
            for gap in range(plan["year"], plan["year"] + 3):
                distance = (slot + direction * gap) // dates
                by_distance.setdefault(distance, set()).add(slot)
        for distance in sorted(by_distance):
            slots = sorted(by_distance[distance])
            wanted_by = (me - distance) * dates + jnp.array(slots, dtype=jnp.int32)
            inside = (wanted_by >= 0) & (wanted_by < total)
            local = jnp.take(annual_of, jnp.clip(wanted_by, 0, total - 1)) - me * dates
            usable = inside & (local >= 0) & (local < dates)
            packed = jnp.take(slc, jnp.clip(local, 0, dates - 1), axis=1)
            packed = jnp.where(usable[None, :, None, None], packed, jnp.zeros_like(packed))
            route = [(i + distance, i) for i in range(devices) if 0 <= i + distance < devices]
            arrived = lax.ppermute(packed, "date", route)
            for n, slot in enumerate(slots):
                part = arrived[:, n]
                sums[slot] = part if sums[slot] is None else sums[slot] + part
    return jnp.stack(sums, axis=1)


def payload_of(images, rim, strip):
    planes, count, rows, cols = images.shape
    edges = jnp.where(strip == 0, rim[..., :HALO], rim[..., TILE - HALO :])
    edges = jnp.transpose(edges, (2, 1, 0, 3)).reshape(rows, count * planes * HALO)
    edges = jnp.pad(edges, ((0, 0), (0, TILE - edges.shape[1])))
    part = rows * TILE // cols
    edges = jnp.transpose(edges.reshape(rows // part, part, TILE), (1, 0, 2)).reshape(part, cols)
    stacked = jnp.transpose(images, (1, 0, 2, 3)).reshape(count * planes * rows, cols)
    return jnp.concatenate([stacked, edges], axis=0)


def body(slc, pair_list, az_half, rng_half):
    planes, dates, rows, cols = slc.shape
    devices = lax.axis_size("date")
    total = dates * devices
    per_date = pair_list.shape[0] // total
    year = min(YEAR, total // 2 - 2)
    half = devices // 2
    late = half * dates - year
    halves = devices % 2 == 0 and 0 < late <= NEAR and 2 * late <= dates
    halves = halves and 2 * (dates - late) * HALO <= TILE
    plan = {
        "dates": dates,
        "devices": devices,
        "per_date": per_date,
        "year": year,
        "late": late,
        "rows": rows,
        "cols": cols,
        "pairs": total * per_date,
        "halves": halves,
    }
    dtype = slc.dtype
    rim_rows = rows * TILE // cols
    lists = (pair_list.T, az_half, rng_half)
    swap_strips = [(0, 1), (1, 0)]

    def images(count):
        return jax.ShapeDtypeStruct((planes, count, rows, cols), dtype)

    def rim_shape(count):
        return jax.ShapeDtypeStruct((planes, count, rows, TILE), dtype)

    def payload_shape(count):
        return jax.ShapeDtypeStruct((planes * count * rows + rim_rows, cols), dtype)

    def swapped_rims(values):
        out = pl.pallas_call(
            rim_kernel,
            out_shape=rim_shape(values.shape[1]),
            in_specs=[ANY],
            out_specs=VMEM,
            scratch_shapes=[pltpu.SemaphoreType.DMA],
            compiler_params=limit(WORK_MIB),
            name="rim_blocks",
        )(values)
        return lax.ppermute(out, "strip", swap_strips)

    wide = cols // 2
    widths = HALO - REACH_LO + 1
    band_shape = (2, 2 * wide + 2 * TILE, wide)
    bands = pl.pallas_call(
        functools.partial(bands_kernel, cols),
        grid=(widths,),
        out_shape=jax.ShapeDtypeStruct((widths, *band_shape), jnp.bfloat16),
        out_specs=pl.BlockSpec((1, *band_shape), lambda n: (n, 0, 0, 0)),
        compiler_params=limit(WORK_MIB),
        name="range_bands",
    )()
    if halves:
        swap = [(i, (i + half) % devices) for i in range(devices)]

        def on_strip(route, strip):
            return [(2 * a + strip, 2 * b + strip) for a, b in route]

        both = ("date", "strip")
        early, rim, strips = pl.pallas_call(
            functools.partial(early_kernel, plan),
            out_shape=(
                images(dates - late),
                rim_shape(dates),
                jax.ShapeDtypeStruct((rows, TILE), dtype),
            ),
            in_specs=[ANY, SMEM],
            out_specs=(VMEM, VMEM, VMEM),
            scratch_shapes=[
                pltpu.VMEM((dates - late, planes, rows, TILE), dtype),
                pltpu.SemaphoreType.DMA((dates - late,)),
                pltpu.SemaphoreType.DMA((dates - late,)),
                pltpu.SemaphoreType.DMA,
            ],
            compiler_params=limit(FIRST_MIB),
            name="early_images",
        )(slc, lists[0])
        early = lax.ppermute(early, both, on_strip(swap, 0))
        rim = lax.ppermute(rim, "strip", swap_strips)
        inner, outer, more = pl.pallas_call(
            functools.partial(beside_kernel, plan),
            out_shape=(
                payload_shape(NEAR),
                payload_shape(NEAR),
                images(dates - late),
            ),
            in_specs=[ANY, SMEM, VMEM],
            out_specs=(VMEM, VMEM, VMEM),
            scratch_shapes=[
                pltpu.SemaphoreType.DMA((2, NEAR, 2)),
                pltpu.SemaphoreType.DMA((dates - late,)),
            ],
            compiler_params=limit(WORK_MIB),
            name="beside_images",
        )(slc, lists[0], rim)
        down = [(i, (i - 1) % half) for i in range(half)]
        down += [(half + i, half + (i + 1) % half) for i in range(half)]
        middle = lax.ppermute(outer, "date", [(half - 1, half), (half, half - 1)])
        more = lax.ppermute(more, both, on_strip(swap, 1))
        strips = lax.ppermute(
            strips, both, [(2 * a + s, 2 * b + 1 - s) for a, b in swap for s in (0, 1)]
        )
        inner = lax.ppermute(inner, "date", down)
        outer = lax.ppermute(outer, "date", [(b, a) for a, b in down])
    else:
        rim = swapped_rims(slc)
        annual = arrivals_by_distance(slc, pair_list, plan)
        strip = lax.axis_index("strip")
        ups = [(i, i + 1) for i in range(devices - 1)]
        inner = payload_of(slc[:, dates - NEAR :], rim[:, dates - NEAR :], strip)
        outer = payload_of(slc[:, :NEAR], rim[:, :NEAR], strip)
        inner = lax.ppermute(inner, "date", ups)
        outer = lax.ppermute(outer, "date", [(b, a) for a, b in ups])
        middle = inner

    out_shape = jax.ShapeDtypeStruct((planes, dates * per_date, rows, cols), jnp.float32)
    depth = 2 * band_shape[1]
    scratch = [
        pltpu.VMEM((2, 4 * rows, depth), jnp.bfloat16),
        pltpu.VMEM((2, 4, 2 * rows, cols), jnp.bfloat16),
        pltpu.VMEM((2, planes, rows, cols), dtype),
        pltpu.VMEM((2, planes, rows, TILE), dtype),
        pltpu.VMEM((2, 2, planes, rows, cols), jnp.float32),
        pltpu.SMEM((dates * NEAR + 1,), jnp.int32),
        pltpu.SemaphoreType.DMA((2, 2)),
    ]

    def cost(flops):
        return pl.CostEstimate(flops=flops, bytes_accessed=1, transcendentals=0)

    out, powers = pl.pallas_call(
        lambda *refs: own_kernel(plan, refs[:3], *refs[3:]),
        out_shape=(out_shape, jax.ShapeDtypeStruct((dates, rows, depth), jnp.bfloat16)),
        in_specs=[SMEM] * 3 + [VMEM] * 3,
        out_specs=(ANY, VMEM),
        scratch_shapes=scratch,
        compiler_params=limit(WORK_MIB),
        cost_estimate=cost(20_000_000_000),
        name="own_pairs",
    )(*lists, slc, rim, bands)

    def more_pairs(kernel, out, others, name):
        return pl.pallas_call(
            lambda *refs: kernel(plan, refs[:3], *refs[3:]),
            out_shape=out_shape,
            in_specs=[SMEM] * 3 + [VMEM] * (4 + len(others)) + [ANY],
            out_specs=ANY,
            scratch_shapes=scratch,
            input_output_aliases={7 + len(others): 0},
            compiler_params=limit(WORK_MIB),
            cost_estimate=cost(1),
            name=name,
        )(*lists, slc, rim, bands, powers, *others, out)

    if halves:
        payload = pl.pallas_call(
            functools.partial(late_kernel, plan),
            out_shape=payload_shape(late),
            in_specs=[VMEM, VMEM, VMEM, SMEM, ANY, ANY],
            out_specs=VMEM,
            scratch_shapes=[pltpu.VMEM((late, planes, rows, TILE), dtype)],
            compiler_params=limit(WORK_MIB),
            name="late_images",
        )(slc, rim, inner, lists[0], powers, strips)
        payload = lax.ppermute(payload, "date", swap)
    out = more_pairs(rest_kernel, out, (inner, outer, middle), "near_pairs")
    if halves:
        kernel = lambda plan, *refs: annual_kernel(plan, False, *refs)
        out = more_pairs(kernel, out, (inner, outer, early, more, strips), "annual_pairs")
        kernel = lambda plan, *refs: annual_kernel(plan, True, *refs)
        out = more_pairs(kernel, out, (inner, outer, payload, payload, strips), "last_pairs")
    else:
        out = more_pairs(plain_kernel, out, (annual, swapped_rims(annual)), "annual_pairs")
    return out


def solution(mesh):
    placed = (P(None, "date", "groups", "strip"), P(), P(), P())
    return jax.shard_map(
        body,
        mesh=mesh,
        in_specs=placed,
        out_specs=P(None, "date", "groups", "strip"),
        check_vma=False,
    )
```

```python
import functools

import jax
import jax.numpy as jnp
from jax import lax
from jax.experimental import pallas as pl
from jax.experimental.pallas import tpu as pltpu
from jax.sharding import PartitionSpec as P

HALO = 16
REACH_LO = 12
NEAR = 3
YEAR = 29
EPSILON = 1e-06
TILE = 128
INNER = TILE // 2
PARTNER, HEIGHT, REACH = 1, 2, 3
WORK_MIB = 16
FIRST_MIB = 56
ANY = pl.BlockSpec(memory_space=pl.ANY)
SMEM = pl.BlockSpec(memory_space=pltpu.SMEM)
VMEM = pl.BlockSpec(memory_space=pltpu.VMEM)


def limit(mebibytes):
    return pltpu.CompilerParams(vmem_limit_bytes=mebibytes * 1024 * 1024)


def run_copies(copies):
    for copy in copies:
        copy.start()
    for copy in copies:
        copy.wait()


def gather_strips(tiles, side):
    lane = lax.broadcasted_iota(jnp.int32, tiles[0].shape, 1)
    packed = jnp.zeros(tiles[0].shape, jnp.float32)
    for n, tile in enumerate(tiles):
        spot = n * HALO
        moved = pltpu.roll(tile.astype(jnp.float32), spot + side * HALO, 1)
        packed = jnp.where((lane >= spot) & (lane < spot + HALO), moved, packed)
    return packed.astype(jnp.bfloat16)


def place_strip(packed, n, side):
    shift = 2 * TILE - (n + side) * HALO
    return pltpu.roll(packed.astype(jnp.float32), lax.rem(shift, TILE), 1).astype(jnp.bfloat16)


def write_strips(out_ref, packed):
    rows, cols = packed.shape[0], out_ref.shape[1]
    part = rows * TILE // cols
    base = out_ref.shape[0] - part
    for n in range(rows // part):
        out_ref[base:, n * TILE : (n + 1) * TILE] = packed[n * part : (n + 1) * part]


def read_strips(ref, rows):
    cols = ref.shape[1]
    base = ref.shape[0] - rows * TILE // cols
    return jnp.concatenate(
        [ref[base:, n * TILE : (n + 1) * TILE] for n in range(cols // TILE)], axis=0
    )


def wanted_images(plan, pairs_ref):
    me = lax.axis_index("date")
    dates, half = plan["dates"], plan["devices"] // 2
    mate = lax.rem(me + half, 2 * half)
    wanted = []
    for k in range(dates - plan["late"]):
        date = mate * dates + jnp.where(mate < half, plan["late"], 0) + k
        at = pairs_ref[PARTNER, date * plan["per_date"] + NEAR] - me * dates
        wanted.append(jnp.clip(at, 0, dates - 1))
    return wanted


def image_copies(slc_ref, wanted, early_ref, sems):
    return [
        pltpu.make_async_copy(slc_ref.at[:, at], early_ref.at[:, k], sems.at[k])
        for k, at in enumerate(wanted)
    ]


def early_kernel(plan, slc_ref, pairs_ref, early_ref, rim_ref, strips_ref, tiles_ref, sems,
                 tile_sems, rim_sem):
    strip, cols = lax.axis_index("strip"), plan["cols"]
    start = pl.multiple_of(jnp.where(strip == 0, cols - TILE, 0), TILE)
    wanted = wanted_images(plan, pairs_ref)
    rim_copy = pltpu.make_async_copy(slc_ref.at[:, :, :, pl.ds(start, TILE)], rim_ref, rim_sem)
    early_copies = image_copies(slc_ref, wanted, early_ref, sems)
    tile_copies = [
        pltpu.make_async_copy(
            slc_ref.at[:, at, :, pl.ds(start, TILE)], tiles_ref.at[k], tile_sems.at[k]
        )
        for k, at in enumerate(wanted)
    ]
    for copy in tile_copies + [rim_copy]:
        copy.start()

    @pl.when(strip == 0)
    def _():
        for copy in early_copies:
            copy.start()

    for copy in tile_copies:
        copy.wait()
    tiles = [tiles_ref[k, c] for k in range(len(wanted)) for c in range(2)]
    strips_ref[...] = gather_strips(tiles, 1 - strip)
    rim_copy.wait()

    @pl.when(strip == 0)
    def _():
        for copy in early_copies:
            copy.wait()


def rim_kernel(slc_ref, rim_ref, sem):
    cols = slc_ref.shape[3]
    start = pl.multiple_of(jnp.where(lax.axis_index("strip") == 0, cols - TILE, 0), TILE)
    run_copies([pltpu.make_async_copy(slc_ref.at[:, :, :, pl.ds(start, TILE)], rim_ref, sem)])


def beside_kernel(plan, slc_ref, pairs_ref, rim_ref, inner_ref, outer_ref, early_ref, sems,
                  early_sems):
    me, strip = lax.axis_index("date"), lax.axis_index("strip")
    dates, rows = plan["dates"], plan["rows"]
    upper = me >= plan["devices"] // 2
    last = dates - NEAR
    copies = []
    firsts = (jnp.where(upper, last, 0), jnp.where(upper, 0, last))
    for r, (out_ref, first) in enumerate(zip((inner_ref, outer_ref), firsts)):
        for k in range(NEAR):
            for c in range(2):
                here = out_ref.at[pl.ds((2 * k + c) * rows, rows)]
                copies.append(
                    pltpu.make_async_copy(slc_ref.at[c, first + k], here, sems.at[r, k, c])
                )
    for copy in copies:
        copy.start()
    early_copies = image_copies(
        slc_ref, wanted_images(plan, pairs_ref), early_ref, early_sems
    )

    @pl.when(strip == 1)
    def _():
        for copy in early_copies:
            copy.start()

    for out_ref, first in zip((inner_ref, outer_ref), firsts):
        tiles = [rim_ref[c, first + k] for k in range(NEAR) for c in range(2)]
        write_strips(out_ref, gather_strips(tiles, strip))
    for copy in copies:
        copy.wait()

    @pl.when(strip == 1)
    def _():
        for copy in early_copies:
            copy.wait()


def late_kernel(plan, slc_ref, rim_ref, inner_ref, outgoing_ref, pairs_ref, *refs):
    late_ref, middle_ref, tiles_ref, sem = refs[-4:]
    copy = pltpu.make_async_copy(outgoing_ref, middle_ref, sem)
    copy.start()
    me, strip = lax.axis_index("date"), lax.axis_index("strip")
    dates, late, rows = plan["dates"], plan["late"], plan["rows"]
    half = plan["devices"] // 2
    mate = lax.rem(me + half, 2 * half)
    mate_slot = jnp.where(mate < half, 0, dates - late)
    packed = read_strips(inner_ref, rows)
    for k in range(late):
        date = mate * dates + mate_slot + k
        wanted = pairs_ref[PARTNER, date * plan["per_date"] + NEAR] - me * dates
        own = (wanted >= 0) & (wanted < dates)
        own_at = jnp.clip(wanted, 0, dates - 1)
        other_at = jnp.clip(jnp.where(me < half, wanted - dates, wanted + NEAR), 0, NEAR - 1)
        for c in range(2):
            here = pl.ds((2 * k + c) * rows, rows)

            @pl.when(own)
            def _():
                late_ref[here] = slc_ref[c, own_at]
                tiles_ref[k, c] = rim_ref[c, own_at]

            @pl.when(jnp.logical_not(own))
            def _():
                there = pl.multiple_of((2 * other_at + c) * rows, rows)
                late_ref[here] = inner_ref[pl.ds(there, rows)]
                tiles_ref[k, c] = place_strip(packed, 2 * other_at + c, strip)

    tiles = [tiles_ref[k, c] for k in range(late) for c in range(2)]
    write_strips(late_ref, gather_strips(tiles, strip))
    copy.wait()


def bands_kernel(cols, out_ref):
    strip = lax.axis_index("strip")
    wide = out_ref.shape[3]
    reach = pl.program_id(0) + REACH_LO

    def band(places, targets):
        return (jnp.abs(places - targets) <= reach).astype(jnp.float32).astype(jnp.bfloat16)

    def indices(shape):
        return lax.broadcasted_iota(jnp.int32, shape, 0), lax.broadcasted_iota(jnp.int32, shape, 1)

    inside = band(*indices((wide, wide)))
    row, col = indices((TILE, wide))
    beyond = jnp.where(strip == 0, cols + row, row - TILE)
    first = band(jnp.where(row < INNER, wide + row, beyond), col)
    second = band(jnp.where(row < INNER, beyond, wide - TILE + row), col + wide)
    for n, part in enumerate((first, second)):
        out_ref[0, n, 0:wide] = inside
        out_ref[0, n, wide : 2 * wide] = inside
        out_ref[0, n, 2 * wide : 2 * wide + TILE] = part
        out_ref[0, n, 2 * wide + TILE : 2 * wide + 2 * TILE] = part


def split(values):
    high = values.astype(jnp.bfloat16)
    low = (values - high.astype(jnp.float32)).astype(jnp.bfloat16)
    return high, low


def put(ref, here, t, values):
    wide = 2 * TILE
    depth = 2 * wide + 2 * TILE
    for low, part in enumerate(split(values)):
        side = [n * depth + 2 * wide + low * TILE for n in range(2)]
        if t < 4:
            at = (t // 2) * depth + low * wide + (t % 2) * TILE
            ref[*here, at : at + TILE] = part
        if t == 2:
            ref[*here, side[0] : side[0] + INNER] = part[:, :INNER]
        if t == 1:
            ref[*here, side[1] + INNER : side[1] + TILE] = part[:, INNER:]
        if t == 4:
            ref[*here, side[0] + INNER : side[0] + TILE] = part[:, INNER:]
            ref[*here, side[1] : side[1] + INNER] = part[:, :INNER]


def tile_of(main, rim, t):
    return [
        (rim(c) if t == 4 else main(c, slice(t * TILE, (t + 1) * TILE))).astype(jnp.float32)
        for c in range(2)
    ]


class Pairs:
    def __init__(self, plan, lists, slc_ref, rim_ref, bands_ref, powers_ref, out_ref, scratch):
        self.plan = plan
        self.lists = lists
        self.slc_ref, self.rim_ref = slc_ref, rim_ref
        self.bands_ref, self.powers_ref, self.out_ref = bands_ref, powers_ref, out_ref
        (self.left_ref, self.stack_ref, self.other_ref, self.other_rim_ref, self.stage_ref,
         self.list_ref, self.sems) = scratch
        self.me, self.strip = lax.axis_index("date"), lax.axis_index("strip")

    def partner(self, pair):
        return self.lists[PARTNER, pair]

    def near_item(self, n):
        slot, kind = n // NEAR, lax.rem(n, NEAR)
        dates = self.plan["dates"]
        pair = (self.me * dates + slot) * self.plan["per_date"] + kind
        return slot, kind, self.partner(pair) - self.me * dates

    def near_list(self, chosen):
        count = 0
        for n in range(self.plan["dates"] * NEAR):
            self.list_ref[count] = n
            count = count + jnp.where(chosen(self.near_item(n)[2]), 1, 0)
        return count

    def own(self, local):
        return (local >= 0) & (local < self.plan["dates"])

    def in_middle(self, local):
        half, dates = self.plan["devices"] // 2, self.plan["dates"]
        if not self.plan["halves"]:
            return False
        return ((self.me == half) & (local < 0)) | ((self.me == half - 1) & (local >= dates))

    def own_other(self, index):
        return (
            lambda c, cols: self.slc_ref[c, index, :, cols],
            lambda c: self.rim_ref[c, index],
        )

    def fetched_other(self, x):
        return (
            lambda c, cols: self.other_ref[x, c, :, cols],
            lambda c: self.other_rim_ref[x, c],
        )

    def fetch_payload(self, x, ref, index):
        rows = self.plan["rows"]
        packed = read_strips(ref, rows)
        for c in range(2):
            at = pl.multiple_of((2 * index + c) * rows, rows)
            self.other_ref[x, c] = ref[pl.ds(at, rows)]
            self.other_rim_ref[x, c] = place_strip(packed, 2 * index + c, self.strip)

    def out_copy(self, stage, x, pair):
        return pltpu.make_async_copy(
            self.stage_ref.at[stage, x], self.out_ref.at[:, pair], self.sems.at[stage, x]
        )

    def run(self, count, work):
        steps = (count + 1) // 2

        def step(n, carry):
            stage = lax.rem(n, 2)

            @pl.when(n >= 2)
            def _():
                for x in range(2):
                    self.out_copy(stage, x, 0).wait()

            items = [work(x, jnp.minimum(2 * n + x, count - 1)) for x in range(2)]
            self.compute(stage, items)
            for x, (slot, kind, _, _) in enumerate(items):
                copy = self.out_copy(stage, x, slot * self.plan["per_date"] + kind)
                pl.when(2 * n + x < count)(copy.start)
            return carry

        lax.fori_loop(0, steps, step, 0)
        for back in (2, 1):
            for x in range(2):
                used = (steps >= back) & (2 * (steps - back) + x < count)
                pl.when(used)(self.out_copy(lax.rem(steps + back, 2), x, 0).wait)

    def compute(self, stage, items):
        plan = self.plan
        rows, dates, per_date = plan["rows"], plan["dates"], plan["per_date"]
        part = [(pl.ds(f * rows, rows),) for f in range(4)]
        depth = self.bands_ref.shape[2]
        wide = self.bands_ref.shape[3]
        heights, widths = [], []
        for slot, kind, _, _ in items:
            pair = (self.me * dates + slot) * per_date + kind
            heights.append(self.lists[HEIGHT, pair])
            widths.append(jnp.clip(self.lists[REACH, pair] - REACH_LO, 0, HALO - REACH_LO))
        for x, (slot, kind, other, other_power) in enumerate(items):
            left_ref = self.left_ref.at[x]
            left_ref[*part[2]] = self.powers_ref[slot]
            if other_power is not None:
                left_ref[*part[3]] = self.powers_ref[other_power]
            first = self.own_other(slot)
            for t in range(5):
                a_real, a_imag = tile_of(*first, t)
                b_real, b_imag = tile_of(*other, t)
                put(left_ref, part[0], t, a_real * b_real + a_imag * b_imag)
                put(left_ref, part[1], t, a_imag * b_real - a_real * b_imag)
                if other_power is None:
                    put(left_ref, part[3], t, b_real * b_real + b_imag * b_imag)
        for n in range(2):
            for x in range(2):
                ranged = jnp.dot(
                    self.left_ref[x, :, n * depth : (n + 1) * depth],
                    self.bands_ref[widths[x], n],
                    preferred_element_type=jnp.float32,
                )
                there = slice(n * wide, (n + 1) * wide)
                for low, values in enumerate(split(ranged)):
                    for f in range(4):
                        self.stack_ref[x, f, low * rows : (low + 1) * rows, there] = values[
                            f * rows : (f + 1) * rows
                        ]
        row = lax.broadcasted_iota(jnp.int32, (rows, 2 * rows), 0)
        col = lax.broadcasted_iota(jnp.int32, (rows, 2 * rows), 1)
        col = jnp.where(col < rows, col, col - rows)
        for x in range(2):
            band = (jnp.abs(row - col) <= heights[x]).astype(jnp.float32).astype(jnp.bfloat16)
            looked = [
                jnp.dot(band, self.stack_ref[x, f], preferred_element_type=jnp.float32)
                for f in range(4)
            ]
            inverse = lax.rsqrt(looked[2] * looked[3] + EPSILON)
            for c in range(2):
                self.stage_ref[stage, x, c] = looked[c] * inverse


def own_kernel(plan, lists, slc_ref, rim_ref, bands_ref, *refs):
    out_ref, powers_ref, *scratch = refs[1 if plan["halves"] else 0 :]
    pairs = Pairs(plan, lists, slc_ref, rim_ref, bands_ref, powers_ref, out_ref, scratch)
    dates = plan["dates"]

    def power(slot, carry):
        for t in range(5):
            real, imag = tile_of(*pairs.own_other(slot), t)
            put(powers_ref, (slot, slice(None)), t, real * real + imag * imag)
        return carry

    lax.fori_loop(0, dates, power, 0)

    def work(x, n):
        slot, kind, local = pairs.near_item(pairs.list_ref[n])
        return slot, kind, pairs.own_other(local), local

    pairs.run(pairs.near_list(pairs.own), work)


def rest_kernel(plan, lists, slc_ref, rim_ref, bands_ref, powers_ref, inner_ref, outer_ref, _,
                out_ref, *scratch):
    pairs = Pairs(plan, lists, slc_ref, rim_ref, bands_ref, powers_ref, out_ref, scratch)
    dates = plan["dates"]
    upper = pairs.me >= plan["devices"] // 2 if plan["halves"] else True

    def work(x, n):
        slot, kind, local = pairs.near_item(pairs.list_ref[n])
        below = local < 0
        index = jnp.clip(jnp.where(below, local + NEAR, local - dates), 0, NEAR - 1)
        inner = below == upper
        pl.when(inner)(lambda: pairs.fetch_payload(x, inner_ref, index))
        pl.when(jnp.logical_not(inner))(lambda: pairs.fetch_payload(x, outer_ref, index))
        return slot, kind, pairs.fetched_other(x), None

    def chosen(local):
        return jnp.logical_not(pairs.own(local) | pairs.in_middle(local))

    pairs.run(pairs.near_list(chosen), work)


def middle_kernel(plan, lists, slc_ref, rim_ref, bands_ref, powers_ref, middle_ref, _, out_ref,
                  *scratch):
    pairs = Pairs(plan, lists, slc_ref, rim_ref, bands_ref, powers_ref, out_ref, scratch)
    dates = plan["dates"]

    def work(x, n):
        slot, kind, local = pairs.near_item(pairs.list_ref[n])
        index = jnp.clip(jnp.where(local < 0, local + NEAR, local - dates), 0, NEAR - 1)
        pairs.fetch_payload(x, middle_ref, index)
        return slot, kind, pairs.fetched_other(x), None

    pairs.run(pairs.near_list(pairs.in_middle), work)


def annual_kernel(plan, is_late, lists, slc_ref, rim_ref, bands_ref, powers_ref, inner_ref,
                  outer_ref, images_ref, more_ref, strips_ref, _, out_ref, *scratch):
    pairs = Pairs(plan, lists, slc_ref, rim_ref, bands_ref, powers_ref, out_ref, scratch)
    dates, late = plan["dates"], plan["late"]
    half = plan["devices"] // 2
    me, split_date = pairs.me, half * dates
    lower = me < half
    if is_late:
        base, count = jnp.where(lower, 0, dates - late), late
    else:
        base, count = jnp.where(lower, late, 0), dates - late

    def fetch_early(x, k, ref):
        packed = strips_ref[...]
        for c in range(2):
            pairs.other_ref[x, c] = ref[c, k]
            pairs.other_rim_ref[x, c] = place_strip(packed, 2 * k + c, pairs.strip)

    def work(x, k):
        slot = base + k
        date = me * dates + slot
        other = pairs.partner(date * plan["per_date"] + NEAR)
        far = (other < split_date) == lower
        from_inner = jnp.where(lower, me != 0, me == half)
        inner_at = jnp.where(lower, other, other - (2 * split_date - NEAR))
        outer_at = jnp.where(lower, other - (split_date - NEAR), other - split_date)
        inner_at, outer_at = jnp.clip(inner_at, 0, NEAR - 1), jnp.clip(outer_at, 0, NEAR - 1)
        fetch = pairs.fetch_payload
        pl.when(far & from_inner)(lambda: fetch(x, inner_ref, inner_at))
        pl.when(far & jnp.logical_not(from_inner))(lambda: fetch(x, outer_ref, outer_at))
        near_side = jnp.logical_not(far)
        if is_late:
            pl.when(near_side)(lambda: fetch(x, images_ref, k))
        else:
            first = pairs.strip == 0
            pl.when(near_side & first)(lambda: fetch_early(x, k, images_ref))
            pl.when(near_side & jnp.logical_not(first))(lambda: fetch_early(x, k, more_ref))
        return slot, NEAR, pairs.fetched_other(x), None

    pairs.run(count, work)


def plain_kernel(plan, lists, slc_ref, rim_ref, bands_ref, powers_ref, images_ref,
                 image_rim_ref, _, out_ref, *scratch):
    pairs = Pairs(plan, lists, slc_ref, rim_ref, bands_ref, powers_ref, out_ref, scratch)

    def work(x, slot):
        other = (
            lambda c, cols: images_ref[c, slot, :, cols],
            lambda c: image_rim_ref[c, slot],
        )
        return slot, NEAR, other, None

    pairs.run(plan["dates"], work)


def arrivals_by_distance(slc, pair_list, plan):
    dates, per_date, devices = plan["dates"], plan["per_date"], plan["devices"]
    total = dates * devices
    me = lax.axis_index("date")
    annual_of = pair_list[:, 1].reshape(total, per_date)[:, per_date - 1]
    sums = [None] * dates
    for direction in (1, -1):
        by_distance = {}
        for slot in range(dates):
            for gap in range(plan["year"], plan["year"] + 3):
                distance = (slot + direction * gap) // dates
                by_distance.setdefault(distance, set()).add(slot)
        for distance in sorted(by_distance):
            slots = sorted(by_distance[distance])
            wanted_by = (me - distance) * dates + jnp.array(slots, dtype=jnp.int32)
            inside = (wanted_by >= 0) & (wanted_by < total)
            local = jnp.take(annual_of, jnp.clip(wanted_by, 0, total - 1)) - me * dates
            usable = inside & (local >= 0) & (local < dates)
            packed = jnp.take(slc, jnp.clip(local, 0, dates - 1), axis=1)
            packed = jnp.where(usable[None, :, None, None], packed, jnp.zeros_like(packed))
            route = [(i + distance, i) for i in range(devices) if 0 <= i + distance < devices]
            arrived = lax.ppermute(packed, "date", route)
            for n, slot in enumerate(slots):
                part = arrived[:, n]
                sums[slot] = part if sums[slot] is None else sums[slot] + part
    return jnp.stack(sums, axis=1)


def payload_of(images, rim, strip):
    planes, count, rows, cols = images.shape
    edges = jnp.where(strip == 0, rim[..., :HALO], rim[..., TILE - HALO :])
    edges = jnp.transpose(edges, (2, 1, 0, 3)).reshape(rows, count * planes * HALO)
    edges = jnp.pad(edges, ((0, 0), (0, TILE - edges.shape[1])))
    part = rows * TILE // cols
    edges = jnp.transpose(edges.reshape(rows // part, part, TILE), (1, 0, 2)).reshape(part, cols)
    stacked = jnp.transpose(images, (1, 0, 2, 3)).reshape(count * planes * rows, cols)
    return jnp.concatenate([stacked, edges], axis=0)


def body(slc, pair_list, az_half, rng_half):
    planes, dates, rows, cols = slc.shape
    devices = lax.axis_size("date")
    total = dates * devices
    per_date = pair_list.shape[0] // total
    year = min(YEAR, total // 2 - 2)
    half = devices // 2
    late = half * dates - year
    halves = devices % 2 == 0 and 0 < late <= NEAR and 2 * late <= dates
    halves = halves and 2 * (dates - late) * HALO <= TILE
    plan = {
        "dates": dates,
        "devices": devices,
        "per_date": per_date,
        "year": year,
        "late": late,
        "rows": rows,
        "cols": cols,
        "pairs": total * per_date,
        "halves": halves,
    }
    dtype = slc.dtype
    rim_rows = rows * TILE // cols
    pairs = pair_list.T
    lists = jnp.concatenate([pairs, az_half[None], rng_half[None]])
    swap_strips = [(0, 1), (1, 0)]

    def images(count):
        return jax.ShapeDtypeStruct((planes, count, rows, cols), dtype)

    def rim_shape(count):
        return jax.ShapeDtypeStruct((planes, count, rows, TILE), dtype)

    def payload_shape(count):
        return jax.ShapeDtypeStruct((planes * count * rows + rim_rows, cols), dtype)

    def swapped_rims(values):
        out = pl.pallas_call(
            rim_kernel,
            out_shape=rim_shape(values.shape[1]),
            in_specs=[ANY],
            out_specs=VMEM,
            scratch_shapes=[pltpu.SemaphoreType.DMA],
            compiler_params=limit(WORK_MIB),
            name="rim_blocks",
        )(values)
        return lax.ppermute(out, "strip", swap_strips)

    def cost(flops):
        return pl.CostEstimate(flops=flops, bytes_accessed=1, transcendentals=0)

    wide = cols // 2
    widths = HALO - REACH_LO + 1
    band_shape = (2, 2 * wide + 2 * TILE, wide)
    bands = pl.pallas_call(
        functools.partial(bands_kernel, cols),
        grid=(widths,),
        out_shape=jax.ShapeDtypeStruct((widths, *band_shape), jnp.bfloat16),
        out_specs=pl.BlockSpec((1, *band_shape), lambda n: (n, 0, 0, 0)),
        compiler_params=limit(WORK_MIB),
        cost_estimate=cost(20_000_000_000),
        name="range_bands",
    )()
    if halves:
        swap = [(i, (i + half) % devices) for i in range(devices)]

        def on_strip(route, strip):
            return [(2 * a + strip, 2 * b + strip) for a, b in route]

        both = ("date", "strip")
        early, rim, strips = pl.pallas_call(
            functools.partial(early_kernel, plan),
            out_shape=(
                images(dates - late),
                rim_shape(dates),
                jax.ShapeDtypeStruct((rows, TILE), dtype),
            ),
            in_specs=[ANY, SMEM],
            out_specs=(VMEM, VMEM, VMEM),
            scratch_shapes=[
                pltpu.VMEM((dates - late, planes, rows, TILE), dtype),
                pltpu.SemaphoreType.DMA((dates - late,)),
                pltpu.SemaphoreType.DMA((dates - late,)),
                pltpu.SemaphoreType.DMA,
            ],
            compiler_params=limit(FIRST_MIB),
            name="early_images",
        )(slc, pairs)
        early = lax.ppermute(early, both, on_strip(swap, 0))
        rim = lax.ppermute(rim, "strip", swap_strips)
        inner, outer, more = pl.pallas_call(
            functools.partial(beside_kernel, plan),
            out_shape=(
                payload_shape(NEAR),
                payload_shape(NEAR),
                images(dates - late),
            ),
            in_specs=[ANY, SMEM, VMEM],
            out_specs=(VMEM, VMEM, VMEM),
            scratch_shapes=[
                pltpu.SemaphoreType.DMA((2, NEAR, 2)),
                pltpu.SemaphoreType.DMA((dates - late,)),
            ],
            compiler_params=limit(WORK_MIB),
            name="beside_images",
        )(slc, lists, rim)
        down = [(i, (i - 1) % half) for i in range(half)]
        down += [(half + i, half + (i + 1) % half) for i in range(half)]
        more = lax.ppermute(more, both, on_strip(swap, 1))
        strips = lax.ppermute(
            strips, both, [(2 * a + s, 2 * b + 1 - s) for a, b in swap for s in (0, 1)]
        )
        outgoing = outer
        outer = lax.ppermute(outer, "date", [(b, a) for a, b in down])
        inner = lax.ppermute(inner, "date", down)
    else:
        rim = swapped_rims(slc)
        annual = arrivals_by_distance(slc, pair_list, plan)
        strip = lax.axis_index("strip")
        ups = [(i, i + 1) for i in range(devices - 1)]
        inner = payload_of(slc[:, dates - NEAR :], rim[:, dates - NEAR :], strip)
        outer = payload_of(slc[:, :NEAR], rim[:, :NEAR], strip)
        inner = lax.ppermute(inner, "date", ups)
        outer = lax.ppermute(outer, "date", [(b, a) for a, b in ups])

    out_shape = jax.ShapeDtypeStruct((planes, dates * per_date, rows, cols), jnp.float32)
    depth = 2 * band_shape[1]
    scratch = [
        pltpu.VMEM((2, 4 * rows, depth), jnp.bfloat16),
        pltpu.VMEM((2, 4, 2 * rows, cols), jnp.bfloat16),
        pltpu.VMEM((2, planes, rows, cols), dtype),
        pltpu.VMEM((2, planes, rows, TILE), dtype),
        pltpu.VMEM((2, 2, planes, rows, cols), jnp.float32),
        pltpu.SMEM((dates * NEAR + 1,), jnp.int32),
        pltpu.SemaphoreType.DMA((2, 2)),
    ]

    if halves:
        payload, middle = pl.pallas_call(
            functools.partial(late_kernel, plan),
            out_shape=(payload_shape(late), payload_shape(NEAR)),
            in_specs=[VMEM, VMEM, VMEM, ANY, SMEM, ANY, ANY],
            out_specs=(VMEM, VMEM),
            scratch_shapes=[
                pltpu.VMEM((late, planes, rows, TILE), dtype),
                pltpu.SemaphoreType.DMA,
            ],
            compiler_params=limit(WORK_MIB),
            name="late_images",
        )(slc, rim, inner, outgoing, lists, bands, strips)
        after = (payload,)
        middle = lax.ppermute(middle, "date", [(half - 1, half), (half, half - 1)])
        payload = lax.ppermute(payload, "date", swap)
    else:
        after = ()

    out, powers = pl.pallas_call(
        functools.partial(own_kernel, plan),
        out_shape=(out_shape, jax.ShapeDtypeStruct((dates, rows, depth), jnp.bfloat16)),
        in_specs=[SMEM] + [VMEM] * 3 + [ANY] * len(after),
        out_specs=(ANY, VMEM),
        scratch_shapes=scratch,
        compiler_params=limit(WORK_MIB),
        cost_estimate=cost(1),
        name="own_pairs",
    )(lists, slc, rim, bands, *after)

    def more_pairs(kernel, out, others, name):
        return pl.pallas_call(
            functools.partial(kernel, plan),
            out_shape=out_shape,
            in_specs=[SMEM] + [VMEM] * (4 + len(others)) + [ANY],
            out_specs=ANY,
            scratch_shapes=scratch,
            input_output_aliases={5 + len(others): 0},
            compiler_params=limit(WORK_MIB),
            cost_estimate=cost(1),
            name=name,
        )(lists, slc, rim, bands, powers, *others, out)

    out = more_pairs(rest_kernel, out, (inner, outer), "near_pairs")
    if halves:
        kernel = lambda plan, *refs: annual_kernel(plan, False, *refs)
        out = more_pairs(kernel, out, (inner, outer, early, more, strips), "annual_pairs")
        out = more_pairs(middle_kernel, out, (middle,), "middle_pairs")
        kernel = lambda plan, *refs: annual_kernel(plan, True, *refs)
        out = more_pairs(kernel, out, (inner, outer, payload, payload, strips), "last_pairs")
    else:
        out = more_pairs(plain_kernel, out, (annual, swapped_rims(annual)), "annual_pairs")
    return out


def solution(mesh):
    placed = (P(None, "date", "groups", "strip"), P(), P(), P())
    return jax.shard_map(
        body,
        mesh=mesh,
        in_specs=placed,
        out_specs=P(None, "date", "groups", "strip"),
        check_vma=False,
    )
```

```python
import functools

import jax
import jax.numpy as jnp
from jax import lax
from jax.experimental import pallas as pl
from jax.experimental.pallas import tpu as pltpu
from jax.sharding import PartitionSpec as P

HALO = 16
REACH_LO = 12
NEAR = 3
YEAR = 29
EPSILON = 1e-06
TILE = 128
INNER = TILE // 2
PER_TILE = TILE // HALO
PARTNER, HEIGHT, REACH = 1, 2, 3
WORK_MIB = 16
FIRST_MIB = 56
ANY = pl.BlockSpec(memory_space=pl.ANY)
SMEM = pl.BlockSpec(memory_space=pltpu.SMEM)
VMEM = pl.BlockSpec(memory_space=pltpu.VMEM)


def limit(mebibytes):
    return pltpu.CompilerParams(vmem_limit_bytes=mebibytes * 1024 * 1024)


def run_copies(copies):
    for copy in copies:
        copy.start()
    for copy in copies:
        copy.wait()


def gather_strips(tiles, side):
    lane = lax.broadcasted_iota(jnp.int32, tiles[0].shape, 1)
    packed = jnp.zeros(tiles[0].shape, jnp.float32)
    for n, tile in enumerate(tiles):
        spot = n * HALO
        moved = pltpu.roll(tile.astype(jnp.float32), spot + side * HALO, 1)
        packed = jnp.where((lane >= spot) & (lane < spot + HALO), moved, packed)
    return packed.astype(jnp.bfloat16)


def place_strip(packed, n, side):
    shift = 2 * TILE - (n + side) * HALO
    return pltpu.roll(packed.astype(jnp.float32), lax.rem(shift, TILE), 1).astype(jnp.bfloat16)


def write_strips(out_ref, packed):
    rows, cols = packed.shape[0], out_ref.shape[1]
    part = rows * TILE // cols
    base = out_ref.shape[0] - part
    for n in range(rows // part):
        out_ref[base:, n * TILE : (n + 1) * TILE] = packed[n * part : (n + 1) * part]


def read_strips(ref, rows):
    cols = ref.shape[1]
    base = ref.shape[0] - rows * TILE // cols
    return jnp.concatenate(
        [ref[base:, n * TILE : (n + 1) * TILE] for n in range(cols // TILE)], axis=0
    )


def rim_kernel(slc_ref, rim_ref, sem):
    cols = slc_ref.shape[3]
    start = pl.multiple_of(jnp.where(lax.axis_index("strip") == 0, cols - TILE, 0), TILE)
    run_copies([pltpu.make_async_copy(slc_ref.at[:, :, :, pl.ds(start, TILE)], rim_ref, sem)])


def beside_kernel(plan, slc_ref, rim_ref, inner_ref, outer_ref, strips_ref, whole_ref, sems, sem):
    me, strip = lax.axis_index("date"), lax.axis_index("strip")
    dates, rows = plan["dates"], plan["rows"]
    upper = me >= plan["devices"] // 2
    last = dates - NEAR
    copies = [pltpu.make_async_copy(slc_ref, whole_ref, sem)]
    firsts = (jnp.where(upper, last, 0), jnp.where(upper, 0, last))
    for r, (out_ref, first) in enumerate(zip((inner_ref, outer_ref), firsts)):
        for k in range(NEAR):
            for c in range(2):
                here = out_ref.at[pl.ds((2 * k + c) * rows, rows)]
                copies.append(
                    pltpu.make_async_copy(slc_ref.at[c, first + k], here, sems.at[r, k, c])
                )
    for copy in copies:
        copy.start()
    for out_ref, first in zip((inner_ref, outer_ref), firsts):
        tiles = [rim_ref[c, first + k] for k in range(NEAR) for c in range(2)]
        write_strips(out_ref, gather_strips(tiles, strip))
    tiles = [rim_ref[c, k] for k in range(dates) for c in range(2)]
    for n in range(2):
        part = tiles[n * PER_TILE : (n + 1) * PER_TILE]
        strips_ref[n] = gather_strips(part, strip)
    for copy in copies:
        copy.wait()


def opposite_strip(strips_ref, index, c, strip):
    n = 2 * index + c
    return place_strip(strips_ref[n // PER_TILE], lax.rem(n, PER_TILE), strip)


def pass_kernel(plan, first_ref, second_ref, strips_ref, _, pass_ref, middle_ref, sems):
    me, strip = lax.axis_index("date"), lax.axis_index("strip")
    dates, late, rows = plan["dates"], plan["late"], plan["rows"]
    lower = me < plan["devices"] // 2
    routes = (
        (pass_ref, late, jnp.where(lower, dates - late, 0)),
        (middle_ref, NEAR, jnp.where(lower, 0, dates - NEAR)),
    )
    for source_strip, source in enumerate((first_ref, second_ref)):

        @pl.when(strip == source_strip)
        def _():
            copies = []
            for out_ref, count, start in routes:
                for k in range(count):
                    for c in range(2):
                        here = out_ref.at[pl.ds((2 * k + c) * rows, rows)]
                        sem = sems.at[len(copies)]
                        copies.append(pltpu.make_async_copy(source.at[c, start + k], here, sem))
            run_copies(copies)

    for out_ref, count, start in routes:
        tiles = [
            opposite_strip(strips_ref, start + k, c, strip) for k in range(count) for c in range(2)
        ]
        write_strips(out_ref, gather_strips(tiles, strip))


def bands_kernel(cols, out_ref):
    strip = lax.axis_index("strip")
    wide = out_ref.shape[3]
    reach = pl.program_id(0) + REACH_LO

    def band(places, targets):
        return (jnp.abs(places - targets) <= reach).astype(jnp.float32).astype(jnp.bfloat16)

    def indices(shape):
        return lax.broadcasted_iota(jnp.int32, shape, 0), lax.broadcasted_iota(jnp.int32, shape, 1)

    inside = band(*indices((wide, wide)))
    row, col = indices((TILE, wide))
    beyond = jnp.where(strip == 0, cols + row, row - TILE)
    first = band(jnp.where(row < INNER, wide + row, beyond), col)
    second = band(jnp.where(row < INNER, beyond, wide - TILE + row), col + wide)
    for n, part in enumerate((first, second)):
        out_ref[0, n, 0:wide] = inside
        out_ref[0, n, wide : 2 * wide] = inside
        out_ref[0, n, 2 * wide : 2 * wide + TILE] = part
        out_ref[0, n, 2 * wide + TILE : 2 * wide + 2 * TILE] = part


def split(values):
    high = values.astype(jnp.bfloat16)
    low = (values - high.astype(jnp.float32)).astype(jnp.bfloat16)
    return high, low


def put(ref, here, t, values):
    wide = 2 * TILE
    depth = 2 * wide + 2 * TILE
    for low, part in enumerate(split(values)):
        side = [n * depth + 2 * wide + low * TILE for n in range(2)]
        if t < 4:
            at = (t // 2) * depth + low * wide + (t % 2) * TILE
            ref[*here, at : at + TILE] = part
        if t == 2:
            ref[*here, side[0] : side[0] + INNER] = part[:, :INNER]
        if t == 1:
            ref[*here, side[1] + INNER : side[1] + TILE] = part[:, INNER:]
        if t == 4:
            ref[*here, side[0] + INNER : side[0] + TILE] = part[:, INNER:]
            ref[*here, side[1] : side[1] + INNER] = part[:, :INNER]


def tile_of(main, rim, t):
    return [
        (rim(c) if t == 4 else main(c, slice(t * TILE, (t + 1) * TILE))).astype(jnp.float32)
        for c in range(2)
    ]


class Pairs:
    def __init__(self, plan, lists, slc_ref, rim_ref, bands_ref, powers_ref, out_ref, scratch):
        self.plan = plan
        self.lists = lists
        self.slc_ref, self.rim_ref = slc_ref, rim_ref
        self.bands_ref, self.powers_ref, self.out_ref = bands_ref, powers_ref, out_ref
        (self.left_ref, self.stack_ref, self.other_ref, self.other_rim_ref, self.stage_ref,
         self.list_ref, self.sems) = scratch
        self.me, self.strip = lax.axis_index("date"), lax.axis_index("strip")

    def partner(self, pair):
        return self.lists[PARTNER, pair]

    def item(self, n):
        slot, kind = n // self.plan["per_date"], lax.rem(n, self.plan["per_date"])
        first = self.me * self.plan["dates"]
        pair = first * self.plan["per_date"] + n
        return slot, kind, self.partner(pair) - first

    def chosen(self, test):
        count = 0
        for n in range(self.plan["dates"] * self.plan["per_date"]):
            self.list_ref[count] = n
            local = self.item(n)[2]
            near = n % self.plan["per_date"] < NEAR
            count = count + jnp.where(test(near, local), 1, 0)
        return count

    def own(self, local):
        return (local >= 0) & (local < self.plan["dates"])

    def in_middle(self, local):
        half, dates = self.plan["devices"] // 2, self.plan["dates"]
        if not self.plan["halves"]:
            return False
        return ((self.me == half) & (local < 0)) | ((self.me == half - 1) & (local >= dates))

    def opposite(self, local):
        half, dates = self.plan["devices"] // 2, self.plan["dates"]
        return local - jnp.where(self.me < half, half * dates, -half * dates)

    def in_half(self, local):
        half, dates = self.plan["devices"] // 2, self.plan["dates"]
        return (local + self.me * dates < half * dates) == (self.me < half)

    def passed(self, local):
        return jnp.logical_not(self.in_half(local) | self.own(self.opposite(local)))

    def own_other(self, index):
        return (
            lambda c, cols: self.slc_ref[c, index, :, cols],
            lambda c: self.rim_ref[c, index],
        )

    def fetched_other(self, x):
        return (
            lambda c, cols: self.other_ref[x, c, :, cols],
            lambda c: self.other_rim_ref[x, c],
        )

    def fetch_payload(self, x, ref, index):
        rows = self.plan["rows"]
        packed = read_strips(ref, rows)
        for c in range(2):
            at = pl.multiple_of((2 * index + c) * rows, rows)
            self.other_ref[x, c] = ref[pl.ds(at, rows)]
            self.other_rim_ref[x, c] = place_strip(packed, 2 * index + c, self.strip)

    def out_copy(self, stage, x, pair):
        return pltpu.make_async_copy(
            self.stage_ref.at[stage, x], self.out_ref.at[:, pair], self.sems.at[stage, x]
        )

    def run(self, count, work):
        steps = (count + 1) // 2

        def step(n, carry):
            stage = lax.rem(n, 2)

            @pl.when(n >= 2)
            def _():
                for x in range(2):
                    self.out_copy(stage, x, 0).wait()

            items = [work(x, jnp.minimum(2 * n + x, count - 1)) for x in range(2)]
            self.compute(stage, items)
            for x, (slot, kind, _, _) in enumerate(items):
                copy = self.out_copy(stage, x, slot * self.plan["per_date"] + kind)
                pl.when(2 * n + x < count)(copy.start)
            return carry

        lax.fori_loop(0, steps, step, 0)
        for back in (2, 1):
            for x in range(2):
                used = (steps >= back) & (2 * (steps - back) + x < count)
                pl.when(used)(self.out_copy(lax.rem(steps + back, 2), x, 0).wait)

    def compute(self, stage, items):
        plan = self.plan
        rows, dates, per_date = plan["rows"], plan["dates"], plan["per_date"]
        part = [(pl.ds(f * rows, rows),) for f in range(4)]
        depth = self.bands_ref.shape[2]
        wide = self.bands_ref.shape[3]
        heights, widths = [], []
        for slot, kind, _, _ in items:
            pair = (self.me * dates + slot) * per_date + kind
            heights.append(self.lists[HEIGHT, pair])
            widths.append(jnp.clip(self.lists[REACH, pair] - REACH_LO, 0, HALO - REACH_LO))
        for x, (slot, kind, other, other_power) in enumerate(items):
            left_ref = self.left_ref.at[x]
            left_ref[*part[2]] = self.powers_ref[slot]
            if other_power is not None:
                left_ref[*part[3]] = self.powers_ref[other_power]
            first = self.own_other(slot)
            for t in range(5):
                a_real, a_imag = tile_of(*first, t)
                b_real, b_imag = tile_of(*other, t)
                put(left_ref, part[0], t, a_real * b_real + a_imag * b_imag)
                put(left_ref, part[1], t, a_imag * b_real - a_real * b_imag)
                if other_power is None:
                    put(left_ref, part[3], t, b_real * b_real + b_imag * b_imag)
        for n in range(2):
            for x in range(2):
                ranged = jnp.dot(
                    self.left_ref[x, :, n * depth : (n + 1) * depth],
                    self.bands_ref[widths[x], n],
                    preferred_element_type=jnp.float32,
                )
                there = slice(n * wide, (n + 1) * wide)
                for low, values in enumerate(split(ranged)):
                    for f in range(4):
                        self.stack_ref[x, f, low * rows : (low + 1) * rows, there] = values[
                            f * rows : (f + 1) * rows
                        ]
        row = lax.broadcasted_iota(jnp.int32, (rows, 2 * rows), 0)
        col = lax.broadcasted_iota(jnp.int32, (rows, 2 * rows), 1)
        col = jnp.where(col < rows, col, col - rows)
        for x in range(2):
            band = (jnp.abs(row - col) <= heights[x]).astype(jnp.float32).astype(jnp.bfloat16)
            looked = [
                jnp.dot(band, self.stack_ref[x, f], preferred_element_type=jnp.float32)
                for f in range(4)
            ]
            inverse = lax.rsqrt(looked[2] * looked[3] + EPSILON)
            for c in range(2):
                self.stage_ref[stage, x, c] = looked[c] * inverse


def own_kernel(plan, lists, slc_ref, rim_ref, bands_ref, out_ref, powers_ref, *scratch):
    pairs = Pairs(plan, lists, slc_ref, rim_ref, bands_ref, powers_ref, out_ref, scratch)
    dates = plan["dates"]

    def power(slot, carry):
        for t in range(5):
            real, imag = tile_of(*pairs.own_other(slot), t)
            put(powers_ref, (slot, slice(None)), t, real * real + imag * imag)
        return carry

    lax.fori_loop(0, dates, power, 0)

    def work(x, n):
        slot, kind, local = pairs.item(pairs.list_ref[n])
        return slot, kind, pairs.own_other(local), local

    pairs.run(pairs.chosen(lambda near, local: near and pairs.own(local)), work)


def rest_kernel(plan, lists, slc_ref, rim_ref, bands_ref, powers_ref, inner_ref, outer_ref, _,
                out_ref, mark_ref, *scratch):
    mark_ref[...] = jnp.zeros_like(mark_ref)
    pairs = Pairs(plan, lists, slc_ref, rim_ref, bands_ref, powers_ref, out_ref, scratch)
    dates = plan["dates"]
    upper = pairs.me >= plan["devices"] // 2 if plan["halves"] else True

    def work(x, n):
        slot, kind, local = pairs.item(pairs.list_ref[n])
        below = local < 0
        index = jnp.clip(jnp.where(below, local + NEAR, local - dates), 0, NEAR - 1)
        inner = below == upper
        pl.when(inner)(lambda: pairs.fetch_payload(x, inner_ref, index))
        pl.when(jnp.logical_not(inner))(lambda: pairs.fetch_payload(x, outer_ref, index))
        return slot, kind, pairs.fetched_other(x), None

    def test(near, local):
        return near and jnp.logical_not(pairs.own(local) | pairs.in_middle(local))

    pairs.run(pairs.chosen(test), work)


def annual_kernel(plan, lists, slc_ref, rim_ref, bands_ref, powers_ref, inner_ref, outer_ref,
                  first_ref, second_ref, strips_ref, _, out_ref, *scratch):
    pairs = Pairs(plan, lists, slc_ref, rim_ref, bands_ref, powers_ref, out_ref, scratch)
    dates, half = plan["dates"], plan["devices"] // 2
    me, strip = pairs.me, pairs.strip
    lower = me < half

    def fetch_opposite(x, ref, at):
        for c in range(2):
            pairs.other_ref[x, c] = ref[c, at]
            pairs.other_rim_ref[x, c] = opposite_strip(strips_ref, at, c, strip)

    def work(x, n):
        slot, kind, local = pairs.item(pairs.list_ref[n])
        far = pairs.in_half(local)
        from_inner = jnp.where(lower, me != 0, me == half)
        other, split_date = local + me * dates, half * dates
        inner_at = jnp.where(lower, other, other - (2 * split_date - NEAR))
        outer_at = jnp.where(lower, other - (split_date - NEAR), other - split_date)
        inner_at, outer_at = jnp.clip(inner_at, 0, NEAR - 1), jnp.clip(outer_at, 0, NEAR - 1)
        at = jnp.clip(pairs.opposite(local), 0, dates - 1)
        pl.when(far & from_inner)(lambda: pairs.fetch_payload(x, inner_ref, inner_at))
        pl.when(far & jnp.logical_not(from_inner))(
            lambda: pairs.fetch_payload(x, outer_ref, outer_at)
        )
        across = jnp.logical_not(far)
        pl.when(across & (strip == 0))(lambda: fetch_opposite(x, first_ref, at))
        pl.when(across & (strip == 1))(lambda: fetch_opposite(x, second_ref, at))
        return slot, kind, pairs.fetched_other(x), None

    def test(near, local):
        return not near and jnp.logical_not(pairs.passed(local))

    pairs.run(pairs.chosen(test), work)


def last_kernel(plan, lists, slc_ref, rim_ref, bands_ref, powers_ref, pass_ref, middle_ref, _,
                out_ref, *scratch):
    pairs = Pairs(plan, lists, slc_ref, rim_ref, bands_ref, powers_ref, out_ref, scratch)
    dates, late = plan["dates"], plan["late"]

    def work(x, n):
        slot, kind, local = pairs.item(pairs.list_ref[n])
        across = pairs.opposite(local)
        pass_at = jnp.clip(jnp.where(across < 0, across + late, across - dates), 0, late - 1)
        middle_at = jnp.clip(jnp.where(local < 0, local + NEAR, local - dates), 0, NEAR - 1)
        pl.when(kind < NEAR)(lambda: pairs.fetch_payload(x, middle_ref, middle_at))
        pl.when(kind == NEAR)(lambda: pairs.fetch_payload(x, pass_ref, pass_at))
        return slot, kind, pairs.fetched_other(x), None

    def test(near, local):
        return pairs.in_middle(local) if near else pairs.passed(local)

    pairs.run(pairs.chosen(test), work)


def plain_kernel(plan, lists, slc_ref, rim_ref, bands_ref, powers_ref, images_ref,
                 image_rim_ref, _, out_ref, *scratch):
    pairs = Pairs(plan, lists, slc_ref, rim_ref, bands_ref, powers_ref, out_ref, scratch)

    def work(x, slot):
        other = (
            lambda c, cols: images_ref[c, slot, :, cols],
            lambda c: image_rim_ref[c, slot],
        )
        return slot, NEAR, other, None

    pairs.run(plan["dates"], work)


def arrivals_by_distance(slc, pair_list, plan):
    dates, per_date, devices = plan["dates"], plan["per_date"], plan["devices"]
    total = dates * devices
    me = lax.axis_index("date")
    annual_of = pair_list[:, 1].reshape(total, per_date)[:, per_date - 1]
    sums = [None] * dates
    for direction in (1, -1):
        by_distance = {}
        for slot in range(dates):
            for gap in range(plan["year"], plan["year"] + 3):
                distance = (slot + direction * gap) // dates
                by_distance.setdefault(distance, set()).add(slot)
        for distance in sorted(by_distance):
            slots = sorted(by_distance[distance])
            wanted_by = (me - distance) * dates + jnp.array(slots, dtype=jnp.int32)
            inside = (wanted_by >= 0) & (wanted_by < total)
            local = jnp.take(annual_of, jnp.clip(wanted_by, 0, total - 1)) - me * dates
            usable = inside & (local >= 0) & (local < dates)
            packed = jnp.take(slc, jnp.clip(local, 0, dates - 1), axis=1)
            packed = jnp.where(usable[None, :, None, None], packed, jnp.zeros_like(packed))
            route = [(i + distance, i) for i in range(devices) if 0 <= i + distance < devices]
            arrived = lax.ppermute(packed, "date", route)
            for n, slot in enumerate(slots):
                part = arrived[:, n]
                sums[slot] = part if sums[slot] is None else sums[slot] + part
    return jnp.stack(sums, axis=1)


def payload_of(images, rim, strip):
    planes, count, rows, cols = images.shape
    edges = jnp.where(strip == 0, rim[..., :HALO], rim[..., TILE - HALO :])
    edges = jnp.transpose(edges, (2, 1, 0, 3)).reshape(rows, count * planes * HALO)
    edges = jnp.pad(edges, ((0, 0), (0, TILE - edges.shape[1])))
    part = rows * TILE // cols
    edges = jnp.transpose(edges.reshape(rows // part, part, TILE), (1, 0, 2)).reshape(part, cols)
    stacked = jnp.transpose(images, (1, 0, 2, 3)).reshape(count * planes * rows, cols)
    return jnp.concatenate([stacked, edges], axis=0)


def body(slc, pair_list, az_half, rng_half):
    planes, dates, rows, cols = slc.shape
    devices = lax.axis_size("date")
    total = dates * devices
    per_date = pair_list.shape[0] // total
    year = min(YEAR, total // 2 - 2)
    half = devices // 2
    late = half * dates - year
    halves = devices % 2 == 0 and 0 < late <= NEAR and 2 * late <= dates
    halves = halves and dates <= PER_TILE
    plan = {
        "dates": dates,
        "devices": devices,
        "per_date": per_date,
        "year": year,
        "late": late,
        "rows": rows,
        "cols": cols,
        "pairs": total * per_date,
        "halves": halves,
    }
    dtype = slc.dtype
    rim_rows = rows * TILE // cols
    lists = jnp.concatenate([pair_list.T, az_half[None], rng_half[None]])
    swap_strips = [(0, 1), (1, 0)]

    def images(count):
        return jax.ShapeDtypeStruct((planes, count, rows, cols), dtype)

    def rim_shape(count):
        return jax.ShapeDtypeStruct((planes, count, rows, TILE), dtype)

    def payload_shape(count):
        return jax.ShapeDtypeStruct((planes * count * rows + rim_rows, cols), dtype)

    def swapped_rims(values):
        out = pl.pallas_call(
            rim_kernel,
            out_shape=rim_shape(values.shape[1]),
            in_specs=[ANY],
            out_specs=VMEM,
            scratch_shapes=[pltpu.SemaphoreType.DMA],
            compiler_params=limit(FIRST_MIB),
            name="rim_blocks",
        )(values)
        return lax.ppermute(out, "strip", swap_strips)

    def cost(flops):
        return pl.CostEstimate(flops=flops, bytes_accessed=1, transcendentals=0)

    wide = cols // 2
    widths = HALO - REACH_LO + 1
    band_shape = (2, 2 * wide + 2 * TILE, wide)
    bands = pl.pallas_call(
        functools.partial(bands_kernel, cols),
        grid=(widths,),
        out_shape=jax.ShapeDtypeStruct((widths, *band_shape), jnp.bfloat16),
        out_specs=pl.BlockSpec((1, *band_shape), lambda n: (n, 0, 0, 0)),
        compiler_params=limit(WORK_MIB),
        cost_estimate=cost(1),
        name="range_bands",
    )()
    if halves:
        swap = [(i, (i + half) % devices) for i in range(devices)]

        def on_strip(route, strip):
            return [(2 * a + strip, 2 * b + strip) for a, b in route]

        both = ("date", "strip")
        first = lax.ppermute(slc, both, on_strip(swap, 0))
        rim = swapped_rims(slc)
        inner, outer, strips, whole = pl.pallas_call(
            functools.partial(beside_kernel, plan),
            out_shape=(
                payload_shape(NEAR),
                payload_shape(NEAR),
                jax.ShapeDtypeStruct((2, rows, TILE), dtype),
                images(dates),
            ),
            in_specs=[ANY, VMEM],
            out_specs=(VMEM, VMEM, VMEM, VMEM),
            scratch_shapes=[pltpu.SemaphoreType.DMA((2, NEAR, 2)), pltpu.SemaphoreType.DMA],
            compiler_params=limit(WORK_MIB),
            name="beside_images",
        )(slc, rim)
        down = [(i, (i - 1) % half) for i in range(half)]
        down += [(half + i, half + (i + 1) % half) for i in range(half)]
        outer = lax.ppermute(outer, "date", [(b, a) for a, b in down])
        inner = lax.ppermute(inner, "date", down)
        strips = lax.ppermute(strips, "date", swap)
        second = lax.ppermute(whole, both, on_strip(swap, 1))
    else:
        rim = swapped_rims(slc)
        annual = arrivals_by_distance(slc, pair_list, plan)
        strip = lax.axis_index("strip")
        ups = [(i, i + 1) for i in range(devices - 1)]
        inner = payload_of(slc[:, dates - NEAR :], rim[:, dates - NEAR :], strip)
        outer = payload_of(slc[:, :NEAR], rim[:, :NEAR], strip)
        inner = lax.ppermute(inner, "date", ups)
        outer = lax.ppermute(outer, "date", [(b, a) for a, b in ups])

    out_shape = jax.ShapeDtypeStruct((planes, dates * per_date, rows, cols), jnp.float32)
    depth = 2 * band_shape[1]
    scratch = [
        pltpu.VMEM((2, 4 * rows, depth), jnp.bfloat16),
        pltpu.VMEM((2, 4, 2 * rows, cols), jnp.bfloat16),
        pltpu.VMEM((2, planes, rows, cols), dtype),
        pltpu.VMEM((2, planes, rows, TILE), dtype),
        pltpu.VMEM((2, 2, planes, rows, cols), jnp.float32),
        pltpu.SMEM((dates * per_date + 1,), jnp.int32),
        pltpu.SemaphoreType.DMA((2, 2)),
    ]

    out, powers = pl.pallas_call(
        functools.partial(own_kernel, plan),
        out_shape=(out_shape, jax.ShapeDtypeStruct((dates, rows, depth), jnp.bfloat16)),
        in_specs=[SMEM] + [VMEM] * 3,
        out_specs=(ANY, VMEM),
        scratch_shapes=scratch,
        compiler_params=limit(WORK_MIB),
        cost_estimate=cost(20_000_000_000),
        name="own_pairs",
    )(lists, slc, rim, bands)

    mark_shape = jax.ShapeDtypeStruct((8, TILE), jnp.float32)

    def more_pairs(kernel, out, others, name, marks=()):
        return pl.pallas_call(
            functools.partial(kernel, plan),
            out_shape=(out_shape, *marks),
            in_specs=[SMEM] + [VMEM] * (4 + len(others)) + [ANY],
            out_specs=(ANY, *[VMEM for mark in marks]),
            scratch_shapes=scratch,
            input_output_aliases={5 + len(others): 0},
            compiler_params=limit(WORK_MIB),
            cost_estimate=cost(1),
            name=name,
        )(lists, slc, rim, bands, powers, *others, out)

    out, mark = more_pairs(rest_kernel, out, (inner, outer), "near_pairs", (mark_shape,))
    if halves:
        passed, middle = pl.pallas_call(
            functools.partial(pass_kernel, plan),
            out_shape=(payload_shape(late), payload_shape(NEAR)),
            in_specs=[ANY, ANY, VMEM, ANY],
            out_specs=(VMEM, VMEM),
            scratch_shapes=[pltpu.SemaphoreType.DMA((2 * (late + NEAR),))],
            compiler_params=limit(WORK_MIB),
            name="passed_images",
        )(first, second, strips, mark)
        along = [(i, i + 1) for i in range(half - 1)]
        along += [(half + i + 1, half + i) for i in range(half - 1)]
        middle = lax.ppermute(middle, "date", [(0, half - 1), (devices - 1, half)])
        passed = lax.ppermute(passed, "date", along)
        others = (inner, outer, first, second, strips)
        (out,) = more_pairs(annual_kernel, out, others, "annual_pairs")
        (out,) = more_pairs(last_kernel, out, (passed, middle), "last_pairs")
    else:
        (out,) = more_pairs(plain_kernel, out, (annual, swapped_rims(annual)), "annual_pairs")
    return out


def solution(mesh):
    placed = (P(None, "date", "groups", "strip"), P(), P(), P())
    return jax.shard_map(
        body,
        mesh=mesh,
        in_specs=placed,
        out_specs=P(None, "date", "groups", "strip"),
        check_vma=False,
    )
```

```python
import functools

import jax
import jax.numpy as jnp
from jax import lax
from jax.experimental import pallas as pl
from jax.experimental.pallas import tpu as pltpu
from jax.sharding import PartitionSpec as P

HALO = 16
REACH_LO = 12
NEAR = 3
YEAR = 29
EPSILON = 1e-06
TILE = 128
INNER = TILE // 2
PER_TILE = TILE // HALO
PARTNER, HEIGHT, REACH = 1, 2, 3
WORK_MIB = 16
FIRST_MIB = 56
ANY = pl.BlockSpec(memory_space=pl.ANY)
SMEM = pl.BlockSpec(memory_space=pltpu.SMEM)
VMEM = pl.BlockSpec(memory_space=pltpu.VMEM)


def limit(mebibytes):
    return pltpu.CompilerParams(vmem_limit_bytes=mebibytes * 1024 * 1024)


def run_copies(copies):
    for copy in copies:
        copy.start()
    for copy in copies:
        copy.wait()


def gather_strips(tiles, side):
    lane = lax.broadcasted_iota(jnp.int32, tiles[0].shape, 1)
    packed = jnp.zeros(tiles[0].shape, jnp.float32)
    for n, tile in enumerate(tiles):
        spot = n * HALO
        moved = pltpu.roll(tile.astype(jnp.float32), spot + side * HALO, 1)
        packed = jnp.where((lane >= spot) & (lane < spot + HALO), moved, packed)
    return packed.astype(jnp.bfloat16)


def place_strip(packed, n, side):
    shift = 2 * TILE - (n + side) * HALO
    return pltpu.roll(packed.astype(jnp.float32), lax.rem(shift, TILE), 1).astype(jnp.bfloat16)


def write_strips(out_ref, packed):
    rows, cols = packed.shape[0], out_ref.shape[1]
    part = rows * TILE // cols
    base = out_ref.shape[0] - part
    for n in range(rows // part):
        out_ref[base:, n * TILE : (n + 1) * TILE] = packed[n * part : (n + 1) * part]


def read_strips(ref, rows):
    cols = ref.shape[1]
    base = ref.shape[0] - rows * TILE // cols
    return jnp.concatenate(
        [ref[base:, n * TILE : (n + 1) * TILE] for n in range(cols // TILE)], axis=0
    )


def rim_kernel(slc_ref, rim_ref, sem):
    cols = slc_ref.shape[3]
    start = pl.multiple_of(jnp.where(lax.axis_index("strip") == 0, cols - TILE, 0), TILE)
    run_copies([pltpu.make_async_copy(slc_ref.at[:, :, :, pl.ds(start, TILE)], rim_ref, sem)])


def shared_copies(plan, slc_ref, shared_ref, sems):
    dates, late = plan["dates"], plan["late"]
    lower = lax.axis_index("date") < plan["devices"] // 2
    parts = (
        (jnp.where(lower, 0, dates - late), 0, late),
        (jnp.where(lower, dates - NEAR, 0), late, NEAR),
    )
    return [
        pltpu.make_async_copy(
            slc_ref.at[:, pl.ds(start, count)], shared_ref.at[:, pl.ds(at, count)], sems.at[n]
        )
        for n, (start, at, count) in enumerate(parts)
    ]


def early_kernel(plan, slc_ref, shared_ref, rim_ref, sems, rim_sem):
    strip, cols = lax.axis_index("strip"), plan["cols"]
    start = pl.multiple_of(jnp.where(strip == 0, cols - TILE, 0), TILE)
    rim_copy = pltpu.make_async_copy(slc_ref.at[:, :, :, pl.ds(start, TILE)], rim_ref, rim_sem)
    rim_copy.start()
    pl.when(strip == 0)(lambda: run_copies(shared_copies(plan, slc_ref, shared_ref, sems)))
    rim_copy.wait()


def beside_kernel(plan, slc_ref, rim_ref, inner_ref, outer_ref, strips_ref, shared_ref, single_ref,
                  sems, shared_sems, sem):
    me, strip = lax.axis_index("date"), lax.axis_index("strip")
    dates, late, rows = plan["dates"], plan["late"], plan["rows"]
    upper = me >= plan["devices"] // 2
    last = dates - NEAR
    rest = pl.ds(jnp.where(upper, NEAR, late), dates - NEAR - late)
    copies = [pltpu.make_async_copy(slc_ref.at[:, rest], single_ref, sem)]
    firsts = (jnp.where(upper, last, 0), jnp.where(upper, 0, last))
    for r, (out_ref, first) in enumerate(zip((inner_ref, outer_ref), firsts)):
        for k in range(NEAR):
            for c in range(2):
                here = out_ref.at[pl.ds((2 * k + c) * rows, rows)]
                copies.append(
                    pltpu.make_async_copy(slc_ref.at[c, first + k], here, sems.at[r, k, c])
                )
    for copy in copies:
        copy.start()
    pl.when(strip == 1)(
        lambda: run_copies(shared_copies(plan, slc_ref, shared_ref, shared_sems))
    )
    for out_ref, first in zip((inner_ref, outer_ref), firsts):
        tiles = [rim_ref[c, first + k] for k in range(NEAR) for c in range(2)]
        write_strips(out_ref, gather_strips(tiles, strip))
    tiles = [rim_ref[c, k] for k in range(dates) for c in range(2)]
    for n in range(2):
        part = tiles[n * PER_TILE : (n + 1) * PER_TILE]
        strips_ref[n] = gather_strips(part, strip)
    for copy in copies:
        copy.wait()


def opposite_strip(strips_ref, index, c, strip):
    n = 2 * index + c
    return place_strip(strips_ref[n // PER_TILE], lax.rem(n, PER_TILE), strip)


def pass_kernel(plan, first_ref, second_ref, strips_ref, _, pass_ref, middle_ref, sems):
    me, strip = lax.axis_index("date"), lax.axis_index("strip")
    dates, late, rows = plan["dates"], plan["late"], plan["rows"]
    lower = me < plan["devices"] // 2
    routes = (
        (pass_ref, late, 0, jnp.where(lower, dates - late, 0)),
        (middle_ref, NEAR, late, jnp.where(lower, 0, dates - NEAR)),
    )
    for source_strip, source in enumerate((first_ref, second_ref)):

        @pl.when(strip == source_strip)
        def _():
            copies = []
            for out_ref, count, at, _ in routes:
                for k in range(count):
                    for c in range(2):
                        here = out_ref.at[pl.ds((2 * k + c) * rows, rows)]
                        sem = sems.at[len(copies)]
                        copies.append(pltpu.make_async_copy(source.at[c, at + k], here, sem))
            run_copies(copies)

    for out_ref, count, _, start in routes:
        tiles = [
            opposite_strip(strips_ref, start + k, c, strip) for k in range(count) for c in range(2)
        ]
        write_strips(out_ref, gather_strips(tiles, strip))


def bands_kernel(cols, out_ref):
    strip = lax.axis_index("strip")
    wide = out_ref.shape[3]
    reach = pl.program_id(0) + REACH_LO

    def band(places, targets):
        return (jnp.abs(places - targets) <= reach).astype(jnp.float32).astype(jnp.bfloat16)

    def indices(shape):
        return lax.broadcasted_iota(jnp.int32, shape, 0), lax.broadcasted_iota(jnp.int32, shape, 1)

    inside = band(*indices((wide, wide)))
    row, col = indices((TILE, wide))
    beyond = jnp.where(strip == 0, cols + row, row - TILE)
    first = band(jnp.where(row < INNER, wide + row, beyond), col)
    second = band(jnp.where(row < INNER, beyond, wide - TILE + row), col + wide)
    for n, part in enumerate((first, second)):
        out_ref[0, n, 0:wide] = inside
        out_ref[0, n, wide : 2 * wide] = inside
        out_ref[0, n, 2 * wide : 2 * wide + TILE] = part
        out_ref[0, n, 2 * wide + TILE : 2 * wide + 2 * TILE] = part


def split(values):
    high = values.astype(jnp.bfloat16)
    low = (values - high.astype(jnp.float32)).astype(jnp.bfloat16)
    return high, low


def put(ref, here, t, values):
    wide = 2 * TILE
    depth = 2 * wide + 2 * TILE
    for low, part in enumerate(split(values)):
        side = [n * depth + 2 * wide + low * TILE for n in range(2)]
        if t < 4:
            at = (t // 2) * depth + low * wide + (t % 2) * TILE
            ref[*here, at : at + TILE] = part
        if t == 2:
            ref[*here, side[0] : side[0] + INNER] = part[:, :INNER]
        if t == 1:
            ref[*here, side[1] + INNER : side[1] + TILE] = part[:, INNER:]
        if t == 4:
            ref[*here, side[0] + INNER : side[0] + TILE] = part[:, INNER:]
            ref[*here, side[1] : side[1] + INNER] = part[:, :INNER]


def tile_of(main, rim, t):
    return [
        (rim(c) if t == 4 else main(c, slice(t * TILE, (t + 1) * TILE))).astype(jnp.float32)
        for c in range(2)
    ]


class Pairs:
    def __init__(self, plan, lists, slc_ref, rim_ref, bands_ref, powers_ref, out_ref, scratch):
        self.plan = plan
        self.lists = lists
        self.slc_ref, self.rim_ref = slc_ref, rim_ref
        self.bands_ref, self.powers_ref, self.out_ref = bands_ref, powers_ref, out_ref
        (self.left_ref, self.stack_ref, self.other_ref, self.other_rim_ref, self.stage_ref,
         self.list_ref, self.sems) = scratch
        self.me, self.strip = lax.axis_index("date"), lax.axis_index("strip")

    def partner(self, pair):
        return self.lists[PARTNER, pair]

    def item(self, n):
        slot, kind = n // self.plan["per_date"], lax.rem(n, self.plan["per_date"])
        first = self.me * self.plan["dates"]
        pair = first * self.plan["per_date"] + n
        return slot, kind, self.partner(pair) - first

    def chosen(self, test):
        count = 0
        for n in range(self.plan["dates"] * self.plan["per_date"]):
            self.list_ref[count] = n
            local = self.item(n)[2]
            near = n % self.plan["per_date"] < NEAR
            count = count + jnp.where(test(near, local), 1, 0)
        return count

    def own(self, local):
        return (local >= 0) & (local < self.plan["dates"])

    def in_middle(self, local):
        half, dates = self.plan["devices"] // 2, self.plan["dates"]
        if not self.plan["halves"]:
            return False
        return ((self.me == half) & (local < 0)) | ((self.me == half - 1) & (local >= dates))

    def opposite(self, local):
        half, dates = self.plan["devices"] // 2, self.plan["dates"]
        return local - jnp.where(self.me < half, half * dates, -half * dates)

    def in_half(self, local):
        half, dates = self.plan["devices"] // 2, self.plan["dates"]
        return (local + self.me * dates < half * dates) == (self.me < half)

    def passed(self, local):
        return jnp.logical_not(self.in_half(local) | self.own(self.opposite(local)))

    def own_other(self, index):
        return (
            lambda c, cols: self.slc_ref[c, index, :, cols],
            lambda c: self.rim_ref[c, index],
        )

    def fetched_other(self, x):
        return (
            lambda c, cols: self.other_ref[x, c, :, cols],
            lambda c: self.other_rim_ref[x, c],
        )

    def fetch_payload(self, x, ref, index):
        rows = self.plan["rows"]
        packed = read_strips(ref, rows)
        for c in range(2):
            at = pl.multiple_of((2 * index + c) * rows, rows)
            self.other_ref[x, c] = ref[pl.ds(at, rows)]
            self.other_rim_ref[x, c] = place_strip(packed, 2 * index + c, self.strip)

    def out_copy(self, stage, x, pair):
        return pltpu.make_async_copy(
            self.stage_ref.at[stage, x], self.out_ref.at[:, pair], self.sems.at[stage, x]
        )

    def run(self, count, work):
        steps = (count + 1) // 2

        def step(n, carry):
            stage = lax.rem(n, 2)

            @pl.when(n >= 2)
            def _():
                for x in range(2):
                    self.out_copy(stage, x, 0).wait()

            items = [work(x, jnp.minimum(2 * n + x, count - 1)) for x in range(2)]
            self.compute(stage, items)
            for x, (slot, kind, _, _) in enumerate(items):
                copy = self.out_copy(stage, x, slot * self.plan["per_date"] + kind)
                pl.when(2 * n + x < count)(copy.start)
            return carry

        lax.fori_loop(0, steps, step, 0)
        for back in (2, 1):
            for x in range(2):
                used = (steps >= back) & (2 * (steps - back) + x < count)
                pl.when(used)(self.out_copy(lax.rem(steps + back, 2), x, 0).wait)

    def compute(self, stage, items):
        plan = self.plan
        rows, dates, per_date = plan["rows"], plan["dates"], plan["per_date"]
        part = [(pl.ds(f * rows, rows),) for f in range(4)]
        depth = self.bands_ref.shape[2]
        wide = self.bands_ref.shape[3]
        heights, widths = [], []
        for slot, kind, _, _ in items:
            pair = (self.me * dates + slot) * per_date + kind
            heights.append(self.lists[HEIGHT, pair])
            widths.append(jnp.clip(self.lists[REACH, pair] - REACH_LO, 0, HALO - REACH_LO))
        for x, (slot, kind, other, other_power) in enumerate(items):
            left_ref = self.left_ref.at[x]
            left_ref[*part[2]] = self.powers_ref[slot]
            if other_power is not None:
                left_ref[*part[3]] = self.powers_ref[other_power]
            first = self.own_other(slot)
            for t in range(5):
                a_real, a_imag = tile_of(*first, t)
                b_real, b_imag = tile_of(*other, t)
                put(left_ref, part[0], t, a_real * b_real + a_imag * b_imag)
                put(left_ref, part[1], t, a_imag * b_real - a_real * b_imag)
                if other_power is None:
                    put(left_ref, part[3], t, b_real * b_real + b_imag * b_imag)
        for n in range(2):
            for x in range(2):
                ranged = jnp.dot(
                    self.left_ref[x, :, n * depth : (n + 1) * depth],
                    self.bands_ref[widths[x], n],
                    preferred_element_type=jnp.float32,
                )
                there = slice(n * wide, (n + 1) * wide)
                for low, values in enumerate(split(ranged)):
                    for f in range(4):
                        self.stack_ref[x, f, low * rows : (low + 1) * rows, there] = values[
                            f * rows : (f + 1) * rows
                        ]
        row = lax.broadcasted_iota(jnp.int32, (rows, 2 * rows), 0)
        col = lax.broadcasted_iota(jnp.int32, (rows, 2 * rows), 1)
        col = jnp.where(col < rows, col, col - rows)
        for x in range(2):
            band = (jnp.abs(row - col) <= heights[x]).astype(jnp.float32).astype(jnp.bfloat16)
            looked = [
                jnp.dot(band, self.stack_ref[x, f], preferred_element_type=jnp.float32)
                for f in range(4)
            ]
            inverse = lax.rsqrt(looked[2] * looked[3] + EPSILON)
            for c in range(2):
                self.stage_ref[stage, x, c] = looked[c] * inverse


def own_kernel(plan, lists, slc_ref, rim_ref, bands_ref, out_ref, powers_ref, *scratch):
    pairs = Pairs(plan, lists, slc_ref, rim_ref, bands_ref, powers_ref, out_ref, scratch)
    dates = plan["dates"]

    def power(slot, carry):
        for t in range(5):
            real, imag = tile_of(*pairs.own_other(slot), t)
            put(powers_ref, (slot, slice(None)), t, real * real + imag * imag)
        return carry

    lax.fori_loop(0, dates, power, 0)

    def work(x, n):
        slot, kind, local = pairs.item(pairs.list_ref[n])
        return slot, kind, pairs.own_other(local), local

    pairs.run(pairs.chosen(lambda near, local: near and pairs.own(local)), work)


def rest_kernel(plan, lists, slc_ref, rim_ref, bands_ref, powers_ref, inner_ref, outer_ref, _sent,
                _, out_ref, *scratch):
    pairs = Pairs(plan, lists, slc_ref, rim_ref, bands_ref, powers_ref, out_ref, scratch)
    dates = plan["dates"]
    upper = pairs.me >= plan["devices"] // 2 if plan["halves"] else True

    def work(x, n):
        slot, kind, local = pairs.item(pairs.list_ref[n])
        below = local < 0
        index = jnp.clip(jnp.where(below, local + NEAR, local - dates), 0, NEAR - 1)
        inner = below == upper
        pl.when(inner)(lambda: pairs.fetch_payload(x, inner_ref, index))
        pl.when(jnp.logical_not(inner))(lambda: pairs.fetch_payload(x, outer_ref, index))
        return slot, kind, pairs.fetched_other(x), None

    def test(near, local):
        return near and jnp.logical_not(pairs.own(local) | pairs.in_middle(local))

    pairs.run(pairs.chosen(test), work)


def annual_kernel(plan, lists, slc_ref, rim_ref, bands_ref, powers_ref, inner_ref, outer_ref,
                  first_ref, second_ref, single_ref, strips_ref, _, out_ref, *scratch):
    pairs = Pairs(plan, lists, slc_ref, rim_ref, bands_ref, powers_ref, out_ref, scratch)
    dates, half = plan["dates"], plan["devices"] // 2
    me, strip = pairs.me, pairs.strip
    lower = me < half

    late = plan["late"]

    def fetch_opposite(x, ref, at, index):
        for c in range(2):
            pairs.other_ref[x, c] = ref[c, index]
            pairs.other_rim_ref[x, c] = opposite_strip(strips_ref, at, c, strip)

    def work(x, n):
        slot, kind, local = pairs.item(pairs.list_ref[n])
        far = pairs.in_half(local)
        from_inner = jnp.where(lower, me != 0, me == half)
        other, split_date = local + me * dates, half * dates
        inner_at = jnp.where(lower, other, other - (2 * split_date - NEAR))
        outer_at = jnp.where(lower, other - (split_date - NEAR), other - split_date)
        inner_at, outer_at = jnp.clip(inner_at, 0, NEAR - 1), jnp.clip(outer_at, 0, NEAR - 1)
        at = jnp.clip(pairs.opposite(local), 0, dates - 1)
        pl.when(far & from_inner)(lambda: pairs.fetch_payload(x, inner_ref, inner_at))
        pl.when(far & jnp.logical_not(from_inner))(
            lambda: pairs.fetch_payload(x, outer_ref, outer_at)
        )
        across = jnp.logical_not(far)
        beside_at = at - jnp.where(lower, dates - late, 0)
        middle_at = at - jnp.where(lower, 0, dates - NEAR)
        single_at = at - jnp.where(lower, NEAR, late)
        is_beside = (beside_at >= 0) & (beside_at < late)
        is_middle = (middle_at >= 0) & (middle_at < NEAR)
        shared = across & (is_beside | is_middle)
        index = jnp.where(is_beside, beside_at, middle_at + late)
        index = jnp.clip(index, 0, late + NEAR - 1)
        single_at = jnp.clip(single_at, 0, dates - late - NEAR - 1)
        pl.when(shared & (strip == 0))(lambda: fetch_opposite(x, first_ref, at, index))
        pl.when(shared & (strip == 1))(lambda: fetch_opposite(x, second_ref, at, index))
        pl.when(across & jnp.logical_not(shared))(
            lambda: fetch_opposite(x, single_ref, at, single_at)
        )
        return slot, kind, pairs.fetched_other(x), None

    def test(near, local):
        return not near and jnp.logical_not(pairs.passed(local))

    pairs.run(pairs.chosen(test), work)


def last_kernel(plan, lists, slc_ref, rim_ref, bands_ref, powers_ref, pass_ref, middle_ref, _,
                out_ref, *scratch):
    pairs = Pairs(plan, lists, slc_ref, rim_ref, bands_ref, powers_ref, out_ref, scratch)
    dates, late = plan["dates"], plan["late"]

    def work(x, n):
        slot, kind, local = pairs.item(pairs.list_ref[n])
        across = pairs.opposite(local)
        pass_at = jnp.clip(jnp.where(across < 0, across + late, across - dates), 0, late - 1)
        middle_at = jnp.clip(jnp.where(local < 0, local + NEAR, local - dates), 0, NEAR - 1)
        pl.when(kind < NEAR)(lambda: pairs.fetch_payload(x, middle_ref, middle_at))
        pl.when(kind == NEAR)(lambda: pairs.fetch_payload(x, pass_ref, pass_at))
        return slot, kind, pairs.fetched_other(x), None

    def test(near, local):
        return pairs.in_middle(local) if near else pairs.passed(local)

    pairs.run(pairs.chosen(test), work)


def plain_kernel(plan, lists, slc_ref, rim_ref, bands_ref, powers_ref, images_ref,
                 image_rim_ref, _, out_ref, *scratch):
    pairs = Pairs(plan, lists, slc_ref, rim_ref, bands_ref, powers_ref, out_ref, scratch)

    def work(x, slot):
        other = (
            lambda c, cols: images_ref[c, slot, :, cols],
            lambda c: image_rim_ref[c, slot],
        )
        return slot, NEAR, other, None

    pairs.run(plan["dates"], work)


def arrivals_by_distance(slc, pair_list, plan):
    dates, per_date, devices = plan["dates"], plan["per_date"], plan["devices"]
    total = dates * devices
    me = lax.axis_index("date")
    annual_of = pair_list[:, 1].reshape(total, per_date)[:, per_date - 1]
    sums = [None] * dates
    for direction in (1, -1):
        by_distance = {}
        for slot in range(dates):
            for gap in range(plan["year"], plan["year"] + 3):
                distance = (slot + direction * gap) // dates
                by_distance.setdefault(distance, set()).add(slot)
        for distance in sorted(by_distance):
            slots = sorted(by_distance[distance])
            wanted_by = (me - distance) * dates + jnp.array(slots, dtype=jnp.int32)
            inside = (wanted_by >= 0) & (wanted_by < total)
            local = jnp.take(annual_of, jnp.clip(wanted_by, 0, total - 1)) - me * dates
            usable = inside & (local >= 0) & (local < dates)
            packed = jnp.take(slc, jnp.clip(local, 0, dates - 1), axis=1)
            packed = jnp.where(usable[None, :, None, None], packed, jnp.zeros_like(packed))
            route = [(i + distance, i) for i in range(devices) if 0 <= i + distance < devices]
            arrived = lax.ppermute(packed, "date", route)
            for n, slot in enumerate(slots):
                part = arrived[:, n]
                sums[slot] = part if sums[slot] is None else sums[slot] + part
    return jnp.stack(sums, axis=1)


def payload_of(images, rim, strip):
    planes, count, rows, cols = images.shape
    edges = jnp.where(strip == 0, rim[..., :HALO], rim[..., TILE - HALO :])
    edges = jnp.transpose(edges, (2, 1, 0, 3)).reshape(rows, count * planes * HALO)
    edges = jnp.pad(edges, ((0, 0), (0, TILE - edges.shape[1])))
    part = rows * TILE // cols
    edges = jnp.transpose(edges.reshape(rows // part, part, TILE), (1, 0, 2)).reshape(part, cols)
    stacked = jnp.transpose(images, (1, 0, 2, 3)).reshape(count * planes * rows, cols)
    return jnp.concatenate([stacked, edges], axis=0)


def body(slc, pair_list, az_half, rng_half):
    planes, dates, rows, cols = slc.shape
    devices = lax.axis_size("date")
    total = dates * devices
    per_date = pair_list.shape[0] // total
    year = min(YEAR, total // 2 - 2)
    half = devices // 2
    late = half * dates - year
    halves = devices % 2 == 0 and 0 < late <= NEAR and 2 * late <= dates
    halves = halves and late + NEAR < dates <= PER_TILE
    plan = {
        "dates": dates,
        "devices": devices,
        "per_date": per_date,
        "year": year,
        "late": late,
        "rows": rows,
        "cols": cols,
        "pairs": total * per_date,
        "halves": halves,
    }
    dtype = slc.dtype
    rim_rows = rows * TILE // cols
    lists = jnp.concatenate([pair_list.T, az_half[None], rng_half[None]])
    swap_strips = [(0, 1), (1, 0)]

    def images(count):
        return jax.ShapeDtypeStruct((planes, count, rows, cols), dtype)

    def rim_shape(count):
        return jax.ShapeDtypeStruct((planes, count, rows, TILE), dtype)

    def payload_shape(count):
        return jax.ShapeDtypeStruct((planes * count * rows + rim_rows, cols), dtype)

    def swapped_rims(values):
        out = pl.pallas_call(
            rim_kernel,
            out_shape=rim_shape(values.shape[1]),
            in_specs=[ANY],
            out_specs=VMEM,
            scratch_shapes=[pltpu.SemaphoreType.DMA],
            compiler_params=limit(FIRST_MIB),
            name="rim_blocks",
        )(values)
        return lax.ppermute(out, "strip", swap_strips)

    def cost(flops):
        return pl.CostEstimate(flops=flops, bytes_accessed=1, transcendentals=0)

    wide = cols // 2
    widths = HALO - REACH_LO + 1
    band_shape = (2, 2 * wide + 2 * TILE, wide)
    bands = pl.pallas_call(
        functools.partial(bands_kernel, cols),
        grid=(widths,),
        out_shape=jax.ShapeDtypeStruct((widths, *band_shape), jnp.bfloat16),
        out_specs=pl.BlockSpec((1, *band_shape), lambda n: (n, 0, 0, 0)),
        compiler_params=limit(WORK_MIB),
        cost_estimate=cost(1),
        name="range_bands",
    )()
    if halves:
        swap = [(i, (i + half) % devices) for i in range(devices)]

        def on_strip(route, strip):
            return [(2 * a + strip, 2 * b + strip) for a, b in route]

        both = ("date", "strip")
        first, rim = pl.pallas_call(
            functools.partial(early_kernel, plan),
            out_shape=(images(late + NEAR), rim_shape(dates)),
            in_specs=[ANY],
            out_specs=(VMEM, VMEM),
            scratch_shapes=[pltpu.SemaphoreType.DMA((2,)), pltpu.SemaphoreType.DMA],
            compiler_params=limit(FIRST_MIB),
            name="early_images",
        )(slc)
        first = lax.ppermute(first, both, on_strip(swap, 0))
        rim = lax.ppermute(rim, "strip", swap_strips)
        inner, outer, strips, second, single = pl.pallas_call(
            functools.partial(beside_kernel, plan),
            out_shape=(
                payload_shape(NEAR),
                payload_shape(NEAR),
                jax.ShapeDtypeStruct((2, rows, TILE), dtype),
                images(late + NEAR),
                images(dates - late - NEAR),
            ),
            in_specs=[ANY, VMEM],
            out_specs=(VMEM,) * 5,
            scratch_shapes=[
                pltpu.SemaphoreType.DMA((2, NEAR, 2)),
                pltpu.SemaphoreType.DMA((2,)),
                pltpu.SemaphoreType.DMA,
            ],
            compiler_params=limit(WORK_MIB),
            name="beside_images",
        )(slc, rim)
        down = [(i, (i - 1) % half) for i in range(half)]
        down += [(half + i, half + (i + 1) % half) for i in range(half)]
        outer = lax.ppermute(outer, "date", [(b, a) for a, b in down])
        inner = lax.ppermute(inner, "date", down)
        strips = lax.ppermute(strips, "date", swap)
        second = lax.ppermute(second, both, on_strip(swap, 1))
        single = lax.ppermute(single, "date", swap)
    else:
        rim = swapped_rims(slc)
        annual = arrivals_by_distance(slc, pair_list, plan)
        strip = lax.axis_index("strip")
        ups = [(i, i + 1) for i in range(devices - 1)]
        inner = payload_of(slc[:, dates - NEAR :], rim[:, dates - NEAR :], strip)
        outer = payload_of(slc[:, :NEAR], rim[:, :NEAR], strip)
        inner = lax.ppermute(inner, "date", ups)
        outer = lax.ppermute(outer, "date", [(b, a) for a, b in ups])

    out_shape = jax.ShapeDtypeStruct((planes, dates * per_date, rows, cols), jnp.float32)
    depth = 2 * band_shape[1]
    scratch = [
        pltpu.VMEM((2, 4 * rows, depth), jnp.bfloat16),
        pltpu.VMEM((2, 4, 2 * rows, cols), jnp.bfloat16),
        pltpu.VMEM((2, planes, rows, cols), dtype),
        pltpu.VMEM((2, planes, rows, TILE), dtype),
        pltpu.VMEM((2, 2, planes, rows, cols), jnp.float32),
        pltpu.SMEM((dates * per_date + 1,), jnp.int32),
        pltpu.SemaphoreType.DMA((2, 2)),
    ]

    out, powers = pl.pallas_call(
        functools.partial(own_kernel, plan),
        out_shape=(out_shape, jax.ShapeDtypeStruct((dates, rows, depth), jnp.bfloat16)),
        in_specs=[SMEM] + [VMEM] * 3,
        out_specs=(ANY, VMEM),
        scratch_shapes=scratch,
        compiler_params=limit(WORK_MIB),
        cost_estimate=cost(20_000_000_000),
        name="own_pairs",
    )(lists, slc, rim, bands)

    def more_pairs(kernel, out, others, name):
        return pl.pallas_call(
            functools.partial(kernel, plan),
            out_shape=out_shape,
            in_specs=[SMEM] + [VMEM] * (4 + len(others)) + [ANY],
            out_specs=ANY,
            scratch_shapes=scratch,
            input_output_aliases={5 + len(others): 0},
            compiler_params=limit(WORK_MIB),
            cost_estimate=cost(1),
            name=name,
        )(lists, slc, rim, bands, powers, *others, out)

    if halves:
        passed, middle = pl.pallas_call(
            functools.partial(pass_kernel, plan),
            out_shape=(payload_shape(late), payload_shape(NEAR)),
            in_specs=[ANY, ANY, VMEM, ANY],
            out_specs=(VMEM, VMEM),
            scratch_shapes=[pltpu.SemaphoreType.DMA((2 * (late + NEAR),))],
            compiler_params=limit(WORK_MIB),
            name="passed_images",
        )(first, second, strips, powers)
        along = [(i, i + 1) for i in range(half - 1)]
        along += [(half + i + 1, half + i) for i in range(half - 1)]
        sent = passed
        middle = lax.ppermute(middle, "date", [(0, half - 1), (devices - 1, half)])
        passed = lax.ppermute(passed, "date", along)
    else:
        sent = inner
    out = more_pairs(rest_kernel, out, (inner, outer, sent), "near_pairs")
    if halves:
        others = (inner, outer, first, second, single, strips)
        out = more_pairs(annual_kernel, out, others, "annual_pairs")
        out = more_pairs(last_kernel, out, (passed, middle), "last_pairs")
    else:
        out = more_pairs(plain_kernel, out, (annual, swapped_rims(annual)), "annual_pairs")
    return out


def solution(mesh):
    placed = (P(None, "date", "groups", "strip"), P(), P(), P())
    return jax.shard_map(
        body,
        mesh=mesh,
        in_specs=placed,
        out_specs=P(None, "date", "groups", "strip"),
        check_vma=False,
    )
```

```python
import functools

import jax
import jax.numpy as jnp
from jax import lax
from jax.experimental import pallas as pl
from jax.experimental.pallas import tpu as pltpu
from jax.sharding import PartitionSpec as P

HALO = 16
REACH_LO = 12
NEAR = 3
YEAR = 29
EPSILON = 1e-06
TILE = 128
INNER = TILE // 2
PARTNER, HEIGHT, REACH = 1, 2, 3
WORK_MIB = 16
FIRST_MIB = 56
ANY = pl.BlockSpec(memory_space=pl.ANY)
SMEM = pl.BlockSpec(memory_space=pltpu.SMEM)
VMEM = pl.BlockSpec(memory_space=pltpu.VMEM)


def limit(mebibytes):
    return pltpu.CompilerParams(vmem_limit_bytes=mebibytes * 1024 * 1024)


def run_copies(copies):
    for copy in copies:
        copy.start()
    for copy in copies:
        copy.wait()


def gather_strips(tiles, side):
    lane = lax.broadcasted_iota(jnp.int32, tiles[0].shape, 1)
    packed = jnp.zeros(tiles[0].shape, jnp.float32)
    for n, tile in enumerate(tiles):
        spot = n * HALO
        moved = pltpu.roll(tile.astype(jnp.float32), spot + side * HALO, 1)
        packed = jnp.where((lane >= spot) & (lane < spot + HALO), moved, packed)
    return packed.astype(jnp.bfloat16)


def place_strip(packed, n, side):
    shift = 2 * TILE - (n + side) * HALO
    return pltpu.roll(packed.astype(jnp.float32), lax.rem(shift, TILE), 1).astype(jnp.bfloat16)


def write_strips(out_ref, packed):
    rows, cols = packed.shape[0], out_ref.shape[1]
    part = rows * TILE // cols
    base = out_ref.shape[0] - part
    for n in range(rows // part):
        out_ref[base:, n * TILE : (n + 1) * TILE] = packed[n * part : (n + 1) * part]


def read_strips(ref, rows):
    cols = ref.shape[1]
    base = ref.shape[0] - rows * TILE // cols
    return jnp.concatenate(
        [ref[base:, n * TILE : (n + 1) * TILE] for n in range(cols // TILE)], axis=0
    )


def wanted_images(plan, pairs_ref):
    me = lax.axis_index("date")
    dates, half = plan["dates"], plan["devices"] // 2
    mate = lax.rem(me + half, 2 * half)
    wanted = []
    for k in range(dates - plan["late"]):
        date = mate * dates + jnp.where(mate < half, plan["late"], 0) + k
        at = pairs_ref[PARTNER, date * plan["per_date"] + NEAR] - me * dates
        wanted.append(jnp.clip(at, 0, dates - 1))
    return wanted


def image_copies(slc_ref, wanted, early_ref, sems):
    return [
        pltpu.make_async_copy(slc_ref.at[:, at], early_ref.at[:, k], sems.at[k])
        for k, at in enumerate(wanted)
    ]


def early_kernel(plan, slc_ref, pairs_ref, early_ref, rim_ref, strips_ref, tiles_ref, sems,
                 tile_sems, rim_sem):
    strip, cols = lax.axis_index("strip"), plan["cols"]
    start = pl.multiple_of(jnp.where(strip == 0, cols - TILE, 0), TILE)
    wanted = wanted_images(plan, pairs_ref)
    rim_copy = pltpu.make_async_copy(slc_ref.at[:, :, :, pl.ds(start, TILE)], rim_ref, rim_sem)
    early_copies = image_copies(slc_ref, wanted, early_ref, sems)
    tile_copies = [
        pltpu.make_async_copy(
            slc_ref.at[:, at, :, pl.ds(start, TILE)], tiles_ref.at[k], tile_sems.at[k]
        )
        for k, at in enumerate(wanted)
    ]
    for copy in tile_copies + [rim_copy] + early_copies:
        copy.start()
    for copy in tile_copies:
        copy.wait()
    tiles = [tiles_ref[k, c] for k in range(len(wanted)) for c in range(2)]
    strips_ref[...] = gather_strips(tiles, 1 - strip)
    for copy in [rim_copy] + early_copies:
        copy.wait()


def rim_kernel(slc_ref, rim_ref, sem):
    cols = slc_ref.shape[3]
    start = pl.multiple_of(jnp.where(lax.axis_index("strip") == 0, cols - TILE, 0), TILE)
    run_copies([pltpu.make_async_copy(slc_ref.at[:, :, :, pl.ds(start, TILE)], rim_ref, sem)])


def beside_kernel(plan, slc_ref, rim_ref, inner_ref, outer_ref, sems):
    me, strip = lax.axis_index("date"), lax.axis_index("strip")
    dates, rows = plan["dates"], plan["rows"]
    upper = me >= plan["devices"] // 2
    last = dates - NEAR
    copies = []
    firsts = (jnp.where(upper, last, 0), jnp.where(upper, 0, last))
    for r, (out_ref, first) in enumerate(zip((inner_ref, outer_ref), firsts)):
        for k in range(NEAR):
            for c in range(2):
                here = out_ref.at[pl.ds((2 * k + c) * rows, rows)]
                copies.append(
                    pltpu.make_async_copy(slc_ref.at[c, first + k], here, sems.at[r, k, c])
                )
    for copy in copies:
        copy.start()
    for out_ref, first in zip((inner_ref, outer_ref), firsts):
        tiles = [rim_ref[c, first + k] for k in range(NEAR) for c in range(2)]
        write_strips(out_ref, gather_strips(tiles, strip))
    for copy in copies:
        copy.wait()


def late_kernel(plan, slc_ref, rim_ref, inner_ref, pairs_ref, *refs):
    late_ref, tiles_ref = refs[-2:]
    me, strip = lax.axis_index("date"), lax.axis_index("strip")
    dates, late, rows = plan["dates"], plan["late"], plan["rows"]
    half = plan["devices"] // 2
    mate = lax.rem(me + half, 2 * half)
    mate_slot = jnp.where(mate < half, 0, dates - late)
    packed = read_strips(inner_ref, rows)
    for k in range(late):
        date = mate * dates + mate_slot + k
        wanted = pairs_ref[PARTNER, date * plan["per_date"] + NEAR] - me * dates
        own = (wanted >= 0) & (wanted < dates)
        own_at = jnp.clip(wanted, 0, dates - 1)
        other_at = jnp.clip(jnp.where(me < half, wanted - dates, wanted + NEAR), 0, NEAR - 1)
        for c in range(2):
            here = pl.ds((2 * k + c) * rows, rows)

            @pl.when(own)
            def _():
                late_ref[here] = slc_ref[c, own_at]
                tiles_ref[k, c] = rim_ref[c, own_at]

            @pl.when(jnp.logical_not(own))
            def _():
                there = pl.multiple_of((2 * other_at + c) * rows, rows)
                late_ref[here] = inner_ref[pl.ds(there, rows)]
                tiles_ref[k, c] = place_strip(packed, 2 * other_at + c, strip)

    tiles = [tiles_ref[k, c] for k in range(late) for c in range(2)]
    write_strips(late_ref, gather_strips(tiles, strip))


def bands_kernel(cols, out_ref):
    strip = lax.axis_index("strip")
    wide = out_ref.shape[3]
    reach = pl.program_id(0) + REACH_LO

    def band(places, targets):
        return (jnp.abs(places - targets) <= reach).astype(jnp.float32).astype(jnp.bfloat16)

    def indices(shape):
        return lax.broadcasted_iota(jnp.int32, shape, 0), lax.broadcasted_iota(jnp.int32, shape, 1)

    inside = band(*indices((wide, wide)))
    row, col = indices((TILE, wide))
    beyond = jnp.where(strip == 0, cols + row, row - TILE)
    first = band(jnp.where(row < INNER, wide + row, beyond), col)
    second = band(jnp.where(row < INNER, beyond, wide - TILE + row), col + wide)
    for n, part in enumerate((first, second)):
        out_ref[0, n, 0:wide] = inside
        out_ref[0, n, wide : 2 * wide] = inside
        out_ref[0, n, 2 * wide : 2 * wide + TILE] = part
        out_ref[0, n, 2 * wide + TILE : 2 * wide + 2 * TILE] = part


def split(values):
    high = values.astype(jnp.bfloat16)
    low = (values - high.astype(jnp.float32)).astype(jnp.bfloat16)
    return high, low


def put(ref, here, t, values):
    wide = 2 * TILE
    depth = 2 * wide + 2 * TILE
    for low, part in enumerate(split(values)):
        side = [n * depth + 2 * wide + low * TILE for n in range(2)]
        if t < 4:
            at = (t // 2) * depth + low * wide + (t % 2) * TILE
            ref[*here, at : at + TILE] = part
        if t == 2:
            ref[*here, side[0] : side[0] + INNER] = part[:, :INNER]
        if t == 1:
            ref[*here, side[1] + INNER : side[1] + TILE] = part[:, INNER:]
        if t == 4:
            ref[*here, side[0] + INNER : side[0] + TILE] = part[:, INNER:]
            ref[*here, side[1] : side[1] + INNER] = part[:, :INNER]


def tile_of(main, rim, t):
    return [
        (rim(c) if t == 4 else main(c, slice(t * TILE, (t + 1) * TILE))).astype(jnp.float32)
        for c in range(2)
    ]


class Pairs:
    def __init__(self, plan, lists, slc_ref, rim_ref, bands_ref, powers_ref, out_ref, scratch):
        self.plan = plan
        self.lists = lists
        self.slc_ref, self.rim_ref = slc_ref, rim_ref
        self.bands_ref, self.powers_ref, self.out_ref = bands_ref, powers_ref, out_ref
        (self.left_ref, self.stack_ref, self.other_ref, self.other_rim_ref, self.stage_ref,
         self.list_ref, self.sems) = scratch
        self.me, self.strip = lax.axis_index("date"), lax.axis_index("strip")

    def partner(self, pair):
        return self.lists[PARTNER, pair]

    def near_item(self, n):
        slot, kind = n // NEAR, lax.rem(n, NEAR)
        dates = self.plan["dates"]
        pair = (self.me * dates + slot) * self.plan["per_date"] + kind
        return slot, kind, self.partner(pair) - self.me * dates

    def near_list(self, chosen):
        count = 0
        for n in range(self.plan["dates"] * NEAR):
            self.list_ref[count] = n
            count = count + jnp.where(chosen(self.near_item(n)[2]), 1, 0)
        return count

    def own(self, local):
        return (local >= 0) & (local < self.plan["dates"])

    def in_middle(self, local):
        half, dates = self.plan["devices"] // 2, self.plan["dates"]
        if not self.plan["halves"]:
            return False
        return ((self.me == half) & (local < 0)) | ((self.me == half - 1) & (local >= dates))

    def own_other(self, index):
        return (
            lambda c, cols: self.slc_ref[c, index, :, cols],
            lambda c: self.rim_ref[c, index],
        )

    def fetched_other(self, x):
        return (
            lambda c, cols: self.other_ref[x, c, :, cols],
            lambda c: self.other_rim_ref[x, c],
        )

    def fetch_payload(self, x, ref, index):
        rows = self.plan["rows"]
        packed = read_strips(ref, rows)
        for c in range(2):
            at = pl.multiple_of((2 * index + c) * rows, rows)
            self.other_ref[x, c] = ref[pl.ds(at, rows)]
            self.other_rim_ref[x, c] = place_strip(packed, 2 * index + c, self.strip)

    def out_copy(self, stage, x, pair):
        return pltpu.make_async_copy(
            self.stage_ref.at[stage, x], self.out_ref.at[:, pair], self.sems.at[stage, x]
        )

    def run(self, count, work):
        steps = (count + 1) // 2

        def step(n, carry):
            stage = lax.rem(n, 2)

            @pl.when(n >= 2)
            def _():
                for x in range(2):
                    self.out_copy(stage, x, 0).wait()

            items = [work(x, jnp.minimum(2 * n + x, count - 1)) for x in range(2)]
            self.compute(stage, items)
            for x, (slot, kind, _, _) in enumerate(items):
                copy = self.out_copy(stage, x, slot * self.plan["per_date"] + kind)
                pl.when(2 * n + x < count)(copy.start)
            return carry

        lax.fori_loop(0, steps, step, 0)
        for back in (2, 1):
            for x in range(2):
                used = (steps >= back) & (2 * (steps - back) + x < count)
                pl.when(used)(self.out_copy(lax.rem(steps + back, 2), x, 0).wait)

    def compute(self, stage, items):
        plan = self.plan
        rows, dates, per_date = plan["rows"], plan["dates"], plan["per_date"]
        part = [(pl.ds(f * rows, rows),) for f in range(4)]
        depth = self.bands_ref.shape[2]
        wide = self.bands_ref.shape[3]
        heights, widths = [], []
        for slot, kind, _, _ in items:
            pair = (self.me * dates + slot) * per_date + kind
            heights.append(self.lists[HEIGHT, pair])
            widths.append(jnp.clip(self.lists[REACH, pair] - REACH_LO, 0, HALO - REACH_LO))
        for x, (slot, kind, other, other_power) in enumerate(items):
            left_ref = self.left_ref.at[x]
            left_ref[*part[2]] = self.powers_ref[slot]
            if other_power is not None:
                left_ref[*part[3]] = self.powers_ref[other_power]
            first = self.own_other(slot)
            for t in range(5):
                a_real, a_imag = tile_of(*first, t)
                b_real, b_imag = tile_of(*other, t)
                put(left_ref, part[0], t, a_real * b_real + a_imag * b_imag)
                put(left_ref, part[1], t, a_imag * b_real - a_real * b_imag)
                if other_power is None:
                    put(left_ref, part[3], t, b_real * b_real + b_imag * b_imag)
        for n in range(2):
            for x in range(2):
                ranged = jnp.dot(
                    self.left_ref[x, :, n * depth : (n + 1) * depth],
                    self.bands_ref[widths[x], n],
                    preferred_element_type=jnp.float32,
                )
                there = slice(n * wide, (n + 1) * wide)
                for low, values in enumerate(split(ranged)):
                    for f in range(4):
                        self.stack_ref[x, f, low * rows : (low + 1) * rows, there] = values[
                            f * rows : (f + 1) * rows
                        ]
        row = lax.broadcasted_iota(jnp.int32, (rows, 2 * rows), 0)
        col = lax.broadcasted_iota(jnp.int32, (rows, 2 * rows), 1)
        col = jnp.where(col < rows, col, col - rows)
        for x in range(2):
            band = (jnp.abs(row - col) <= heights[x]).astype(jnp.float32).astype(jnp.bfloat16)
            looked = [
                jnp.dot(band, self.stack_ref[x, f], preferred_element_type=jnp.float32)
                for f in range(4)
            ]
            inverse = lax.rsqrt(looked[2] * looked[3] + EPSILON)
            for c in range(2):
                self.stage_ref[stage, x, c] = looked[c] * inverse


def own_kernel(plan, lists, slc_ref, rim_ref, bands_ref, out_ref, powers_ref, *scratch):
    pairs = Pairs(plan, lists, slc_ref, rim_ref, bands_ref, powers_ref, out_ref, scratch)
    dates = plan["dates"]

    def power(slot, carry):
        for t in range(5):
            real, imag = tile_of(*pairs.own_other(slot), t)
            put(powers_ref, (slot, slice(None)), t, real * real + imag * imag)
        return carry

    lax.fori_loop(0, dates, power, 0)

    def work(x, n):
        slot, kind, local = pairs.near_item(pairs.list_ref[n])
        return slot, kind, pairs.own_other(local), local

    pairs.run(pairs.near_list(pairs.own), work)


def rest_kernel(plan, lists, slc_ref, rim_ref, bands_ref, powers_ref, inner_ref, outer_ref, _sent,
                _, out_ref, *scratch):
    pairs = Pairs(plan, lists, slc_ref, rim_ref, bands_ref, powers_ref, out_ref, scratch)
    dates = plan["dates"]
    upper = pairs.me >= plan["devices"] // 2 if plan["halves"] else True

    def work(x, n):
        slot, kind, local = pairs.near_item(pairs.list_ref[n])
        below = local < 0
        index = jnp.clip(jnp.where(below, local + NEAR, local - dates), 0, NEAR - 1)
        inner = below == upper
        pl.when(inner)(lambda: pairs.fetch_payload(x, inner_ref, index))
        pl.when(jnp.logical_not(inner))(lambda: pairs.fetch_payload(x, outer_ref, index))
        return slot, kind, pairs.fetched_other(x), None

    def chosen(local):
        return jnp.logical_not(pairs.own(local) | pairs.in_middle(local))

    pairs.run(pairs.near_list(chosen), work)


def middle_kernel(plan, lists, slc_ref, rim_ref, bands_ref, powers_ref, middle_ref, _, out_ref,
                  *scratch):
    pairs = Pairs(plan, lists, slc_ref, rim_ref, bands_ref, powers_ref, out_ref, scratch)
    dates = plan["dates"]

    def work(x, n):
        slot, kind, local = pairs.near_item(pairs.list_ref[n])
        index = jnp.clip(jnp.where(local < 0, local + NEAR, local - dates), 0, NEAR - 1)
        pairs.fetch_payload(x, middle_ref, index)
        return slot, kind, pairs.fetched_other(x), None

    pairs.run(pairs.near_list(pairs.in_middle), work)


def annual_kernel(plan, is_late, lists, slc_ref, rim_ref, bands_ref, powers_ref, inner_ref,
                  outer_ref, images_ref, strips_ref, _, out_ref, *scratch):
    pairs = Pairs(plan, lists, slc_ref, rim_ref, bands_ref, powers_ref, out_ref, scratch)
    dates, late = plan["dates"], plan["late"]
    half = plan["devices"] // 2
    me, split_date = pairs.me, half * dates
    lower = me < half
    if is_late:
        base, count = jnp.where(lower, 0, dates - late), late
    else:
        base, count = jnp.where(lower, late, 0), dates - late

    def fetch_early(x, k, ref):
        packed = strips_ref[...]
        for c in range(2):
            pairs.other_ref[x, c] = ref[c, k]
            pairs.other_rim_ref[x, c] = place_strip(packed, 2 * k + c, pairs.strip)

    def work(x, k):
        slot = base + k
        date = me * dates + slot
        other = pairs.partner(date * plan["per_date"] + NEAR)
        far = (other < split_date) == lower
        from_inner = jnp.where(lower, me != 0, me == half)
        inner_at = jnp.where(lower, other, other - (2 * split_date - NEAR))
        outer_at = jnp.where(lower, other - (split_date - NEAR), other - split_date)
        inner_at, outer_at = jnp.clip(inner_at, 0, NEAR - 1), jnp.clip(outer_at, 0, NEAR - 1)
        fetch = pairs.fetch_payload
        pl.when(far & from_inner)(lambda: fetch(x, inner_ref, inner_at))
        pl.when(far & jnp.logical_not(from_inner))(lambda: fetch(x, outer_ref, outer_at))
        near_side = jnp.logical_not(far)
        if is_late:
            pl.when(near_side)(lambda: fetch(x, images_ref, k))
        else:
            pl.when(near_side)(lambda: fetch_early(x, k, images_ref))
        return slot, NEAR, pairs.fetched_other(x), None

    pairs.run(count, work)


def plain_kernel(plan, lists, slc_ref, rim_ref, bands_ref, powers_ref, images_ref,
                 image_rim_ref, _, out_ref, *scratch):
    pairs = Pairs(plan, lists, slc_ref, rim_ref, bands_ref, powers_ref, out_ref, scratch)

    def work(x, slot):
        other = (
            lambda c, cols: images_ref[c, slot, :, cols],
            lambda c: image_rim_ref[c, slot],
        )
        return slot, NEAR, other, None

    pairs.run(plan["dates"], work)


def arrivals_by_distance(slc, pair_list, plan):
    dates, per_date, devices = plan["dates"], plan["per_date"], plan["devices"]
    total = dates * devices
    me = lax.axis_index("date")
    annual_of = pair_list[:, 1].reshape(total, per_date)[:, per_date - 1]
    sums = [None] * dates
    for direction in (1, -1):
        by_distance = {}
        for slot in range(dates):
            for gap in range(plan["year"], plan["year"] + 3):
                distance = (slot + direction * gap) // dates
                by_distance.setdefault(distance, set()).add(slot)
        for distance in sorted(by_distance):
            slots = sorted(by_distance[distance])
            wanted_by = (me - distance) * dates + jnp.array(slots, dtype=jnp.int32)
            inside = (wanted_by >= 0) & (wanted_by < total)
            local = jnp.take(annual_of, jnp.clip(wanted_by, 0, total - 1)) - me * dates
            usable = inside & (local >= 0) & (local < dates)
            packed = jnp.take(slc, jnp.clip(local, 0, dates - 1), axis=1)
            packed = jnp.where(usable[None, :, None, None], packed, jnp.zeros_like(packed))
            route = [(i + distance, i) for i in range(devices) if 0 <= i + distance < devices]
            arrived = lax.ppermute(packed, "date", route)
            for n, slot in enumerate(slots):
                part = arrived[:, n]
                sums[slot] = part if sums[slot] is None else sums[slot] + part
    return jnp.stack(sums, axis=1)


def payload_of(images, rim, strip):
    planes, count, rows, cols = images.shape
    edges = jnp.where(strip == 0, rim[..., :HALO], rim[..., TILE - HALO :])
    edges = jnp.transpose(edges, (2, 1, 0, 3)).reshape(rows, count * planes * HALO)
    edges = jnp.pad(edges, ((0, 0), (0, TILE - edges.shape[1])))
    part = rows * TILE // cols
    edges = jnp.transpose(edges.reshape(rows // part, part, TILE), (1, 0, 2)).reshape(part, cols)
    stacked = jnp.transpose(images, (1, 0, 2, 3)).reshape(count * planes * rows, cols)
    return jnp.concatenate([stacked, edges], axis=0)


def body(slc, pair_list, az_half, rng_half):
    planes, dates, rows, cols = slc.shape
    devices = lax.axis_size("date")
    total = dates * devices
    per_date = pair_list.shape[0] // total
    year = min(YEAR, total // 2 - 2)
    half = devices // 2
    late = half * dates - year
    halves = devices % 2 == 0 and 0 < late <= NEAR and 2 * late <= dates
    halves = halves and 2 * (dates - late) * HALO <= TILE
    plan = {
        "dates": dates,
        "devices": devices,
        "per_date": per_date,
        "year": year,
        "late": late,
        "rows": rows,
        "cols": cols,
        "pairs": total * per_date,
        "halves": halves,
    }
    dtype = slc.dtype
    rim_rows = rows * TILE // cols
    pairs = pair_list.T
    lists = jnp.concatenate([pairs, az_half[None], rng_half[None]])
    swap_strips = [(0, 1), (1, 0)]

    def images(count):
        return jax.ShapeDtypeStruct((planes, count, rows, cols), dtype)

    def rim_shape(count):
        return jax.ShapeDtypeStruct((planes, count, rows, TILE), dtype)

    def payload_shape(count):
        return jax.ShapeDtypeStruct((planes * count * rows + rim_rows, cols), dtype)

    def swapped_rims(values):
        out = pl.pallas_call(
            rim_kernel,
            out_shape=rim_shape(values.shape[1]),
            in_specs=[ANY],
            out_specs=VMEM,
            scratch_shapes=[pltpu.SemaphoreType.DMA],
            compiler_params=limit(WORK_MIB),
            name="rim_blocks",
        )(values)
        return lax.ppermute(out, "strip", swap_strips)

    def cost(flops):
        return pl.CostEstimate(flops=flops, bytes_accessed=1, transcendentals=0)

    wide = cols // 2
    widths = HALO - REACH_LO + 1
    band_shape = (2, 2 * wide + 2 * TILE, wide)
    bands = pl.pallas_call(
        functools.partial(bands_kernel, cols),
        grid=(widths,),
        out_shape=jax.ShapeDtypeStruct((widths, *band_shape), jnp.bfloat16),
        out_specs=pl.BlockSpec((1, *band_shape), lambda n: (n, 0, 0, 0)),
        compiler_params=limit(WORK_MIB),
        cost_estimate=cost(1),
        name="range_bands",
    )()
    if halves:
        swap = [(i, (i + half) % devices) for i in range(devices)]
        both = ("date", "strip")
        early, rim, strips = pl.pallas_call(
            functools.partial(early_kernel, plan),
            out_shape=(
                images(dates - late),
                rim_shape(dates),
                jax.ShapeDtypeStruct((rows, TILE), dtype),
            ),
            in_specs=[ANY, SMEM],
            out_specs=(VMEM, VMEM, VMEM),
            scratch_shapes=[
                pltpu.VMEM((dates - late, planes, rows, TILE), dtype),
                pltpu.SemaphoreType.DMA((dates - late,)),
                pltpu.SemaphoreType.DMA((dates - late,)),
                pltpu.SemaphoreType.DMA,
            ],
            compiler_params=limit(FIRST_MIB),
            name="early_images",
        )(slc, pairs)
        early = lax.ppermute(early, "date", swap)
        rim = lax.ppermute(rim, "strip", swap_strips)
        inner, outer = pl.pallas_call(
            functools.partial(beside_kernel, plan),
            out_shape=(payload_shape(NEAR), payload_shape(NEAR)),
            in_specs=[ANY, VMEM],
            out_specs=(VMEM, VMEM),
            scratch_shapes=[pltpu.SemaphoreType.DMA((2, NEAR, 2))],
            compiler_params=limit(WORK_MIB),
            name="beside_images",
        )(slc, rim)
        down = [(i, (i - 1) % half) for i in range(half)]
        down += [(half + i, half + (i + 1) % half) for i in range(half)]
        strips = lax.ppermute(
            strips, both, [(2 * a + s, 2 * b + 1 - s) for a, b in swap for s in (0, 1)]
        )
        middle = lax.ppermute(outer, "date", [(half - 1, half), (half, half - 1)])
        outer = lax.ppermute(outer, "date", [(b, a) for a, b in down])
        inner = lax.ppermute(inner, "date", down)
    else:
        rim = swapped_rims(slc)
        annual = arrivals_by_distance(slc, pair_list, plan)
        strip = lax.axis_index("strip")
        ups = [(i, i + 1) for i in range(devices - 1)]
        inner = payload_of(slc[:, dates - NEAR :], rim[:, dates - NEAR :], strip)
        outer = payload_of(slc[:, :NEAR], rim[:, :NEAR], strip)
        inner = lax.ppermute(inner, "date", ups)
        outer = lax.ppermute(outer, "date", [(b, a) for a, b in ups])

    out_shape = jax.ShapeDtypeStruct((planes, dates * per_date, rows, cols), jnp.float32)
    depth = 2 * band_shape[1]
    scratch = [
        pltpu.VMEM((2, 4 * rows, depth), jnp.bfloat16),
        pltpu.VMEM((2, 4, 2 * rows, cols), jnp.bfloat16),
        pltpu.VMEM((2, planes, rows, cols), dtype),
        pltpu.VMEM((2, planes, rows, TILE), dtype),
        pltpu.VMEM((2, 2, planes, rows, cols), jnp.float32),
        pltpu.SMEM((dates * NEAR + 1,), jnp.int32),
        pltpu.SemaphoreType.DMA((2, 2)),
    ]

    out, powers = pl.pallas_call(
        functools.partial(own_kernel, plan),
        out_shape=(out_shape, jax.ShapeDtypeStruct((dates, rows, depth), jnp.bfloat16)),
        in_specs=[SMEM] + [VMEM] * 3,
        out_specs=(ANY, VMEM),
        scratch_shapes=scratch,
        compiler_params=limit(WORK_MIB),
        cost_estimate=cost(20_000_000_000),
        name="own_pairs",
    )(lists, slc, rim, bands)

    def more_pairs(kernel, out, others, name):
        return pl.pallas_call(
            functools.partial(kernel, plan),
            out_shape=out_shape,
            in_specs=[SMEM] + [VMEM] * (4 + len(others)) + [ANY],
            out_specs=ANY,
            scratch_shapes=scratch,
            input_output_aliases={5 + len(others): 0},
            compiler_params=limit(WORK_MIB),
            cost_estimate=cost(1),
            name=name,
        )(lists, slc, rim, bands, powers, *others, out)

    if halves:
        payload = sent = pl.pallas_call(
            functools.partial(late_kernel, plan),
            out_shape=payload_shape(late),
            in_specs=[VMEM, VMEM, VMEM, SMEM, ANY, ANY],
            out_specs=VMEM,
            scratch_shapes=[pltpu.VMEM((late, planes, rows, TILE), dtype)],
            compiler_params=limit(WORK_MIB),
            name="late_images",
        )(slc, rim, inner, lists, powers, strips)
        payload = lax.ppermute(payload, "date", swap)
    else:
        sent = inner
    out = more_pairs(rest_kernel, out, (inner, outer, sent), "near_pairs")
    if halves:
        kernel = lambda plan, *refs: annual_kernel(plan, False, *refs)
        out = more_pairs(kernel, out, (inner, outer, early, strips), "annual_pairs")
        out = more_pairs(middle_kernel, out, (middle,), "middle_pairs")
        kernel = lambda plan, *refs: annual_kernel(plan, True, *refs)
        out = more_pairs(kernel, out, (inner, outer, payload, strips), "last_pairs")
    else:
        out = more_pairs(plain_kernel, out, (annual, swapped_rims(annual)), "annual_pairs")
    return out


def solution(mesh):
    placed = (P(None, "date", "groups", "strip"), P(), P(), P())
    return jax.shard_map(
        body,
        mesh=mesh,
        in_specs=placed,
        out_specs=P(None, "date", "groups", "strip"),
        check_vma=False,
    )
```

```python
import functools

import jax
import jax.numpy as jnp
from jax import lax
from jax.experimental import pallas as pl
from jax.experimental.pallas import tpu as pltpu
from jax.sharding import PartitionSpec as P

HALO = 16
REACH_LO = 12
NEAR = 3
YEAR = 29
EPSILON = 1e-06
TILE = 128
INNER = TILE // 2
PARTNER, HEIGHT, REACH = 1, 2, 3
WORK_MIB = 16
FIRST_MIB = 56
ANY = pl.BlockSpec(memory_space=pl.ANY)
SMEM = pl.BlockSpec(memory_space=pltpu.SMEM)
VMEM = pl.BlockSpec(memory_space=pltpu.VMEM)


def limit(mebibytes):
    return pltpu.CompilerParams(vmem_limit_bytes=mebibytes * 1024 * 1024)


def run_copies(copies):
    for copy in copies:
        copy.start()
    for copy in copies:
        copy.wait()


def gather_strips(tiles, side):
    lane = lax.broadcasted_iota(jnp.int32, tiles[0].shape, 1)
    packed = jnp.zeros(tiles[0].shape, jnp.float32)
    for n, tile in enumerate(tiles):
        spot = n * HALO
        moved = pltpu.roll(tile.astype(jnp.float32), spot + side * HALO, 1)
        packed = jnp.where((lane >= spot) & (lane < spot + HALO), moved, packed)
    return packed.astype(jnp.bfloat16)


def place_strip(packed, n, side):
    shift = 2 * TILE - (n + side) * HALO
    return pltpu.roll(packed.astype(jnp.float32), lax.rem(shift, TILE), 1).astype(jnp.bfloat16)


def write_strips(out_ref, packed):
    rows, cols = packed.shape[0], out_ref.shape[1]
    part = rows * TILE // cols
    base = out_ref.shape[0] - part
    for n in range(rows // part):
        out_ref[base:, n * TILE : (n + 1) * TILE] = packed[n * part : (n + 1) * part]


def read_strips(ref, rows):
    cols = ref.shape[1]
    base = ref.shape[0] - rows * TILE // cols
    return jnp.concatenate(
        [ref[base:, n * TILE : (n + 1) * TILE] for n in range(cols // TILE)], axis=0
    )


def wanted_images(plan, pairs_ref):
    me = lax.axis_index("date")
    dates, half = plan["dates"], plan["devices"] // 2
    mate = lax.rem(me + half, 2 * half)
    wanted = []
    for k in range(dates - plan["late"]):
        date = mate * dates + jnp.where(mate < half, plan["late"], 0) + k
        at = pairs_ref[PARTNER, date * plan["per_date"] + NEAR] - me * dates
        wanted.append(jnp.clip(at, 0, dates - 1))
    return wanted


def image_copies(slc_ref, wanted, early_ref, sems):
    return [
        pltpu.make_async_copy(slc_ref.at[:, at], early_ref.at[:, k], sems.at[k])
        for k, at in enumerate(wanted)
    ]


def early_kernel(plan, slc_ref, pairs_ref, early_ref, rim_ref, strips_ref, tiles_ref, sems,
                 tile_sems, rim_sem):
    strip, cols = lax.axis_index("strip"), plan["cols"]
    start = pl.multiple_of(jnp.where(strip == 0, cols - TILE, 0), TILE)
    wanted = wanted_images(plan, pairs_ref)
    rim_copy = pltpu.make_async_copy(slc_ref.at[:, :, :, pl.ds(start, TILE)], rim_ref, rim_sem)
    early_copies = image_copies(slc_ref, wanted, early_ref, sems)
    tile_copies = [
        pltpu.make_async_copy(
            slc_ref.at[:, at, :, pl.ds(start, TILE)], tiles_ref.at[k], tile_sems.at[k]
        )
        for k, at in enumerate(wanted)
    ]
    for copy in tile_copies + [rim_copy] + early_copies:
        copy.start()
    for copy in tile_copies:
        copy.wait()
    tiles = [tiles_ref[k, c] for k in range(len(wanted)) for c in range(2)]
    strips_ref[...] = gather_strips(tiles, 1 - strip)
    for copy in [rim_copy] + early_copies:
        copy.wait()


def rim_kernel(slc_ref, rim_ref, sem):
    cols = slc_ref.shape[3]
    start = pl.multiple_of(jnp.where(lax.axis_index("strip") == 0, cols - TILE, 0), TILE)
    run_copies([pltpu.make_async_copy(slc_ref.at[:, :, :, pl.ds(start, TILE)], rim_ref, sem)])


def beside_kernel(plan, slc_ref, rim_ref, inner_ref, outer_ref, sems):
    me, strip = lax.axis_index("date"), lax.axis_index("strip")
    dates, rows = plan["dates"], plan["rows"]
    upper = me >= plan["devices"] // 2
    last = dates - NEAR
    copies = []
    firsts = (jnp.where(upper, last, 0), jnp.where(upper, 0, last))
    for r, (out_ref, first) in enumerate(zip((inner_ref, outer_ref), firsts)):
        for k in range(NEAR):
            for c in range(2):
                here = out_ref.at[pl.ds((2 * k + c) * rows, rows)]
                copies.append(
                    pltpu.make_async_copy(slc_ref.at[c, first + k], here, sems.at[r, k, c])
                )
    for copy in copies:
        copy.start()
    for out_ref, first in zip((inner_ref, outer_ref), firsts):
        tiles = [rim_ref[c, first + k] for k in range(NEAR) for c in range(2)]
        write_strips(out_ref, gather_strips(tiles, strip))
    for copy in copies:
        copy.wait()


def late_kernel(plan, slc_ref, rim_ref, inner_ref, held_ref, pairs_ref, *refs):
    late_ref, outer_ref, tiles_ref, sem = refs[-4:]
    copy = pltpu.make_async_copy(held_ref, outer_ref, sem)
    copy.start()
    me, strip = lax.axis_index("date"), lax.axis_index("strip")
    dates, late, rows = plan["dates"], plan["late"], plan["rows"]
    half = plan["devices"] // 2
    mate = lax.rem(me + half, 2 * half)
    mate_slot = jnp.where(mate < half, 0, dates - late)
    packed = read_strips(inner_ref, rows)
    for k in range(late):
        date = mate * dates + mate_slot + k
        wanted = pairs_ref[PARTNER, date * plan["per_date"] + NEAR] - me * dates
        own = (wanted >= 0) & (wanted < dates)
        own_at = jnp.clip(wanted, 0, dates - 1)
        other_at = jnp.clip(jnp.where(me < half, wanted - dates, wanted + NEAR), 0, NEAR - 1)
        for c in range(2):
            here = pl.ds((2 * k + c) * rows, rows)

            @pl.when(own)
            def _():
                late_ref[here] = slc_ref[c, own_at]
                tiles_ref[k, c] = rim_ref[c, own_at]

            @pl.when(jnp.logical_not(own))
            def _():
                there = pl.multiple_of((2 * other_at + c) * rows, rows)
                late_ref[here] = inner_ref[pl.ds(there, rows)]
                tiles_ref[k, c] = place_strip(packed, 2 * other_at + c, strip)

    tiles = [tiles_ref[k, c] for k in range(late) for c in range(2)]
    write_strips(late_ref, gather_strips(tiles, strip))
    copy.wait()


def bands_kernel(cols, out_ref):
    strip = lax.axis_index("strip")
    wide = out_ref.shape[3]
    reach = pl.program_id(0) + REACH_LO

    def band(places, targets):
        return (jnp.abs(places - targets) <= reach).astype(jnp.float32).astype(jnp.bfloat16)

    def indices(shape):
        return lax.broadcasted_iota(jnp.int32, shape, 0), lax.broadcasted_iota(jnp.int32, shape, 1)

    inside = band(*indices((wide, wide)))
    row, col = indices((TILE, wide))
    beyond = jnp.where(strip == 0, cols + row, row - TILE)
    first = band(jnp.where(row < INNER, wide + row, beyond), col)
    second = band(jnp.where(row < INNER, beyond, wide - TILE + row), col + wide)
    for n, part in enumerate((first, second)):
        out_ref[0, n, 0:wide] = inside
        out_ref[0, n, wide : 2 * wide] = inside
        out_ref[0, n, 2 * wide : 2 * wide + TILE] = part
        out_ref[0, n, 2 * wide + TILE : 2 * wide + 2 * TILE] = part


def split(values):
    high = values.astype(jnp.bfloat16)
    low = (values - high.astype(jnp.float32)).astype(jnp.bfloat16)
    return high, low


def put(ref, here, t, values):
    wide = 2 * TILE
    depth = 2 * wide + 2 * TILE
    for low, part in enumerate(split(values)):
        side = [n * depth + 2 * wide + low * TILE for n in range(2)]
        if t < 4:
            at = (t // 2) * depth + low * wide + (t % 2) * TILE
            ref[*here, at : at + TILE] = part
        if t == 2:
            ref[*here, side[0] : side[0] + INNER] = part[:, :INNER]
        if t == 1:
            ref[*here, side[1] + INNER : side[1] + TILE] = part[:, INNER:]
        if t == 4:
            ref[*here, side[0] + INNER : side[0] + TILE] = part[:, INNER:]
            ref[*here, side[1] : side[1] + INNER] = part[:, :INNER]


def tile_of(main, rim, t):
    return [
        (rim(c) if t == 4 else main(c, slice(t * TILE, (t + 1) * TILE))).astype(jnp.float32)
        for c in range(2)
    ]


class Pairs:
    def __init__(self, plan, lists, slc_ref, rim_ref, bands_ref, powers_ref, out_ref, scratch):
        self.plan = plan
        self.lists = lists
        self.slc_ref, self.rim_ref = slc_ref, rim_ref
        self.bands_ref, self.powers_ref, self.out_ref = bands_ref, powers_ref, out_ref
        (self.left_ref, self.stack_ref, self.other_ref, self.other_rim_ref, self.stage_ref,
         self.list_ref, self.sems) = scratch
        self.me, self.strip = lax.axis_index("date"), lax.axis_index("strip")

    def partner(self, pair):
        return self.lists[PARTNER, pair]

    def near_item(self, n):
        slot, kind = n // NEAR, lax.rem(n, NEAR)
        dates = self.plan["dates"]
        pair = (self.me * dates + slot) * self.plan["per_date"] + kind
        return slot, kind, self.partner(pair) - self.me * dates

    def near_list(self, chosen):
        count = 0
        for n in range(self.plan["dates"] * NEAR):
            self.list_ref[count] = n
            count = count + jnp.where(chosen(self.near_item(n)[2]), 1, 0)
        return count

    def own(self, local):
        return (local >= 0) & (local < self.plan["dates"])

    def in_middle(self, local):
        half, dates = self.plan["devices"] // 2, self.plan["dates"]
        if not self.plan["halves"]:
            return False
        return ((self.me == half) & (local < 0)) | ((self.me == half - 1) & (local >= dates))

    def own_other(self, index):
        return (
            lambda c, cols: self.slc_ref[c, index, :, cols],
            lambda c: self.rim_ref[c, index],
        )

    def fetched_other(self, x):
        return (
            lambda c, cols: self.other_ref[x, c, :, cols],
            lambda c: self.other_rim_ref[x, c],
        )

    def fetch_payload(self, x, ref, index):
        rows = self.plan["rows"]
        packed = read_strips(ref, rows)
        for c in range(2):
            at = pl.multiple_of((2 * index + c) * rows, rows)
            self.other_ref[x, c] = ref[pl.ds(at, rows)]
            self.other_rim_ref[x, c] = place_strip(packed, 2 * index + c, self.strip)

    def out_copy(self, stage, x, pair):
        return pltpu.make_async_copy(
            self.stage_ref.at[stage, x], self.out_ref.at[:, pair], self.sems.at[stage, x]
        )

    def run(self, count, work):
        steps = (count + 1) // 2

        def step(n, carry):
            stage = lax.rem(n, 2)

            @pl.when(n >= 2)
            def _():
                for x in range(2):
                    self.out_copy(stage, x, 0).wait()

            items = [work(x, jnp.minimum(2 * n + x, count - 1)) for x in range(2)]
            self.compute(stage, items)
            for x, (slot, kind, _, _) in enumerate(items):
                copy = self.out_copy(stage, x, slot * self.plan["per_date"] + kind)
                pl.when(2 * n + x < count)(copy.start)
            return carry

        lax.fori_loop(0, steps, step, 0)
        for back in (2, 1):
            for x in range(2):
                used = (steps >= back) & (2 * (steps - back) + x < count)
                pl.when(used)(self.out_copy(lax.rem(steps + back, 2), x, 0).wait)

    def compute(self, stage, items):
        plan = self.plan
        rows, dates, per_date = plan["rows"], plan["dates"], plan["per_date"]
        part = [(pl.ds(f * rows, rows),) for f in range(4)]
        depth = self.bands_ref.shape[2]
        wide = self.bands_ref.shape[3]
        heights, widths = [], []
        for slot, kind, _, _ in items:
            pair = (self.me * dates + slot) * per_date + kind
            heights.append(self.lists[HEIGHT, pair])
            widths.append(jnp.clip(self.lists[REACH, pair] - REACH_LO, 0, HALO - REACH_LO))
        for x, (slot, kind, other, other_power) in enumerate(items):
            left_ref = self.left_ref.at[x]
            left_ref[*part[2]] = self.powers_ref[slot]
            if other_power is not None:
                left_ref[*part[3]] = self.powers_ref[other_power]
            first = self.own_other(slot)
            for t in range(5):
                a_real, a_imag = tile_of(*first, t)
                b_real, b_imag = tile_of(*other, t)
                put(left_ref, part[0], t, a_real * b_real + a_imag * b_imag)
                put(left_ref, part[1], t, a_imag * b_real - a_real * b_imag)
                if other_power is None:
                    put(left_ref, part[3], t, b_real * b_real + b_imag * b_imag)
        for n in range(2):
            for x in range(2):
                ranged = jnp.dot(
                    self.left_ref[x, :, n * depth : (n + 1) * depth],
                    self.bands_ref[widths[x], n],
                    preferred_element_type=jnp.float32,
                )
                there = slice(n * wide, (n + 1) * wide)
                for low, values in enumerate(split(ranged)):
                    for f in range(4):
                        self.stack_ref[x, f, low * rows : (low + 1) * rows, there] = values[
                            f * rows : (f + 1) * rows
                        ]
        row = lax.broadcasted_iota(jnp.int32, (rows, 2 * rows), 0)
        col = lax.broadcasted_iota(jnp.int32, (rows, 2 * rows), 1)
        col = jnp.where(col < rows, col, col - rows)
        for x in range(2):
            band = (jnp.abs(row - col) <= heights[x]).astype(jnp.float32).astype(jnp.bfloat16)
            looked = [
                jnp.dot(band, self.stack_ref[x, f], preferred_element_type=jnp.float32)
                for f in range(4)
            ]
            inverse = lax.rsqrt(looked[2] * looked[3] + EPSILON)
            for c in range(2):
                self.stage_ref[stage, x, c] = looked[c] * inverse


def own_kernel(plan, lists, slc_ref, rim_ref, bands_ref, out_ref, powers_ref, *scratch):
    pairs = Pairs(plan, lists, slc_ref, rim_ref, bands_ref, powers_ref, out_ref, scratch)
    dates = plan["dates"]

    def power(slot, carry):
        for t in range(5):
            real, imag = tile_of(*pairs.own_other(slot), t)
            put(powers_ref, (slot, slice(None)), t, real * real + imag * imag)
        return carry

    lax.fori_loop(0, dates, power, 0)

    def work(x, n):
        slot, kind, local = pairs.near_item(pairs.list_ref[n])
        return slot, kind, pairs.own_other(local), local

    pairs.run(pairs.near_list(pairs.own), work)


def rest_kernel(plan, lists, slc_ref, rim_ref, bands_ref, powers_ref, inner_ref, outer_ref,
                middle_ref, _, out_ref, *scratch):
    pairs = Pairs(plan, lists, slc_ref, rim_ref, bands_ref, powers_ref, out_ref, scratch)
    dates = plan["dates"]
    upper = pairs.me >= plan["devices"] // 2 if plan["halves"] else True

    def work(x, n):
        slot, kind, local = pairs.near_item(pairs.list_ref[n])
        below = local < 0
        index = jnp.clip(jnp.where(below, local + NEAR, local - dates), 0, NEAR - 1)
        inner, middle = below == upper, pairs.in_middle(local)
        sources = (
            (jnp.logical_not(inner), outer_ref),
            (inner & jnp.logical_not(middle), inner_ref),
            (inner & middle, middle_ref),
        )
        for chosen, ref in sources:
            pl.when(chosen)(functools.partial(pairs.fetch_payload, x, ref, index))
        return slot, kind, pairs.fetched_other(x), None

    pairs.run(pairs.near_list(lambda local: jnp.logical_not(pairs.own(local))), work)


def annual_kernel(plan, lists, slc_ref, rim_ref, bands_ref, powers_ref, ring_ref,
                  images_ref, strips_ref, _, out_ref, *scratch, is_late):
    pairs = Pairs(plan, lists, slc_ref, rim_ref, bands_ref, powers_ref, out_ref, scratch)
    dates, late = plan["dates"], plan["late"]
    half = plan["devices"] // 2
    me, split_date = pairs.me, half * dates
    lower = me < half
    if is_late:
        base, count = jnp.where(lower, 0, dates - late), late
    else:
        base, count = jnp.where(lower, late, 0), dates - late

    def fetch_early(x, k, ref):
        packed = strips_ref[...]
        for c in range(2):
            pairs.other_ref[x, c] = ref[c, k]
            pairs.other_rim_ref[x, c] = place_strip(packed, 2 * k + c, pairs.strip)

    def work(x, k):
        slot = base + k
        date = me * dates + slot
        other = pairs.partner(date * plan["per_date"] + NEAR)
        far = (other < split_date) == lower
        end = 2 * split_date
        if is_late:
            ring_at = jnp.where(lower, other - (split_date - NEAR), other - split_date)
        else:
            ring_at = jnp.where(lower, other, other - (end - NEAR))
        ring_at = jnp.clip(ring_at, 0, NEAR - 1)
        fetch = pairs.fetch_payload
        pl.when(far)(lambda: fetch(x, ring_ref, ring_at))
        near_side = jnp.logical_not(far)
        if is_late:
            pl.when(near_side)(lambda: fetch(x, images_ref, k))
        else:
            pl.when(near_side)(lambda: fetch_early(x, k, images_ref))
        return slot, NEAR, pairs.fetched_other(x), None

    pairs.run(count, work)


def plain_kernel(plan, lists, slc_ref, rim_ref, bands_ref, powers_ref, images_ref,
                 image_rim_ref, _, out_ref, *scratch):
    pairs = Pairs(plan, lists, slc_ref, rim_ref, bands_ref, powers_ref, out_ref, scratch)

    def work(x, slot):
        other = (
            lambda c, cols: images_ref[c, slot, :, cols],
            lambda c: image_rim_ref[c, slot],
        )
        return slot, NEAR, other, None

    pairs.run(plan["dates"], work)


def arrivals_by_distance(slc, pair_list, plan):
    dates, per_date, devices = plan["dates"], plan["per_date"], plan["devices"]
    total = dates * devices
    me = lax.axis_index("date")
    annual_of = pair_list[:, 1].reshape(total, per_date)[:, per_date - 1]
    sums = [None] * dates
    for direction in (1, -1):
        by_distance = {}
        for slot in range(dates):
            for gap in range(plan["year"], plan["year"] + 3):
                distance = (slot + direction * gap) // dates
                by_distance.setdefault(distance, set()).add(slot)
        for distance in sorted(by_distance):
            slots = sorted(by_distance[distance])
            wanted_by = (me - distance) * dates + jnp.array(slots, dtype=jnp.int32)
            inside = (wanted_by >= 0) & (wanted_by < total)
            local = jnp.take(annual_of, jnp.clip(wanted_by, 0, total - 1)) - me * dates
            usable = inside & (local >= 0) & (local < dates)
            packed = jnp.take(slc, jnp.clip(local, 0, dates - 1), axis=1)
            packed = jnp.where(usable[None, :, None, None], packed, jnp.zeros_like(packed))
            route = [(i + distance, i) for i in range(devices) if 0 <= i + distance < devices]
            arrived = lax.ppermute(packed, "date", route)
            for n, slot in enumerate(slots):
                part = arrived[:, n]
                sums[slot] = part if sums[slot] is None else sums[slot] + part
    return jnp.stack(sums, axis=1)


def payload_of(images, rim, strip):
    planes, count, rows, cols = images.shape
    edges = jnp.where(strip == 0, rim[..., :HALO], rim[..., TILE - HALO :])
    edges = jnp.transpose(edges, (2, 1, 0, 3)).reshape(rows, count * planes * HALO)
    edges = jnp.pad(edges, ((0, 0), (0, TILE - edges.shape[1])))
    part = rows * TILE // cols
    edges = jnp.transpose(edges.reshape(rows // part, part, TILE), (1, 0, 2)).reshape(part, cols)
    stacked = jnp.transpose(images, (1, 0, 2, 3)).reshape(count * planes * rows, cols)
    return jnp.concatenate([stacked, edges], axis=0)


def body(slc, pair_list, az_half, rng_half):
    planes, dates, rows, cols = slc.shape
    devices = lax.axis_size("date")
    total = dates * devices
    per_date = pair_list.shape[0] // total
    year = min(YEAR, total // 2 - 2)
    half = devices // 2
    late = half * dates - year
    halves = devices % 2 == 0 and 0 < late <= NEAR and 2 * late <= dates
    halves = halves and 2 * (dates - late) * HALO <= TILE
    plan = {
        "dates": dates,
        "devices": devices,
        "per_date": per_date,
        "year": year,
        "late": late,
        "rows": rows,
        "cols": cols,
        "pairs": total * per_date,
        "halves": halves,
    }
    dtype = slc.dtype
    rim_rows = rows * TILE // cols
    pairs = pair_list.T
    lists = jnp.concatenate([pairs, az_half[None], rng_half[None]])
    swap_strips = [(0, 1), (1, 0)]

    def images(count):
        return jax.ShapeDtypeStruct((planes, count, rows, cols), dtype)

    def rim_shape(count):
        return jax.ShapeDtypeStruct((planes, count, rows, TILE), dtype)

    def payload_shape(count):
        return jax.ShapeDtypeStruct((planes * count * rows + rim_rows, cols), dtype)

    def swapped_rims(values):
        out = pl.pallas_call(
            rim_kernel,
            out_shape=rim_shape(values.shape[1]),
            in_specs=[ANY],
            out_specs=VMEM,
            scratch_shapes=[pltpu.SemaphoreType.DMA],
            compiler_params=limit(WORK_MIB),
            name="rim_blocks",
        )(values)
        return lax.ppermute(out, "strip", swap_strips)

    def cost(flops):
        return pl.CostEstimate(flops=flops, bytes_accessed=1, transcendentals=0)

    wide = cols // 2
    widths = HALO - REACH_LO + 1
    band_shape = (2, 2 * wide + 2 * TILE, wide)
    bands = pl.pallas_call(
        functools.partial(bands_kernel, cols),
        grid=(widths,),
        out_shape=jax.ShapeDtypeStruct((widths, *band_shape), jnp.bfloat16),
        out_specs=pl.BlockSpec((1, *band_shape), lambda n: (n, 0, 0, 0)),
        compiler_params=limit(WORK_MIB),
        cost_estimate=cost(1),
        name="range_bands",
    )()
    if halves:
        swap = [(i, (i + half) % devices) for i in range(devices)]
        both = ("date", "strip")
        early, rim, strips = pl.pallas_call(
            functools.partial(early_kernel, plan),
            out_shape=(
                images(dates - late),
                rim_shape(dates),
                jax.ShapeDtypeStruct((rows, TILE), dtype),
            ),
            in_specs=[ANY, SMEM],
            out_specs=(VMEM, VMEM, VMEM),
            scratch_shapes=[
                pltpu.VMEM((dates - late, planes, rows, TILE), dtype),
                pltpu.SemaphoreType.DMA((dates - late,)),
                pltpu.SemaphoreType.DMA((dates - late,)),
                pltpu.SemaphoreType.DMA,
            ],
            compiler_params=limit(FIRST_MIB),
            name="early_images",
        )(slc, pairs)
        early = lax.ppermute(early, "date", swap)
        rim = lax.ppermute(rim, "strip", swap_strips)
        inner, outer = pl.pallas_call(
            functools.partial(beside_kernel, plan),
            out_shape=(payload_shape(NEAR), payload_shape(NEAR)),
            in_specs=[ANY, VMEM],
            out_specs=(VMEM, VMEM),
            scratch_shapes=[pltpu.SemaphoreType.DMA((2, NEAR, 2))],
            compiler_params=limit(WORK_MIB),
            name="beside_images",
        )(slc, rim)
        down = [(i, (i - 1) % half) for i in range(half)]
        down += [(half + i, half + (i + 1) % half) for i in range(half)]
        strips = lax.ppermute(
            strips, both, [(2 * a + s, 2 * b + 1 - s) for a, b in swap for s in (0, 1)]
        )
        middle = lax.ppermute(outer, "date", [(half - 1, half), (half, half - 1)])
        inner = lax.ppermute(inner, "date", down)
    else:
        rim = swapped_rims(slc)
        annual = arrivals_by_distance(slc, pair_list, plan)
        strip = lax.axis_index("strip")
        ups = [(i, i + 1) for i in range(devices - 1)]
        inner = payload_of(slc[:, dates - NEAR :], rim[:, dates - NEAR :], strip)
        outer = payload_of(slc[:, :NEAR], rim[:, :NEAR], strip)
        inner = lax.ppermute(inner, "date", ups)
        outer = lax.ppermute(outer, "date", [(b, a) for a, b in ups])

    out_shape = jax.ShapeDtypeStruct((planes, dates * per_date, rows, cols), jnp.float32)
    depth = 2 * band_shape[1]
    scratch = [
        pltpu.VMEM((2, 4 * rows, depth), jnp.bfloat16),
        pltpu.VMEM((2, 4, 2 * rows, cols), jnp.bfloat16),
        pltpu.VMEM((2, planes, rows, cols), dtype),
        pltpu.VMEM((2, planes, rows, TILE), dtype),
        pltpu.VMEM((2, 2, planes, rows, cols), jnp.float32),
        pltpu.SMEM((dates * NEAR + 1,), jnp.int32),
        pltpu.SemaphoreType.DMA((2, 2)),
    ]

    out, powers = pl.pallas_call(
        functools.partial(own_kernel, plan),
        out_shape=(out_shape, jax.ShapeDtypeStruct((dates, rows, depth), jnp.bfloat16)),
        in_specs=[SMEM] + [VMEM] * 3,
        out_specs=(ANY, VMEM),
        scratch_shapes=scratch,
        compiler_params=limit(WORK_MIB),
        cost_estimate=cost(20_000_000_000),
        name="own_pairs",
    )(lists, slc, rim, bands)

    def more_pairs(kernel, out, others, name):
        return pl.pallas_call(
            functools.partial(kernel, plan),
            out_shape=out_shape,
            in_specs=[SMEM] + [VMEM] * (4 + len(others)) + [ANY],
            out_specs=ANY,
            scratch_shapes=scratch,
            input_output_aliases={5 + len(others): 0},
            compiler_params=limit(WORK_MIB),
            cost_estimate=cost(1),
            name=name,
        )(lists, slc, rim, bands, powers, *others, out)

    if halves:
        payload, outer = pl.pallas_call(
            functools.partial(late_kernel, plan),
            out_shape=(payload_shape(late), payload_shape(NEAR)),
            in_specs=[VMEM, VMEM, VMEM, ANY, SMEM, ANY, ANY],
            out_specs=(VMEM, VMEM),
            scratch_shapes=[
                pltpu.VMEM((late, planes, rows, TILE), dtype),
                pltpu.SemaphoreType.DMA,
            ],
            compiler_params=limit(WORK_MIB),
            name="late_images",
        )(slc, rim, inner, outer, lists, powers, strips)
        payload = lax.ppermute(payload, "date", swap)
        outer = lax.ppermute(outer, "date", [(b, a) for a, b in down])
    if halves:
        early_pairs = functools.partial(annual_kernel, is_late=False)
        out = more_pairs(early_pairs, out, (inner, early, strips), "annual_pairs")
        out = more_pairs(rest_kernel, out, (inner, outer, middle), "near_pairs")
        late_pairs = functools.partial(annual_kernel, is_late=True)
        out = more_pairs(late_pairs, out, (outer, payload, strips), "last_pairs")
    else:
        out = more_pairs(rest_kernel, out, (inner, outer, inner), "near_pairs")
        out = more_pairs(plain_kernel, out, (annual, swapped_rims(annual)), "annual_pairs")
    return out


def solution(mesh):
    placed = (P(None, "date", "groups", "strip"), P(), P(), P())
    return jax.shard_map(
        body,
        mesh=mesh,
        in_specs=placed,
        out_specs=P(None, "date", "groups", "strip"),
        check_vma=False,
    )
```

```python
import functools

import jax
import jax.numpy as jnp
from jax import lax
from jax.experimental import pallas as pl
from jax.experimental.pallas import tpu as pltpu
from jax.sharding import PartitionSpec as P

HALO = 16
REACH_LO = 12
NEAR = 3
YEAR = 29
EPSILON = 1e-06
TILE = 128
INNER = TILE // 2
PER_TILE = TILE // HALO
PARTNER, HEIGHT, REACH = 1, 2, 3
WORK_MIB = 16
FIRST_MIB = 56
ANY = pl.BlockSpec(memory_space=pl.ANY)
SMEM = pl.BlockSpec(memory_space=pltpu.SMEM)
VMEM = pl.BlockSpec(memory_space=pltpu.VMEM)


def limit(mebibytes):
    return pltpu.CompilerParams(vmem_limit_bytes=mebibytes * 1024 * 1024)


def run_copies(copies):
    for copy in copies:
        copy.start()
    for copy in copies:
        copy.wait()


def gather_strips(tiles, side):
    lane = lax.broadcasted_iota(jnp.int32, tiles[0].shape, 1)
    packed = jnp.zeros(tiles[0].shape, jnp.float32)
    for n, tile in enumerate(tiles):
        spot = n * HALO
        moved = pltpu.roll(tile.astype(jnp.float32), spot + side * HALO, 1)
        packed = jnp.where((lane >= spot) & (lane < spot + HALO), moved, packed)
    return packed.astype(jnp.bfloat16)


def place_strip(packed, n, side):
    shift = 2 * TILE - (n + side) * HALO
    return pltpu.roll(packed.astype(jnp.float32), lax.rem(shift, TILE), 1).astype(jnp.bfloat16)


def write_strips(out_ref, packed):
    rows, cols = packed.shape[0], out_ref.shape[1]
    part = rows * TILE // cols
    base = out_ref.shape[0] - part
    for n in range(rows // part):
        out_ref[base:, n * TILE : (n + 1) * TILE] = packed[n * part : (n + 1) * part]


def read_strips(ref, rows):
    cols = ref.shape[1]
    base = ref.shape[0] - rows * TILE // cols
    return jnp.concatenate(
        [ref[base:, n * TILE : (n + 1) * TILE] for n in range(cols // TILE)], axis=0
    )


def wanted_images(plan, pairs_ref):
    me = lax.axis_index("date")
    dates, half = plan["dates"], plan["devices"] // 2
    mate = lax.rem(me + half, 2 * half)
    wanted = []
    for k in range(dates - plan["late"]):
        date = mate * dates + jnp.where(mate < half, plan["late"], 0) + k
        at = pairs_ref[PARTNER, date * plan["per_date"] + NEAR] - me * dates
        wanted.append(jnp.clip(at, 0, dates - 1))
    return wanted


def image_copies(slc_ref, wanted, early_ref, sems):
    return [
        pltpu.make_async_copy(slc_ref.at[:, at], early_ref.at[:, k], sems.at[k])
        for k, at in enumerate(wanted)
    ]


def gather_all(tiles, side):
    return [gather_strips(tiles[n * PER_TILE : (n + 1) * PER_TILE], side) for n in range(2)]


def early_kernel(plan, slc_ref, pairs_ref, early_ref, packed_ref, strips_ref, tiles_ref, sems,
                 tile_sem):
    strip, cols = lax.axis_index("strip"), plan["cols"]
    start = pl.multiple_of(jnp.where(strip == 0, cols - TILE, 0), TILE)
    wanted = wanted_images(plan, pairs_ref)
    tile_copy = pltpu.make_async_copy(
        slc_ref.at[:, :, :, pl.ds(start, TILE)], tiles_ref, tile_sem
    )
    early_copies = image_copies(slc_ref, wanted, early_ref, sems)
    for copy in [tile_copy] + early_copies:
        copy.start()
    tile_copy.wait()
    tiles = [tiles_ref[c, k] for k in range(plan["dates"]) for c in range(2)]
    for n, packed in enumerate(gather_all(tiles, 1 - strip)):
        packed_ref[n] = packed
    tiles = [tiles_ref[c, at] for at in wanted for c in range(2)]
    strips_ref[...] = gather_strips(tiles, 1 - strip)
    for copy in early_copies:
        copy.wait()


def rim_kernel(slc_ref, rim_ref, sem):
    cols = slc_ref.shape[3]
    start = pl.multiple_of(jnp.where(lax.axis_index("strip") == 0, cols - TILE, 0), TILE)
    run_copies([pltpu.make_async_copy(slc_ref.at[:, :, :, pl.ds(start, TILE)], rim_ref, sem)])


def beside_kernel(plan, slc_ref, packed_ref, inner_ref, outer_ref, rim_ref, sems):
    me, strip = lax.axis_index("date"), lax.axis_index("strip")
    dates, rows = plan["dates"], plan["rows"]
    upper = me >= plan["devices"] // 2
    last = dates - NEAR
    copies = []
    firsts = (jnp.where(upper, last, 0), jnp.where(upper, 0, last))
    for r, (out_ref, first) in enumerate(zip((inner_ref, outer_ref), firsts)):
        for k in range(NEAR):
            for c in range(2):
                here = out_ref.at[pl.ds((2 * k + c) * rows, rows)]
                copies.append(
                    pltpu.make_async_copy(slc_ref.at[c, first + k], here, sems.at[r, k, c])
                )
    for copy in copies:
        copy.start()
    for k in range(dates):
        for c in range(2):
            tile, n = divmod(2 * k + c, PER_TILE)
            rim_ref[c, k] = place_strip(packed_ref[tile], n, strip)
    for out_ref, first in zip((inner_ref, outer_ref), firsts):
        tiles = [rim_ref[c, first + k] for k in range(NEAR) for c in range(2)]
        write_strips(out_ref, gather_strips(tiles, strip))
    for copy in copies:
        copy.wait()


def late_kernel(plan, slc_ref, rim_ref, inner_ref, middle_ref, held_ref, pairs_ref, *refs):
    late_ref, outer_ref, tiles_ref, sem = refs[-4:]
    copy = pltpu.make_async_copy(held_ref, outer_ref, sem)
    copy.start()
    me, strip = lax.axis_index("date"), lax.axis_index("strip")
    dates, late, rows = plan["dates"], plan["late"], plan["rows"]
    half = plan["devices"] // 2
    mate = lax.rem(me + half, 2 * half)
    mate_slot = jnp.where(mate < half, 0, dates - late)
    in_middle = (me == half) | (me == half - 1)
    for k in range(late):
        date = mate * dates + mate_slot + k
        wanted = pairs_ref[PARTNER, date * plan["per_date"] + NEAR] - me * dates
        own = (wanted >= 0) & (wanted < dates)
        own_at = jnp.clip(wanted, 0, dates - 1)
        other_at = jnp.clip(jnp.where(me < half, wanted - dates, wanted + NEAR), 0, NEAR - 1)
        for c in range(2):
            here = pl.ds((2 * k + c) * rows, rows)

            @pl.when(own)
            def _():
                late_ref[here] = slc_ref[c, own_at]
                tiles_ref[k, c] = rim_ref[c, own_at]

            for chosen, ref in ((in_middle, middle_ref), (jnp.logical_not(in_middle), inner_ref)):

                @pl.when(chosen & jnp.logical_not(own))
                def _():
                    there = pl.multiple_of((2 * other_at + c) * rows, rows)
                    late_ref[here] = ref[pl.ds(there, rows)]
                    packed = read_strips(ref, rows)
                    tiles_ref[k, c] = place_strip(packed, 2 * other_at + c, strip)

    tiles = [tiles_ref[k, c] for k in range(late) for c in range(2)]
    write_strips(late_ref, gather_strips(tiles, strip))
    copy.wait()


def bands_kernel(cols, out_ref):
    strip = lax.axis_index("strip")
    wide = out_ref.shape[3]
    reach = pl.program_id(0) + REACH_LO

    def band(places, targets):
        return (jnp.abs(places - targets) <= reach).astype(jnp.float32).astype(jnp.bfloat16)

    def indices(shape):
        return lax.broadcasted_iota(jnp.int32, shape, 0), lax.broadcasted_iota(jnp.int32, shape, 1)

    inside = band(*indices((wide, wide)))
    row, col = indices((TILE, wide))
    beyond = jnp.where(strip == 0, cols + row, row - TILE)
    first = band(jnp.where(row < INNER, wide + row, beyond), col)
    second = band(jnp.where(row < INNER, beyond, wide - TILE + row), col + wide)
    for n, part in enumerate((first, second)):
        out_ref[0, n, 0:wide] = inside
        out_ref[0, n, wide : 2 * wide] = inside
        out_ref[0, n, 2 * wide : 2 * wide + TILE] = part
        out_ref[0, n, 2 * wide + TILE : 2 * wide + 2 * TILE] = part


def split(values):
    high = values.astype(jnp.bfloat16)
    low = (values - high.astype(jnp.float32)).astype(jnp.bfloat16)
    return high, low


def put(ref, here, t, values):
    wide = 2 * TILE
    depth = 2 * wide + 2 * TILE
    for low, part in enumerate(split(values)):
        side = [n * depth + 2 * wide + low * TILE for n in range(2)]
        if t < 4:
            at = (t // 2) * depth + low * wide + (t % 2) * TILE
            ref[*here, at : at + TILE] = part
        if t == 2:
            ref[*here, side[0] : side[0] + INNER] = part[:, :INNER]
        if t == 1:
            ref[*here, side[1] + INNER : side[1] + TILE] = part[:, INNER:]
        if t == 4:
            ref[*here, side[0] + INNER : side[0] + TILE] = part[:, INNER:]
            ref[*here, side[1] : side[1] + INNER] = part[:, :INNER]


def tile_of(main, rim, t):
    return [
        (rim(c) if t == 4 else main(c, slice(t * TILE, (t + 1) * TILE))).astype(jnp.float32)
        for c in range(2)
    ]


class Pairs:
    def __init__(self, plan, lists, slc_ref, rim_ref, bands_ref, powers_ref, out_ref, scratch):
        self.plan = plan
        self.lists = lists
        self.slc_ref, self.rim_ref = slc_ref, rim_ref
        self.bands_ref, self.powers_ref, self.out_ref = bands_ref, powers_ref, out_ref
        (self.left_ref, self.stack_ref, self.other_ref, self.other_rim_ref, self.stage_ref,
         self.list_ref, self.sems) = scratch
        self.me, self.strip = lax.axis_index("date"), lax.axis_index("strip")

    def partner(self, pair):
        return self.lists[PARTNER, pair]

    def near_item(self, n):
        slot, kind = n // NEAR, lax.rem(n, NEAR)
        dates = self.plan["dates"]
        pair = (self.me * dates + slot) * self.plan["per_date"] + kind
        return slot, kind, self.partner(pair) - self.me * dates

    def near_list(self, chosen):
        count = 0
        for n in range(self.plan["dates"] * NEAR):
            self.list_ref[count] = n
            count = count + jnp.where(chosen(self.near_item(n)[2]), 1, 0)
        return count

    def own(self, local):
        return (local >= 0) & (local < self.plan["dates"])

    def in_middle(self, local):
        half, dates = self.plan["devices"] // 2, self.plan["dates"]
        if not self.plan["halves"]:
            return False
        return ((self.me == half) & (local < 0)) | ((self.me == half - 1) & (local >= dates))

    def own_other(self, index):
        return (
            lambda c, cols: self.slc_ref[c, index, :, cols],
            lambda c: self.rim_ref[c, index],
        )

    def fetched_other(self, x):
        return (
            lambda c, cols: self.other_ref[x, c, :, cols],
            lambda c: self.other_rim_ref[x, c],
        )

    def fetch_payload(self, x, ref, index):
        rows = self.plan["rows"]
        packed = read_strips(ref, rows)
        for c in range(2):
            at = pl.multiple_of((2 * index + c) * rows, rows)
            self.other_ref[x, c] = ref[pl.ds(at, rows)]
            self.other_rim_ref[x, c] = place_strip(packed, 2 * index + c, self.strip)

    def out_copy(self, stage, x, pair):
        return pltpu.make_async_copy(
            self.stage_ref.at[stage, x], self.out_ref.at[:, pair], self.sems.at[stage, x]
        )

    def run(self, count, work):
        steps = (count + 1) // 2

        def step(n, carry):
            stage = lax.rem(n, 2)

            @pl.when(n >= 2)
            def _():
                for x in range(2):
                    self.out_copy(stage, x, 0).wait()

            items = [work(x, jnp.minimum(2 * n + x, count - 1)) for x in range(2)]
            self.compute(stage, items)
            for x, (slot, kind, _, _) in enumerate(items):
                copy = self.out_copy(stage, x, slot * self.plan["per_date"] + kind)
                pl.when(2 * n + x < count)(copy.start)
            return carry

        lax.fori_loop(0, steps, step, 0)
        for back in (2, 1):
            for x in range(2):
                used = (steps >= back) & (2 * (steps - back) + x < count)
                pl.when(used)(self.out_copy(lax.rem(steps + back, 2), x, 0).wait)

    def compute(self, stage, items):
        plan = self.plan
        rows, dates, per_date = plan["rows"], plan["dates"], plan["per_date"]
        part = [(pl.ds(f * rows, rows),) for f in range(4)]
        depth = self.bands_ref.shape[2]
        wide = self.bands_ref.shape[3]
        heights, widths = [], []
        for slot, kind, _, _ in items:
            pair = (self.me * dates + slot) * per_date + kind
            heights.append(self.lists[HEIGHT, pair])
            widths.append(jnp.clip(self.lists[REACH, pair] - REACH_LO, 0, HALO - REACH_LO))
        for x, (slot, kind, other, other_power) in enumerate(items):
            left_ref = self.left_ref.at[x]
            left_ref[*part[2]] = self.powers_ref[slot]
            if other_power is not None:
                left_ref[*part[3]] = self.powers_ref[other_power]
            first = self.own_other(slot)
            for t in range(5):
                a_real, a_imag = tile_of(*first, t)
                b_real, b_imag = tile_of(*other, t)
                put(left_ref, part[0], t, a_real * b_real + a_imag * b_imag)
                put(left_ref, part[1], t, a_imag * b_real - a_real * b_imag)
                if other_power is None:
                    put(left_ref, part[3], t, b_real * b_real + b_imag * b_imag)
        for n in range(2):
            for x in range(2):
                ranged = jnp.dot(
                    self.left_ref[x, :, n * depth : (n + 1) * depth],
                    self.bands_ref[widths[x], n],
                    preferred_element_type=jnp.float32,
                )
                there = slice(n * wide, (n + 1) * wide)
                for low, values in enumerate(split(ranged)):
                    for f in range(4):
                        self.stack_ref[x, f, low * rows : (low + 1) * rows, there] = values[
                            f * rows : (f + 1) * rows
                        ]
        row = lax.broadcasted_iota(jnp.int32, (rows, 2 * rows), 0)
        col = lax.broadcasted_iota(jnp.int32, (rows, 2 * rows), 1)
        col = jnp.where(col < rows, col, col - rows)
        for x in range(2):
            band = (jnp.abs(row - col) <= heights[x]).astype(jnp.float32).astype(jnp.bfloat16)
            looked = [
                jnp.dot(band, self.stack_ref[x, f], preferred_element_type=jnp.float32)
                for f in range(4)
            ]
            inverse = lax.rsqrt(looked[2] * looked[3] + EPSILON)
            for c in range(2):
                self.stage_ref[stage, x, c] = looked[c] * inverse


def own_kernel(plan, lists, slc_ref, rim_ref, bands_ref, out_ref, powers_ref, *scratch):
    pairs = Pairs(plan, lists, slc_ref, rim_ref, bands_ref, powers_ref, out_ref, scratch)
    dates = plan["dates"]

    def power(slot, carry):
        for t in range(5):
            real, imag = tile_of(*pairs.own_other(slot), t)
            put(powers_ref, (slot, slice(None)), t, real * real + imag * imag)
        return carry

    lax.fori_loop(0, dates, power, 0)

    def work(x, n):
        slot, kind, local = pairs.near_item(pairs.list_ref[n])
        return slot, kind, pairs.own_other(local), local

    pairs.run(pairs.near_list(pairs.own), work)


def rest_kernel(plan, lists, slc_ref, rim_ref, bands_ref, powers_ref, inner_ref, outer_ref,
                middle_ref, _, out_ref, *scratch):
    pairs = Pairs(plan, lists, slc_ref, rim_ref, bands_ref, powers_ref, out_ref, scratch)
    dates = plan["dates"]
    upper = pairs.me >= plan["devices"] // 2 if plan["halves"] else True

    def work(x, n):
        slot, kind, local = pairs.near_item(pairs.list_ref[n])
        below = local < 0
        index = jnp.clip(jnp.where(below, local + NEAR, local - dates), 0, NEAR - 1)
        inner, middle = below == upper, pairs.in_middle(local)
        sources = (
            (jnp.logical_not(inner), outer_ref),
            (inner & jnp.logical_not(middle), inner_ref),
            (inner & middle, middle_ref),
        )
        for chosen, ref in sources:
            pl.when(chosen)(functools.partial(pairs.fetch_payload, x, ref, index))
        return slot, kind, pairs.fetched_other(x), None

    pairs.run(pairs.near_list(lambda local: jnp.logical_not(pairs.own(local))), work)


def annual_kernel(plan, lists, slc_ref, rim_ref, bands_ref, powers_ref, ring_ref,
                  images_ref, strips_ref, _, out_ref, *scratch, is_late):
    pairs = Pairs(plan, lists, slc_ref, rim_ref, bands_ref, powers_ref, out_ref, scratch)
    dates, late = plan["dates"], plan["late"]
    half = plan["devices"] // 2
    me, split_date = pairs.me, half * dates
    lower = me < half
    if is_late:
        base, count = jnp.where(lower, 0, dates - late), late
    else:
        base, count = jnp.where(lower, late, 0), dates - late

    def fetch_early(x, k, ref):
        packed = strips_ref[...]
        for c in range(2):
            pairs.other_ref[x, c] = ref[c, k]
            pairs.other_rim_ref[x, c] = place_strip(packed, 2 * k + c, pairs.strip)

    def work(x, k):
        slot = base + k
        date = me * dates + slot
        other = pairs.partner(date * plan["per_date"] + NEAR)
        if is_late:
            pairs.fetch_payload(x, images_ref, k)
        else:
            far = (other < split_date) == lower
            ring_at = jnp.where(lower, other, other - (2 * split_date - NEAR))
            ring_at = jnp.clip(ring_at, 0, NEAR - 1)
            pl.when(far)(lambda: pairs.fetch_payload(x, ring_ref, ring_at))
            pl.when(jnp.logical_not(far))(lambda: fetch_early(x, k, images_ref))
        return slot, NEAR, pairs.fetched_other(x), None

    pairs.run(count, work)


def plain_kernel(plan, lists, slc_ref, rim_ref, bands_ref, powers_ref, images_ref,
                 image_rim_ref, _, out_ref, *scratch):
    pairs = Pairs(plan, lists, slc_ref, rim_ref, bands_ref, powers_ref, out_ref, scratch)

    def work(x, slot):
        other = (
            lambda c, cols: images_ref[c, slot, :, cols],
            lambda c: image_rim_ref[c, slot],
        )
        return slot, NEAR, other, None

    pairs.run(plan["dates"], work)


def arrivals_by_distance(slc, pair_list, plan):
    dates, per_date, devices = plan["dates"], plan["per_date"], plan["devices"]
    total = dates * devices
    me = lax.axis_index("date")
    annual_of = pair_list[:, 1].reshape(total, per_date)[:, per_date - 1]
    sums = [None] * dates
    for direction in (1, -1):
        by_distance = {}
        for slot in range(dates):
            for gap in range(plan["year"], plan["year"] + 3):
                distance = (slot + direction * gap) // dates
                by_distance.setdefault(distance, set()).add(slot)
        for distance in sorted(by_distance):
            slots = sorted(by_distance[distance])
            wanted_by = (me - distance) * dates + jnp.array(slots, dtype=jnp.int32)
            inside = (wanted_by >= 0) & (wanted_by < total)
            local = jnp.take(annual_of, jnp.clip(wanted_by, 0, total - 1)) - me * dates
            usable = inside & (local >= 0) & (local < dates)
            packed = jnp.take(slc, jnp.clip(local, 0, dates - 1), axis=1)
            packed = jnp.where(usable[None, :, None, None], packed, jnp.zeros_like(packed))
            route = [(i + distance, i) for i in range(devices) if 0 <= i + distance < devices]
            arrived = lax.ppermute(packed, "date", route)
            for n, slot in enumerate(slots):
                part = arrived[:, n]
                sums[slot] = part if sums[slot] is None else sums[slot] + part
    return jnp.stack(sums, axis=1)


def payload_of(images, rim, strip):
    planes, count, rows, cols = images.shape
    edges = jnp.where(strip == 0, rim[..., :HALO], rim[..., TILE - HALO :])
    edges = jnp.transpose(edges, (2, 1, 0, 3)).reshape(rows, count * planes * HALO)
    edges = jnp.pad(edges, ((0, 0), (0, TILE - edges.shape[1])))
    part = rows * TILE // cols
    edges = jnp.transpose(edges.reshape(rows // part, part, TILE), (1, 0, 2)).reshape(part, cols)
    stacked = jnp.transpose(images, (1, 0, 2, 3)).reshape(count * planes * rows, cols)
    return jnp.concatenate([stacked, edges], axis=0)


def body(slc, pair_list, az_half, rng_half):
    planes, dates, rows, cols = slc.shape
    devices = lax.axis_size("date")
    total = dates * devices
    per_date = pair_list.shape[0] // total
    year = min(YEAR, total // 2 - 2)
    half = devices // 2
    late = half * dates - year
    halves = devices % 2 == 0 and 0 < late <= NEAR and 2 * late <= dates
    halves = halves and dates - late <= PER_TILE // 2 and dates <= PER_TILE
    plan = {
        "dates": dates,
        "devices": devices,
        "per_date": per_date,
        "year": year,
        "late": late,
        "rows": rows,
        "cols": cols,
        "pairs": total * per_date,
        "halves": halves,
    }
    dtype = slc.dtype
    rim_rows = rows * TILE // cols
    pairs = pair_list.T
    lists = jnp.concatenate([pairs, az_half[None], rng_half[None]])
    swap_strips = [(0, 1), (1, 0)]

    def images(count):
        return jax.ShapeDtypeStruct((planes, count, rows, cols), dtype)

    def rim_shape(count):
        return jax.ShapeDtypeStruct((planes, count, rows, TILE), dtype)

    def payload_shape(count):
        return jax.ShapeDtypeStruct((planes * count * rows + rim_rows, cols), dtype)

    def swapped_rims(values):
        out = pl.pallas_call(
            rim_kernel,
            out_shape=rim_shape(values.shape[1]),
            in_specs=[ANY],
            out_specs=VMEM,
            scratch_shapes=[pltpu.SemaphoreType.DMA],
            compiler_params=limit(WORK_MIB),
            name="rim_blocks",
        )(values)
        return lax.ppermute(out, "strip", swap_strips)

    def cost(flops):
        return pl.CostEstimate(flops=flops, bytes_accessed=1, transcendentals=0)

    wide = cols // 2
    widths = HALO - REACH_LO + 1
    band_shape = (2, 2 * wide + 2 * TILE, wide)
    bands = pl.pallas_call(
        functools.partial(bands_kernel, cols),
        grid=(widths,),
        out_shape=jax.ShapeDtypeStruct((widths, *band_shape), jnp.bfloat16),
        out_specs=pl.BlockSpec((1, *band_shape), lambda n: (n, 0, 0, 0)),
        compiler_params=limit(WORK_MIB),
        cost_estimate=cost(1),
        name="range_bands",
    )()
    if halves:
        swap = [(i, (i + half) % devices) for i in range(devices)]
        both = ("date", "strip")
        early, packed, strips = pl.pallas_call(
            functools.partial(early_kernel, plan),
            out_shape=(
                images(dates - late),
                jax.ShapeDtypeStruct((2, rows, TILE), dtype),
                jax.ShapeDtypeStruct((rows, TILE), dtype),
            ),
            in_specs=[ANY, SMEM],
            out_specs=(VMEM, VMEM, VMEM),
            scratch_shapes=[
                pltpu.VMEM((planes, dates, rows, TILE), dtype),
                pltpu.SemaphoreType.DMA((dates - late,)),
                pltpu.SemaphoreType.DMA,
            ],
            compiler_params=limit(FIRST_MIB),
            name="early_images",
        )(slc, pairs)
        early = lax.ppermute(early, "date", swap)
        packed = lax.ppermute(packed, "strip", swap_strips)
        inner, outer, rim = pl.pallas_call(
            functools.partial(beside_kernel, plan),
            out_shape=(payload_shape(NEAR), payload_shape(NEAR), rim_shape(dates)),
            in_specs=[ANY, VMEM],
            out_specs=(VMEM, VMEM, VMEM),
            scratch_shapes=[pltpu.SemaphoreType.DMA((2, NEAR, 2))],
            compiler_params=limit(WORK_MIB),
            name="beside_images",
        )(slc, packed)
        down = [(i, (i - 1) % half) for i in range(half)]
        down += [(half + i, half + (i + 1) % half) for i in range(half)]
        strips = lax.ppermute(
            strips, both, [(2 * a + s, 2 * b + 1 - s) for a, b in swap for s in (0, 1)]
        )
        middle = lax.ppermute(outer, "date", [(half - 1, half), (half, half - 1)])
        inner = lax.ppermute(inner, "date", down)
    else:
        rim = swapped_rims(slc)
        annual = arrivals_by_distance(slc, pair_list, plan)
        strip = lax.axis_index("strip")
        ups = [(i, i + 1) for i in range(devices - 1)]
        inner = payload_of(slc[:, dates - NEAR :], rim[:, dates - NEAR :], strip)
        outer = payload_of(slc[:, :NEAR], rim[:, :NEAR], strip)
        inner = lax.ppermute(inner, "date", ups)
        outer = lax.ppermute(outer, "date", [(b, a) for a, b in ups])

    out_shape = jax.ShapeDtypeStruct((planes, dates * per_date, rows, cols), jnp.float32)
    depth = 2 * band_shape[1]
    scratch = [
        pltpu.VMEM((2, 4 * rows, depth), jnp.bfloat16),
        pltpu.VMEM((2, 4, 2 * rows, cols), jnp.bfloat16),
        pltpu.VMEM((2, planes, rows, cols), dtype),
        pltpu.VMEM((2, planes, rows, TILE), dtype),
        pltpu.VMEM((2, 2, planes, rows, cols), jnp.float32),
        pltpu.SMEM((dates * NEAR + 1,), jnp.int32),
        pltpu.SemaphoreType.DMA((2, 2)),
    ]

    out, powers = pl.pallas_call(
        functools.partial(own_kernel, plan),
        out_shape=(out_shape, jax.ShapeDtypeStruct((dates, rows, depth), jnp.bfloat16)),
        in_specs=[SMEM] + [VMEM] * 3,
        out_specs=(ANY, VMEM),
        scratch_shapes=scratch,
        compiler_params=limit(WORK_MIB),
        cost_estimate=cost(20_000_000_000),
        name="own_pairs",
    )(lists, slc, rim, bands)

    def more_pairs(kernel, out, others, name):
        return pl.pallas_call(
            functools.partial(kernel, plan),
            out_shape=out_shape,
            in_specs=[SMEM] + [VMEM] * (4 + len(others)) + [ANY],
            out_specs=ANY,
            scratch_shapes=scratch,
            input_output_aliases={5 + len(others): 0},
            compiler_params=limit(WORK_MIB),
            cost_estimate=cost(1),
            name=name,
        )(lists, slc, rim, bands, powers, *others, out)

    if halves:
        payload, outer = pl.pallas_call(
            functools.partial(late_kernel, plan),
            out_shape=(payload_shape(late), payload_shape(NEAR)),
            in_specs=[VMEM, VMEM, VMEM, VMEM, ANY, SMEM, ANY, ANY],
            out_specs=(VMEM, VMEM),
            scratch_shapes=[
                pltpu.VMEM((late, planes, rows, TILE), dtype),
                pltpu.SemaphoreType.DMA,
            ],
            compiler_params=limit(WORK_MIB),
            name="late_images",
        )(slc, rim, inner, middle, outer, lists, powers, strips)
        up = [(b, a) for a, b in down if b not in (half - 1, half)]
        outer = lax.ppermute(outer, "date", up)
        payload = lax.ppermute(payload, "date", swap)
    if halves:
        early_pairs = functools.partial(annual_kernel, is_late=False)
        out = more_pairs(early_pairs, out, (inner, early, strips), "annual_pairs")
        out = more_pairs(rest_kernel, out, (inner, outer, middle), "near_pairs")
        late_pairs = functools.partial(annual_kernel, is_late=True)
        out = more_pairs(late_pairs, out, (inner, payload, strips), "last_pairs")
    else:
        out = more_pairs(rest_kernel, out, (inner, outer, inner), "near_pairs")
        out = more_pairs(plain_kernel, out, (annual, swapped_rims(annual)), "annual_pairs")
    return out


def solution(mesh):
    placed = (P(None, "date", "groups", "strip"), P(), P(), P())
    return jax.shard_map(
        body,
        mesh=mesh,
        in_specs=placed,
        out_specs=P(None, "date", "groups", "strip"),
        check_vma=False,
    )
```

```python
import functools

import jax
import jax.numpy as jnp
from jax import lax
from jax.experimental import pallas as pl
from jax.experimental.pallas import tpu as pltpu
from jax.sharding import PartitionSpec as P

HALO = 16
REACH_LO = 12
NEAR = 3
YEAR = 29
EPSILON = 1e-06
TILE = 128
INNER = TILE // 2
PER_TILE = TILE // HALO
PARTNER, HEIGHT, REACH = 1, 2, 3
WORK_MIB = 16
FIRST_MIB = 56
ANY = pl.BlockSpec(memory_space=pl.ANY)
SMEM = pl.BlockSpec(memory_space=pltpu.SMEM)
VMEM = pl.BlockSpec(memory_space=pltpu.VMEM)


def limit(mebibytes):
    return pltpu.CompilerParams(vmem_limit_bytes=mebibytes * 1024 * 1024)


def run_copies(copies):
    for copy in copies:
        copy.start()
    for copy in copies:
        copy.wait()


def gather_strips(tiles, side):
    lane = lax.broadcasted_iota(jnp.int32, tiles[0].shape, 1)
    packed = jnp.zeros(tiles[0].shape, jnp.float32)
    for n, tile in enumerate(tiles):
        spot = n * HALO
        moved = pltpu.roll(tile.astype(jnp.float32), spot + side * HALO, 1)
        packed = jnp.where((lane >= spot) & (lane < spot + HALO), moved, packed)
    return packed.astype(jnp.bfloat16)


def place_strip(packed, n, side):
    shift = 2 * TILE - (n + side) * HALO
    return pltpu.roll(packed.astype(jnp.float32), lax.rem(shift, TILE), 1).astype(jnp.bfloat16)


def write_strips(out_ref, packed):
    rows, cols = packed.shape[0], out_ref.shape[1]
    part = rows * TILE // cols
    base = out_ref.shape[0] - part
    for n in range(rows // part):
        out_ref[base:, n * TILE : (n + 1) * TILE] = packed[n * part : (n + 1) * part]


def read_strips(ref, rows):
    cols = ref.shape[1]
    base = ref.shape[0] - rows * TILE // cols
    return jnp.concatenate(
        [ref[base:, n * TILE : (n + 1) * TILE] for n in range(cols // TILE)], axis=0
    )


def wanted_images(plan, pairs_ref):
    me = lax.axis_index("date")
    dates, half = plan["dates"], plan["devices"] // 2
    mate = lax.rem(me + half, 2 * half)
    wanted = []
    for k in range(dates - plan["late"]):
        date = mate * dates + jnp.where(mate < half, plan["late"], 0) + k
        at = pairs_ref[PARTNER, date * plan["per_date"] + NEAR] - me * dates
        wanted.append(jnp.clip(at, 0, dates - 1))
    return wanted


def image_copies(slc_ref, wanted, early_ref, sems):
    return [
        pltpu.make_async_copy(slc_ref.at[:, at], early_ref.at[:, k], sems.at[k])
        for k, at in enumerate(wanted)
    ]


def gather_all(tiles, side):
    return [gather_strips(tiles[n * PER_TILE : (n + 1) * PER_TILE], side) for n in range(2)]


def early_kernel(plan, slc_ref, pairs_ref, early_ref, packed_ref, strips_ref, tiles_ref, sems,
                 tile_sem):
    strip, cols = lax.axis_index("strip"), plan["cols"]
    start = pl.multiple_of(jnp.where(strip == 0, cols - TILE, 0), TILE)
    wanted = wanted_images(plan, pairs_ref)
    tile_copy = pltpu.make_async_copy(
        slc_ref.at[:, :, :, pl.ds(start, TILE)], tiles_ref, tile_sem
    )
    early_copies = image_copies(slc_ref, wanted, early_ref, sems)
    for copy in [tile_copy] + early_copies:
        copy.start()
    tile_copy.wait()
    tiles = [tiles_ref[c, k] for k in range(plan["dates"]) for c in range(2)]
    for n, packed in enumerate(gather_all(tiles, 1 - strip)):
        packed_ref[n] = packed
    tiles = [tiles_ref[c, at] for at in wanted for c in range(2)]
    strips_ref[...] = gather_strips(tiles, 1 - strip)
    for copy in early_copies:
        copy.wait()


def rim_kernel(slc_ref, rim_ref, sem):
    cols = slc_ref.shape[3]
    start = pl.multiple_of(jnp.where(lax.axis_index("strip") == 0, cols - TILE, 0), TILE)
    run_copies([pltpu.make_async_copy(slc_ref.at[:, :, :, pl.ds(start, TILE)], rim_ref, sem)])


def beside_kernel(plan, slc_ref, packed_ref, inner_ref, outer_ref, rim_ref, sems):
    me, strip = lax.axis_index("date"), lax.axis_index("strip")
    dates, rows = plan["dates"], plan["rows"]
    upper = me >= plan["devices"] // 2
    last = dates - NEAR
    copies = []
    firsts = (jnp.where(upper, last, 0), jnp.where(upper, 0, last))
    for r, (out_ref, first) in enumerate(zip((inner_ref, outer_ref), firsts)):
        for k in range(NEAR):
            for c in range(2):
                here = out_ref.at[pl.ds((2 * k + c) * rows, rows)]
                copies.append(
                    pltpu.make_async_copy(slc_ref.at[c, first + k], here, sems.at[r, k, c])
                )
    for copy in copies:
        copy.start()
    for k in range(dates):
        for c in range(2):
            tile, n = divmod(2 * k + c, PER_TILE)
            rim_ref[c, k] = place_strip(packed_ref[tile], n, strip)
    for out_ref, first in zip((inner_ref, outer_ref), firsts):
        tiles = [rim_ref[c, first + k] for k in range(NEAR) for c in range(2)]
        write_strips(out_ref, gather_strips(tiles, strip))
    for copy in copies:
        copy.wait()


def late_kernel(plan, slc_ref, rim_ref, inner_ref, middle_ref, pairs_ref, *refs):
    late_ref, tiles_ref = refs[-2:]
    me, strip = lax.axis_index("date"), lax.axis_index("strip")
    dates, late, rows = plan["dates"], plan["late"], plan["rows"]
    half = plan["devices"] // 2
    mate = lax.rem(me + half, 2 * half)
    mate = jnp.where(me == half - 1, 0, jnp.where(me == half, 2 * half - 1, mate))
    mate_slot = jnp.where(mate < half, 0, dates - late)
    in_middle = (me == half) | (me == half - 1)
    for k in range(late):
        date = mate * dates + mate_slot + k
        wanted = pairs_ref[PARTNER, date * plan["per_date"] + NEAR] - me * dates
        own = (wanted >= 0) & (wanted < dates)
        own_at = jnp.clip(wanted, 0, dates - 1)
        other_at = jnp.clip(jnp.where(me < half, wanted - dates, wanted + NEAR), 0, NEAR - 1)
        for c in range(2):
            here = pl.ds((2 * k + c) * rows, rows)

            @pl.when(own)
            def _():
                late_ref[here] = slc_ref[c, own_at]
                tiles_ref[k, c] = rim_ref[c, own_at]

            for chosen, ref in ((in_middle, middle_ref), (jnp.logical_not(in_middle), inner_ref)):

                @pl.when(chosen & jnp.logical_not(own))
                def _():
                    there = pl.multiple_of((2 * other_at + c) * rows, rows)
                    late_ref[here] = ref[pl.ds(there, rows)]
                    packed = read_strips(ref, rows)
                    tiles_ref[k, c] = place_strip(packed, 2 * other_at + c, strip)

    tiles = [tiles_ref[k, c] for k in range(late) for c in range(2)]
    write_strips(late_ref, gather_strips(tiles, strip))


def bands_kernel(cols, out_ref):
    strip = lax.axis_index("strip")
    wide = out_ref.shape[3]
    reach = pl.program_id(0) + REACH_LO

    def band(places, targets):
        return (jnp.abs(places - targets) <= reach).astype(jnp.float32).astype(jnp.bfloat16)

    def indices(shape):
        return lax.broadcasted_iota(jnp.int32, shape, 0), lax.broadcasted_iota(jnp.int32, shape, 1)

    inside = band(*indices((wide, wide)))
    row, col = indices((TILE, wide))
    beyond = jnp.where(strip == 0, cols + row, row - TILE)
    first = band(jnp.where(row < INNER, wide + row, beyond), col)
    second = band(jnp.where(row < INNER, beyond, wide - TILE + row), col + wide)
    for n, part in enumerate((first, second)):
        out_ref[0, n, 0:wide] = inside
        out_ref[0, n, wide : 2 * wide] = inside
        out_ref[0, n, 2 * wide : 2 * wide + TILE] = part
        out_ref[0, n, 2 * wide + TILE : 2 * wide + 2 * TILE] = part


def split(values):
    high = values.astype(jnp.bfloat16)
    low = (values - high.astype(jnp.float32)).astype(jnp.bfloat16)
    return high, low


def put(ref, here, t, values):
    wide = 2 * TILE
    depth = 2 * wide + 2 * TILE
    for low, part in enumerate(split(values)):
        side = [n * depth + 2 * wide + low * TILE for n in range(2)]
        if t < 4:
            at = (t // 2) * depth + low * wide + (t % 2) * TILE
            ref[*here, at : at + TILE] = part
        if t == 2:
            ref[*here, side[0] : side[0] + INNER] = part[:, :INNER]
        if t == 1:
            ref[*here, side[1] + INNER : side[1] + TILE] = part[:, INNER:]
        if t == 4:
            ref[*here, side[0] + INNER : side[0] + TILE] = part[:, INNER:]
            ref[*here, side[1] : side[1] + INNER] = part[:, :INNER]


def tile_of(main, rim, t):
    return [
        (rim(c) if t == 4 else main(c, slice(t * TILE, (t + 1) * TILE))).astype(jnp.float32)
        for c in range(2)
    ]


class Pairs:
    def __init__(self, plan, lists, slc_ref, rim_ref, bands_ref, powers_ref, out_ref, scratch):
        self.plan = plan
        self.lists = lists
        self.slc_ref, self.rim_ref = slc_ref, rim_ref
        self.bands_ref, self.powers_ref, self.out_ref = bands_ref, powers_ref, out_ref
        (self.left_ref, self.stack_ref, self.other_ref, self.other_rim_ref, self.stage_ref,
         self.list_ref, self.sems) = scratch
        self.me, self.strip = lax.axis_index("date"), lax.axis_index("strip")

    def partner(self, pair):
        return self.lists[PARTNER, pair]

    def near_item(self, n):
        slot, kind = n // NEAR, lax.rem(n, NEAR)
        dates = self.plan["dates"]
        pair = (self.me * dates + slot) * self.plan["per_date"] + kind
        return slot, kind, self.partner(pair) - self.me * dates

    def near_list(self, chosen):
        count = 0
        for n in range(self.plan["dates"] * NEAR):
            self.list_ref[count] = n
            count = count + jnp.where(chosen(self.near_item(n)[2]), 1, 0)
        return count

    def own(self, local):
        return (local >= 0) & (local < self.plan["dates"])

    def in_middle(self, local):
        half, dates = self.plan["devices"] // 2, self.plan["dates"]
        if not self.plan["halves"]:
            return False
        return ((self.me == half) & (local < 0)) | ((self.me == half - 1) & (local >= dates))

    def own_other(self, index):
        return (
            lambda c, cols: self.slc_ref[c, index, :, cols],
            lambda c: self.rim_ref[c, index],
        )

    def fetched_other(self, x):
        return (
            lambda c, cols: self.other_ref[x, c, :, cols],
            lambda c: self.other_rim_ref[x, c],
        )

    def fetch_payload(self, x, ref, index):
        rows = self.plan["rows"]
        packed = read_strips(ref, rows)
        for c in range(2):
            at = pl.multiple_of((2 * index + c) * rows, rows)
            self.other_ref[x, c] = ref[pl.ds(at, rows)]
            self.other_rim_ref[x, c] = place_strip(packed, 2 * index + c, self.strip)

    def out_copy(self, stage, x, pair):
        return pltpu.make_async_copy(
            self.stage_ref.at[stage, x], self.out_ref.at[:, pair], self.sems.at[stage, x]
        )

    def run(self, count, work):
        steps = (count + 1) // 2

        def step(n, carry):
            stage = lax.rem(n, 2)

            @pl.when(n >= 2)
            def _():
                for x in range(2):
                    self.out_copy(stage, x, 0).wait()

            items = [work(x, jnp.minimum(2 * n + x, count - 1)) for x in range(2)]
            self.compute(stage, items)
            for x, (slot, kind, _, _) in enumerate(items):
                copy = self.out_copy(stage, x, slot * self.plan["per_date"] + kind)
                pl.when(2 * n + x < count)(copy.start)
            return carry

        lax.fori_loop(0, steps, step, 0)
        for back in (2, 1):
            for x in range(2):
                used = (steps >= back) & (2 * (steps - back) + x < count)
                pl.when(used)(self.out_copy(lax.rem(steps + back, 2), x, 0).wait)

    def compute(self, stage, items):
        plan = self.plan
        rows, dates, per_date = plan["rows"], plan["dates"], plan["per_date"]
        part = [(pl.ds(f * rows, rows),) for f in range(4)]
        depth = self.bands_ref.shape[2]
        wide = self.bands_ref.shape[3]
        heights, widths = [], []
        for slot, kind, _, _ in items:
            pair = (self.me * dates + slot) * per_date + kind
            heights.append(self.lists[HEIGHT, pair])
            widths.append(jnp.clip(self.lists[REACH, pair] - REACH_LO, 0, HALO - REACH_LO))
        for x, (slot, kind, other, other_power) in enumerate(items):
            left_ref = self.left_ref.at[x]
            left_ref[*part[2]] = self.powers_ref[slot]
            if other_power is not None:
                left_ref[*part[3]] = self.powers_ref[other_power]
            first = self.own_other(slot)
            for t in range(5):
                a_real, a_imag = tile_of(*first, t)
                b_real, b_imag = tile_of(*other, t)
                put(left_ref, part[0], t, a_real * b_real + a_imag * b_imag)
                put(left_ref, part[1], t, a_imag * b_real - a_real * b_imag)
                if other_power is None:
                    put(left_ref, part[3], t, b_real * b_real + b_imag * b_imag)
        for n in range(2):
            for x in range(2):
                ranged = jnp.dot(
                    self.left_ref[x, :, n * depth : (n + 1) * depth],
                    self.bands_ref[widths[x], n],
                    preferred_element_type=jnp.float32,
                )
                there = slice(n * wide, (n + 1) * wide)
                for low, values in enumerate(split(ranged)):
                    for f in range(4):
                        self.stack_ref[x, f, low * rows : (low + 1) * rows, there] = values[
                            f * rows : (f + 1) * rows
                        ]
        row = lax.broadcasted_iota(jnp.int32, (rows, 2 * rows), 0)
        col = lax.broadcasted_iota(jnp.int32, (rows, 2 * rows), 1)
        col = jnp.where(col < rows, col, col - rows)
        for x in range(2):
            band = (jnp.abs(row - col) <= heights[x]).astype(jnp.float32).astype(jnp.bfloat16)
            looked = [
                jnp.dot(band, self.stack_ref[x, f], preferred_element_type=jnp.float32)
                for f in range(4)
            ]
            inverse = lax.rsqrt(looked[2] * looked[3] + EPSILON)
            for c in range(2):
                self.stage_ref[stage, x, c] = looked[c] * inverse


def own_kernel(plan, lists, slc_ref, rim_ref, bands_ref, out_ref, powers_ref, *scratch):
    pairs = Pairs(plan, lists, slc_ref, rim_ref, bands_ref, powers_ref, out_ref, scratch)
    dates = plan["dates"]

    def power(slot, carry):
        for t in range(5):
            real, imag = tile_of(*pairs.own_other(slot), t)
            put(powers_ref, (slot, slice(None)), t, real * real + imag * imag)
        return carry

    lax.fori_loop(0, dates, power, 0)

    def work(x, n):
        slot, kind, local = pairs.near_item(pairs.list_ref[n])
        return slot, kind, pairs.own_other(local), local

    pairs.run(pairs.near_list(pairs.own), work)


def rest_kernel(plan, lists, slc_ref, rim_ref, bands_ref, powers_ref, inner_ref, outer_ref,
                middle_ref, _, out_ref, *scratch):
    pairs = Pairs(plan, lists, slc_ref, rim_ref, bands_ref, powers_ref, out_ref, scratch)
    dates = plan["dates"]
    upper = pairs.me >= plan["devices"] // 2 if plan["halves"] else True

    def work(x, n):
        slot, kind, local = pairs.near_item(pairs.list_ref[n])
        below = local < 0
        index = jnp.clip(jnp.where(below, local + NEAR, local - dates), 0, NEAR - 1)
        inner, middle = below == upper, pairs.in_middle(local)
        sources = (
            (jnp.logical_not(inner), outer_ref),
            (inner & jnp.logical_not(middle), inner_ref),
            (inner & middle, middle_ref),
        )
        for chosen, ref in sources:
            pl.when(chosen)(functools.partial(pairs.fetch_payload, x, ref, index))
        return slot, kind, pairs.fetched_other(x), None

    pairs.run(pairs.near_list(lambda local: jnp.logical_not(pairs.own(local))), work)


def annual_kernel(plan, lists, slc_ref, rim_ref, bands_ref, powers_ref, ring_ref,
                  images_ref, strips_ref, _sent, _, out_ref, *scratch, is_late):
    pairs = Pairs(plan, lists, slc_ref, rim_ref, bands_ref, powers_ref, out_ref, scratch)
    dates, late = plan["dates"], plan["late"]
    half = plan["devices"] // 2
    me, split_date = pairs.me, half * dates
    lower = me < half
    if is_late:
        base, count = jnp.where(lower, 0, dates - late), late
    else:
        base, count = jnp.where(lower, late, 0), dates - late

    def fetch_early(x, k, ref):
        packed = strips_ref[...]
        for c in range(2):
            pairs.other_ref[x, c] = ref[c, k]
            pairs.other_rim_ref[x, c] = place_strip(packed, 2 * k + c, pairs.strip)

    def work(x, k):
        slot = base + k
        date = me * dates + slot
        other = pairs.partner(date * plan["per_date"] + NEAR)
        if is_late:
            pairs.fetch_payload(x, images_ref, k)
        else:
            far = (other < split_date) == lower
            ring_at = jnp.where(lower, other, other - (2 * split_date - NEAR))
            ring_at = jnp.clip(ring_at, 0, NEAR - 1)
            pl.when(far)(lambda: pairs.fetch_payload(x, ring_ref, ring_at))
            pl.when(jnp.logical_not(far))(lambda: fetch_early(x, k, images_ref))
        return slot, NEAR, pairs.fetched_other(x), None

    pairs.run(count, work)


def plain_kernel(plan, lists, slc_ref, rim_ref, bands_ref, powers_ref, images_ref,
                 image_rim_ref, _, out_ref, *scratch):
    pairs = Pairs(plan, lists, slc_ref, rim_ref, bands_ref, powers_ref, out_ref, scratch)

    def work(x, slot):
        other = (
            lambda c, cols: images_ref[c, slot, :, cols],
            lambda c: image_rim_ref[c, slot],
        )
        return slot, NEAR, other, None

    pairs.run(plan["dates"], work)


def arrivals_by_distance(slc, pair_list, plan):
    dates, per_date, devices = plan["dates"], plan["per_date"], plan["devices"]
    total = dates * devices
    me = lax.axis_index("date")
    annual_of = pair_list[:, 1].reshape(total, per_date)[:, per_date - 1]
    sums = [None] * dates
    for direction in (1, -1):
        by_distance = {}
        for slot in range(dates):
            for gap in range(plan["year"], plan["year"] + 3):
                distance = (slot + direction * gap) // dates
                by_distance.setdefault(distance, set()).add(slot)
        for distance in sorted(by_distance):
            slots = sorted(by_distance[distance])
            wanted_by = (me - distance) * dates + jnp.array(slots, dtype=jnp.int32)
            inside = (wanted_by >= 0) & (wanted_by < total)
            local = jnp.take(annual_of, jnp.clip(wanted_by, 0, total - 1)) - me * dates
            usable = inside & (local >= 0) & (local < dates)
            packed = jnp.take(slc, jnp.clip(local, 0, dates - 1), axis=1)
            packed = jnp.where(usable[None, :, None, None], packed, jnp.zeros_like(packed))
            route = [(i + distance, i) for i in range(devices) if 0 <= i + distance < devices]
            arrived = lax.ppermute(packed, "date", route)
            for n, slot in enumerate(slots):
                part = arrived[:, n]
                sums[slot] = part if sums[slot] is None else sums[slot] + part
    return jnp.stack(sums, axis=1)


def payload_of(images, rim, strip):
    planes, count, rows, cols = images.shape
    edges = jnp.where(strip == 0, rim[..., :HALO], rim[..., TILE - HALO :])
    edges = jnp.transpose(edges, (2, 1, 0, 3)).reshape(rows, count * planes * HALO)
    edges = jnp.pad(edges, ((0, 0), (0, TILE - edges.shape[1])))
    part = rows * TILE // cols
    edges = jnp.transpose(edges.reshape(rows // part, part, TILE), (1, 0, 2)).reshape(part, cols)
    stacked = jnp.transpose(images, (1, 0, 2, 3)).reshape(count * planes * rows, cols)
    return jnp.concatenate([stacked, edges], axis=0)


def body(slc, pair_list, az_half, rng_half):
    planes, dates, rows, cols = slc.shape
    devices = lax.axis_size("date")
    total = dates * devices
    per_date = pair_list.shape[0] // total
    year = min(YEAR, total // 2 - 2)
    half = devices // 2
    late = half * dates - year
    halves = devices % 2 == 0 and 0 < late <= NEAR and 2 * late <= dates
    halves = halves and dates - late <= PER_TILE // 2 and dates <= PER_TILE
    plan = {
        "dates": dates,
        "devices": devices,
        "per_date": per_date,
        "year": year,
        "late": late,
        "rows": rows,
        "cols": cols,
        "pairs": total * per_date,
        "halves": halves,
    }
    dtype = slc.dtype
    rim_rows = rows * TILE // cols
    pairs = pair_list.T
    lists = jnp.concatenate([pairs, az_half[None], rng_half[None]])
    swap_strips = [(0, 1), (1, 0)]

    def images(count):
        return jax.ShapeDtypeStruct((planes, count, rows, cols), dtype)

    def rim_shape(count):
        return jax.ShapeDtypeStruct((planes, count, rows, TILE), dtype)

    def payload_shape(count):
        return jax.ShapeDtypeStruct((planes * count * rows + rim_rows, cols), dtype)

    def swapped_rims(values):
        out = pl.pallas_call(
            rim_kernel,
            out_shape=rim_shape(values.shape[1]),
            in_specs=[ANY],
            out_specs=VMEM,
            scratch_shapes=[pltpu.SemaphoreType.DMA],
            compiler_params=limit(WORK_MIB),
            name="rim_blocks",
        )(values)
        return lax.ppermute(out, "strip", swap_strips)

    def cost(flops):
        return pl.CostEstimate(flops=flops, bytes_accessed=1, transcendentals=0)

    wide = cols // 2
    widths = HALO - REACH_LO + 1
    band_shape = (2, 2 * wide + 2 * TILE, wide)
    bands = pl.pallas_call(
        functools.partial(bands_kernel, cols),
        grid=(widths,),
        out_shape=jax.ShapeDtypeStruct((widths, *band_shape), jnp.bfloat16),
        out_specs=pl.BlockSpec((1, *band_shape), lambda n: (n, 0, 0, 0)),
        compiler_params=limit(WORK_MIB),
        cost_estimate=cost(1),
        name="range_bands",
    )()
    if halves:
        swap = [(i, (i + half) % devices) for i in range(devices)]
        both = ("date", "strip")
        early, packed, strips = pl.pallas_call(
            functools.partial(early_kernel, plan),
            out_shape=(
                images(dates - late),
                jax.ShapeDtypeStruct((2, rows, TILE), dtype),
                jax.ShapeDtypeStruct((rows, TILE), dtype),
            ),
            in_specs=[ANY, SMEM],
            out_specs=(VMEM, VMEM, VMEM),
            scratch_shapes=[
                pltpu.VMEM((planes, dates, rows, TILE), dtype),
                pltpu.SemaphoreType.DMA((dates - late,)),
                pltpu.SemaphoreType.DMA,
            ],
            compiler_params=limit(FIRST_MIB),
            name="early_images",
        )(slc, pairs)
        early = lax.ppermute(early, "date", swap)
        packed = lax.ppermute(packed, "strip", swap_strips)
        inner, outer, rim = pl.pallas_call(
            functools.partial(beside_kernel, plan),
            out_shape=(payload_shape(NEAR), payload_shape(NEAR), rim_shape(dates)),
            in_specs=[ANY, VMEM],
            out_specs=(VMEM, VMEM, VMEM),
            scratch_shapes=[pltpu.SemaphoreType.DMA((2, NEAR, 2))],
            compiler_params=limit(WORK_MIB),
            name="beside_images",
        )(slc, packed)
        down = [(i, (i - 1) % half) for i in range(half)]
        down += [(half + i, half + (i + 1) % half) for i in range(half)]
        strips = lax.ppermute(
            strips, both, [(2 * a + s, 2 * b + 1 - s) for a, b in swap for s in (0, 1)]
        )
        up = [(b, a) for a, b in down if b not in (half - 1, half)]
        middle = lax.ppermute(outer, "date", [(half - 1, half), (half, half - 1)])
        outer = lax.ppermute(outer, "date", up)
        inner = lax.ppermute(inner, "date", down)
    else:
        rim = swapped_rims(slc)
        annual = arrivals_by_distance(slc, pair_list, plan)
        strip = lax.axis_index("strip")
        ups = [(i, i + 1) for i in range(devices - 1)]
        inner = payload_of(slc[:, dates - NEAR :], rim[:, dates - NEAR :], strip)
        outer = payload_of(slc[:, :NEAR], rim[:, :NEAR], strip)
        inner = lax.ppermute(inner, "date", ups)
        outer = lax.ppermute(outer, "date", [(b, a) for a, b in ups])

    out_shape = jax.ShapeDtypeStruct((planes, dates * per_date, rows, cols), jnp.float32)
    depth = 2 * band_shape[1]
    scratch = [
        pltpu.VMEM((2, 4 * rows, depth), jnp.bfloat16),
        pltpu.VMEM((2, 4, 2 * rows, cols), jnp.bfloat16),
        pltpu.VMEM((2, planes, rows, cols), dtype),
        pltpu.VMEM((2, planes, rows, TILE), dtype),
        pltpu.VMEM((2, 2, planes, rows, cols), jnp.float32),
        pltpu.SMEM((dates * NEAR + 1,), jnp.int32),
        pltpu.SemaphoreType.DMA((2, 2)),
    ]

    out, powers = pl.pallas_call(
        functools.partial(own_kernel, plan),
        out_shape=(out_shape, jax.ShapeDtypeStruct((dates, rows, depth), jnp.bfloat16)),
        in_specs=[SMEM] + [VMEM] * 3,
        out_specs=(ANY, VMEM),
        scratch_shapes=scratch,
        compiler_params=limit(WORK_MIB),
        cost_estimate=cost(20_000_000_000),
        name="own_pairs",
    )(lists, slc, rim, bands)

    def more_pairs(kernel, out, others, name):
        return pl.pallas_call(
            functools.partial(kernel, plan),
            out_shape=out_shape,
            in_specs=[SMEM] + [VMEM] * (4 + len(others)) + [ANY],
            out_specs=ANY,
            scratch_shapes=scratch,
            input_output_aliases={5 + len(others): 0},
            compiler_params=limit(WORK_MIB),
            cost_estimate=cost(1),
            name=name,
        )(lists, slc, rim, bands, powers, *others, out)

    if halves:
        payload = sent = pl.pallas_call(
            functools.partial(late_kernel, plan),
            out_shape=payload_shape(late),
            in_specs=[VMEM, VMEM, VMEM, VMEM, SMEM, ANY, ANY],
            out_specs=VMEM,
            scratch_shapes=[pltpu.VMEM((late, planes, rows, TILE), dtype)],
            compiler_params=limit(WORK_MIB),
            name="late_images",
        )(slc, rim, inner, middle, lists, powers, strips)
        late_swap = [(a, b) for a, b in swap if a not in (half - 1, half)]
        late_swap += [(half - 1, 0), (half, devices - 1)]
        payload = lax.ppermute(payload, "date", late_swap)
    if halves:
        early_pairs = functools.partial(annual_kernel, is_late=False)
        out = more_pairs(early_pairs, out, (inner, early, strips, sent), "annual_pairs")
        out = more_pairs(rest_kernel, out, (inner, outer, middle), "near_pairs")
        late_pairs = functools.partial(annual_kernel, is_late=True)
        out = more_pairs(late_pairs, out, (inner, payload, strips, sent), "last_pairs")
    else:
        out = more_pairs(rest_kernel, out, (inner, outer, inner), "near_pairs")
        out = more_pairs(plain_kernel, out, (annual, swapped_rims(annual)), "annual_pairs")
    return out


def solution(mesh):
    placed = (P(None, "date", "groups", "strip"), P(), P(), P())
    return jax.shard_map(
        body,
        mesh=mesh,
        in_specs=placed,
        out_specs=P(None, "date", "groups", "strip"),
        check_vma=False,
    )
```

```python
import functools

import jax
import jax.numpy as jnp
from jax import lax
from jax.experimental import pallas as pl
from jax.experimental.pallas import tpu as pltpu
from jax.sharding import PartitionSpec as P

HALO = 16
REACH_LO = 12
NEAR = 3
YEAR = 29
EPSILON = 1e-06
TILE = 128
INNER = TILE // 2
PER_TILE = TILE // HALO
PARTNER, HEIGHT, REACH = 1, 2, 3
WORK_MIB = 16
FIRST_MIB = 56
ANY = pl.BlockSpec(memory_space=pl.ANY)
SMEM = pl.BlockSpec(memory_space=pltpu.SMEM)
VMEM = pl.BlockSpec(memory_space=pltpu.VMEM)


def limit(mebibytes):
    return pltpu.CompilerParams(vmem_limit_bytes=mebibytes * 1024 * 1024)


def run_copies(copies):
    for copy in copies:
        copy.start()
    for copy in copies:
        copy.wait()


def gather_strips(tiles, side):
    lane = lax.broadcasted_iota(jnp.int32, tiles[0].shape, 1)
    packed = jnp.zeros(tiles[0].shape, jnp.float32)
    for n, tile in enumerate(tiles):
        spot = n * HALO
        moved = pltpu.roll(tile.astype(jnp.float32), spot + side * HALO, 1)
        packed = jnp.where((lane >= spot) & (lane < spot + HALO), moved, packed)
    return packed.astype(jnp.bfloat16)


def place_strip(packed, n, side):
    shift = 2 * TILE - (n + side) * HALO
    return pltpu.roll(packed.astype(jnp.float32), lax.rem(shift, TILE), 1).astype(jnp.bfloat16)


def write_strips(out_ref, packed):
    rows, cols = packed.shape[0], out_ref.shape[1]
    part = rows * TILE // cols
    base = out_ref.shape[0] - part
    for n in range(rows // part):
        out_ref[base:, n * TILE : (n + 1) * TILE] = packed[n * part : (n + 1) * part]


def read_strips(ref, rows):
    cols = ref.shape[1]
    base = ref.shape[0] - rows * TILE // cols
    return jnp.concatenate(
        [ref[base:, n * TILE : (n + 1) * TILE] for n in range(cols // TILE)], axis=0
    )


def wanted_images(plan, pairs_ref):
    me = lax.axis_index("date")
    dates, half = plan["dates"], plan["devices"] // 2
    mate = lax.rem(me + half, 2 * half)
    wanted = []
    for k in range(dates - plan["late"]):
        date = mate * dates + jnp.where(mate < half, plan["late"], 0) + k
        at = pairs_ref[PARTNER, date * plan["per_date"] + NEAR] - me * dates
        wanted.append(jnp.clip(at, 0, dates - 1))
    return wanted


def image_copies(slc_ref, wanted, early_ref, sems):
    return [
        pltpu.make_async_copy(slc_ref.at[:, at], early_ref.at[:, k], sems.at[k])
        for k, at in enumerate(wanted)
    ]


def gather_all(tiles, side):
    return [gather_strips(tiles[n * PER_TILE : (n + 1) * PER_TILE], side) for n in range(2)]


def early_kernel(plan, slc_ref, pairs_ref, early_ref, middle_ref, packed_ref, strips_ref,
                 tiles_ref, sems, middle_sem, tile_sem):
    strip, cols = lax.axis_index("strip"), plan["cols"]
    start = pl.multiple_of(jnp.where(strip == 0, cols - TILE, 0), TILE)
    wanted = wanted_images(plan, pairs_ref)
    tile_copy = pltpu.make_async_copy(
        slc_ref.at[:, :, :, pl.ds(start, TILE)], tiles_ref, tile_sem
    )
    early_copies = image_copies(slc_ref, wanted, early_ref, sems)
    for copy in [tile_copy] + early_copies:
        copy.start()
    me, half = lax.axis_index("date"), plan["devices"] // 2
    first = jnp.where(me < half, plan["dates"] - NEAR, 0)
    middle_copy = pltpu.make_async_copy(
        slc_ref.at[:, pl.ds(first, NEAR)], middle_ref, middle_sem
    )
    in_middle = (me == half) | (me == half - 1)
    pl.when(in_middle)(lambda: middle_copy.start())
    tile_copy.wait()
    tiles = [tiles_ref[c, k] for k in range(plan["dates"]) for c in range(2)]
    for n, packed in enumerate(gather_all(tiles, 1 - strip)):
        packed_ref[n] = packed
    tiles = [tiles_ref[c, at] for at in wanted for c in range(2)]
    strips_ref[...] = gather_strips(tiles, 1 - strip)
    for copy in early_copies:
        copy.wait()
    pl.when(in_middle)(lambda: middle_copy.wait())


def rim_kernel(slc_ref, rim_ref, sem):
    cols = slc_ref.shape[3]
    start = pl.multiple_of(jnp.where(lax.axis_index("strip") == 0, cols - TILE, 0), TILE)
    run_copies([pltpu.make_async_copy(slc_ref.at[:, :, :, pl.ds(start, TILE)], rim_ref, sem)])


def beside_kernel(plan, slc_ref, packed_ref, inner_ref, outer_ref, rim_ref, edges_ref, sems):
    me, strip = lax.axis_index("date"), lax.axis_index("strip")
    dates, rows = plan["dates"], plan["rows"]
    upper = me >= plan["devices"] // 2
    last = dates - NEAR
    copies = []
    firsts = (jnp.where(upper, last, 0), jnp.where(upper, 0, last))
    for r, (out_ref, first) in enumerate(zip((inner_ref, outer_ref), firsts)):
        for k in range(NEAR):
            for c in range(2):
                here = out_ref.at[pl.ds((2 * k + c) * rows, rows)]
                copies.append(
                    pltpu.make_async_copy(slc_ref.at[c, first + k], here, sems.at[r, k, c])
                )
    for copy in copies:
        copy.start()
    for k in range(dates):
        for c in range(2):
            tile, n = divmod(2 * k + c, PER_TILE)
            rim_ref[c, k] = place_strip(packed_ref[tile], n, strip)
    for out_ref, first in zip((inner_ref, outer_ref), firsts):
        tiles = [rim_ref[c, first + k] for k in range(NEAR) for c in range(2)]
        edges_ref[...] = gather_strips(tiles, strip)
        write_strips(out_ref, edges_ref[...])
    for copy in copies:
        copy.wait()


def late_kernel(plan, slc_ref, rim_ref, inner_ref, middle_ref, edges_ref, pairs_ref, *refs):
    late_ref, tiles_ref = refs[-2:]
    me, strip = lax.axis_index("date"), lax.axis_index("strip")
    dates, late, rows = plan["dates"], plan["late"], plan["rows"]
    half = plan["devices"] // 2
    mate = lax.rem(me + half, 2 * half)
    mate = jnp.where(me == half - 1, 0, jnp.where(me == half, 2 * half - 1, mate))
    mate_slot = jnp.where(mate < half, 0, dates - late)
    in_middle = (me == half) | (me == half - 1)
    for k in range(late):
        date = mate * dates + mate_slot + k
        wanted = pairs_ref[PARTNER, date * plan["per_date"] + NEAR] - me * dates
        own = (wanted >= 0) & (wanted < dates)
        own_at = jnp.clip(wanted, 0, dates - 1)
        other_at = jnp.clip(jnp.where(me < half, wanted - dates, wanted + NEAR), 0, NEAR - 1)
        for c in range(2):
            here = pl.ds((2 * k + c) * rows, rows)

            @pl.when(own)
            def _():
                late_ref[here] = slc_ref[c, own_at]
                tiles_ref[k, c] = rim_ref[c, own_at]

            @pl.when(jnp.logical_not(own | in_middle))
            def _():
                there = pl.multiple_of((2 * other_at + c) * rows, rows)
                late_ref[here] = inner_ref[pl.ds(there, rows)]
                packed = read_strips(inner_ref, rows)
                tiles_ref[k, c] = place_strip(packed, 2 * other_at + c, strip)

            @pl.when(jnp.logical_not(own) & in_middle)
            def _():
                late_ref[here] = middle_ref[c, other_at]
                tiles_ref[k, c] = place_strip(edges_ref[...], 2 * other_at + c, strip)

    tiles = [tiles_ref[k, c] for k in range(late) for c in range(2)]
    write_strips(late_ref, gather_strips(tiles, strip))


def bands_kernel(cols, out_ref):
    strip = lax.axis_index("strip")
    wide = out_ref.shape[3]
    reach = pl.program_id(0) + REACH_LO

    def band(places, targets):
        return (jnp.abs(places - targets) <= reach).astype(jnp.float32).astype(jnp.bfloat16)

    def indices(shape):
        return lax.broadcasted_iota(jnp.int32, shape, 0), lax.broadcasted_iota(jnp.int32, shape, 1)

    inside = band(*indices((wide, wide)))
    row, col = indices((TILE, wide))
    beyond = jnp.where(strip == 0, cols + row, row - TILE)
    first = band(jnp.where(row < INNER, wide + row, beyond), col)
    second = band(jnp.where(row < INNER, beyond, wide - TILE + row), col + wide)
    for n, part in enumerate((first, second)):
        out_ref[0, n, 0:wide] = inside
        out_ref[0, n, wide : 2 * wide] = inside
        out_ref[0, n, 2 * wide : 2 * wide + TILE] = part
        out_ref[0, n, 2 * wide + TILE : 2 * wide + 2 * TILE] = part


def split(values):
    high = values.astype(jnp.bfloat16)
    low = (values - high.astype(jnp.float32)).astype(jnp.bfloat16)
    return high, low


def put(ref, here, t, values):
    wide = 2 * TILE
    depth = 2 * wide + 2 * TILE
    for low, part in enumerate(split(values)):
        side = [n * depth + 2 * wide + low * TILE for n in range(2)]
        if t < 4:
            at = (t // 2) * depth + low * wide + (t % 2) * TILE
            ref[*here, at : at + TILE] = part
        if t == 2:
            ref[*here, side[0] : side[0] + INNER] = part[:, :INNER]
        if t == 1:
            ref[*here, side[1] + INNER : side[1] + TILE] = part[:, INNER:]
        if t == 4:
            ref[*here, side[0] + INNER : side[0] + TILE] = part[:, INNER:]
            ref[*here, side[1] : side[1] + INNER] = part[:, :INNER]


def tile_of(main, rim, t):
    return [
        (rim(c) if t == 4 else main(c, slice(t * TILE, (t + 1) * TILE))).astype(jnp.float32)
        for c in range(2)
    ]


class Pairs:
    def __init__(self, plan, lists, slc_ref, rim_ref, bands_ref, powers_ref, out_ref, scratch):
        self.plan = plan
        self.lists = lists
        self.slc_ref, self.rim_ref = slc_ref, rim_ref
        self.bands_ref, self.powers_ref, self.out_ref = bands_ref, powers_ref, out_ref
        (self.left_ref, self.stack_ref, self.other_ref, self.other_rim_ref, self.stage_ref,
         self.list_ref, self.sems) = scratch
        self.me, self.strip = lax.axis_index("date"), lax.axis_index("strip")

    def partner(self, pair):
        return self.lists[PARTNER, pair]

    def near_item(self, n):
        slot, kind = n // NEAR, lax.rem(n, NEAR)
        dates = self.plan["dates"]
        pair = (self.me * dates + slot) * self.plan["per_date"] + kind
        return slot, kind, self.partner(pair) - self.me * dates

    def near_list(self, chosen):
        count = 0
        for n in range(self.plan["dates"] * NEAR):
            self.list_ref[count] = n
            count = count + jnp.where(chosen(self.near_item(n)[2]), 1, 0)
        return count

    def own(self, local):
        return (local >= 0) & (local < self.plan["dates"])

    def in_middle(self, local):
        half, dates = self.plan["devices"] // 2, self.plan["dates"]
        if not self.plan["halves"]:
            return False
        return ((self.me == half) & (local < 0)) | ((self.me == half - 1) & (local >= dates))

    def own_other(self, index):
        return (
            lambda c, cols: self.slc_ref[c, index, :, cols],
            lambda c: self.rim_ref[c, index],
        )

    def fetched_other(self, x):
        return (
            lambda c, cols: self.other_ref[x, c, :, cols],
            lambda c: self.other_rim_ref[x, c],
        )

    def fetch_payload(self, x, ref, index):
        rows = self.plan["rows"]
        packed = read_strips(ref, rows)
        for c in range(2):
            at = pl.multiple_of((2 * index + c) * rows, rows)
            self.other_ref[x, c] = ref[pl.ds(at, rows)]
            self.other_rim_ref[x, c] = place_strip(packed, 2 * index + c, self.strip)

    def fetch_images(self, x, ref, packed_ref, index):
        packed = packed_ref[...]
        for c in range(2):
            self.other_ref[x, c] = ref[c, index]
            self.other_rim_ref[x, c] = place_strip(packed, 2 * index + c, self.strip)

    def out_copy(self, stage, x, pair):
        return pltpu.make_async_copy(
            self.stage_ref.at[stage, x], self.out_ref.at[:, pair], self.sems.at[stage, x]
        )

    def run(self, count, work):
        steps = (count + 1) // 2

        def step(n, carry):
            stage = lax.rem(n, 2)

            @pl.when(n >= 2)
            def _():
                for x in range(2):
                    self.out_copy(stage, x, 0).wait()

            items = [work(x, jnp.minimum(2 * n + x, count - 1)) for x in range(2)]
            self.compute(stage, items)
            for x, (slot, kind, _, _) in enumerate(items):
                copy = self.out_copy(stage, x, slot * self.plan["per_date"] + kind)
                pl.when(2 * n + x < count)(copy.start)
            return carry

        lax.fori_loop(0, steps, step, 0)
        for back in (2, 1):
            for x in range(2):
                used = (steps >= back) & (2 * (steps - back) + x < count)
                pl.when(used)(self.out_copy(lax.rem(steps + back, 2), x, 0).wait)

    def compute(self, stage, items):
        plan = self.plan
        rows, dates, per_date = plan["rows"], plan["dates"], plan["per_date"]
        part = [(pl.ds(f * rows, rows),) for f in range(4)]
        depth = self.bands_ref.shape[2]
        wide = self.bands_ref.shape[3]
        heights, widths = [], []
        for slot, kind, _, _ in items:
            pair = (self.me * dates + slot) * per_date + kind
            heights.append(self.lists[HEIGHT, pair])
            widths.append(jnp.clip(self.lists[REACH, pair] - REACH_LO, 0, HALO - REACH_LO))
        for x, (slot, kind, other, other_power) in enumerate(items):
            left_ref = self.left_ref.at[x]
            left_ref[*part[2]] = self.powers_ref[slot]
            if other_power is not None:
                left_ref[*part[3]] = self.powers_ref[other_power]
            first = self.own_other(slot)
            for t in range(5):
                a_real, a_imag = tile_of(*first, t)
                b_real, b_imag = tile_of(*other, t)
                put(left_ref, part[0], t, a_real * b_real + a_imag * b_imag)
                put(left_ref, part[1], t, a_imag * b_real - a_real * b_imag)
                if other_power is None:
                    put(left_ref, part[3], t, b_real * b_real + b_imag * b_imag)
        for n in range(2):
            for x in range(2):
                ranged = jnp.dot(
                    self.left_ref[x, :, n * depth : (n + 1) * depth],
                    self.bands_ref[widths[x], n],
                    preferred_element_type=jnp.float32,
                )
                there = slice(n * wide, (n + 1) * wide)
                for low, values in enumerate(split(ranged)):
                    for f in range(4):
                        self.stack_ref[x, f, low * rows : (low + 1) * rows, there] = values[
                            f * rows : (f + 1) * rows
                        ]
        row = lax.broadcasted_iota(jnp.int32, (rows, 2 * rows), 0)
        col = lax.broadcasted_iota(jnp.int32, (rows, 2 * rows), 1)
        col = jnp.where(col < rows, col, col - rows)
        for x in range(2):
            band = (jnp.abs(row - col) <= heights[x]).astype(jnp.float32).astype(jnp.bfloat16)
            looked = [
                jnp.dot(band, self.stack_ref[x, f], preferred_element_type=jnp.float32)
                for f in range(4)
            ]
            inverse = lax.rsqrt(looked[2] * looked[3] + EPSILON)
            for c in range(2):
                self.stage_ref[stage, x, c] = looked[c] * inverse


def own_kernel(plan, lists, slc_ref, rim_ref, bands_ref, out_ref, powers_ref, *scratch):
    pairs = Pairs(plan, lists, slc_ref, rim_ref, bands_ref, powers_ref, out_ref, scratch)
    dates = plan["dates"]

    def power(slot, carry):
        for t in range(5):
            real, imag = tile_of(*pairs.own_other(slot), t)
            put(powers_ref, (slot, slice(None)), t, real * real + imag * imag)
        return carry

    lax.fori_loop(0, dates, power, 0)

    def work(x, n):
        slot, kind, local = pairs.near_item(pairs.list_ref[n])
        return slot, kind, pairs.own_other(local), local

    pairs.run(pairs.near_list(pairs.own), work)


def rest_kernel(plan, lists, slc_ref, rim_ref, bands_ref, powers_ref, inner_ref, outer_ref,
                middle_ref, edges_ref, _, out_ref, *scratch):
    pairs = Pairs(plan, lists, slc_ref, rim_ref, bands_ref, powers_ref, out_ref, scratch)
    dates = plan["dates"]
    upper = pairs.me >= plan["devices"] // 2 if plan["halves"] else True

    def work(x, n):
        slot, kind, local = pairs.near_item(pairs.list_ref[n])
        below = local < 0
        index = jnp.clip(jnp.where(below, local + NEAR, local - dates), 0, NEAR - 1)
        inner, middle = below == upper, pairs.in_middle(local)
        fetch = pairs.fetch_payload
        pl.when(jnp.logical_not(inner))(lambda: fetch(x, outer_ref, index))
        pl.when(inner & jnp.logical_not(middle))(lambda: fetch(x, inner_ref, index))
        pl.when(inner & middle)(lambda: pairs.fetch_images(x, middle_ref, edges_ref, index))
        return slot, kind, pairs.fetched_other(x), None

    pairs.run(pairs.near_list(lambda local: jnp.logical_not(pairs.own(local))), work)


def annual_kernel(plan, lists, slc_ref, rim_ref, bands_ref, powers_ref, ring_ref,
                  images_ref, strips_ref, _sent, _, out_ref, *scratch, is_late):
    pairs = Pairs(plan, lists, slc_ref, rim_ref, bands_ref, powers_ref, out_ref, scratch)
    dates, late = plan["dates"], plan["late"]
    half = plan["devices"] // 2
    me, split_date = pairs.me, half * dates
    lower = me < half
    if is_late:
        base, count = jnp.where(lower, 0, dates - late), late
    else:
        base, count = jnp.where(lower, late, 0), dates - late

    def work(x, k):
        slot = base + k
        date = me * dates + slot
        other = pairs.partner(date * plan["per_date"] + NEAR)
        if is_late:
            pairs.fetch_payload(x, images_ref, k)
        else:
            far = (other < split_date) == lower
            ring_at = jnp.where(lower, other, other - (2 * split_date - NEAR))
            ring_at = jnp.clip(ring_at, 0, NEAR - 1)
            pl.when(far)(lambda: pairs.fetch_payload(x, ring_ref, ring_at))
            pl.when(jnp.logical_not(far))(lambda: pairs.fetch_images(x, images_ref, strips_ref, k))
        return slot, NEAR, pairs.fetched_other(x), None

    pairs.run(count, work)


def plain_kernel(plan, lists, slc_ref, rim_ref, bands_ref, powers_ref, images_ref,
                 image_rim_ref, _, out_ref, *scratch):
    pairs = Pairs(plan, lists, slc_ref, rim_ref, bands_ref, powers_ref, out_ref, scratch)

    def work(x, slot):
        other = (
            lambda c, cols: images_ref[c, slot, :, cols],
            lambda c: image_rim_ref[c, slot],
        )
        return slot, NEAR, other, None

    pairs.run(plan["dates"], work)


def arrivals_by_distance(slc, pair_list, plan):
    dates, per_date, devices = plan["dates"], plan["per_date"], plan["devices"]
    total = dates * devices
    me = lax.axis_index("date")
    annual_of = pair_list[:, 1].reshape(total, per_date)[:, per_date - 1]
    sums = [None] * dates
    for direction in (1, -1):
        by_distance = {}
        for slot in range(dates):
            for gap in range(plan["year"], plan["year"] + 3):
                distance = (slot + direction * gap) // dates
                by_distance.setdefault(distance, set()).add(slot)
        for distance in sorted(by_distance):
            slots = sorted(by_distance[distance])
            wanted_by = (me - distance) * dates + jnp.array(slots, dtype=jnp.int32)
            inside = (wanted_by >= 0) & (wanted_by < total)
            local = jnp.take(annual_of, jnp.clip(wanted_by, 0, total - 1)) - me * dates
            usable = inside & (local >= 0) & (local < dates)
            packed = jnp.take(slc, jnp.clip(local, 0, dates - 1), axis=1)
            packed = jnp.where(usable[None, :, None, None], packed, jnp.zeros_like(packed))
            route = [(i + distance, i) for i in range(devices) if 0 <= i + distance < devices]
            arrived = lax.ppermute(packed, "date", route)
            for n, slot in enumerate(slots):
                part = arrived[:, n]
                sums[slot] = part if sums[slot] is None else sums[slot] + part
    return jnp.stack(sums, axis=1)


def payload_of(images, rim, strip):
    planes, count, rows, cols = images.shape
    edges = jnp.where(strip == 0, rim[..., :HALO], rim[..., TILE - HALO :])
    edges = jnp.transpose(edges, (2, 1, 0, 3)).reshape(rows, count * planes * HALO)
    edges = jnp.pad(edges, ((0, 0), (0, TILE - edges.shape[1])))
    part = rows * TILE // cols
    edges = jnp.transpose(edges.reshape(rows // part, part, TILE), (1, 0, 2)).reshape(part, cols)
    stacked = jnp.transpose(images, (1, 0, 2, 3)).reshape(count * planes * rows, cols)
    return jnp.concatenate([stacked, edges], axis=0)


def body(slc, pair_list, az_half, rng_half):
    planes, dates, rows, cols = slc.shape
    devices = lax.axis_size("date")
    total = dates * devices
    per_date = pair_list.shape[0] // total
    year = min(YEAR, total // 2 - 2)
    half = devices // 2
    late = half * dates - year
    halves = devices % 2 == 0 and 0 < late <= NEAR and 2 * late <= dates
    halves = halves and dates - late <= PER_TILE // 2 and dates <= PER_TILE
    plan = {
        "dates": dates,
        "devices": devices,
        "per_date": per_date,
        "year": year,
        "late": late,
        "rows": rows,
        "cols": cols,
        "pairs": total * per_date,
        "halves": halves,
    }
    dtype = slc.dtype
    rim_rows = rows * TILE // cols
    pairs = pair_list.T
    lists = jnp.concatenate([pairs, az_half[None], rng_half[None]])
    swap_strips = [(0, 1), (1, 0)]

    def images(count):
        return jax.ShapeDtypeStruct((planes, count, rows, cols), dtype)

    def rim_shape(count):
        return jax.ShapeDtypeStruct((planes, count, rows, TILE), dtype)

    def payload_shape(count):
        return jax.ShapeDtypeStruct((planes * count * rows + rim_rows, cols), dtype)

    def swapped_rims(values):
        out = pl.pallas_call(
            rim_kernel,
            out_shape=rim_shape(values.shape[1]),
            in_specs=[ANY],
            out_specs=VMEM,
            scratch_shapes=[pltpu.SemaphoreType.DMA],
            compiler_params=limit(WORK_MIB),
            name="rim_blocks",
        )(values)
        return lax.ppermute(out, "strip", swap_strips)

    def cost(flops):
        return pl.CostEstimate(flops=flops, bytes_accessed=1, transcendentals=0)

    wide = cols // 2
    widths = HALO - REACH_LO + 1
    band_shape = (2, 2 * wide + 2 * TILE, wide)
    bands = pl.pallas_call(
        functools.partial(bands_kernel, cols),
        grid=(widths,),
        out_shape=jax.ShapeDtypeStruct((widths, *band_shape), jnp.bfloat16),
        out_specs=pl.BlockSpec((1, *band_shape), lambda n: (n, 0, 0, 0)),
        compiler_params=limit(WORK_MIB),
        cost_estimate=cost(1),
        name="range_bands",
    )()
    if halves:
        swap = [(i, (i + half) % devices) for i in range(devices)]
        both = ("date", "strip")
        early, middle, packed, strips = pl.pallas_call(
            functools.partial(early_kernel, plan),
            out_shape=(
                images(dates - late),
                images(NEAR),
                jax.ShapeDtypeStruct((2, rows, TILE), dtype),
                jax.ShapeDtypeStruct((rows, TILE), dtype),
            ),
            in_specs=[ANY, SMEM],
            out_specs=(VMEM, VMEM, VMEM, VMEM),
            scratch_shapes=[
                pltpu.VMEM((planes, dates, rows, TILE), dtype),
                pltpu.SemaphoreType.DMA((dates - late,)),
                pltpu.SemaphoreType.DMA,
                pltpu.SemaphoreType.DMA,
            ],
            compiler_params=limit(FIRST_MIB),
            name="early_images",
        )(slc, pairs)
        early = lax.ppermute(early, "date", swap)
        packed = lax.ppermute(packed, "strip", swap_strips)
        inner, outer, rim, edges = pl.pallas_call(
            functools.partial(beside_kernel, plan),
            out_shape=(
                payload_shape(NEAR),
                payload_shape(NEAR),
                rim_shape(dates),
                jax.ShapeDtypeStruct((rows, TILE), dtype),
            ),
            in_specs=[ANY, VMEM],
            out_specs=(VMEM, VMEM, VMEM, VMEM),
            scratch_shapes=[pltpu.SemaphoreType.DMA((2, NEAR, 2))],
            compiler_params=limit(WORK_MIB),
            name="beside_images",
        )(slc, packed)
        down = [(i, (i - 1) % half) for i in range(half)]
        down += [(half + i, half + (i + 1) % half) for i in range(half)]
        strips = lax.ppermute(
            strips, both, [(2 * a + s, 2 * b + 1 - s) for a, b in swap for s in (0, 1)]
        )
        up = [(b, a) for a, b in down if b not in (half - 1, half)]
        across = [(half - 1, half), (half, half - 1)]
        middle = lax.ppermute(middle, "date", across)
        edges = lax.ppermute(edges, "date", across)
        outer = lax.ppermute(outer, "date", up)
        inner = lax.ppermute(inner, "date", down)
    else:
        rim = swapped_rims(slc)
        annual = arrivals_by_distance(slc, pair_list, plan)
        strip = lax.axis_index("strip")
        ups = [(i, i + 1) for i in range(devices - 1)]
        inner = payload_of(slc[:, dates - NEAR :], rim[:, dates - NEAR :], strip)
        outer = payload_of(slc[:, :NEAR], rim[:, :NEAR], strip)
        inner = lax.ppermute(inner, "date", ups)
        outer = lax.ppermute(outer, "date", [(b, a) for a, b in ups])

    out_shape = jax.ShapeDtypeStruct((planes, dates * per_date, rows, cols), jnp.float32)
    depth = 2 * band_shape[1]
    scratch = [
        pltpu.VMEM((2, 4 * rows, depth), jnp.bfloat16),
        pltpu.VMEM((2, 4, 2 * rows, cols), jnp.bfloat16),
        pltpu.VMEM((2, planes, rows, cols), dtype),
        pltpu.VMEM((2, planes, rows, TILE), dtype),
        pltpu.VMEM((2, 2, planes, rows, cols), jnp.float32),
        pltpu.SMEM((dates * NEAR + 1,), jnp.int32),
        pltpu.SemaphoreType.DMA((2, 2)),
    ]

    out, powers = pl.pallas_call(
        functools.partial(own_kernel, plan),
        out_shape=(out_shape, jax.ShapeDtypeStruct((dates, rows, depth), jnp.bfloat16)),
        in_specs=[SMEM] + [VMEM] * 3,
        out_specs=(ANY, VMEM),
        scratch_shapes=scratch,
        compiler_params=limit(WORK_MIB),
        cost_estimate=cost(20_000_000_000),
        name="own_pairs",
    )(lists, slc, rim, bands)

    def more_pairs(kernel, out, others, name):
        return pl.pallas_call(
            functools.partial(kernel, plan),
            out_shape=out_shape,
            in_specs=[SMEM] + [VMEM] * (4 + len(others)) + [ANY],
            out_specs=ANY,
            scratch_shapes=scratch,
            input_output_aliases={5 + len(others): 0},
            compiler_params=limit(WORK_MIB),
            cost_estimate=cost(1),
            name=name,
        )(lists, slc, rim, bands, powers, *others, out)

    if halves:
        payload = sent = pl.pallas_call(
            functools.partial(late_kernel, plan),
            out_shape=payload_shape(late),
            in_specs=[VMEM] * 5 + [SMEM, ANY, ANY],
            out_specs=VMEM,
            scratch_shapes=[pltpu.VMEM((late, planes, rows, TILE), dtype)],
            compiler_params=limit(WORK_MIB),
            name="late_images",
        )(slc, rim, inner, middle, edges, lists, powers, strips)
        late_swap = [(a, b) for a, b in swap if a not in (half - 1, half)]
        late_swap += [(half - 1, 0), (half, devices - 1)]
        payload = lax.ppermute(payload, "date", late_swap)
    if halves:
        early_pairs = functools.partial(annual_kernel, is_late=False)
        out = more_pairs(early_pairs, out, (inner, early, strips, sent), "annual_pairs")
        out = more_pairs(rest_kernel, out, (inner, outer, middle, edges), "near_pairs")
        late_pairs = functools.partial(annual_kernel, is_late=True)
        out = more_pairs(late_pairs, out, (inner, payload, strips, sent), "last_pairs")
    else:
        out = more_pairs(rest_kernel, out, (inner, outer, annual, rim[0, 0]), "near_pairs")
        out = more_pairs(plain_kernel, out, (annual, swapped_rims(annual)), "annual_pairs")
    return out


def solution(mesh):
    placed = (P(None, "date", "groups", "strip"), P(), P(), P())
    return jax.shard_map(
        body,
        mesh=mesh,
        in_specs=placed,
        out_specs=P(None, "date", "groups", "strip"),
        check_vma=False,
    )
```

```python
import functools

import jax
import jax.numpy as jnp
from jax import lax
from jax.experimental import pallas as pl
from jax.experimental.pallas import tpu as pltpu
from jax.sharding import PartitionSpec as P

HALO = 16
REACH_LO = 12
NEAR = 3
YEAR = 29
EPSILON = 1e-06
TILE = 128
INNER = TILE // 2
OWN_FLOPS = 4_000_000_000
ANNUAL_FLOPS = 8_000_000_000
PARTNER, HEIGHT, REACH = 1, 2, 3
WORK_MIB = 16
FIRST_MIB = 56
ANY = pl.BlockSpec(memory_space=pl.ANY)
SMEM = pl.BlockSpec(memory_space=pltpu.SMEM)
VMEM = pl.BlockSpec(memory_space=pltpu.VMEM)


def limit(mebibytes):
    return pltpu.CompilerParams(vmem_limit_bytes=mebibytes * 1024 * 1024)


def run_copies(copies):
    for copy in copies:
        copy.start()
    for copy in copies:
        copy.wait()


def gather_strips(tiles, side):
    lane = lax.broadcasted_iota(jnp.int32, tiles[0].shape, 1)
    packed = jnp.zeros(tiles[0].shape, jnp.float32)
    for n, tile in enumerate(tiles):
        spot = n * HALO
        moved = pltpu.roll(tile.astype(jnp.float32), spot + side * HALO, 1)
        packed = jnp.where((lane >= spot) & (lane < spot + HALO), moved, packed)
    return packed.astype(jnp.bfloat16)


def place_strip(packed, n, side):
    shift = 2 * TILE - (n + side) * HALO
    return pltpu.roll(packed.astype(jnp.float32), lax.rem(shift, TILE), 1).astype(jnp.bfloat16)


def write_strips(out_ref, packed):
    rows, cols = packed.shape[0], out_ref.shape[1]
    part = rows * TILE // cols
    base = out_ref.shape[0] - part
    for n in range(rows // part):
        out_ref[base:, n * TILE : (n + 1) * TILE] = packed[n * part : (n + 1) * part]


def read_strips(ref, rows):
    cols = ref.shape[1]
    base = ref.shape[0] - rows * TILE // cols
    return jnp.concatenate(
        [ref[base:, n * TILE : (n + 1) * TILE] for n in range(cols // TILE)], axis=0
    )


def wanted_images(plan, pairs_ref):
    me = lax.axis_index("date")
    dates, half = plan["dates"], plan["devices"] // 2
    mate = lax.rem(me + half, 2 * half)
    wanted = []
    for k in range(dates - plan["late"]):
        date = mate * dates + jnp.where(mate < half, plan["late"], 0) + k
        at = pairs_ref[PARTNER, date * plan["per_date"] + NEAR] - me * dates
        wanted.append(jnp.clip(at, 0, dates - 1))
    return wanted


def image_copies(slc_ref, wanted, early_ref, sems):
    return [
        pltpu.make_async_copy(slc_ref.at[:, at], early_ref.at[:, k], sems.at[k])
        for k, at in enumerate(wanted)
    ]


def early_kernel(plan, slc_ref, pairs_ref, early_ref, rim_ref, strips_ref, tiles_ref, sems,
                 tile_sems, rim_sem):
    strip, cols = lax.axis_index("strip"), plan["cols"]
    start = pl.multiple_of(jnp.where(strip == 0, cols - TILE, 0), TILE)
    wanted = wanted_images(plan, pairs_ref)
    rim_copy = pltpu.make_async_copy(slc_ref.at[:, :, :, pl.ds(start, TILE)], rim_ref, rim_sem)
    early_copies = image_copies(slc_ref, wanted, early_ref, sems)
    tile_copies = [
        pltpu.make_async_copy(
            slc_ref.at[:, at, :, pl.ds(start, TILE)], tiles_ref.at[k], tile_sems.at[k]
        )
        for k, at in enumerate(wanted)
    ]
    for copy in tile_copies + [rim_copy] + early_copies:
        copy.start()
    for copy in tile_copies:
        copy.wait()
    tiles = [tiles_ref[k, c] for k in range(len(wanted)) for c in range(2)]
    strips_ref[...] = gather_strips(tiles, 1 - strip)
    for copy in [rim_copy] + early_copies:
        copy.wait()


def rim_kernel(slc_ref, rim_ref, sem):
    cols = slc_ref.shape[3]
    start = pl.multiple_of(jnp.where(lax.axis_index("strip") == 0, cols - TILE, 0), TILE)
    run_copies([pltpu.make_async_copy(slc_ref.at[:, :, :, pl.ds(start, TILE)], rim_ref, sem)])


def beside_kernel(plan, slc_ref, rim_ref, inner_ref, outer_ref, sems):
    me, strip = lax.axis_index("date"), lax.axis_index("strip")
    dates, rows = plan["dates"], plan["rows"]
    upper = me >= plan["devices"] // 2
    last = dates - NEAR
    copies = []
    firsts = (jnp.where(upper, last, 0), jnp.where(upper, 0, last))
    for r, (out_ref, first) in enumerate(zip((inner_ref, outer_ref), firsts)):
        for k in range(NEAR):
            for c in range(2):
                here = out_ref.at[pl.ds((2 * k + c) * rows, rows)]
                copies.append(
                    pltpu.make_async_copy(slc_ref.at[c, first + k], here, sems.at[r, k, c])
                )
    for copy in copies:
        copy.start()
    for out_ref, first in zip((inner_ref, outer_ref), firsts):
        tiles = [rim_ref[c, first + k] for k in range(NEAR) for c in range(2)]
        write_strips(out_ref, gather_strips(tiles, strip))
    for copy in copies:
        copy.wait()


def late_kernel(plan, slc_ref, rim_ref, inner_ref, pairs_ref, *refs):
    late_ref, tiles_ref = refs[-2:]
    me, strip = lax.axis_index("date"), lax.axis_index("strip")
    dates, late, rows = plan["dates"], plan["late"], plan["rows"]
    half = plan["devices"] // 2
    mate = lax.rem(me + half, 2 * half)
    mate_slot = jnp.where(mate < half, 0, dates - late)
    packed = read_strips(inner_ref, rows)
    for k in range(late):
        date = mate * dates + mate_slot + k
        wanted = pairs_ref[PARTNER, date * plan["per_date"] + NEAR] - me * dates
        own = (wanted >= 0) & (wanted < dates)
        own_at = jnp.clip(wanted, 0, dates - 1)
        other_at = jnp.clip(jnp.where(me < half, wanted - dates, wanted + NEAR), 0, NEAR - 1)
        for c in range(2):
            here = pl.ds((2 * k + c) * rows, rows)

            @pl.when(own)
            def _():
                late_ref[here] = slc_ref[c, own_at]
                tiles_ref[k, c] = rim_ref[c, own_at]

            @pl.when(jnp.logical_not(own))
            def _():
                there = pl.multiple_of((2 * other_at + c) * rows, rows)
                late_ref[here] = inner_ref[pl.ds(there, rows)]
                tiles_ref[k, c] = place_strip(packed, 2 * other_at + c, strip)

    tiles = [tiles_ref[k, c] for k in range(late) for c in range(2)]
    write_strips(late_ref, gather_strips(tiles, strip))


def bands_kernel(cols, out_ref):
    strip = lax.axis_index("strip")
    wide = out_ref.shape[3]
    reach = pl.program_id(0) + REACH_LO

    def band(places, targets):
        return (jnp.abs(places - targets) <= reach).astype(jnp.float32).astype(jnp.bfloat16)

    def indices(shape):
        return lax.broadcasted_iota(jnp.int32, shape, 0), lax.broadcasted_iota(jnp.int32, shape, 1)

    inside = band(*indices((wide, wide)))
    row, col = indices((TILE, wide))
    beyond = jnp.where(strip == 0, cols + row, row - TILE)
    first = band(jnp.where(row < INNER, wide + row, beyond), col)
    second = band(jnp.where(row < INNER, beyond, wide - TILE + row), col + wide)
    for n, part in enumerate((first, second)):
        out_ref[0, n, 0:wide] = inside
        out_ref[0, n, wide : 2 * wide] = inside
        out_ref[0, n, 2 * wide : 2 * wide + TILE] = part
        out_ref[0, n, 2 * wide + TILE : 2 * wide + 2 * TILE] = part


def split(values):
    high = values.astype(jnp.bfloat16)
    low = (values - high.astype(jnp.float32)).astype(jnp.bfloat16)
    return high, low


def put(ref, here, t, values):
    wide = 2 * TILE
    depth = 2 * wide + 2 * TILE
    for low, part in enumerate(split(values)):
        side = [n * depth + 2 * wide + low * TILE for n in range(2)]
        if t < 4:
            at = (t // 2) * depth + low * wide + (t % 2) * TILE
            ref[*here, at : at + TILE] = part
        if t == 2:
            ref[*here, side[0] : side[0] + INNER] = part[:, :INNER]
        if t == 1:
            ref[*here, side[1] + INNER : side[1] + TILE] = part[:, INNER:]
        if t == 4:
            ref[*here, side[0] + INNER : side[0] + TILE] = part[:, INNER:]
            ref[*here, side[1] : side[1] + INNER] = part[:, :INNER]


def tile_of(main, rim, t):
    return [
        (rim(c) if t == 4 else main(c, slice(t * TILE, (t + 1) * TILE))).astype(jnp.float32)
        for c in range(2)
    ]


class Pairs:
    def __init__(self, plan, lists, slc_ref, rim_ref, bands_ref, powers_ref, out_ref, scratch):
        self.plan = plan
        self.lists = lists
        self.slc_ref, self.rim_ref = slc_ref, rim_ref
        self.bands_ref, self.powers_ref, self.out_ref = bands_ref, powers_ref, out_ref
        (self.left_ref, self.stack_ref, self.other_ref, self.other_rim_ref, self.stage_ref,
         self.list_ref, self.sems) = scratch
        self.me, self.strip = lax.axis_index("date"), lax.axis_index("strip")

    def partner(self, pair):
        return self.lists[PARTNER, pair]

    def near_item(self, n):
        slot, kind = n // NEAR, lax.rem(n, NEAR)
        dates = self.plan["dates"]
        pair = (self.me * dates + slot) * self.plan["per_date"] + kind
        return slot, kind, self.partner(pair) - self.me * dates

    def near_list(self, chosen):
        count = 0
        for n in range(self.plan["dates"] * NEAR):
            self.list_ref[count] = n
            count = count + jnp.where(chosen(self.near_item(n)[2]), 1, 0)
        return count

    def own(self, local):
        return (local >= 0) & (local < self.plan["dates"])

    def in_middle(self, local):
        half, dates = self.plan["devices"] // 2, self.plan["dates"]
        if not self.plan["halves"]:
            return False
        return ((self.me == half) & (local < 0)) | ((self.me == half - 1) & (local >= dates))

    def own_other(self, index):
        return (
            lambda c, cols: self.slc_ref[c, index, :, cols],
            lambda c: self.rim_ref[c, index],
        )

    def fetched_other(self, x):
        return (
            lambda c, cols: self.other_ref[x, c, :, cols],
            lambda c: self.other_rim_ref[x, c],
        )

    def fetch_payload(self, x, ref, index):
        rows = self.plan["rows"]
        packed = read_strips(ref, rows)
        for c in range(2):
            at = pl.multiple_of((2 * index + c) * rows, rows)
            self.other_ref[x, c] = ref[pl.ds(at, rows)]
            self.other_rim_ref[x, c] = place_strip(packed, 2 * index + c, self.strip)

    def out_copy(self, stage, x, pair):
        return pltpu.make_async_copy(
            self.stage_ref.at[stage, x], self.out_ref.at[:, pair], self.sems.at[stage, x]
        )

    def run(self, count, work):
        steps = (count + 1) // 2

        def step(n, carry):
            stage = lax.rem(n, 2)

            @pl.when(n >= 2)
            def _():
                for x in range(2):
                    self.out_copy(stage, x, 0).wait()

            items = [work(x, jnp.minimum(2 * n + x, count - 1)) for x in range(2)]
            self.compute(stage, items)
            for x, (slot, kind, _, _) in enumerate(items):
                copy = self.out_copy(stage, x, slot * self.plan["per_date"] + kind)
                pl.when(2 * n + x < count)(copy.start)
            return carry

        lax.fori_loop(0, steps, step, 0)
        for back in (2, 1):
            for x in range(2):
                used = (steps >= back) & (2 * (steps - back) + x < count)
                pl.when(used)(self.out_copy(lax.rem(steps + back, 2), x, 0).wait)

    def compute(self, stage, items):
        plan = self.plan
        rows, dates, per_date = plan["rows"], plan["dates"], plan["per_date"]
        part = [(pl.ds(f * rows, rows),) for f in range(4)]
        depth = self.bands_ref.shape[2]
        wide = self.bands_ref.shape[3]
        heights, widths = [], []
        for slot, kind, _, _ in items:
            pair = (self.me * dates + slot) * per_date + kind
            heights.append(self.lists[HEIGHT, pair])
            widths.append(jnp.clip(self.lists[REACH, pair] - REACH_LO, 0, HALO - REACH_LO))
        for x, (slot, kind, other, other_power) in enumerate(items):
            left_ref = self.left_ref.at[x]
            left_ref[*part[2]] = self.powers_ref[slot]
            if other_power is not None:
                left_ref[*part[3]] = self.powers_ref[other_power]
            first = self.own_other(slot)
            for t in range(5):
                a_real, a_imag = tile_of(*first, t)
                b_real, b_imag = tile_of(*other, t)
                put(left_ref, part[0], t, a_real * b_real + a_imag * b_imag)
                put(left_ref, part[1], t, a_imag * b_real - a_real * b_imag)
                if other_power is None:
                    put(left_ref, part[3], t, b_real * b_real + b_imag * b_imag)
        for n in range(2):
            for x in range(2):
                ranged = jnp.dot(
                    self.left_ref[x, :, n * depth : (n + 1) * depth],
                    self.bands_ref[widths[x], n],
                    preferred_element_type=jnp.float32,
                )
                there = slice(n * wide, (n + 1) * wide)
                for low, values in enumerate(split(ranged)):
                    for f in range(4):
                        self.stack_ref[x, f, low * rows : (low + 1) * rows, there] = values[
                            f * rows : (f + 1) * rows
                        ]
        row = lax.broadcasted_iota(jnp.int32, (rows, 2 * rows), 0)
        col = lax.broadcasted_iota(jnp.int32, (rows, 2 * rows), 1)
        col = jnp.where(col < rows, col, col - rows)
        for x in range(2):
            band = (jnp.abs(row - col) <= heights[x]).astype(jnp.float32).astype(jnp.bfloat16)
            looked = [
                jnp.dot(band, self.stack_ref[x, f], preferred_element_type=jnp.float32)
                for f in range(4)
            ]
            inverse = lax.rsqrt(looked[2] * looked[3] + EPSILON)
            for c in range(2):
                self.stage_ref[stage, x, c] = looked[c] * inverse


def own_kernel(plan, lists, slc_ref, rim_ref, bands_ref, out_ref, powers_ref, *scratch):
    pairs = Pairs(plan, lists, slc_ref, rim_ref, bands_ref, powers_ref, out_ref, scratch)
    dates = plan["dates"]

    def power(slot, carry):
        for t in range(5):
            real, imag = tile_of(*pairs.own_other(slot), t)
            put(powers_ref, (slot, slice(None)), t, real * real + imag * imag)
        return carry

    lax.fori_loop(0, dates, power, 0)

    def work(x, n):
        slot, kind, local = pairs.near_item(pairs.list_ref[n])
        return slot, kind, pairs.own_other(local), local

    pairs.run(pairs.near_list(pairs.own), work)


def rest_kernel(plan, lists, slc_ref, rim_ref, bands_ref, powers_ref, inner_ref, outer_ref,
                middle_ref, _, out_ref, *scratch):
    pairs = Pairs(plan, lists, slc_ref, rim_ref, bands_ref, powers_ref, out_ref, scratch)
    dates = plan["dates"]
    upper = pairs.me >= plan["devices"] // 2 if plan["halves"] else True

    def work(x, n):
        slot, kind, local = pairs.near_item(pairs.list_ref[n])
        below = local < 0
        index = jnp.clip(jnp.where(below, local + NEAR, local - dates), 0, NEAR - 1)
        inner, middle = below == upper, pairs.in_middle(local)
        sources = (
            (jnp.logical_not(inner), outer_ref),
            (inner & jnp.logical_not(middle), inner_ref),
            (inner & middle, middle_ref),
        )
        for chosen, ref in sources:
            pl.when(chosen)(functools.partial(pairs.fetch_payload, x, ref, index))
        return slot, kind, pairs.fetched_other(x), None

    pairs.run(pairs.near_list(lambda local: jnp.logical_not(pairs.own(local))), work)


def annual_kernel(plan, lists, slc_ref, rim_ref, bands_ref, powers_ref, ring_ref,
                  images_ref, strips_ref, _sent, _, out_ref, *scratch, is_late):
    pairs = Pairs(plan, lists, slc_ref, rim_ref, bands_ref, powers_ref, out_ref, scratch)
    dates, late = plan["dates"], plan["late"]
    half = plan["devices"] // 2
    me, split_date = pairs.me, half * dates
    lower = me < half
    if is_late:
        base, count = jnp.where(lower, 0, dates - late), late
    else:
        base, count = jnp.where(lower, late, 0), dates - late

    def fetch_early(x, k, ref):
        packed = strips_ref[...]
        for c in range(2):
            pairs.other_ref[x, c] = ref[c, k]
            pairs.other_rim_ref[x, c] = place_strip(packed, 2 * k + c, pairs.strip)

    def work(x, k):
        slot = base + k
        date = me * dates + slot
        other = pairs.partner(date * plan["per_date"] + NEAR)
        far = (other < split_date) == lower
        end = 2 * split_date
        if is_late:
            ring_at = jnp.where(lower, other - (split_date - NEAR), other - split_date)
        else:
            ring_at = jnp.where(lower, other, other - (end - NEAR))
        ring_at = jnp.clip(ring_at, 0, NEAR - 1)
        fetch = pairs.fetch_payload
        pl.when(far)(lambda: fetch(x, ring_ref, ring_at))
        near_side = jnp.logical_not(far)
        if is_late:
            pl.when(near_side)(lambda: fetch(x, images_ref, k))
        else:
            pl.when(near_side)(lambda: fetch_early(x, k, images_ref))
        return slot, NEAR, pairs.fetched_other(x), None

    pairs.run(count, work)


def plain_kernel(plan, lists, slc_ref, rim_ref, bands_ref, powers_ref, images_ref,
                 image_rim_ref, _, out_ref, *scratch):
    pairs = Pairs(plan, lists, slc_ref, rim_ref, bands_ref, powers_ref, out_ref, scratch)

    def work(x, slot):
        other = (
            lambda c, cols: images_ref[c, slot, :, cols],
            lambda c: image_rim_ref[c, slot],
        )
        return slot, NEAR, other, None

    pairs.run(plan["dates"], work)


def arrivals_by_distance(slc, pair_list, plan):
    dates, per_date, devices = plan["dates"], plan["per_date"], plan["devices"]
    total = dates * devices
    me = lax.axis_index("date")
    annual_of = pair_list[:, 1].reshape(total, per_date)[:, per_date - 1]
    sums = [None] * dates
    for direction in (1, -1):
        by_distance = {}
        for slot in range(dates):
            for gap in range(plan["year"], plan["year"] + 3):
                distance = (slot + direction * gap) // dates
                by_distance.setdefault(distance, set()).add(slot)
        for distance in sorted(by_distance):
            slots = sorted(by_distance[distance])
            wanted_by = (me - distance) * dates + jnp.array(slots, dtype=jnp.int32)
            inside = (wanted_by >= 0) & (wanted_by < total)
            local = jnp.take(annual_of, jnp.clip(wanted_by, 0, total - 1)) - me * dates
            usable = inside & (local >= 0) & (local < dates)
            packed = jnp.take(slc, jnp.clip(local, 0, dates - 1), axis=1)
            packed = jnp.where(usable[None, :, None, None], packed, jnp.zeros_like(packed))
            route = [(i + distance, i) for i in range(devices) if 0 <= i + distance < devices]
            arrived = lax.ppermute(packed, "date", route)
            for n, slot in enumerate(slots):
                part = arrived[:, n]
                sums[slot] = part if sums[slot] is None else sums[slot] + part
    return jnp.stack(sums, axis=1)


def payload_of(images, rim, strip):
    planes, count, rows, cols = images.shape
    edges = jnp.where(strip == 0, rim[..., :HALO], rim[..., TILE - HALO :])
    edges = jnp.transpose(edges, (2, 1, 0, 3)).reshape(rows, count * planes * HALO)
    edges = jnp.pad(edges, ((0, 0), (0, TILE - edges.shape[1])))
    part = rows * TILE // cols
    edges = jnp.transpose(edges.reshape(rows // part, part, TILE), (1, 0, 2)).reshape(part, cols)
    stacked = jnp.transpose(images, (1, 0, 2, 3)).reshape(count * planes * rows, cols)
    return jnp.concatenate([stacked, edges], axis=0)


def body(slc, pair_list, az_half, rng_half):
    planes, dates, rows, cols = slc.shape
    devices = lax.axis_size("date")
    total = dates * devices
    per_date = pair_list.shape[0] // total
    year = min(YEAR, total // 2 - 2)
    half = devices // 2
    late = half * dates - year
    halves = devices % 2 == 0 and 0 < late <= NEAR and 2 * late <= dates
    halves = halves and 2 * (dates - late) * HALO <= TILE
    plan = {
        "dates": dates,
        "devices": devices,
        "per_date": per_date,
        "year": year,
        "late": late,
        "rows": rows,
        "cols": cols,
        "pairs": total * per_date,
        "halves": halves,
    }
    dtype = slc.dtype
    rim_rows = rows * TILE // cols
    pairs = pair_list.T
    lists = jnp.concatenate([pairs, az_half[None], rng_half[None]])
    swap_strips = [(0, 1), (1, 0)]

    def images(count):
        return jax.ShapeDtypeStruct((planes, count, rows, cols), dtype)

    def rim_shape(count):
        return jax.ShapeDtypeStruct((planes, count, rows, TILE), dtype)

    def payload_shape(count):
        return jax.ShapeDtypeStruct((planes * count * rows + rim_rows, cols), dtype)

    def swapped_rims(values):
        out = pl.pallas_call(
            rim_kernel,
            out_shape=rim_shape(values.shape[1]),
            in_specs=[ANY],
            out_specs=VMEM,
            scratch_shapes=[pltpu.SemaphoreType.DMA],
            compiler_params=limit(WORK_MIB),
            name="rim_blocks",
        )(values)
        return lax.ppermute(out, "strip", swap_strips)

    def cost(flops):
        return pl.CostEstimate(flops=flops, bytes_accessed=1, transcendentals=0)

    wide = cols // 2
    widths = HALO - REACH_LO + 1
    band_shape = (2, 2 * wide + 2 * TILE, wide)
    bands = pl.pallas_call(
        functools.partial(bands_kernel, cols),
        grid=(widths,),
        out_shape=jax.ShapeDtypeStruct((widths, *band_shape), jnp.bfloat16),
        out_specs=pl.BlockSpec((1, *band_shape), lambda n: (n, 0, 0, 0)),
        compiler_params=limit(WORK_MIB),
        cost_estimate=cost(1),
        name="range_bands",
    )()
    if halves:
        swap = [(i, (i + half) % devices) for i in range(devices)]
        both = ("date", "strip")
        early, rim, strips = pl.pallas_call(
            functools.partial(early_kernel, plan),
            out_shape=(
                images(dates - late),
                rim_shape(dates),
                jax.ShapeDtypeStruct((rows, TILE), dtype),
            ),
            in_specs=[ANY, SMEM],
            out_specs=(VMEM, VMEM, VMEM),
            scratch_shapes=[
                pltpu.VMEM((dates - late, planes, rows, TILE), dtype),
                pltpu.SemaphoreType.DMA((dates - late,)),
                pltpu.SemaphoreType.DMA((dates - late,)),
                pltpu.SemaphoreType.DMA,
            ],
            compiler_params=limit(FIRST_MIB),
            name="early_images",
        )(slc, pairs)
        early = lax.ppermute(early, "date", swap)
        rim = lax.ppermute(rim, "strip", swap_strips)
        inner, outer = pl.pallas_call(
            functools.partial(beside_kernel, plan),
            out_shape=(payload_shape(NEAR), payload_shape(NEAR)),
            in_specs=[ANY, VMEM],
            out_specs=(VMEM, VMEM),
            scratch_shapes=[pltpu.SemaphoreType.DMA((2, NEAR, 2))],
            compiler_params=limit(WORK_MIB),
            name="beside_images",
        )(slc, rim)
        down = [(i, (i - 1) % half) for i in range(half)]
        down += [(half + i, half + (i + 1) % half) for i in range(half)]
        strips = lax.ppermute(
            strips, both, [(2 * a + s, 2 * b + 1 - s) for a, b in swap for s in (0, 1)]
        )
        middle = lax.ppermute(outer, "date", [(half - 1, half), (half, half - 1)])
        outer = lax.ppermute(outer, "date", [(b, a) for a, b in down])
        inner = lax.ppermute(inner, "date", down)
    else:
        rim = swapped_rims(slc)
        annual = arrivals_by_distance(slc, pair_list, plan)
        strip = lax.axis_index("strip")
        ups = [(i, i + 1) for i in range(devices - 1)]
        inner = payload_of(slc[:, dates - NEAR :], rim[:, dates - NEAR :], strip)
        outer = payload_of(slc[:, :NEAR], rim[:, :NEAR], strip)
        inner = lax.ppermute(inner, "date", ups)
        outer = lax.ppermute(outer, "date", [(b, a) for a, b in ups])

    out_shape = jax.ShapeDtypeStruct((planes, dates * per_date, rows, cols), jnp.float32)
    depth = 2 * band_shape[1]
    scratch = [
        pltpu.VMEM((2, 4 * rows, depth), jnp.bfloat16),
        pltpu.VMEM((2, 4, 2 * rows, cols), jnp.bfloat16),
        pltpu.VMEM((2, planes, rows, cols), dtype),
        pltpu.VMEM((2, planes, rows, TILE), dtype),
        pltpu.VMEM((2, 2, planes, rows, cols), jnp.float32),
        pltpu.SMEM((dates * NEAR + 1,), jnp.int32),
        pltpu.SemaphoreType.DMA((2, 2)),
    ]

    out, powers = pl.pallas_call(
        functools.partial(own_kernel, plan),
        out_shape=(out_shape, jax.ShapeDtypeStruct((dates, rows, depth), jnp.bfloat16)),
        in_specs=[SMEM] + [VMEM] * 3,
        out_specs=(ANY, VMEM),
        scratch_shapes=scratch,
        compiler_params=limit(WORK_MIB),
        cost_estimate=cost(OWN_FLOPS),
        name="own_pairs",
    )(lists, slc, rim, bands)

    def more_pairs(kernel, out, others, name, flops=1):
        return pl.pallas_call(
            functools.partial(kernel, plan),
            out_shape=out_shape,
            in_specs=[SMEM] + [VMEM] * (4 + len(others)) + [ANY],
            out_specs=ANY,
            scratch_shapes=scratch,
            input_output_aliases={5 + len(others): 0},
            compiler_params=limit(WORK_MIB),
            cost_estimate=cost(flops),
            name=name,
        )(lists, slc, rim, bands, powers, *others, out)

    if halves:
        payload = sent = pl.pallas_call(
            functools.partial(late_kernel, plan),
            out_shape=payload_shape(late),
            in_specs=[VMEM, VMEM, VMEM, SMEM, ANY, ANY],
            out_specs=VMEM,
            scratch_shapes=[pltpu.VMEM((late, planes, rows, TILE), dtype)],
            compiler_params=limit(WORK_MIB),
            name="late_images",
        )(slc, rim, inner, lists, powers, strips)
        payload = lax.ppermute(payload, "date", swap)
    if halves:
        early_pairs = functools.partial(annual_kernel, is_late=False)
        out = more_pairs(early_pairs, out, (inner, early, strips, sent), "annual_pairs", ANNUAL_FLOPS)
        out = more_pairs(rest_kernel, out, (inner, outer, middle), "near_pairs")
        late_pairs = functools.partial(annual_kernel, is_late=True)
        out = more_pairs(late_pairs, out, (outer, payload, strips, sent), "last_pairs")
    else:
        out = more_pairs(rest_kernel, out, (inner, outer, inner), "near_pairs")
        out = more_pairs(plain_kernel, out, (annual, swapped_rims(annual)), "annual_pairs")
    return out


def solution(mesh):
    placed = (P(None, "date", "groups", "strip"), P(), P(), P())
    return jax.shard_map(
        body,
        mesh=mesh,
        in_specs=placed,
        out_specs=P(None, "date", "groups", "strip"),
        check_vma=False,
    )
```

```python
import functools

import jax
import jax.numpy as jnp
from jax import lax
from jax.experimental import pallas as pl
from jax.experimental.pallas import tpu as pltpu
from jax.sharding import PartitionSpec as P

HALO = 16
REACH_LO = 12
NEAR = 3
YEAR = 29
EPSILON = 1e-06
TILE = 128
INNER = TILE // 2
OWN_FLOPS = 4_000_000_000
ANNUAL_FLOPS = 8_000_000_000
PARTNER, HEIGHT, REACH = 1, 2, 3
WORK_MIB = 16
FIRST_MIB = 56
ANY = pl.BlockSpec(memory_space=pl.ANY)
SMEM = pl.BlockSpec(memory_space=pltpu.SMEM)
VMEM = pl.BlockSpec(memory_space=pltpu.VMEM)


def limit(mebibytes):
    return pltpu.CompilerParams(vmem_limit_bytes=mebibytes * 1024 * 1024)


def run_copies(copies):
    for copy in copies:
        copy.start()
    for copy in copies:
        copy.wait()


def gather_strips(tiles, side):
    lane = lax.broadcasted_iota(jnp.int32, tiles[0].shape, 1)
    packed = jnp.zeros(tiles[0].shape, jnp.float32)
    for n, tile in enumerate(tiles):
        spot = n * HALO
        moved = pltpu.roll(tile.astype(jnp.float32), spot + side * HALO, 1)
        packed = jnp.where((lane >= spot) & (lane < spot + HALO), moved, packed)
    return packed.astype(jnp.bfloat16)


def place_strip(packed, n, side):
    shift = 2 * TILE - (n + side) * HALO
    return pltpu.roll(packed.astype(jnp.float32), lax.rem(shift, TILE), 1).astype(jnp.bfloat16)


def write_strips(out_ref, packed):
    rows, cols = packed.shape[0], out_ref.shape[1]
    part = rows * TILE // cols
    base = out_ref.shape[0] - part
    for n in range(rows // part):
        out_ref[base:, n * TILE : (n + 1) * TILE] = packed[n * part : (n + 1) * part]


def read_strips(ref, rows):
    cols = ref.shape[1]
    base = ref.shape[0] - rows * TILE // cols
    return jnp.concatenate(
        [ref[base:, n * TILE : (n + 1) * TILE] for n in range(cols // TILE)], axis=0
    )


def wanted_images(plan, pairs_ref):
    me = lax.axis_index("date")
    dates, half = plan["dates"], plan["devices"] // 2
    mate = lax.rem(me + half, 2 * half)
    wanted = []
    for k in range(dates - plan["late"]):
        date = mate * dates + jnp.where(mate < half, plan["late"], 0) + k
        at = pairs_ref[PARTNER, date * plan["per_date"] + NEAR] - me * dates
        wanted.append(jnp.clip(at, 0, dates - 1))
    return wanted


def image_copies(slc_ref, wanted, early_ref, sems):
    return [
        pltpu.make_async_copy(slc_ref.at[:, at], early_ref.at[:, k], sems.at[k])
        for k, at in enumerate(wanted)
    ]


def early_kernel(plan, slc_ref, pairs_ref, early_ref, rim_ref, strips_ref, tiles_ref, sems,
                 tile_sems, rim_sem):
    strip, cols = lax.axis_index("strip"), plan["cols"]
    start = pl.multiple_of(jnp.where(strip == 0, cols - TILE, 0), TILE)
    wanted = wanted_images(plan, pairs_ref)
    rim_copy = pltpu.make_async_copy(slc_ref.at[:, :, :, pl.ds(start, TILE)], rim_ref, rim_sem)
    early_copies = image_copies(slc_ref, wanted, early_ref, sems)
    tile_copies = [
        pltpu.make_async_copy(
            slc_ref.at[:, at, :, pl.ds(start, TILE)], tiles_ref.at[k], tile_sems.at[k]
        )
        for k, at in enumerate(wanted)
    ]
    for copy in tile_copies + [rim_copy] + early_copies:
        copy.start()
    for copy in tile_copies:
        copy.wait()
    tiles = [tiles_ref[k, c] for k in range(len(wanted)) for c in range(2)]
    strips_ref[...] = gather_strips(tiles, 1 - strip)
    for copy in [rim_copy] + early_copies:
        copy.wait()


def rim_kernel(slc_ref, rim_ref, sem):
    cols = slc_ref.shape[3]
    start = pl.multiple_of(jnp.where(lax.axis_index("strip") == 0, cols - TILE, 0), TILE)
    run_copies([pltpu.make_async_copy(slc_ref.at[:, :, :, pl.ds(start, TILE)], rim_ref, sem)])


def beside_kernel(plan, slc_ref, rim_ref, inner_ref, outer_ref, sems):
    me, strip = lax.axis_index("date"), lax.axis_index("strip")
    dates, rows = plan["dates"], plan["rows"]
    upper = me >= plan["devices"] // 2
    last = dates - NEAR
    copies = []
    firsts = (jnp.where(upper, last, 0), jnp.where(upper, 0, last))
    for r, (out_ref, first) in enumerate(zip((inner_ref, outer_ref), firsts)):
        for k in range(NEAR):
            for c in range(2):
                here = out_ref.at[pl.ds((2 * k + c) * rows, rows)]
                copies.append(
                    pltpu.make_async_copy(slc_ref.at[c, first + k], here, sems.at[r, k, c])
                )
    for copy in copies:
        copy.start()
    for out_ref, first in zip((inner_ref, outer_ref), firsts):
        tiles = [rim_ref[c, first + k] for k in range(NEAR) for c in range(2)]
        write_strips(out_ref, gather_strips(tiles, strip))
    for copy in copies:
        copy.wait()


def late_kernel(plan, slc_ref, rim_ref, inner_ref, pairs_ref, *refs):
    late_ref, end_ref, tiles_ref = refs[-3:]
    me, strip = lax.axis_index("date"), lax.axis_index("strip")
    dates, late, rows = plan["dates"], plan["late"], plan["rows"]
    half = plan["devices"] // 2
    mate = lax.rem(me + half, 2 * half)
    mate_slot = jnp.where(mate < half, 0, dates - late)
    packed = read_strips(inner_ref, rows)
    for k in range(late):
        date = mate * dates + mate_slot + k
        wanted = pairs_ref[PARTNER, date * plan["per_date"] + NEAR] - me * dates
        own = (wanted >= 0) & (wanted < dates)
        own_at = jnp.clip(wanted, 0, dates - 1)
        other_at = jnp.clip(jnp.where(me < half, wanted - dates, wanted + NEAR), 0, NEAR - 1)
        for c in range(2):
            here = pl.ds((2 * k + c) * rows, rows)

            @pl.when(own)
            def _():
                late_ref[here] = slc_ref[c, own_at]
                tiles_ref[k, c] = rim_ref[c, own_at]

            @pl.when(jnp.logical_not(own))
            def _():
                there = pl.multiple_of((2 * other_at + c) * rows, rows)
                late_ref[here] = inner_ref[pl.ds(there, rows)]
                tiles_ref[k, c] = place_strip(packed, 2 * other_at + c, strip)

    tiles = [tiles_ref[k, c] for k in range(late) for c in range(2)]
    write_strips(late_ref, gather_strips(tiles, strip))

    @pl.when((me == half) | (me == half - 1))
    def _():
        end = jnp.where(me < half, 0, 2 * half - 1)
        end_slot = jnp.where(me < half, 0, dates - late)
        tiles = []
        for k in range(late):
            date = end * dates + end_slot + k
            at = pairs_ref[PARTNER, date * plan["per_date"] + NEAR] - me * dates
            at = jnp.clip(at, 0, dates - 1)
            for c in range(2):
                end_ref[pl.ds((2 * k + c) * rows, rows)] = slc_ref[c, at]
                tiles.append(rim_ref[c, at])
        write_strips(end_ref, gather_strips(tiles, strip))


def bands_kernel(cols, out_ref):
    strip = lax.axis_index("strip")
    wide = out_ref.shape[3]
    reach = pl.program_id(0) + REACH_LO

    def band(places, targets):
        return (jnp.abs(places - targets) <= reach).astype(jnp.float32).astype(jnp.bfloat16)

    def indices(shape):
        return lax.broadcasted_iota(jnp.int32, shape, 0), lax.broadcasted_iota(jnp.int32, shape, 1)

    inside = band(*indices((wide, wide)))
    row, col = indices((TILE, wide))
    beyond = jnp.where(strip == 0, cols + row, row - TILE)
    first = band(jnp.where(row < INNER, wide + row, beyond), col)
    second = band(jnp.where(row < INNER, beyond, wide - TILE + row), col + wide)
    for n, part in enumerate((first, second)):
        out_ref[0, n, 0:wide] = inside
        out_ref[0, n, wide : 2 * wide] = inside
        out_ref[0, n, 2 * wide : 2 * wide + TILE] = part
        out_ref[0, n, 2 * wide + TILE : 2 * wide + 2 * TILE] = part


def split(values):
    high = values.astype(jnp.bfloat16)
    low = (values - high.astype(jnp.float32)).astype(jnp.bfloat16)
    return high, low


def put(ref, here, t, values):
    wide = 2 * TILE
    depth = 2 * wide + 2 * TILE
    for low, part in enumerate(split(values)):
        side = [n * depth + 2 * wide + low * TILE for n in range(2)]
        if t < 4:
            at = (t // 2) * depth + low * wide + (t % 2) * TILE
            ref[*here, at : at + TILE] = part
        if t == 2:
            ref[*here, side[0] : side[0] + INNER] = part[:, :INNER]
        if t == 1:
            ref[*here, side[1] + INNER : side[1] + TILE] = part[:, INNER:]
        if t == 4:
            ref[*here, side[0] + INNER : side[0] + TILE] = part[:, INNER:]
            ref[*here, side[1] : side[1] + INNER] = part[:, :INNER]


def tile_of(main, rim, t):
    return [
        (rim(c) if t == 4 else main(c, slice(t * TILE, (t + 1) * TILE))).astype(jnp.float32)
        for c in range(2)
    ]


class Pairs:
    def __init__(self, plan, lists, slc_ref, rim_ref, bands_ref, powers_ref, out_ref, scratch):
        self.plan = plan
        self.lists = lists
        self.slc_ref, self.rim_ref = slc_ref, rim_ref
        self.bands_ref, self.powers_ref, self.out_ref = bands_ref, powers_ref, out_ref
        (self.left_ref, self.stack_ref, self.other_ref, self.other_rim_ref, self.stage_ref,
         self.list_ref, self.sems) = scratch
        self.me, self.strip = lax.axis_index("date"), lax.axis_index("strip")

    def partner(self, pair):
        return self.lists[PARTNER, pair]

    def near_item(self, n):
        slot, kind = n // NEAR, lax.rem(n, NEAR)
        dates = self.plan["dates"]
        pair = (self.me * dates + slot) * self.plan["per_date"] + kind
        return slot, kind, self.partner(pair) - self.me * dates

    def near_list(self, chosen):
        count = 0
        for n in range(self.plan["dates"] * NEAR):
            self.list_ref[count] = n
            count = count + jnp.where(chosen(self.near_item(n)[2]), 1, 0)
        return count

    def own(self, local):
        return (local >= 0) & (local < self.plan["dates"])

    def in_middle(self, local):
        half, dates = self.plan["devices"] // 2, self.plan["dates"]
        if not self.plan["halves"]:
            return False
        return ((self.me == half) & (local < 0)) | ((self.me == half - 1) & (local >= dates))

    def own_other(self, index):
        return (
            lambda c, cols: self.slc_ref[c, index, :, cols],
            lambda c: self.rim_ref[c, index],
        )

    def fetched_other(self, x):
        return (
            lambda c, cols: self.other_ref[x, c, :, cols],
            lambda c: self.other_rim_ref[x, c],
        )

    def fetch_payload(self, x, ref, index):
        rows = self.plan["rows"]
        packed = read_strips(ref, rows)
        for c in range(2):
            at = pl.multiple_of((2 * index + c) * rows, rows)
            self.other_ref[x, c] = ref[pl.ds(at, rows)]
            self.other_rim_ref[x, c] = place_strip(packed, 2 * index + c, self.strip)

    def out_copy(self, stage, x, pair):
        return pltpu.make_async_copy(
            self.stage_ref.at[stage, x], self.out_ref.at[:, pair], self.sems.at[stage, x]
        )

    def run(self, count, work):
        steps = (count + 1) // 2

        def step(n, carry):
            stage = lax.rem(n, 2)

            @pl.when(n >= 2)
            def _():
                for x in range(2):
                    self.out_copy(stage, x, 0).wait()

            items = [work(x, jnp.minimum(2 * n + x, count - 1)) for x in range(2)]
            self.compute(stage, items)
            for x, (slot, kind, _, _) in enumerate(items):
                copy = self.out_copy(stage, x, slot * self.plan["per_date"] + kind)
                pl.when(2 * n + x < count)(copy.start)
            return carry

        lax.fori_loop(0, steps, step, 0)
        for back in (2, 1):
            for x in range(2):
                used = (steps >= back) & (2 * (steps - back) + x < count)
                pl.when(used)(self.out_copy(lax.rem(steps + back, 2), x, 0).wait)

    def compute(self, stage, items):
        plan = self.plan
        rows, dates, per_date = plan["rows"], plan["dates"], plan["per_date"]
        part = [(pl.ds(f * rows, rows),) for f in range(4)]
        depth = self.bands_ref.shape[2]
        wide = self.bands_ref.shape[3]
        heights, widths = [], []
        for slot, kind, _, _ in items:
            pair = (self.me * dates + slot) * per_date + kind
            heights.append(self.lists[HEIGHT, pair])
            widths.append(jnp.clip(self.lists[REACH, pair] - REACH_LO, 0, HALO - REACH_LO))
        for x, (slot, kind, other, other_power) in enumerate(items):
            left_ref = self.left_ref.at[x]
            left_ref[*part[2]] = self.powers_ref[slot]
            if other_power is not None:
                left_ref[*part[3]] = self.powers_ref[other_power]
            first = self.own_other(slot)
            for t in range(5):
                a_real, a_imag = tile_of(*first, t)
                b_real, b_imag = tile_of(*other, t)
                put(left_ref, part[0], t, a_real * b_real + a_imag * b_imag)
                put(left_ref, part[1], t, a_imag * b_real - a_real * b_imag)
                if other_power is None:
                    put(left_ref, part[3], t, b_real * b_real + b_imag * b_imag)
        for n in range(2):
            for x in range(2):
                ranged = jnp.dot(
                    self.left_ref[x, :, n * depth : (n + 1) * depth],
                    self.bands_ref[widths[x], n],
                    preferred_element_type=jnp.float32,
                )
                there = slice(n * wide, (n + 1) * wide)
                for low, values in enumerate(split(ranged)):
                    for f in range(4):
                        self.stack_ref[x, f, low * rows : (low + 1) * rows, there] = values[
                            f * rows : (f + 1) * rows
                        ]
        row = lax.broadcasted_iota(jnp.int32, (rows, 2 * rows), 0)
        col = lax.broadcasted_iota(jnp.int32, (rows, 2 * rows), 1)
        col = jnp.where(col < rows, col, col - rows)
        for x in range(2):
            band = (jnp.abs(row - col) <= heights[x]).astype(jnp.float32).astype(jnp.bfloat16)
            looked = [
                jnp.dot(band, self.stack_ref[x, f], preferred_element_type=jnp.float32)
                for f in range(4)
            ]
            inverse = lax.rsqrt(looked[2] * looked[3] + EPSILON)
            for c in range(2):
                self.stage_ref[stage, x, c] = looked[c] * inverse


def own_kernel(plan, lists, slc_ref, rim_ref, bands_ref, out_ref, powers_ref, *scratch):
    pairs = Pairs(plan, lists, slc_ref, rim_ref, bands_ref, powers_ref, out_ref, scratch)
    dates = plan["dates"]

    def power(slot, carry):
        for t in range(5):
            real, imag = tile_of(*pairs.own_other(slot), t)
            put(powers_ref, (slot, slice(None)), t, real * real + imag * imag)
        return carry

    lax.fori_loop(0, dates, power, 0)

    def work(x, n):
        slot, kind, local = pairs.near_item(pairs.list_ref[n])
        return slot, kind, pairs.own_other(local), local

    pairs.run(pairs.near_list(pairs.own), work)


def rest_kernel(plan, lists, slc_ref, rim_ref, bands_ref, powers_ref, inner_ref, outer_ref,
                middle_ref, _, out_ref, *scratch):
    pairs = Pairs(plan, lists, slc_ref, rim_ref, bands_ref, powers_ref, out_ref, scratch)
    dates = plan["dates"]
    upper = pairs.me >= plan["devices"] // 2 if plan["halves"] else True

    def work(x, n):
        slot, kind, local = pairs.near_item(pairs.list_ref[n])
        below = local < 0
        index = jnp.clip(jnp.where(below, local + NEAR, local - dates), 0, NEAR - 1)
        inner, middle = below == upper, pairs.in_middle(local)
        sources = (
            (jnp.logical_not(inner), outer_ref),
            (inner & jnp.logical_not(middle), inner_ref),
            (inner & middle, middle_ref),
        )
        for chosen, ref in sources:
            pl.when(chosen)(functools.partial(pairs.fetch_payload, x, ref, index))
        return slot, kind, pairs.fetched_other(x), None

    pairs.run(pairs.near_list(lambda local: jnp.logical_not(pairs.own(local))), work)


def annual_kernel(plan, lists, slc_ref, rim_ref, bands_ref, powers_ref, ring_ref,
                  images_ref, strips_ref, _sent, _, out_ref, *scratch, is_late):
    pairs = Pairs(plan, lists, slc_ref, rim_ref, bands_ref, powers_ref, out_ref, scratch)
    dates, late = plan["dates"], plan["late"]
    half = plan["devices"] // 2
    me, split_date = pairs.me, half * dates
    lower = me < half
    if is_late:
        base, count = jnp.where(lower, 0, dates - late), late
    else:
        base, count = jnp.where(lower, late, 0), dates - late

    def fetch_early(x, k, ref):
        packed = strips_ref[...]
        for c in range(2):
            pairs.other_ref[x, c] = ref[c, k]
            pairs.other_rim_ref[x, c] = place_strip(packed, 2 * k + c, pairs.strip)

    def work(x, k):
        slot = base + k
        date = me * dates + slot
        other = pairs.partner(date * plan["per_date"] + NEAR)
        far = (other < split_date) == lower
        end = 2 * split_date
        if is_late:
            ring_at = k
        else:
            ring_at = jnp.where(lower, other, other - (end - NEAR))
        ring_at = jnp.clip(ring_at, 0, NEAR - 1)
        fetch = pairs.fetch_payload
        pl.when(far)(lambda: fetch(x, ring_ref, ring_at))
        near_side = jnp.logical_not(far)
        if is_late:
            pl.when(near_side)(lambda: fetch(x, images_ref, k))
        else:
            pl.when(near_side)(lambda: fetch_early(x, k, images_ref))
        return slot, NEAR, pairs.fetched_other(x), None

    pairs.run(count, work)


def plain_kernel(plan, lists, slc_ref, rim_ref, bands_ref, powers_ref, images_ref,
                 image_rim_ref, _, out_ref, *scratch):
    pairs = Pairs(plan, lists, slc_ref, rim_ref, bands_ref, powers_ref, out_ref, scratch)

    def work(x, slot):
        other = (
            lambda c, cols: images_ref[c, slot, :, cols],
            lambda c: image_rim_ref[c, slot],
        )
        return slot, NEAR, other, None

    pairs.run(plan["dates"], work)


def arrivals_by_distance(slc, pair_list, plan):
    dates, per_date, devices = plan["dates"], plan["per_date"], plan["devices"]
    total = dates * devices
    me = lax.axis_index("date")
    annual_of = pair_list[:, 1].reshape(total, per_date)[:, per_date - 1]
    sums = [None] * dates
    for direction in (1, -1):
        by_distance = {}
        for slot in range(dates):
            for gap in range(plan["year"], plan["year"] + 3):
                distance = (slot + direction * gap) // dates
                by_distance.setdefault(distance, set()).add(slot)
        for distance in sorted(by_distance):
            slots = sorted(by_distance[distance])
            wanted_by = (me - distance) * dates + jnp.array(slots, dtype=jnp.int32)
            inside = (wanted_by >= 0) & (wanted_by < total)
            local = jnp.take(annual_of, jnp.clip(wanted_by, 0, total - 1)) - me * dates
            usable = inside & (local >= 0) & (local < dates)
            packed = jnp.take(slc, jnp.clip(local, 0, dates - 1), axis=1)
            packed = jnp.where(usable[None, :, None, None], packed, jnp.zeros_like(packed))
            route = [(i + distance, i) for i in range(devices) if 0 <= i + distance < devices]
            arrived = lax.ppermute(packed, "date", route)
            for n, slot in enumerate(slots):
                part = arrived[:, n]
                sums[slot] = part if sums[slot] is None else sums[slot] + part
    return jnp.stack(sums, axis=1)


def payload_of(images, rim, strip):
    planes, count, rows, cols = images.shape
    edges = jnp.where(strip == 0, rim[..., :HALO], rim[..., TILE - HALO :])
    edges = jnp.transpose(edges, (2, 1, 0, 3)).reshape(rows, count * planes * HALO)
    edges = jnp.pad(edges, ((0, 0), (0, TILE - edges.shape[1])))
    part = rows * TILE // cols
    edges = jnp.transpose(edges.reshape(rows // part, part, TILE), (1, 0, 2)).reshape(part, cols)
    stacked = jnp.transpose(images, (1, 0, 2, 3)).reshape(count * planes * rows, cols)
    return jnp.concatenate([stacked, edges], axis=0)


def body(slc, pair_list, az_half, rng_half):
    planes, dates, rows, cols = slc.shape
    devices = lax.axis_size("date")
    total = dates * devices
    per_date = pair_list.shape[0] // total
    year = min(YEAR, total // 2 - 2)
    half = devices // 2
    late = half * dates - year
    halves = devices % 2 == 0 and 0 < late <= NEAR and 2 * late <= dates
    halves = halves and 2 * (dates - late) * HALO <= TILE
    plan = {
        "dates": dates,
        "devices": devices,
        "per_date": per_date,
        "year": year,
        "late": late,
        "rows": rows,
        "cols": cols,
        "pairs": total * per_date,
        "halves": halves,
    }
    dtype = slc.dtype
    rim_rows = rows * TILE // cols
    pairs = pair_list.T
    lists = jnp.concatenate([pairs, az_half[None], rng_half[None]])
    swap_strips = [(0, 1), (1, 0)]

    def images(count):
        return jax.ShapeDtypeStruct((planes, count, rows, cols), dtype)

    def rim_shape(count):
        return jax.ShapeDtypeStruct((planes, count, rows, TILE), dtype)

    def payload_shape(count):
        return jax.ShapeDtypeStruct((planes * count * rows + rim_rows, cols), dtype)

    def swapped_rims(values):
        out = pl.pallas_call(
            rim_kernel,
            out_shape=rim_shape(values.shape[1]),
            in_specs=[ANY],
            out_specs=VMEM,
            scratch_shapes=[pltpu.SemaphoreType.DMA],
            compiler_params=limit(WORK_MIB),
            name="rim_blocks",
        )(values)
        return lax.ppermute(out, "strip", swap_strips)

    def cost(flops):
        return pl.CostEstimate(flops=flops, bytes_accessed=1, transcendentals=0)

    wide = cols // 2
    widths = HALO - REACH_LO + 1
    band_shape = (2, 2 * wide + 2 * TILE, wide)
    bands = pl.pallas_call(
        functools.partial(bands_kernel, cols),
        grid=(widths,),
        out_shape=jax.ShapeDtypeStruct((widths, *band_shape), jnp.bfloat16),
        out_specs=pl.BlockSpec((1, *band_shape), lambda n: (n, 0, 0, 0)),
        compiler_params=limit(WORK_MIB),
        cost_estimate=cost(1),
        name="range_bands",
    )()
    if halves:
        swap = [(i, (i + half) % devices) for i in range(devices)]
        both = ("date", "strip")
        early, rim, strips = pl.pallas_call(
            functools.partial(early_kernel, plan),
            out_shape=(
                images(dates - late),
                rim_shape(dates),
                jax.ShapeDtypeStruct((rows, TILE), dtype),
            ),
            in_specs=[ANY, SMEM],
            out_specs=(VMEM, VMEM, VMEM),
            scratch_shapes=[
                pltpu.VMEM((dates - late, planes, rows, TILE), dtype),
                pltpu.SemaphoreType.DMA((dates - late,)),
                pltpu.SemaphoreType.DMA((dates - late,)),
                pltpu.SemaphoreType.DMA,
            ],
            compiler_params=limit(FIRST_MIB),
            name="early_images",
        )(slc, pairs)
        early = lax.ppermute(early, "date", swap)
        rim = lax.ppermute(rim, "strip", swap_strips)
        inner, outer = pl.pallas_call(
            functools.partial(beside_kernel, plan),
            out_shape=(payload_shape(NEAR), payload_shape(NEAR)),
            in_specs=[ANY, VMEM],
            out_specs=(VMEM, VMEM),
            scratch_shapes=[pltpu.SemaphoreType.DMA((2, NEAR, 2))],
            compiler_params=limit(WORK_MIB),
            name="beside_images",
        )(slc, rim)
        down = [(i, (i - 1) % half) for i in range(half)]
        down += [(half + i, half + (i + 1) % half) for i in range(half)]
        strips = lax.ppermute(
            strips, both, [(2 * a + s, 2 * b + 1 - s) for a, b in swap for s in (0, 1)]
        )
        up = [(b, a) for a, b in down if b not in (half - 1, half)]
        across = [(half - 1, half), (half, half - 1)]
        second = outer
        outer = lax.ppermute(second, "date", up)
        middle = lax.ppermute(second, "date", across)
        inner = lax.ppermute(inner, "date", down)
    else:
        rim = swapped_rims(slc)
        annual = arrivals_by_distance(slc, pair_list, plan)
        strip = lax.axis_index("strip")
        ups = [(i, i + 1) for i in range(devices - 1)]
        inner = payload_of(slc[:, dates - NEAR :], rim[:, dates - NEAR :], strip)
        outer = payload_of(slc[:, :NEAR], rim[:, :NEAR], strip)
        inner = lax.ppermute(inner, "date", ups)
        outer = lax.ppermute(outer, "date", [(b, a) for a, b in ups])

    out_shape = jax.ShapeDtypeStruct((planes, dates * per_date, rows, cols), jnp.float32)
    depth = 2 * band_shape[1]
    scratch = [
        pltpu.VMEM((2, 4 * rows, depth), jnp.bfloat16),
        pltpu.VMEM((2, 4, 2 * rows, cols), jnp.bfloat16),
        pltpu.VMEM((2, planes, rows, cols), dtype),
        pltpu.VMEM((2, planes, rows, TILE), dtype),
        pltpu.VMEM((2, 2, planes, rows, cols), jnp.float32),
        pltpu.SMEM((dates * NEAR + 1,), jnp.int32),
        pltpu.SemaphoreType.DMA((2, 2)),
    ]

    out, powers = pl.pallas_call(
        functools.partial(own_kernel, plan),
        out_shape=(out_shape, jax.ShapeDtypeStruct((dates, rows, depth), jnp.bfloat16)),
        in_specs=[SMEM] + [VMEM] * 3,
        out_specs=(ANY, VMEM),
        scratch_shapes=scratch,
        compiler_params=limit(WORK_MIB),
        cost_estimate=cost(OWN_FLOPS),
        name="own_pairs",
    )(lists, slc, rim, bands)

    def more_pairs(kernel, out, others, name, flops=1):
        return pl.pallas_call(
            functools.partial(kernel, plan),
            out_shape=out_shape,
            in_specs=[SMEM] + [VMEM] * (4 + len(others)) + [ANY],
            out_specs=ANY,
            scratch_shapes=scratch,
            input_output_aliases={5 + len(others): 0},
            compiler_params=limit(WORK_MIB),
            cost_estimate=cost(flops),
            name=name,
        )(lists, slc, rim, bands, powers, *others, out)

    if halves:
        payload, ending = pl.pallas_call(
            functools.partial(late_kernel, plan),
            out_shape=(payload_shape(late), payload_shape(late)),
            in_specs=[VMEM, VMEM, VMEM, SMEM, ANY, ANY],
            out_specs=(VMEM, VMEM),
            scratch_shapes=[pltpu.VMEM((late, planes, rows, TILE), dtype)],
            compiler_params=limit(WORK_MIB),
            name="late_images",
        )(slc, rim, inner, lists, powers, strips)
        sent = payload
        payload = lax.ppermute(payload, "date", swap)
        ending = lax.ppermute(ending, "date", [(half - 1, 0), (half, devices - 1)])
    if halves:
        early_pairs = functools.partial(annual_kernel, is_late=False)
        out = more_pairs(early_pairs, out, (inner, early, strips, sent), "annual_pairs", ANNUAL_FLOPS)
        out = more_pairs(rest_kernel, out, (inner, outer, middle), "near_pairs")
        late_pairs = functools.partial(annual_kernel, is_late=True)
        out = more_pairs(late_pairs, out, (ending, payload, strips, sent), "last_pairs")
    else:
        out = more_pairs(rest_kernel, out, (inner, outer, inner), "near_pairs")
        out = more_pairs(plain_kernel, out, (annual, swapped_rims(annual)), "annual_pairs")
    return out


def solution(mesh):
    placed = (P(None, "date", "groups", "strip"), P(), P(), P())
    return jax.shard_map(
        body,
        mesh=mesh,
        in_specs=placed,
        out_specs=P(None, "date", "groups", "strip"),
        check_vma=False,
    )
```

```python
import functools

import jax
import jax.numpy as jnp
from jax import lax
from jax.experimental import pallas as pl
from jax.experimental.pallas import tpu as pltpu
from jax.sharding import PartitionSpec as P

HALO = 16
REACH_LO = 12
NEAR = 3
YEAR = 29
EPSILON = 1e-06
TILE = 128
INNER = TILE // 2
OWN_FLOPS = 4_000_000_000
ANNUAL_FLOPS = 8_000_000_000
PARTNER, HEIGHT, REACH = 1, 2, 3
WORK_MIB = 16
FIRST_MIB = 56
ANY = pl.BlockSpec(memory_space=pl.ANY)
SMEM = pl.BlockSpec(memory_space=pltpu.SMEM)
VMEM = pl.BlockSpec(memory_space=pltpu.VMEM)


def limit(mebibytes):
    return pltpu.CompilerParams(vmem_limit_bytes=mebibytes * 1024 * 1024)


def run_copies(copies):
    for copy in copies:
        copy.start()
    for copy in copies:
        copy.wait()


def gather_strips(tiles, side):
    lane = lax.broadcasted_iota(jnp.int32, tiles[0].shape, 1)
    packed = jnp.zeros(tiles[0].shape, jnp.float32)
    for n, tile in enumerate(tiles):
        spot = n * HALO
        moved = pltpu.roll(tile.astype(jnp.float32), spot + side * HALO, 1)
        packed = jnp.where((lane >= spot) & (lane < spot + HALO), moved, packed)
    return packed.astype(jnp.bfloat16)


def place_strip(packed, n, side):
    shift = 2 * TILE - (n + side) * HALO
    return pltpu.roll(packed.astype(jnp.float32), lax.rem(shift, TILE), 1).astype(jnp.bfloat16)


def write_strips(out_ref, packed):
    rows, cols = packed.shape[0], out_ref.shape[1]
    part = rows * TILE // cols
    base = out_ref.shape[0] - part
    for n in range(rows // part):
        out_ref[base:, n * TILE : (n + 1) * TILE] = packed[n * part : (n + 1) * part]


def read_strips(ref, rows):
    cols = ref.shape[1]
    base = ref.shape[0] - rows * TILE // cols
    return jnp.concatenate(
        [ref[base:, n * TILE : (n + 1) * TILE] for n in range(cols // TILE)], axis=0
    )


def wanted_images(plan, pairs_ref):
    me = lax.axis_index("date")
    dates, half = plan["dates"], plan["devices"] // 2
    mate = lax.rem(me + half, 2 * half)
    wanted = []
    for k in range(dates - plan["late"]):
        date = mate * dates + jnp.where(mate < half, plan["late"], 0) + k
        at = pairs_ref[PARTNER, date * plan["per_date"] + NEAR] - me * dates
        wanted.append(jnp.clip(at, 0, dates - 1))
    return wanted


def image_copies(slc_ref, wanted, early_ref, sems):
    return [
        pltpu.make_async_copy(slc_ref.at[:, at], early_ref.at[:, k], sems.at[k])
        for k, at in enumerate(wanted)
    ]


def early_kernel(plan, slc_ref, pairs_ref, early_ref, rim_ref, strips_ref, tiles_ref, sems,
                 tile_sems, rim_sem):
    strip, cols = lax.axis_index("strip"), plan["cols"]
    start = pl.multiple_of(jnp.where(strip == 0, cols - TILE, 0), TILE)
    wanted = wanted_images(plan, pairs_ref)
    rim_copy = pltpu.make_async_copy(slc_ref.at[:, :, :, pl.ds(start, TILE)], rim_ref, rim_sem)
    early_copies = image_copies(slc_ref, wanted, early_ref, sems)
    tile_copies = [
        pltpu.make_async_copy(
            slc_ref.at[:, at, :, pl.ds(start, TILE)], tiles_ref.at[k], tile_sems.at[k]
        )
        for k, at in enumerate(wanted)
    ]
    for copy in tile_copies + [rim_copy] + early_copies:
        copy.start()
    for copy in tile_copies:
        copy.wait()
    tiles = [tiles_ref[k, c] for k in range(len(wanted)) for c in range(2)]
    strips_ref[...] = gather_strips(tiles, 1 - strip)
    for copy in [rim_copy] + early_copies:
        copy.wait()


def rim_kernel(slc_ref, rim_ref, sem):
    cols = slc_ref.shape[3]
    start = pl.multiple_of(jnp.where(lax.axis_index("strip") == 0, cols - TILE, 0), TILE)
    run_copies([pltpu.make_async_copy(slc_ref.at[:, :, :, pl.ds(start, TILE)], rim_ref, sem)])


def beside_kernel(plan, slc_ref, rim_ref, inner_ref, outer_ref, sems):
    me, strip = lax.axis_index("date"), lax.axis_index("strip")
    dates, rows = plan["dates"], plan["rows"]
    upper = me >= plan["devices"] // 2
    last = dates - NEAR
    copies = []
    firsts = (jnp.where(upper, last, 0), jnp.where(upper, 0, last))
    for r, (out_ref, first) in enumerate(zip((inner_ref, outer_ref), firsts)):
        for k in range(NEAR):
            for c in range(2):
                here = out_ref.at[pl.ds((2 * k + c) * rows, rows)]
                copies.append(
                    pltpu.make_async_copy(slc_ref.at[c, first + k], here, sems.at[r, k, c])
                )
    for copy in copies:
        copy.start()
    for out_ref, first in zip((inner_ref, outer_ref), firsts):
        tiles = [rim_ref[c, first + k] for k in range(NEAR) for c in range(2)]
        write_strips(out_ref, gather_strips(tiles, strip))
    for copy in copies:
        copy.wait()


def late_kernel(plan, slc_ref, rim_ref, inner_ref, pairs_ref, *refs):
    late_ref, tiles_ref = refs[-2:]
    me, strip = lax.axis_index("date"), lax.axis_index("strip")
    dates, late, rows = plan["dates"], plan["late"], plan["rows"]
    half = plan["devices"] // 2
    mate = lax.rem(me + half, 2 * half)
    mate_slot = jnp.where(mate < half, 0, dates - late)
    packed = read_strips(inner_ref, rows)
    for k in range(late):
        date = mate * dates + mate_slot + k
        wanted = pairs_ref[PARTNER, date * plan["per_date"] + NEAR] - me * dates
        own = (wanted >= 0) & (wanted < dates)
        own_at = jnp.clip(wanted, 0, dates - 1)
        other_at = jnp.clip(jnp.where(me < half, wanted - dates, wanted + NEAR), 0, NEAR - 1)
        for c in range(2):
            here = pl.ds((2 * k + c) * rows, rows)

            @pl.when(own)
            def _():
                late_ref[here] = slc_ref[c, own_at]
                tiles_ref[k, c] = rim_ref[c, own_at]

            @pl.when(jnp.logical_not(own))
            def _():
                there = pl.multiple_of((2 * other_at + c) * rows, rows)
                late_ref[here] = inner_ref[pl.ds(there, rows)]
                tiles_ref[k, c] = place_strip(packed, 2 * other_at + c, strip)

    tiles = [tiles_ref[k, c] for k in range(late) for c in range(2)]
    write_strips(late_ref, gather_strips(tiles, strip))


def ending_kernel(plan, slc_ref, rim_ref, middle_ref, pairs_ref, _, end_ref, tiles_ref):
    me, strip = lax.axis_index("date"), lax.axis_index("strip")
    dates, late, rows = plan["dates"], plan["late"], plan["rows"]
    half = plan["devices"] // 2

    @pl.when((me == half) | (me == half - 1))
    def _():
        end = jnp.where(me < half, 0, 2 * half - 1)
        end_slot = jnp.where(me < half, 0, dates - late)
        packed = read_strips(middle_ref, rows)
        for k in range(late):
            date = end * dates + end_slot + k
            wanted = pairs_ref[PARTNER, date * plan["per_date"] + NEAR] - me * dates
            own = (wanted >= 0) & (wanted < dates)
            own_at = jnp.clip(wanted, 0, dates - 1)
            other_at = jnp.where(me < half, wanted - dates, wanted + NEAR)
            other_at = jnp.clip(other_at, 0, NEAR - 1)
            for c in range(2):
                here = pl.ds((2 * k + c) * rows, rows)

                @pl.when(own)
                def _():
                    end_ref[here] = slc_ref[c, own_at]
                    tiles_ref[k, c] = rim_ref[c, own_at]

                @pl.when(jnp.logical_not(own))
                def _():
                    there = pl.multiple_of((2 * other_at + c) * rows, rows)
                    end_ref[here] = middle_ref[pl.ds(there, rows)]
                    tiles_ref[k, c] = place_strip(packed, 2 * other_at + c, strip)

        tiles = [tiles_ref[k, c] for k in range(late) for c in range(2)]
        write_strips(end_ref, gather_strips(tiles, strip))


def bands_kernel(cols, out_ref):
    strip = lax.axis_index("strip")
    wide = out_ref.shape[3]
    reach = pl.program_id(0) + REACH_LO

    def band(places, targets):
        return (jnp.abs(places - targets) <= reach).astype(jnp.float32).astype(jnp.bfloat16)

    def indices(shape):
        return lax.broadcasted_iota(jnp.int32, shape, 0), lax.broadcasted_iota(jnp.int32, shape, 1)

    inside = band(*indices((wide, wide)))
    row, col = indices((TILE, wide))
    beyond = jnp.where(strip == 0, cols + row, row - TILE)
    first = band(jnp.where(row < INNER, wide + row, beyond), col)
    second = band(jnp.where(row < INNER, beyond, wide - TILE + row), col + wide)
    for n, part in enumerate((first, second)):
        out_ref[0, n, 0:wide] = inside
        out_ref[0, n, wide : 2 * wide] = inside
        out_ref[0, n, 2 * wide : 2 * wide + TILE] = part
        out_ref[0, n, 2 * wide + TILE : 2 * wide + 2 * TILE] = part


def split(values):
    high = values.astype(jnp.bfloat16)
    low = (values - high.astype(jnp.float32)).astype(jnp.bfloat16)
    return high, low


def put(ref, here, t, values):
    wide = 2 * TILE
    depth = 2 * wide + 2 * TILE
    for low, part in enumerate(split(values)):
        side = [n * depth + 2 * wide + low * TILE for n in range(2)]
        if t < 4:
            at = (t // 2) * depth + low * wide + (t % 2) * TILE
            ref[*here, at : at + TILE] = part
        if t == 2:
            ref[*here, side[0] : side[0] + INNER] = part[:, :INNER]
        if t == 1:
            ref[*here, side[1] + INNER : side[1] + TILE] = part[:, INNER:]
        if t == 4:
            ref[*here, side[0] + INNER : side[0] + TILE] = part[:, INNER:]
            ref[*here, side[1] : side[1] + INNER] = part[:, :INNER]


def tile_of(main, rim, t):
    return [
        (rim(c) if t == 4 else main(c, slice(t * TILE, (t + 1) * TILE))).astype(jnp.float32)
        for c in range(2)
    ]


class Pairs:
    def __init__(self, plan, lists, slc_ref, rim_ref, bands_ref, powers_ref, out_ref, scratch):
        self.plan = plan
        self.lists = lists
        self.slc_ref, self.rim_ref = slc_ref, rim_ref
        self.bands_ref, self.powers_ref, self.out_ref = bands_ref, powers_ref, out_ref
        (self.left_ref, self.stack_ref, self.other_ref, self.other_rim_ref, self.stage_ref,
         self.list_ref, self.sems) = scratch
        self.me, self.strip = lax.axis_index("date"), lax.axis_index("strip")

    def partner(self, pair):
        return self.lists[PARTNER, pair]

    def near_item(self, n):
        slot, kind = n // NEAR, lax.rem(n, NEAR)
        dates = self.plan["dates"]
        pair = (self.me * dates + slot) * self.plan["per_date"] + kind
        return slot, kind, self.partner(pair) - self.me * dates

    def near_list(self, chosen):
        count = 0
        for n in range(self.plan["dates"] * NEAR):
            self.list_ref[count] = n
            count = count + jnp.where(chosen(self.near_item(n)[2]), 1, 0)
        return count

    def own(self, local):
        return (local >= 0) & (local < self.plan["dates"])

    def in_middle(self, local):
        half, dates = self.plan["devices"] // 2, self.plan["dates"]
        if not self.plan["halves"]:
            return False
        return ((self.me == half) & (local < 0)) | ((self.me == half - 1) & (local >= dates))

    def own_other(self, index):
        return (
            lambda c, cols: self.slc_ref[c, index, :, cols],
            lambda c: self.rim_ref[c, index],
        )

    def fetched_other(self, x):
        return (
            lambda c, cols: self.other_ref[x, c, :, cols],
            lambda c: self.other_rim_ref[x, c],
        )

    def fetch_payload(self, x, ref, index):
        rows = self.plan["rows"]
        packed = read_strips(ref, rows)
        for c in range(2):
            at = pl.multiple_of((2 * index + c) * rows, rows)
            self.other_ref[x, c] = ref[pl.ds(at, rows)]
            self.other_rim_ref[x, c] = place_strip(packed, 2 * index + c, self.strip)

    def out_copy(self, stage, x, pair):
        return pltpu.make_async_copy(
            self.stage_ref.at[stage, x], self.out_ref.at[:, pair], self.sems.at[stage, x]
        )

    def run(self, count, work):
        steps = (count + 1) // 2

        def step(n, carry):
            stage = lax.rem(n, 2)

            @pl.when(n >= 2)
            def _():
                for x in range(2):
                    self.out_copy(stage, x, 0).wait()

            items = [work(x, jnp.minimum(2 * n + x, count - 1)) for x in range(2)]
            self.compute(stage, items)
            for x, (slot, kind, _, _) in enumerate(items):
                copy = self.out_copy(stage, x, slot * self.plan["per_date"] + kind)
                pl.when(2 * n + x < count)(copy.start)
            return carry

        lax.fori_loop(0, steps, step, 0)
        for back in (2, 1):
            for x in range(2):
                used = (steps >= back) & (2 * (steps - back) + x < count)
                pl.when(used)(self.out_copy(lax.rem(steps + back, 2), x, 0).wait)

    def compute(self, stage, items):
        plan = self.plan
        rows, dates, per_date = plan["rows"], plan["dates"], plan["per_date"]
        part = [(pl.ds(f * rows, rows),) for f in range(4)]
        depth = self.bands_ref.shape[2]
        wide = self.bands_ref.shape[3]
        heights, widths = [], []
        for slot, kind, _, _ in items:
            pair = (self.me * dates + slot) * per_date + kind
            heights.append(self.lists[HEIGHT, pair])
            widths.append(jnp.clip(self.lists[REACH, pair] - REACH_LO, 0, HALO - REACH_LO))
        for x, (slot, kind, other, other_power) in enumerate(items):
            left_ref = self.left_ref.at[x]
            left_ref[*part[2]] = self.powers_ref[slot]
            if other_power is not None:
                left_ref[*part[3]] = self.powers_ref[other_power]
            first = self.own_other(slot)
            for t in range(5):
                a_real, a_imag = tile_of(*first, t)
                b_real, b_imag = tile_of(*other, t)
                put(left_ref, part[0], t, a_real * b_real + a_imag * b_imag)
                put(left_ref, part[1], t, a_imag * b_real - a_real * b_imag)
                if other_power is None:
                    put(left_ref, part[3], t, b_real * b_real + b_imag * b_imag)
        for n in range(2):
            for x in range(2):
                ranged = jnp.dot(
                    self.left_ref[x, :, n * depth : (n + 1) * depth],
                    self.bands_ref[widths[x], n],
                    preferred_element_type=jnp.float32,
                )
                there = slice(n * wide, (n + 1) * wide)
                for low, values in enumerate(split(ranged)):
                    for f in range(4):
                        self.stack_ref[x, f, low * rows : (low + 1) * rows, there] = values[
                            f * rows : (f + 1) * rows
                        ]
        row = lax.broadcasted_iota(jnp.int32, (rows, 2 * rows), 0)
        col = lax.broadcasted_iota(jnp.int32, (rows, 2 * rows), 1)
        col = jnp.where(col < rows, col, col - rows)
        for x in range(2):
            band = (jnp.abs(row - col) <= heights[x]).astype(jnp.float32).astype(jnp.bfloat16)
            looked = [
                jnp.dot(band, self.stack_ref[x, f], preferred_element_type=jnp.float32)
                for f in range(4)
            ]
            inverse = lax.rsqrt(looked[2] * looked[3] + EPSILON)
            for c in range(2):
                self.stage_ref[stage, x, c] = looked[c] * inverse


def own_kernel(plan, lists, slc_ref, rim_ref, bands_ref, out_ref, powers_ref, *scratch):
    pairs = Pairs(plan, lists, slc_ref, rim_ref, bands_ref, powers_ref, out_ref, scratch)
    dates = plan["dates"]

    def power(slot, carry):
        for t in range(5):
            real, imag = tile_of(*pairs.own_other(slot), t)
            put(powers_ref, (slot, slice(None)), t, real * real + imag * imag)
        return carry

    lax.fori_loop(0, dates, power, 0)

    def work(x, n):
        slot, kind, local = pairs.near_item(pairs.list_ref[n])
        return slot, kind, pairs.own_other(local), local

    pairs.run(pairs.near_list(pairs.own), work)


def rest_kernel(plan, lists, slc_ref, rim_ref, bands_ref, powers_ref, inner_ref, outer_ref,
                middle_ref, _sent, _late, _, out_ref, *scratch):
    pairs = Pairs(plan, lists, slc_ref, rim_ref, bands_ref, powers_ref, out_ref, scratch)
    dates = plan["dates"]
    upper = pairs.me >= plan["devices"] // 2 if plan["halves"] else True

    def work(x, n):
        slot, kind, local = pairs.near_item(pairs.list_ref[n])
        below = local < 0
        index = jnp.clip(jnp.where(below, local + NEAR, local - dates), 0, NEAR - 1)
        inner, middle = below == upper, pairs.in_middle(local)
        sources = (
            (jnp.logical_not(inner), outer_ref),
            (inner & jnp.logical_not(middle), inner_ref),
            (inner & middle, middle_ref),
        )
        for chosen, ref in sources:
            pl.when(chosen)(functools.partial(pairs.fetch_payload, x, ref, index))
        return slot, kind, pairs.fetched_other(x), None

    pairs.run(pairs.near_list(lambda local: jnp.logical_not(pairs.own(local))), work)


def annual_kernel(plan, lists, slc_ref, rim_ref, bands_ref, powers_ref, ring_ref,
                  images_ref, strips_ref, _sent, _, out_ref, *scratch, is_late):
    mark_ref, *scratch = scratch
    mark_ref[...] = jnp.zeros_like(mark_ref)
    pairs = Pairs(plan, lists, slc_ref, rim_ref, bands_ref, powers_ref, out_ref, scratch)
    dates, late = plan["dates"], plan["late"]
    half = plan["devices"] // 2
    me, split_date = pairs.me, half * dates
    lower = me < half
    if is_late:
        base, count = jnp.where(lower, 0, dates - late), late
    else:
        base, count = jnp.where(lower, late, 0), dates - late

    def fetch_early(x, k, ref):
        packed = strips_ref[...]
        for c in range(2):
            pairs.other_ref[x, c] = ref[c, k]
            pairs.other_rim_ref[x, c] = place_strip(packed, 2 * k + c, pairs.strip)

    def work(x, k):
        slot = base + k
        date = me * dates + slot
        other = pairs.partner(date * plan["per_date"] + NEAR)
        if is_late:
            far = (me == 0) | (me == 2 * half - 1)
            ring_at = k
        else:
            far = (other < split_date) == lower
            ring_at = jnp.where(lower, other, other - (2 * split_date - NEAR))
            ring_at = jnp.clip(ring_at, 0, NEAR - 1)
        fetch = pairs.fetch_payload
        pl.when(far)(lambda: fetch(x, ring_ref, ring_at))
        near_side = jnp.logical_not(far)
        if is_late:
            pl.when(near_side)(lambda: fetch(x, images_ref, k))
        else:
            pl.when(near_side)(lambda: fetch_early(x, k, images_ref))
        return slot, NEAR, pairs.fetched_other(x), None

    pairs.run(count, work)


def plain_kernel(plan, lists, slc_ref, rim_ref, bands_ref, powers_ref, images_ref,
                 image_rim_ref, _, out_ref, *scratch):
    pairs = Pairs(plan, lists, slc_ref, rim_ref, bands_ref, powers_ref, out_ref, scratch)

    def work(x, slot):
        other = (
            lambda c, cols: images_ref[c, slot, :, cols],
            lambda c: image_rim_ref[c, slot],
        )
        return slot, NEAR, other, None

    pairs.run(plan["dates"], work)


def arrivals_by_distance(slc, pair_list, plan):
    dates, per_date, devices = plan["dates"], plan["per_date"], plan["devices"]
    total = dates * devices
    me = lax.axis_index("date")
    annual_of = pair_list[:, 1].reshape(total, per_date)[:, per_date - 1]
    sums = [None] * dates
    for direction in (1, -1):
        by_distance = {}
        for slot in range(dates):
            for gap in range(plan["year"], plan["year"] + 3):
                distance = (slot + direction * gap) // dates
                by_distance.setdefault(distance, set()).add(slot)
        for distance in sorted(by_distance):
            slots = sorted(by_distance[distance])
            wanted_by = (me - distance) * dates + jnp.array(slots, dtype=jnp.int32)
            inside = (wanted_by >= 0) & (wanted_by < total)
            local = jnp.take(annual_of, jnp.clip(wanted_by, 0, total - 1)) - me * dates
            usable = inside & (local >= 0) & (local < dates)
            packed = jnp.take(slc, jnp.clip(local, 0, dates - 1), axis=1)
            packed = jnp.where(usable[None, :, None, None], packed, jnp.zeros_like(packed))
            route = [(i + distance, i) for i in range(devices) if 0 <= i + distance < devices]
            arrived = lax.ppermute(packed, "date", route)
            for n, slot in enumerate(slots):
                part = arrived[:, n]
                sums[slot] = part if sums[slot] is None else sums[slot] + part
    return jnp.stack(sums, axis=1)


def payload_of(images, rim, strip):
    planes, count, rows, cols = images.shape
    edges = jnp.where(strip == 0, rim[..., :HALO], rim[..., TILE - HALO :])
    edges = jnp.transpose(edges, (2, 1, 0, 3)).reshape(rows, count * planes * HALO)
    edges = jnp.pad(edges, ((0, 0), (0, TILE - edges.shape[1])))
    part = rows * TILE // cols
    edges = jnp.transpose(edges.reshape(rows // part, part, TILE), (1, 0, 2)).reshape(part, cols)
    stacked = jnp.transpose(images, (1, 0, 2, 3)).reshape(count * planes * rows, cols)
    return jnp.concatenate([stacked, edges], axis=0)


def body(slc, pair_list, az_half, rng_half):
    planes, dates, rows, cols = slc.shape
    devices = lax.axis_size("date")
    total = dates * devices
    per_date = pair_list.shape[0] // total
    year = min(YEAR, total // 2 - 2)
    half = devices // 2
    late = half * dates - year
    halves = devices % 2 == 0 and 0 < late <= NEAR and 2 * late <= dates
    halves = halves and 2 * (dates - late) * HALO <= TILE
    plan = {
        "dates": dates,
        "devices": devices,
        "per_date": per_date,
        "year": year,
        "late": late,
        "rows": rows,
        "cols": cols,
        "pairs": total * per_date,
        "halves": halves,
    }
    dtype = slc.dtype
    rim_rows = rows * TILE // cols
    pairs = pair_list.T
    lists = jnp.concatenate([pairs, az_half[None], rng_half[None]])
    swap_strips = [(0, 1), (1, 0)]

    def images(count):
        return jax.ShapeDtypeStruct((planes, count, rows, cols), dtype)

    def rim_shape(count):
        return jax.ShapeDtypeStruct((planes, count, rows, TILE), dtype)

    def payload_shape(count):
        return jax.ShapeDtypeStruct((planes * count * rows + rim_rows, cols), dtype)

    def swapped_rims(values):
        out = pl.pallas_call(
            rim_kernel,
            out_shape=rim_shape(values.shape[1]),
            in_specs=[ANY],
            out_specs=VMEM,
            scratch_shapes=[pltpu.SemaphoreType.DMA],
            compiler_params=limit(WORK_MIB),
            name="rim_blocks",
        )(values)
        return lax.ppermute(out, "strip", swap_strips)

    def cost(flops):
        return pl.CostEstimate(flops=flops, bytes_accessed=1, transcendentals=0)

    wide = cols // 2
    widths = HALO - REACH_LO + 1
    band_shape = (2, 2 * wide + 2 * TILE, wide)
    bands = pl.pallas_call(
        functools.partial(bands_kernel, cols),
        grid=(widths,),
        out_shape=jax.ShapeDtypeStruct((widths, *band_shape), jnp.bfloat16),
        out_specs=pl.BlockSpec((1, *band_shape), lambda n: (n, 0, 0, 0)),
        compiler_params=limit(WORK_MIB),
        cost_estimate=cost(1),
        name="range_bands",
    )()
    if halves:
        swap = [(i, (i + half) % devices) for i in range(devices)]
        both = ("date", "strip")
        early, rim, strips = pl.pallas_call(
            functools.partial(early_kernel, plan),
            out_shape=(
                images(dates - late),
                rim_shape(dates),
                jax.ShapeDtypeStruct((rows, TILE), dtype),
            ),
            in_specs=[ANY, SMEM],
            out_specs=(VMEM, VMEM, VMEM),
            scratch_shapes=[
                pltpu.VMEM((dates - late, planes, rows, TILE), dtype),
                pltpu.SemaphoreType.DMA((dates - late,)),
                pltpu.SemaphoreType.DMA((dates - late,)),
                pltpu.SemaphoreType.DMA,
            ],
            compiler_params=limit(FIRST_MIB),
            name="early_images",
        )(slc, pairs)
        early = lax.ppermute(early, "date", swap)
        rim = lax.ppermute(rim, "strip", swap_strips)
        inner, outer = pl.pallas_call(
            functools.partial(beside_kernel, plan),
            out_shape=(payload_shape(NEAR), payload_shape(NEAR)),
            in_specs=[ANY, VMEM],
            out_specs=(VMEM, VMEM),
            scratch_shapes=[pltpu.SemaphoreType.DMA((2, NEAR, 2))],
            compiler_params=limit(WORK_MIB),
            name="beside_images",
        )(slc, rim)
        down = [(i, (i - 1) % half) for i in range(half)]
        down += [(half + i, half + (i + 1) % half) for i in range(half)]
        strips = lax.ppermute(
            strips, both, [(2 * a + s, 2 * b + 1 - s) for a, b in swap for s in (0, 1)]
        )
        up = [(b, a) for a, b in down if b not in (half - 1, half)]
        across = [(half - 1, half), (half, half - 1)]
        second = outer
        outer = lax.ppermute(second, "date", up)
        middle = lax.ppermute(second, "date", across)
        inner = lax.ppermute(inner, "date", down)
    else:
        rim = swapped_rims(slc)
        annual = arrivals_by_distance(slc, pair_list, plan)
        strip = lax.axis_index("strip")
        ups = [(i, i + 1) for i in range(devices - 1)]
        inner = payload_of(slc[:, dates - NEAR :], rim[:, dates - NEAR :], strip)
        outer = payload_of(slc[:, :NEAR], rim[:, :NEAR], strip)
        inner = lax.ppermute(inner, "date", ups)
        outer = lax.ppermute(outer, "date", [(b, a) for a, b in ups])

    out_shape = jax.ShapeDtypeStruct((planes, dates * per_date, rows, cols), jnp.float32)
    depth = 2 * band_shape[1]
    scratch = [
        pltpu.VMEM((2, 4 * rows, depth), jnp.bfloat16),
        pltpu.VMEM((2, 4, 2 * rows, cols), jnp.bfloat16),
        pltpu.VMEM((2, planes, rows, cols), dtype),
        pltpu.VMEM((2, planes, rows, TILE), dtype),
        pltpu.VMEM((2, 2, planes, rows, cols), jnp.float32),
        pltpu.SMEM((dates * NEAR + 1,), jnp.int32),
        pltpu.SemaphoreType.DMA((2, 2)),
    ]

    out, powers = pl.pallas_call(
        functools.partial(own_kernel, plan),
        out_shape=(out_shape, jax.ShapeDtypeStruct((dates, rows, depth), jnp.bfloat16)),
        in_specs=[SMEM] + [VMEM] * 3,
        out_specs=(ANY, VMEM),
        scratch_shapes=scratch,
        compiler_params=limit(WORK_MIB),
        cost_estimate=cost(OWN_FLOPS),
        name="own_pairs",
    )(lists, slc, rim, bands)

    def more_pairs(kernel, out, others, name, flops=1, marks=()):
        return pl.pallas_call(
            functools.partial(kernel, plan),
            out_shape=(out_shape, *marks),
            in_specs=[SMEM] + [VMEM] * (4 + len(others)) + [ANY],
            out_specs=(ANY, *[VMEM for mark in marks]),
            scratch_shapes=scratch,
            input_output_aliases={5 + len(others): 0},
            compiler_params=limit(WORK_MIB),
            cost_estimate=cost(flops),
            name=name,
        )(lists, slc, rim, bands, powers, *others, out)

    if halves:
        payload = sent = pl.pallas_call(
            functools.partial(late_kernel, plan),
            out_shape=payload_shape(late),
            in_specs=[VMEM, VMEM, VMEM, SMEM, ANY, ANY],
            out_specs=VMEM,
            scratch_shapes=[pltpu.VMEM((late, planes, rows, TILE), dtype)],
            compiler_params=limit(WORK_MIB),
            name="late_images",
        )(slc, rim, inner, lists, powers, strips)
        late_swap = [(a, b) for a, b in swap if a not in (half - 1, half)]
        payload = lax.ppermute(payload, "date", late_swap)
    if halves:
        early_pairs = functools.partial(annual_kernel, is_late=False)
        marks = (jax.ShapeDtypeStruct((8, TILE), jnp.float32),)
        others = (inner, early, strips, sent)
        out, mark = more_pairs(early_pairs, out, others, "annual_pairs", ANNUAL_FLOPS, marks)
        ending = ended = pl.pallas_call(
            functools.partial(ending_kernel, plan),
            out_shape=payload_shape(late),
            in_specs=[VMEM, VMEM, VMEM, SMEM, ANY],
            out_specs=VMEM,
            scratch_shapes=[pltpu.VMEM((late, planes, rows, TILE), dtype)],
            compiler_params=limit(WORK_MIB),
            name="ending_images",
        )(slc, rim, middle, lists, mark)
        ending = lax.ppermute(ending, "date", [(half - 1, 0), (half, devices - 1)])
        (out,) = more_pairs(rest_kernel, out, (inner, outer, middle, ended, payload), "near_pairs")
        late_pairs = functools.partial(annual_kernel, is_late=True)
        out, _ = more_pairs(
            late_pairs, out, (ending, payload, strips, sent), "last_pairs", 1, marks
        )
    else:
        (out,) = more_pairs(rest_kernel, out, (inner, outer, inner, inner, inner), "near_pairs")
        (out,) = more_pairs(plain_kernel, out, (annual, swapped_rims(annual)), "annual_pairs")
    return out


def solution(mesh):
    placed = (P(None, "date", "groups", "strip"), P(), P(), P())
    return jax.shard_map(
        body,
        mesh=mesh,
        in_specs=placed,
        out_specs=P(None, "date", "groups", "strip"),
        check_vma=False,
    )
```

```python
import functools

import jax
import jax.numpy as jnp
from jax import lax
from jax.experimental import pallas as pl
from jax.experimental.pallas import tpu as pltpu
from jax.sharding import PartitionSpec as P

HALO = 16
REACH_LO = 12
NEAR = 3
YEAR = 29
EPSILON = 1e-06
TILE = 128
INNER = TILE // 2
OWN_FLOPS = 4_000_000_000
ANNUAL_FLOPS = 8_000_000_000
PARTNER, HEIGHT, REACH = 1, 2, 3
WORK_MIB = 16
FIRST_MIB = 56
ANY = pl.BlockSpec(memory_space=pl.ANY)
SMEM = pl.BlockSpec(memory_space=pltpu.SMEM)
VMEM = pl.BlockSpec(memory_space=pltpu.VMEM)


def limit(mebibytes):
    return pltpu.CompilerParams(vmem_limit_bytes=mebibytes * 1024 * 1024)


def run_copies(copies):
    for copy in copies:
        copy.start()
    for copy in copies:
        copy.wait()


def gather_strips(tiles, side):
    lane = lax.broadcasted_iota(jnp.int32, tiles[0].shape, 1)
    packed = jnp.zeros(tiles[0].shape, jnp.float32)
    for n, tile in enumerate(tiles):
        spot = n * HALO
        moved = pltpu.roll(tile.astype(jnp.float32), spot + side * HALO, 1)
        packed = jnp.where((lane >= spot) & (lane < spot + HALO), moved, packed)
    return packed.astype(jnp.bfloat16)


def place_strip(packed, n, side):
    shift = 2 * TILE - (n + side) * HALO
    return pltpu.roll(packed.astype(jnp.float32), lax.rem(shift, TILE), 1).astype(jnp.bfloat16)


def write_strips(out_ref, packed):
    rows, cols = packed.shape[0], out_ref.shape[1]
    part = rows * TILE // cols
    base = out_ref.shape[0] - part
    for n in range(rows // part):
        out_ref[base:, n * TILE : (n + 1) * TILE] = packed[n * part : (n + 1) * part]


def read_strips(ref, rows):
    cols = ref.shape[1]
    base = ref.shape[0] - rows * TILE // cols
    return jnp.concatenate(
        [ref[base:, n * TILE : (n + 1) * TILE] for n in range(cols // TILE)], axis=0
    )


def wanted_images(plan, pairs_ref):
    me = lax.axis_index("date")
    dates, half = plan["dates"], plan["devices"] // 2
    mate = lax.rem(me + half, 2 * half)
    wanted = []
    for k in range(dates - plan["late"]):
        date = mate * dates + jnp.where(mate < half, plan["late"], 0) + k
        at = pairs_ref[PARTNER, date * plan["per_date"] + NEAR] - me * dates
        wanted.append(jnp.clip(at, 0, dates - 1))
    return wanted


def image_copies(slc_ref, wanted, early_ref, sems):
    return [
        pltpu.make_async_copy(slc_ref.at[:, at], early_ref.at[:, k], sems.at[k])
        for k, at in enumerate(wanted)
    ]


def early_kernel(plan, slc_ref, pairs_ref, early_ref, rim_ref, sems, rim_sem):
    strip, cols = lax.axis_index("strip"), plan["cols"]
    start = pl.multiple_of(jnp.where(strip == 0, cols - TILE, 0), TILE)
    rim_copy = pltpu.make_async_copy(slc_ref.at[:, :, :, pl.ds(start, TILE)], rim_ref, rim_sem)
    early_copies = image_copies(slc_ref, wanted_images(plan, pairs_ref), early_ref, sems)
    run_copies([rim_copy] + early_copies)


def edges_kernel(plan, slc_ref, pairs_ref, _, strips_ref, tiles_ref, tile_sems):
    strip, cols = lax.axis_index("strip"), plan["cols"]
    start = pl.multiple_of(jnp.where(strip == 0, cols - TILE, 0), TILE)
    wanted = wanted_images(plan, pairs_ref)
    run_copies(
        [
            pltpu.make_async_copy(
                slc_ref.at[:, at, :, pl.ds(start, TILE)], tiles_ref.at[k], tile_sems.at[k]
            )
            for k, at in enumerate(wanted)
        ]
    )
    tiles = [tiles_ref[k, c] for k in range(len(wanted)) for c in range(2)]
    strips_ref[...] = gather_strips(tiles, 1 - strip)


def rim_kernel(slc_ref, rim_ref, sem):
    cols = slc_ref.shape[3]
    start = pl.multiple_of(jnp.where(lax.axis_index("strip") == 0, cols - TILE, 0), TILE)
    run_copies([pltpu.make_async_copy(slc_ref.at[:, :, :, pl.ds(start, TILE)], rim_ref, sem)])


def beside_kernel(plan, slc_ref, rim_ref, inner_ref, outer_ref, sems):
    me, strip = lax.axis_index("date"), lax.axis_index("strip")
    dates, rows = plan["dates"], plan["rows"]
    upper = me >= plan["devices"] // 2
    last = dates - NEAR
    copies = []
    firsts = (jnp.where(upper, last, 0), jnp.where(upper, 0, last))
    for r, (out_ref, first) in enumerate(zip((inner_ref, outer_ref), firsts)):
        for k in range(NEAR):
            for c in range(2):
                here = out_ref.at[pl.ds((2 * k + c) * rows, rows)]
                copies.append(
                    pltpu.make_async_copy(slc_ref.at[c, first + k], here, sems.at[r, k, c])
                )
    for copy in copies:
        copy.start()
    for out_ref, first in zip((inner_ref, outer_ref), firsts):
        tiles = [rim_ref[c, first + k] for k in range(NEAR) for c in range(2)]
        write_strips(out_ref, gather_strips(tiles, strip))
    for copy in copies:
        copy.wait()


def late_kernel(plan, slc_ref, rim_ref, inner_ref, pairs_ref, *refs):
    late_ref, tiles_ref = refs[-2:]
    me, strip = lax.axis_index("date"), lax.axis_index("strip")
    dates, late, rows = plan["dates"], plan["late"], plan["rows"]
    half = plan["devices"] // 2
    mate = lax.rem(me + half, 2 * half)
    mate_slot = jnp.where(mate < half, 0, dates - late)
    packed = read_strips(inner_ref, rows)
    for k in range(late):
        date = mate * dates + mate_slot + k
        wanted = pairs_ref[PARTNER, date * plan["per_date"] + NEAR] - me * dates
        own = (wanted >= 0) & (wanted < dates)
        own_at = jnp.clip(wanted, 0, dates - 1)
        other_at = jnp.clip(jnp.where(me < half, wanted - dates, wanted + NEAR), 0, NEAR - 1)
        for c in range(2):
            here = pl.ds((2 * k + c) * rows, rows)

            @pl.when(own)
            def _():
                late_ref[here] = slc_ref[c, own_at]
                tiles_ref[k, c] = rim_ref[c, own_at]

            @pl.when(jnp.logical_not(own))
            def _():
                there = pl.multiple_of((2 * other_at + c) * rows, rows)
                late_ref[here] = inner_ref[pl.ds(there, rows)]
                tiles_ref[k, c] = place_strip(packed, 2 * other_at + c, strip)

    tiles = [tiles_ref[k, c] for k in range(late) for c in range(2)]
    write_strips(late_ref, gather_strips(tiles, strip))


def bands_kernel(cols, out_ref):
    strip = lax.axis_index("strip")
    wide = out_ref.shape[3]
    reach = pl.program_id(0) + REACH_LO

    def band(places, targets):
        return (jnp.abs(places - targets) <= reach).astype(jnp.float32).astype(jnp.bfloat16)

    def indices(shape):
        return lax.broadcasted_iota(jnp.int32, shape, 0), lax.broadcasted_iota(jnp.int32, shape, 1)

    inside = band(*indices((wide, wide)))
    row, col = indices((TILE, wide))
    beyond = jnp.where(strip == 0, cols + row, row - TILE)
    first = band(jnp.where(row < INNER, wide + row, beyond), col)
    second = band(jnp.where(row < INNER, beyond, wide - TILE + row), col + wide)
    for n, part in enumerate((first, second)):
        out_ref[0, n, 0:wide] = inside
        out_ref[0, n, wide : 2 * wide] = inside
        out_ref[0, n, 2 * wide : 2 * wide + TILE] = part
        out_ref[0, n, 2 * wide + TILE : 2 * wide + 2 * TILE] = part


def split(values):
    high = values.astype(jnp.bfloat16)
    low = (values - high.astype(jnp.float32)).astype(jnp.bfloat16)
    return high, low


def put(ref, here, t, values):
    wide = 2 * TILE
    depth = 2 * wide + 2 * TILE
    for low, part in enumerate(split(values)):
        side = [n * depth + 2 * wide + low * TILE for n in range(2)]
        if t < 4:
            at = (t // 2) * depth + low * wide + (t % 2) * TILE
            ref[*here, at : at + TILE] = part
        if t == 2:
            ref[*here, side[0] : side[0] + INNER] = part[:, :INNER]
        if t == 1:
            ref[*here, side[1] + INNER : side[1] + TILE] = part[:, INNER:]
        if t == 4:
            ref[*here, side[0] + INNER : side[0] + TILE] = part[:, INNER:]
            ref[*here, side[1] : side[1] + INNER] = part[:, :INNER]


def tile_of(main, rim, t):
    return [
        (rim(c) if t == 4 else main(c, slice(t * TILE, (t + 1) * TILE))).astype(jnp.float32)
        for c in range(2)
    ]


class Pairs:
    def __init__(self, plan, lists, slc_ref, rim_ref, bands_ref, powers_ref, out_ref, scratch):
        self.plan = plan
        self.lists = lists
        self.slc_ref, self.rim_ref = slc_ref, rim_ref
        self.bands_ref, self.powers_ref, self.out_ref = bands_ref, powers_ref, out_ref
        (self.left_ref, self.stack_ref, self.other_ref, self.other_rim_ref, self.stage_ref,
         self.list_ref, self.sems) = scratch
        self.me, self.strip = lax.axis_index("date"), lax.axis_index("strip")

    def partner(self, pair):
        return self.lists[PARTNER, pair]

    def near_item(self, n):
        slot, kind = n // NEAR, lax.rem(n, NEAR)
        dates = self.plan["dates"]
        pair = (self.me * dates + slot) * self.plan["per_date"] + kind
        return slot, kind, self.partner(pair) - self.me * dates

    def near_list(self, chosen):
        count = 0
        for n in range(self.plan["dates"] * NEAR):
            self.list_ref[count] = n
            count = count + jnp.where(chosen(self.near_item(n)[2]), 1, 0)
        return count

    def own(self, local):
        return (local >= 0) & (local < self.plan["dates"])

    def in_middle(self, local):
        half, dates = self.plan["devices"] // 2, self.plan["dates"]
        if not self.plan["halves"]:
            return False
        return ((self.me == half) & (local < 0)) | ((self.me == half - 1) & (local >= dates))

    def own_other(self, index):
        return (
            lambda c, cols: self.slc_ref[c, index, :, cols],
            lambda c: self.rim_ref[c, index],
        )

    def fetched_other(self, x):
        return (
            lambda c, cols: self.other_ref[x, c, :, cols],
            lambda c: self.other_rim_ref[x, c],
        )

    def fetch_payload(self, x, ref, index):
        rows = self.plan["rows"]
        packed = read_strips(ref, rows)
        for c in range(2):
            at = pl.multiple_of((2 * index + c) * rows, rows)
            self.other_ref[x, c] = ref[pl.ds(at, rows)]
            self.other_rim_ref[x, c] = place_strip(packed, 2 * index + c, self.strip)

    def out_copy(self, stage, x, pair):
        return pltpu.make_async_copy(
            self.stage_ref.at[stage, x], self.out_ref.at[:, pair], self.sems.at[stage, x]
        )

    def run(self, count, work):
        steps = (count + 1) // 2

        def step(n, carry):
            stage = lax.rem(n, 2)

            @pl.when(n >= 2)
            def _():
                for x in range(2):
                    self.out_copy(stage, x, 0).wait()

            items = [work(x, jnp.minimum(2 * n + x, count - 1)) for x in range(2)]
            self.compute(stage, items)
            for x, (slot, kind, _, _) in enumerate(items):
                copy = self.out_copy(stage, x, slot * self.plan["per_date"] + kind)
                pl.when(2 * n + x < count)(copy.start)
            return carry

        lax.fori_loop(0, steps, step, 0)
        for back in (2, 1):
            for x in range(2):
                used = (steps >= back) & (2 * (steps - back) + x < count)
                pl.when(used)(self.out_copy(lax.rem(steps + back, 2), x, 0).wait)

    def compute(self, stage, items):
        plan = self.plan
        rows, dates, per_date = plan["rows"], plan["dates"], plan["per_date"]
        part = [(pl.ds(f * rows, rows),) for f in range(4)]
        depth = self.bands_ref.shape[2]
        wide = self.bands_ref.shape[3]
        heights, widths = [], []
        for slot, kind, _, _ in items:
            pair = (self.me * dates + slot) * per_date + kind
            heights.append(self.lists[HEIGHT, pair])
            widths.append(jnp.clip(self.lists[REACH, pair] - REACH_LO, 0, HALO - REACH_LO))
        for x, (slot, kind, other, other_power) in enumerate(items):
            left_ref = self.left_ref.at[x]
            left_ref[*part[2]] = self.powers_ref[slot]
            if other_power is not None:
                left_ref[*part[3]] = self.powers_ref[other_power]
            first = self.own_other(slot)
            for t in range(5):
                a_real, a_imag = tile_of(*first, t)
                b_real, b_imag = tile_of(*other, t)
                put(left_ref, part[0], t, a_real * b_real + a_imag * b_imag)
                put(left_ref, part[1], t, a_imag * b_real - a_real * b_imag)
                if other_power is None:
                    put(left_ref, part[3], t, b_real * b_real + b_imag * b_imag)
        for n in range(2):
            for x in range(2):
                ranged = jnp.dot(
                    self.left_ref[x, :, n * depth : (n + 1) * depth],
                    self.bands_ref[widths[x], n],
                    preferred_element_type=jnp.float32,
                )
                there = slice(n * wide, (n + 1) * wide)
                for low, values in enumerate(split(ranged)):
                    for f in range(4):
                        self.stack_ref[x, f, low * rows : (low + 1) * rows, there] = values[
                            f * rows : (f + 1) * rows
                        ]
        row = lax.broadcasted_iota(jnp.int32, (rows, 2 * rows), 0)
        col = lax.broadcasted_iota(jnp.int32, (rows, 2 * rows), 1)
        col = jnp.where(col < rows, col, col - rows)
        for x in range(2):
            band = (jnp.abs(row - col) <= heights[x]).astype(jnp.float32).astype(jnp.bfloat16)
            looked = [
                jnp.dot(band, self.stack_ref[x, f], preferred_element_type=jnp.float32)
                for f in range(4)
            ]
            inverse = lax.rsqrt(looked[2] * looked[3] + EPSILON)
            for c in range(2):
                self.stage_ref[stage, x, c] = looked[c] * inverse


def own_kernel(plan, lists, slc_ref, rim_ref, bands_ref, out_ref, powers_ref, *scratch):
    pairs = Pairs(plan, lists, slc_ref, rim_ref, bands_ref, powers_ref, out_ref, scratch)
    dates = plan["dates"]

    def power(slot, carry):
        for t in range(5):
            real, imag = tile_of(*pairs.own_other(slot), t)
            put(powers_ref, (slot, slice(None)), t, real * real + imag * imag)
        return carry

    lax.fori_loop(0, dates, power, 0)

    def work(x, n):
        slot, kind, local = pairs.near_item(pairs.list_ref[n])
        return slot, kind, pairs.own_other(local), local

    pairs.run(pairs.near_list(pairs.own), work)


def rest_kernel(plan, lists, slc_ref, rim_ref, bands_ref, powers_ref, inner_ref, outer_ref,
                middle_ref, _, out_ref, *scratch):
    pairs = Pairs(plan, lists, slc_ref, rim_ref, bands_ref, powers_ref, out_ref, scratch)
    dates = plan["dates"]
    upper = pairs.me >= plan["devices"] // 2 if plan["halves"] else True

    def work(x, n):
        slot, kind, local = pairs.near_item(pairs.list_ref[n])
        below = local < 0
        index = jnp.clip(jnp.where(below, local + NEAR, local - dates), 0, NEAR - 1)
        inner, middle = below == upper, pairs.in_middle(local)
        sources = (
            (jnp.logical_not(inner), outer_ref),
            (inner & jnp.logical_not(middle), inner_ref),
            (inner & middle, middle_ref),
        )
        for chosen, ref in sources:
            pl.when(chosen)(functools.partial(pairs.fetch_payload, x, ref, index))
        return slot, kind, pairs.fetched_other(x), None

    pairs.run(pairs.near_list(lambda local: jnp.logical_not(pairs.own(local))), work)


def annual_kernel(plan, lists, slc_ref, rim_ref, bands_ref, powers_ref, ring_ref,
                  images_ref, strips_ref, _sent, _, out_ref, *scratch, is_late):
    pairs = Pairs(plan, lists, slc_ref, rim_ref, bands_ref, powers_ref, out_ref, scratch)
    dates, late = plan["dates"], plan["late"]
    half = plan["devices"] // 2
    me, split_date = pairs.me, half * dates
    lower = me < half
    if is_late:
        base, count = jnp.where(lower, 0, dates - late), late
    else:
        base, count = jnp.where(lower, late, 0), dates - late

    def fetch_early(x, k, ref):
        packed = strips_ref[...]
        for c in range(2):
            pairs.other_ref[x, c] = ref[c, k]
            pairs.other_rim_ref[x, c] = place_strip(packed, 2 * k + c, pairs.strip)

    def work(x, k):
        slot = base + k
        date = me * dates + slot
        other = pairs.partner(date * plan["per_date"] + NEAR)
        far = (other < split_date) == lower
        end = 2 * split_date
        if is_late:
            ring_at = jnp.where(lower, other - (split_date - NEAR), other - split_date)
        else:
            ring_at = jnp.where(lower, other, other - (end - NEAR))
        ring_at = jnp.clip(ring_at, 0, NEAR - 1)
        fetch = pairs.fetch_payload
        pl.when(far)(lambda: fetch(x, ring_ref, ring_at))
        near_side = jnp.logical_not(far)
        if is_late:
            pl.when(near_side)(lambda: fetch(x, images_ref, k))
        else:
            pl.when(near_side)(lambda: fetch_early(x, k, images_ref))
        return slot, NEAR, pairs.fetched_other(x), None

    pairs.run(count, work)


def plain_kernel(plan, lists, slc_ref, rim_ref, bands_ref, powers_ref, images_ref,
                 image_rim_ref, _, out_ref, *scratch):
    pairs = Pairs(plan, lists, slc_ref, rim_ref, bands_ref, powers_ref, out_ref, scratch)

    def work(x, slot):
        other = (
            lambda c, cols: images_ref[c, slot, :, cols],
            lambda c: image_rim_ref[c, slot],
        )
        return slot, NEAR, other, None

    pairs.run(plan["dates"], work)


def arrivals_by_distance(slc, pair_list, plan):
    dates, per_date, devices = plan["dates"], plan["per_date"], plan["devices"]
    total = dates * devices
    me = lax.axis_index("date")
    annual_of = pair_list[:, 1].reshape(total, per_date)[:, per_date - 1]
    sums = [None] * dates
    for direction in (1, -1):
        by_distance = {}
        for slot in range(dates):
            for gap in range(plan["year"], plan["year"] + 3):
                distance = (slot + direction * gap) // dates
                by_distance.setdefault(distance, set()).add(slot)
        for distance in sorted(by_distance):
            slots = sorted(by_distance[distance])
            wanted_by = (me - distance) * dates + jnp.array(slots, dtype=jnp.int32)
            inside = (wanted_by >= 0) & (wanted_by < total)
            local = jnp.take(annual_of, jnp.clip(wanted_by, 0, total - 1)) - me * dates
            usable = inside & (local >= 0) & (local < dates)
            packed = jnp.take(slc, jnp.clip(local, 0, dates - 1), axis=1)
            packed = jnp.where(usable[None, :, None, None], packed, jnp.zeros_like(packed))
            route = [(i + distance, i) for i in range(devices) if 0 <= i + distance < devices]
            arrived = lax.ppermute(packed, "date", route)
            for n, slot in enumerate(slots):
                part = arrived[:, n]
                sums[slot] = part if sums[slot] is None else sums[slot] + part
    return jnp.stack(sums, axis=1)


def payload_of(images, rim, strip):
    planes, count, rows, cols = images.shape
    edges = jnp.where(strip == 0, rim[..., :HALO], rim[..., TILE - HALO :])
    edges = jnp.transpose(edges, (2, 1, 0, 3)).reshape(rows, count * planes * HALO)
    edges = jnp.pad(edges, ((0, 0), (0, TILE - edges.shape[1])))
    part = rows * TILE // cols
    edges = jnp.transpose(edges.reshape(rows // part, part, TILE), (1, 0, 2)).reshape(part, cols)
    stacked = jnp.transpose(images, (1, 0, 2, 3)).reshape(count * planes * rows, cols)
    return jnp.concatenate([stacked, edges], axis=0)


def body(slc, pair_list, az_half, rng_half):
    planes, dates, rows, cols = slc.shape
    devices = lax.axis_size("date")
    total = dates * devices
    per_date = pair_list.shape[0] // total
    year = min(YEAR, total // 2 - 2)
    half = devices // 2
    late = half * dates - year
    halves = devices % 2 == 0 and 0 < late <= NEAR and 2 * late <= dates
    halves = halves and 2 * (dates - late) * HALO <= TILE
    plan = {
        "dates": dates,
        "devices": devices,
        "per_date": per_date,
        "year": year,
        "late": late,
        "rows": rows,
        "cols": cols,
        "pairs": total * per_date,
        "halves": halves,
    }
    dtype = slc.dtype
    rim_rows = rows * TILE // cols
    pairs = pair_list.T
    lists = jnp.concatenate([pairs, az_half[None], rng_half[None]])
    swap_strips = [(0, 1), (1, 0)]

    def images(count):
        return jax.ShapeDtypeStruct((planes, count, rows, cols), dtype)

    def rim_shape(count):
        return jax.ShapeDtypeStruct((planes, count, rows, TILE), dtype)

    def payload_shape(count):
        return jax.ShapeDtypeStruct((planes * count * rows + rim_rows, cols), dtype)

    def swapped_rims(values):
        out = pl.pallas_call(
            rim_kernel,
            out_shape=rim_shape(values.shape[1]),
            in_specs=[ANY],
            out_specs=VMEM,
            scratch_shapes=[pltpu.SemaphoreType.DMA],
            compiler_params=limit(WORK_MIB),
            name="rim_blocks",
        )(values)
        return lax.ppermute(out, "strip", swap_strips)

    def cost(flops):
        return pl.CostEstimate(flops=flops, bytes_accessed=1, transcendentals=0)

    wide = cols // 2
    widths = HALO - REACH_LO + 1
    band_shape = (2, 2 * wide + 2 * TILE, wide)
    bands = pl.pallas_call(
        functools.partial(bands_kernel, cols),
        grid=(widths,),
        out_shape=jax.ShapeDtypeStruct((widths, *band_shape), jnp.bfloat16),
        out_specs=pl.BlockSpec((1, *band_shape), lambda n: (n, 0, 0, 0)),
        compiler_params=limit(WORK_MIB),
        cost_estimate=cost(1),
        name="range_bands",
    )()
    if halves:
        swap = [(i, (i + half) % devices) for i in range(devices)]
        both = ("date", "strip")
        early, rim = pl.pallas_call(
            functools.partial(early_kernel, plan),
            out_shape=(images(dates - late), rim_shape(dates)),
            in_specs=[ANY, SMEM],
            out_specs=(VMEM, VMEM),
            scratch_shapes=[pltpu.SemaphoreType.DMA((dates - late,)), pltpu.SemaphoreType.DMA],
            compiler_params=limit(FIRST_MIB),
            name="early_images",
        )(slc, pairs)
        strips = pl.pallas_call(
            functools.partial(edges_kernel, plan),
            out_shape=jax.ShapeDtypeStruct((rows, TILE), dtype),
            in_specs=[ANY, SMEM, ANY],
            out_specs=VMEM,
            scratch_shapes=[
                pltpu.VMEM((dates - late, planes, rows, TILE), dtype),
                pltpu.SemaphoreType.DMA((dates - late,)),
            ],
            compiler_params=limit(FIRST_MIB),
            name="early_edges",
        )(slc, pairs, rim)
        early = lax.ppermute(early, "date", swap)
        rim = lax.ppermute(rim, "strip", swap_strips)
        inner, outer = pl.pallas_call(
            functools.partial(beside_kernel, plan),
            out_shape=(payload_shape(NEAR), payload_shape(NEAR)),
            in_specs=[ANY, VMEM],
            out_specs=(VMEM, VMEM),
            scratch_shapes=[pltpu.SemaphoreType.DMA((2, NEAR, 2))],
            compiler_params=limit(WORK_MIB),
            name="beside_images",
        )(slc, rim)
        down = [(i, (i - 1) % half) for i in range(half)]
        down += [(half + i, half + (i + 1) % half) for i in range(half)]
        strips = lax.ppermute(
            strips, both, [(2 * a + s, 2 * b + 1 - s) for a, b in swap for s in (0, 1)]
        )
        middle = lax.ppermute(outer, "date", [(half - 1, half), (half, half - 1)])
        outer = lax.ppermute(outer, "date", [(b, a) for a, b in down])
        inner = lax.ppermute(inner, "date", down)
    else:
        rim = swapped_rims(slc)
        annual = arrivals_by_distance(slc, pair_list, plan)
        strip = lax.axis_index("strip")
        ups = [(i, i + 1) for i in range(devices - 1)]
        inner = payload_of(slc[:, dates - NEAR :], rim[:, dates - NEAR :], strip)
        outer = payload_of(slc[:, :NEAR], rim[:, :NEAR], strip)
        inner = lax.ppermute(inner, "date", ups)
        outer = lax.ppermute(outer, "date", [(b, a) for a, b in ups])

    out_shape = jax.ShapeDtypeStruct((planes, dates * per_date, rows, cols), jnp.float32)
    depth = 2 * band_shape[1]
    scratch = [
        pltpu.VMEM((2, 4 * rows, depth), jnp.bfloat16),
        pltpu.VMEM((2, 4, 2 * rows, cols), jnp.bfloat16),
        pltpu.VMEM((2, planes, rows, cols), dtype),
        pltpu.VMEM((2, planes, rows, TILE), dtype),
        pltpu.VMEM((2, 2, planes, rows, cols), jnp.float32),
        pltpu.SMEM((dates * NEAR + 1,), jnp.int32),
        pltpu.SemaphoreType.DMA((2, 2)),
    ]

    out, powers = pl.pallas_call(
        functools.partial(own_kernel, plan),
        out_shape=(out_shape, jax.ShapeDtypeStruct((dates, rows, depth), jnp.bfloat16)),
        in_specs=[SMEM] + [VMEM] * 3,
        out_specs=(ANY, VMEM),
        scratch_shapes=scratch,
        compiler_params=limit(WORK_MIB),
        cost_estimate=cost(OWN_FLOPS),
        name="own_pairs",
    )(lists, slc, rim, bands)

    def more_pairs(kernel, out, others, name, flops=1):
        return pl.pallas_call(
            functools.partial(kernel, plan),
            out_shape=out_shape,
            in_specs=[SMEM] + [VMEM] * (4 + len(others)) + [ANY],
            out_specs=ANY,
            scratch_shapes=scratch,
            input_output_aliases={5 + len(others): 0},
            compiler_params=limit(WORK_MIB),
            cost_estimate=cost(flops),
            name=name,
        )(lists, slc, rim, bands, powers, *others, out)

    if halves:
        payload = sent = pl.pallas_call(
            functools.partial(late_kernel, plan),
            out_shape=payload_shape(late),
            in_specs=[VMEM, VMEM, VMEM, SMEM, ANY, ANY],
            out_specs=VMEM,
            scratch_shapes=[pltpu.VMEM((late, planes, rows, TILE), dtype)],
            compiler_params=limit(WORK_MIB),
            name="late_images",
        )(slc, rim, inner, lists, powers, strips)
        payload = lax.ppermute(payload, "date", swap)
    if halves:
        early_pairs = functools.partial(annual_kernel, is_late=False)
        out = more_pairs(early_pairs, out, (inner, early, strips, sent), "annual_pairs", ANNUAL_FLOPS)
        out = more_pairs(rest_kernel, out, (inner, outer, middle), "near_pairs")
        late_pairs = functools.partial(annual_kernel, is_late=True)
        out = more_pairs(late_pairs, out, (outer, payload, strips, sent), "last_pairs")
    else:
        out = more_pairs(rest_kernel, out, (inner, outer, inner), "near_pairs")
        out = more_pairs(plain_kernel, out, (annual, swapped_rims(annual)), "annual_pairs")
    return out


def solution(mesh):
    placed = (P(None, "date", "groups", "strip"), P(), P(), P())
    return jax.shard_map(
        body,
        mesh=mesh,
        in_specs=placed,
        out_specs=P(None, "date", "groups", "strip"),
        check_vma=False,
    )
```
